32 devices in a mesh: group: 2 (over y), ctx: 4 (over z), exp: 2 (over x), tp: 2 (over core).
Axes of the slice: x: 2, y: 2, z: 4, core: 2. Of those that a mesh axis runs over, the one named last changes fastest.
Arguments:
- queries: bfloat16 [256, 2, 2048], P(('group', 'ctx'), 'tp', 'exp'), parts along dimension 0, may hold values from -5 to 5
- cached_keys: bfloat16 [16384, 2, 128], P(('group', 'ctx'), 'tp'), parts along dimension 0, may hold values from -5 to 5
- cached_values: bfloat16 [16384, 2, 128], P(('group', 'ctx'), 'tp'), parts along dimension 0, may hold values from -5 to 5
- key_seg: int32 [16384], P(('group', 'ctx')), parts along dimension 0, may hold values from 0 to 63, as said below
- query_seg: int32 [256], P(('group', 'ctx')), parts along dimension 0, may hold values from 0 to 63, as said below
- parent: int32 [128], P('group'), parts along dimension 0, may hold values from 0 to 62, as said below
- out_weight: bfloat16 [2, 2048, 2048], P('tp', 'exp'), may hold values from -0.09375 to 0.09375
- residual: bfloat16 [256, 2048], P(('group', 'ctx'), ('exp', 'tp')), parts along dimension 0, may hold values from -15 to 15
- norm_gain: bfloat16 [2048], P(('exp', 'tp')), may hold values from 0.25 to 1.75
- gate_up_weight: bfloat16 [64, 2048, 1536], P('ctx', ('exp', 'tp')), may hold values from -0.125 to 0.125
- down_weight: bfloat16 [64, 768, 2048], P('ctx', None, ('exp', 'tp')), may hold values from -0.21875 to 0.21875
- expert_ids: int32 [256, 8], P(('group', 'ctx')), parts along dimension 0, may hold values from 0 to 63, all different within a row; in each aligned block of 32 rows (0 to 31, 32 to 63, ...) at most 8 rows name the same one
- route_weight: float32 [256, 8], P(('group', 'ctx')), parts along dimension 0, may hold values from 0.05 to 0.5
Outputs:
- layer_out: bfloat16 [256, 2048], P(('group', 'ctx'), ('exp', 'tp')), parts along dimension 0
The draws below stay inside these ranges and needn't reach their ends.
There are 2 independent parts, one for each index of `group`. The reference program is written for one: setup_inputs(seed, part) draws one part's arguments, and reference() takes and returns one part's arrays. A program takes and returns all parts, laid end to end along the dimension named above; an argument that names none is the same for every part. Nothing has to cross between parts.
Inputs may be any that keep to these rules, and one draw needn't show every extreme that they name: `key_seg`: never falls along the prompt; the first 16 positions are in segment 0; every one of the 64 segments has at least one position. `query_seg`: equals key_seg at the last 128 positions of the prompt, in order. parent[0] = 0 and parent[s] < s for s > 0; every segment reaches 0 within 6 applications of parent, and segment 64 - 1 needs exactly 6. `expert_ids`: each row names 8 different experts; among the 32 rows of one device no expert is named more than 8 times.
All inputs are finite; a program needn't handle non-finite values.
Results may differ from the reference program's by a relative error of at most 0.0085.
Values may be sent and summed in bfloat16 or wider, within the bound.
No kernel may reach another device: no remote copies, remote signals or barrier semaphores. Data moves between devices by JAX's collectives and lax.ppermute only.
A program may use at most 128 MiB of HBM per device.

```python
import math
import jax
import jax.numpy as jnp
import numpy as np
from jax import lax

KVH = 2
QPK = 16
HD = 128
D = 2048
FF_E = 768
E = 64
K = 8
MOST = 8
NSEG = 64
DEPTH = 6
Q_DEV = 32
NEW_TOK = 128
PROMPT = 8192
N_CTX = 4


def prompt_segments(key):
    forced_start = PROMPT - NEW_TOK // 2 - 16
    drawn = jax.random.permutation(key, PROMPT - 17)[:NSEG - 2].astype(jnp.int32)
    drawn = drawn + (drawn >= forced_start).astype(jnp.int32)
    starts_at = jnp.concatenate([drawn, jnp.full((1,), forced_start, jnp.int32)]) + 16
    starts = jnp.zeros((PROMPT,), jnp.int32).at[starts_at].set(1)
    return jnp.cumsum(starts).astype(jnp.int32)


def draw_key_seg(key, part):
    return prompt_segments(key)


def draw_query_seg(key, part):
    return prompt_segments(key)[PROMPT - NEW_TOK:]


def draw_parent(key, part):
    key = jax.random.fold_in(key, 11)
    anchor_key, pick_key = jax.random.split(key)
    anchors = jnp.sort(jax.random.permutation(anchor_key, NSEG - 2)[:DEPTH - 1] + 1).astype(jnp.int32)
    forced = jnp.full((NSEG,), -1, jnp.int32)
    forced = forced.at[anchors[0]].set(0)
    forced = forced.at[anchors[1:]].set(anchors[:-1])
    forced = forced.at[NSEG - 1].set(anchors[-1])
    picks = jax.random.randint(pick_key, (NSEG,), 0, 1 << 20)

    def place(index, state):
        parents, depths = state
        candidate = picks[index] % index
        candidate = jnp.where(depths[candidate] >= DEPTH, parents[candidate], candidate)
        chosen = jnp.where(forced[index] >= 0, forced[index], candidate)
        return (parents.at[index].set(chosen), depths.at[index].set(depths[chosen] + 1))
    start = (jnp.zeros((NSEG,), jnp.int32), jnp.zeros((NSEG,), jnp.int32))
    parents, depths = lax.fori_loop(1, NSEG, place, start)
    return parents


def draw_queries(key, part):
    key = jax.random.fold_in(key, 22)
    shape = (NEW_TOK, KVH, QPK * HD)
    base = jnp.clip(jax.random.normal(key, shape, jnp.float32), -4.5, 4.5)
    return base.astype(jnp.bfloat16)


def draw_cached_keys(key, part):
    key = jax.random.fold_in(key, 23)
    shape = (PROMPT, KVH, HD)
    base = jnp.clip(jax.random.normal(key, shape, jnp.float32), -4.5, 4.5)
    return base.astype(jnp.bfloat16)


def draw_residual(key, part):
    key = jax.random.fold_in(key, 31)
    row_key, value_key = jax.random.split(key)
    columns = jnp.arange(D, dtype=jnp.float32) / D
    row_scale = jnp.exp(jax.random.uniform(row_key, (NEW_TOK, 1), jnp.float32, math.log(0.2), math.log(2.0)))
    column_scale = jnp.exp(math.log(0.3) + math.log(6.0) * columns)
    base = jnp.clip(jax.random.normal(value_key, (NEW_TOK, D), jnp.float32), -4.0, 4.0)
    return (base * row_scale * column_scale[None, :]).astype(jnp.bfloat16)


def block_scale(key, extent, cuts, least, top_value):
    def one(axis_at, parts):
        draws = jax.random.uniform(jax.random.fold_in(jax.random.fold_in(key, 6), axis_at), (parts,), jnp.float32, least / len(cuts), top_value / len(cuts))
        return jnp.repeat(jnp.exp(draws), extent[axis_at] // parts).reshape((-1,) + (1,) * (len(extent) - axis_at - 1))

    factor_of = one(*cuts[0])
    for cut in cuts[1:]:
        factor_of = factor_of * one(*cut)
    return factor_of


def routed_block(key, own, number, rows, count, top, reach, slope):
    ranking = jax.random.permutation(key, count)
    crowded, ordinary = shares(count, rows * top, reach, slope, True), shares(count, rows * top, reach, slope, False)
    places = jnp.arange(count)

    def named(tallies, turn):
        used = int((tallies > 0).sum())
        fixed = max(1, used // 4)
        passed = fixed + (places - fixed + turn * (used - fixed)) % max(1, count - fixed)
        return jnp.zeros((count,), jnp.int32).at[ranking[jnp.where(places < fixed, places, passed)]].set(jnp.asarray(tallies, jnp.int32))

    tallies = jnp.where(number % 4 == 0, named(crowded, number // 4), named(ordinary, number - number // 4 - 1))
    mixed = jax.random.permutation(jax.random.fold_in(own, 3), count)
    source_of, sink = mixed[0:count // 2 * 2:2], mixed[1:count // 2 * 2:2]
    margin = jnp.minimum(tallies[source_of] - 1, reach - tallies[sink]) // 2
    margin = jnp.where((source_of == ranking[0]) | (sink == ranking[0]) | (tallies[sink] == 0), 0, jnp.maximum(margin, 0))
    passed = jax.random.randint(jax.random.fold_in(own, 4), (count // 2,), 0, 1 << 20) % (margin + 1)
    tallies = tallies.at[source_of].add(-passed).at[sink].add(passed)
    items = jnp.searchsorted(jnp.cumsum(tallies), jnp.arange(rows * top), side="right").astype(jnp.int32)
    listing = items.reshape(top, rows).T
    listing = listing[jax.random.permutation(jax.random.fold_in(own, 1), rows)]
    turn = jax.random.randint(jax.random.fold_in(own, 2), (rows, 1), 0, top)
    return jnp.take_along_axis(listing, (jnp.arange(top)[None, :] + turn) % top, axis=1)


def shares(amount, total, bound, slope, full):
    loads = [(1 << 20) // math.isqrt(grade ** slope) + 1 for grade in range(1, amount + 1)]
    largest = bound if full else min(bound, max(-(-total // amount), total * loads[0] // sum(loads)))
    least = 1 if total - largest >= amount - 1 else 0
    given, spare = [largest] + [least] * (amount - 1), total - largest - least * (amount - 1)
    while spare > 0:
        free = [i for i in range(1, amount) if given[i] < largest] or [i for i in range(1, amount) if given[i] < bound]
        whole, left = sum([loads[i] for i in free]), spare
        for i in free:
            extra = min(bound - given[i], max(1, left * loads[i] // whole), spare)
            given[i] = given[i] + extra
            spare = spare - extra
    return np.array(given)


def bell_draw(stream_key, shape, scale, reach, shards=(), held_as=jnp.bfloat16):
    gain = block_scale(stream_key, shape, shards, -0.22, 0.18) if shards else 1.0
    values = jax.random.normal(stream_key, shape, jnp.float32) * scale * gain
    return jnp.minimum(jnp.maximum(values, -reach), reach).astype(held_as)


def setup_inputs(seed: int = 0, part: int = 0) -> dict:
    seeds = jax.random.split(jax.random.key(seed), 14)
    part_splits = jax.random.split(jax.random.fold_in(seeds[13], part), 14)
    queries = draw_queries(jax.random.fold_in(jax.random.fold_in(seeds[13], part), 71), part)
    cached_keys = draw_cached_keys(jax.random.fold_in(jax.random.fold_in(seeds[13], part), 71), part)
    cached_values = bell_draw(part_splits[2], (PROMPT, KVH, HD), 1.0, 5.0, ((0, 4), (1, 2)))
    key_seg = draw_key_seg(jax.random.fold_in(jax.random.fold_in(seeds[13], part), 71), part)
    query_seg = draw_query_seg(jax.random.fold_in(jax.random.fold_in(seeds[13], part), 71), part)
    parent = draw_parent(jax.random.fold_in(jax.random.fold_in(seeds[13], part), 71), part)
    out_weight = bell_draw(seeds[6], (KVH, QPK * HD, D), (KVH * QPK * HD) ** -0.5, 0.09375, ((0, 2), (1, 2)))
    residual = draw_residual(jax.random.fold_in(jax.random.fold_in(seeds[13], part), 71), part)
    norm_gain = jnp.clip(1.0 + 0.15 * jax.random.normal(seeds[8], (D,), jnp.float32), 0.25, 1.75).astype(jnp.bfloat16)
    gate_up_weight = bell_draw(seeds[9], (E, D, 2 * FF_E), D ** -0.5, 0.125, ((0, 4), (1, 4)))
    down_weight = bell_draw(seeds[10], (E, FF_E, D), FF_E ** -0.5, 0.21875, ((0, 4), (2, 4)))
    expert_ids_keys = jax.random.split(jax.random.fold_in(part_splits[11], 1), NEW_TOK // Q_DEV)
    expert_ids_turns = jax.random.permutation(jax.random.fold_in(part_splits[11], 3), NEW_TOK // Q_DEV)
    expert_ids = jax.vmap(lambda own, number: routed_block(jax.random.fold_in(part_splits[11], 2), own, number, Q_DEV, E, K, MOST, 1))(expert_ids_keys, expert_ids_turns).reshape((NEW_TOK, K))
    route_weight = jnp.clip(jnp.exp(math.log(0.5) - 2.3025851 * jax.random.uniform(part_splits[12], (NEW_TOK, K), jnp.float32) ** block_scale(part_splits[12], (NEW_TOK, K), ((0, 4),), -0.2, 0.2)), 0.05, 0.5)
    return {"queries": queries, "cached_keys": cached_keys, "cached_values": cached_values, "key_seg": key_seg, "query_seg": query_seg, "parent": parent, "out_weight": out_weight, "residual": residual, "norm_gain": norm_gain, "gate_up_weight": gate_up_weight, "down_weight": down_weight, "expert_ids": expert_ids, "route_weight": route_weight}


epsilon = 1e-06
masked_score = -1e+30

def ancestor_table(segments, parent):
    labels = jnp.arange(NSEG, dtype=jnp.int32)
    current = segments
    seen = current[:, None] == labels[None, :]
    for level in range(DEPTH):
        current = parent[current]
        seen = seen | (current[:, None] == labels[None, :])
    return seen

def reference(queries, cached_keys, cached_values, key_seg, query_seg, parent, out_weight, residual, norm_gain, gate_up_weight, down_weight, expert_ids, route_weight):
    seen = ancestor_table(query_seg, parent)
    query_pos = PROMPT - NEW_TOK + jnp.arange(NEW_TOK, dtype=jnp.int32)
    key_pos = jnp.arange(PROMPT, dtype=jnp.int32)
    allowed = seen[:, key_seg] & (key_pos[None, :] <= query_pos[:, None])
    head_total = KVH * QPK
    inverse_root = 1.0 / math.sqrt(HD)
    per_head = queries.reshape(NEW_TOK, head_total, HD).transpose(1, 0, 2)
    owners = (jnp.arange(head_total, dtype=jnp.int32) // QPK).astype(jnp.int32)

    def attend(operands):
        query_rows, owner = operands
        key_rows = lax.dynamic_index_in_dim(cached_keys, owner, 1, keepdims=False)
        value_rows = lax.dynamic_index_in_dim(cached_values, owner, 1, keepdims=False)
        scores = jnp.dot(query_rows, key_rows.T, preferred_element_type=jnp.float32) * inverse_root
        scores = jnp.where(allowed, scores, masked_score)
        highest = lax.optimization_barrier(jnp.max(scores, axis=1, keepdims=True))
        probs = jnp.where(allowed, jnp.exp(scores - highest), 0.0)
        totals = lax.optimization_barrier(jnp.sum(probs, axis=1, keepdims=True))
        return jnp.dot(probs.astype(jnp.bfloat16), value_rows, preferred_element_type=jnp.float32) / totals
    attention = lax.map(attend, (per_head, owners))
    attention = attention.transpose(1, 0, 2).reshape(NEW_TOK, head_total * HD).astype(jnp.bfloat16)
    mixed_in = residual.astype(jnp.float32) + jnp.dot(attention, out_weight.reshape(head_total * HD, D), preferred_element_type=jnp.float32)
    mean_square = lax.optimization_barrier(jnp.mean(mixed_in * mixed_in, axis=1, keepdims=True))
    normed = (mixed_in * lax.rsqrt(mean_square + epsilon) * norm_gain.astype(jnp.float32)).astype(jnp.bfloat16)
    flat_ids = expert_ids.reshape(-1)
    flat_weight = route_weight.reshape(-1)
    token_of = (jnp.arange(NEW_TOK * K, dtype=jnp.int32) // K).astype(jnp.int32)
    capacity = N_CTX * MOST
    slot_labels = jnp.arange(capacity, dtype=jnp.int32)

    def add_expert(expert, moe_sum):
        chosen = flat_ids == expert
        picked = jnp.nonzero(chosen, size=capacity, fill_value=0)[0].astype(jnp.int32)
        live = slot_labels < jnp.sum(chosen.astype(jnp.int32))
        tokens = token_of[picked]
        gate_block = lax.dynamic_index_in_dim(gate_up_weight, expert, 0, keepdims=False)
        down_block = lax.dynamic_index_in_dim(down_weight, expert, 0, keepdims=False)
        gate_up = jnp.dot(normed[tokens], gate_block, preferred_element_type=jnp.float32)
        hidden = (jax.nn.silu(gate_up[:, :FF_E]) * gate_up[:, FF_E:]).astype(jnp.bfloat16)
        expert_out = jnp.dot(hidden, down_block, preferred_element_type=jnp.float32).astype(jnp.bfloat16)
        weights = jnp.where(live, flat_weight[picked], 0.0)
        return moe_sum.at[tokens].add(expert_out.astype(jnp.float32) * weights[:, None])
    moe_sum = lax.fori_loop(0, E, add_expert, jnp.zeros((NEW_TOK, D), jnp.float32))
    return (mixed_in + moe_sum).astype(jnp.bfloat16)
```

```python
import functools
import math

import jax
import jax.numpy as jnp
from jax import lax
from jax.experimental import pallas as pl
from jax.experimental.pallas import tpu as pltpu
from jax.sharding import PartitionSpec as P

MOST = 8
DEPTH = 6
LANES = 128

epsilon = 1e-06
masked_score = -1e30
least_high = -1e20

f32 = jnp.float32
bf16 = jnp.bfloat16


def params(megabytes, steps=0):
    semantics = ("arbitrary",) * steps if steps else None
    return pltpu.CompilerParams(
        vmem_limit_bytes=megabytes * 1024 * 1024, dimension_semantics=semantics
    )


def lane_ids(shape):
    return lax.broadcasted_iota(jnp.int32, shape, len(shape) - 1)


def row_ids(shape):
    return lax.broadcasted_iota(jnp.int32, shape, len(shape) - 2)


def dot(left, right, dims=((1,), (0,))):
    return lax.dot_general(left, right, (dims, ((), ())), preferred_element_type=f32)


def in_two(value):
    high = value.astype(bf16).astype(f32)
    return high, value - high


def exchange(pieces, axes):
    return lax.all_to_all(pieces, axes, split_axis=0, concat_axis=0, tiled=True)


def collect(value, axis):
    count = lax.axis_size(axis)
    return exchange(jnp.broadcast_to(value[None], (count,) + value.shape), axis)


def shifted(value, axis, steps):
    count = lax.axis_size(axis)
    pairs = [(source, (source + steps) % count) for source in range(count)]
    return lax.ppermute(value, axis, pairs)


def sight_kernel(parent_ref, key_seg_ref, sight_ref):
    seg_count, key_count = sight_ref.shape
    square = (seg_count, seg_count)
    same = row_ids(square) == lane_ids(square)
    step = (parent_ref[...] == row_ids(square)) | same
    one = step.astype(f32).astype(bf16)
    two = (dot(one, one) > 0.5).astype(f32).astype(bf16)
    four = (dot(two, two) > 0.5).astype(f32).astype(bf16)
    six = (dot(four, two) > 0.5).astype(f32).astype(bf16)
    keys = (key_seg_ref[...] == row_ids((seg_count, key_count))).astype(f32).astype(bf16)
    sight_ref[...] = dot(six, keys, ((0,), (0,))).astype(bf16)


def sight_of(parent, key_seg):
    assert DEPTH == 6
    return pl.pallas_call(
        sight_kernel,
        out_shape=jax.ShapeDtypeStruct((parent.shape[0], key_seg.shape[0]), bf16),
        compiler_params=params(16),
        name="sight",
    )(parent[None, :], key_seg[None, :])


def attend_kernel(heads, scale, lead_ref, queries_ref, keys_ref, values_ref, sight_ref, out_ref):
    rows = queries_ref.shape[0]
    key_count, head_size = keys_ref.shape
    seg_count = sight_ref.shape[0]
    width = heads * head_size
    info = queries_ref[:, width : width + LANES].astype(f32)
    own_seg = info[:, :1].astype(jnp.int32)
    onehot = (own_seg == lane_ids((rows, seg_count))).astype(f32).astype(bf16)
    seen = dot(onehot, sight_ref[...]) > 0.5
    place = (rows, key_count)
    lead = lead_ref[0] + pl.program_id(0) * rows
    causal = lane_ids(place) - row_ids(place) <= lead
    bias = jnp.where(seen & causal, 0.0, masked_score)
    stats = jnp.zeros((rows, LANES), f32)
    lane = lane_ids((rows, LANES))
    for head in range(heads):
        columns = slice(head * head_size, (head + 1) * head_size)
        scores = dot(queries_ref[:, columns], keys_ref[...], ((1,), (1,))) + bias
        high = jnp.maximum(jnp.max(scores, axis=1, keepdims=True), least_high)
        high = high.astype(bf16).astype(f32)
        probs = jnp.exp2((scores - high) * scale)
        total_high, total_low = in_two(jnp.sum(probs, axis=1, keepdims=True))
        out_ref[:, columns] = dot(probs.astype(bf16), values_ref[...]).astype(bf16)
        stats = jnp.where(lane == head, high, stats)
        stats = jnp.where(lane == heads + head, total_high, stats)
        stats = jnp.where(lane == 2 * heads + head, total_low, stats)
    out_ref[:, width : width + LANES] = stats.astype(bf16)


def attend(lead, queries, keys, values, sight, heads, scale):
    token_count, columns = queries.shape
    block = min(token_count, 128)
    key_count, head_size = keys.shape
    work = token_count * heads * key_count
    return pl.pallas_call(
        functools.partial(attend_kernel, heads, scale),
        grid=(token_count // block,),
        in_specs=[
            pl.BlockSpec(memory_space=pltpu.SMEM),
            pl.BlockSpec((block, columns), lambda index: (index, 0)),
            pl.BlockSpec(keys.shape, lambda index: (0, 0)),
            pl.BlockSpec(values.shape, lambda index: (0, 0)),
            pl.BlockSpec(sight.shape, lambda index: (0, 0)),
        ],
        out_specs=pl.BlockSpec((block, columns), lambda index: (index, 0)),
        out_shape=jax.ShapeDtypeStruct((token_count, columns), bf16),
        compiler_params=params(40, 1),
        cost_estimate=pl.CostEstimate(
            flops=4 * work * head_size, bytes_accessed=2**21, transcendentals=work
        ),
        name="attend",
    )(lead, queries, keys, values, sight)


def project_kernel(heads, scale, parts_ref, weight_ref, out_ref, attention_ref):
    source_count = parts_ref.shape[0]
    width = attention_ref.shape[1]
    head_size = width // heads

    @pl.when(pl.program_id(0) == 0)
    def merge():
        stats = [parts_ref[i, :, width : width + LANES].astype(f32) for i in range(source_count)]
        top = functools.reduce(jnp.maximum, stats)
        factors = [jnp.exp2(jnp.minimum((stat - top) * scale, 0.0)) for stat in stats]
        total = 0.0
        for stat, factor in zip(stats, factors):
            high = pltpu.roll(stat, LANES - heads, 1)
            low = pltpu.roll(stat, LANES - 2 * heads, 1)
            total = total + factor * (high + low)
        shares = [factor / total for factor in factors]
        for head in range(heads):
            columns = slice(head * head_size, (head + 1) * head_size)
            merged = 0.0
            for i in range(source_count):
                part = parts_ref[i, :, columns].astype(f32)
                merged = merged + part * shares[i][:, head : head + 1]
            attention_ref[:, columns] = merged.astype(bf16)

    out_ref[0] = dot(attention_ref[...], weight_ref[...]).astype(bf16)


def project(parts, weight, heads, scale, piece_count):
    source_count, rows, columns = parts.shape
    width, model_width = weight.shape
    piece_width = model_width // piece_count
    return pl.pallas_call(
        functools.partial(project_kernel, heads, scale),
        grid=(piece_count,),
        in_specs=[
            pl.BlockSpec(parts.shape, lambda index: (0, 0, 0)),
            pl.BlockSpec((width, piece_width), lambda index: (0, index)),
        ],
        out_specs=pl.BlockSpec((1, rows, piece_width), lambda index: (index, 0, 0)),
        out_shape=jax.ShapeDtypeStruct((piece_count, rows, piece_width), bf16),
        scratch_shapes=[pltpu.VMEM((rows, width), bf16)],
        compiler_params=params(32, 1),
        cost_estimate=pl.CostEstimate(
            flops=2 * rows * width * model_width,
            bytes_accessed=2 * width * model_width,
            transcendentals=0,
        ),
        name="project",
    )(parts, weight)


def mix_kernel(parts_ref, residual_ref, gain_ref, mixed_ref, sent_ref):
    rows, width = mixed_ref.shape
    mixed = residual_ref[...].astype(f32)
    for i in range(parts_ref.shape[0]):
        mixed = mixed + parts_ref[i].astype(f32)
    mixed_ref[...] = mixed
    sent_ref[:, :width] = (mixed * gain_ref[...].astype(f32)).astype(bf16)
    high, low = in_two(jnp.sum(mixed * mixed, axis=1, keepdims=True))
    lane = lane_ids((rows, LANES))
    squares = jnp.where(lane == 0, high, jnp.where(lane == 1, low, 0.0))
    sent_ref[:, width:] = squares.astype(bf16)


def mix(parts, residual, gain):
    rows, width = residual.shape
    return pl.pallas_call(
        mix_kernel,
        out_shape=(
            jax.ShapeDtypeStruct((rows, width), f32),
            jax.ShapeDtypeStruct((rows, width + LANES), bf16),
        ),
        compiler_params=params(16),
        name="mix",
    )(parts, residual, gain[None, :])


def route_kernel(local_experts, choices, first_ref, info_ref, place_ref, high_ref, low_ref):
    piece_count, tokens, slots = place_ref.shape
    info = info_ref[...].astype(f32)
    expert = (lane_ids((tokens, local_experts)) + first_ref[0]).astype(f32)
    member = jnp.zeros((tokens, local_experts), f32)
    weight_high = jnp.zeros((tokens, local_experts), f32)
    weight_low = jnp.zeros((tokens, local_experts), f32)
    for k in range(choices):
        chosen = info[:, 1 + k : 2 + k] == expert
        high = info[:, 1 + choices + k : 2 + choices + k]
        low = info[:, 1 + 2 * choices + k : 2 + 2 * choices + k]
        member = jnp.where(chosen, 1.0, member)
        weight_high = jnp.where(chosen, high, weight_high)
        weight_low = jnp.where(chosen, low, weight_low)
    square = (tokens, tokens)
    earlier = (lane_ids(square) < row_ids(square)).astype(f32).astype(bf16)
    member = member.astype(bf16)
    rank = jnp.where(member > 0.5, dot(earlier, member), -1.0).astype(bf16)
    weight_high = weight_high.astype(bf16)
    weight_low = weight_low.astype(bf16)
    capacity = piece_count * slots // local_experts
    for piece in range(piece_count):
        slot = lane_ids((local_experts, slots)) + piece * slots
        spread = (slot // capacity == row_ids((local_experts, slots))).astype(f32).astype(bf16)
        wanted = (lane_ids((tokens, slots)) + piece * slots) % capacity
        placed = dot(rank, spread) == wanted.astype(f32)
        place_ref[piece] = jnp.where(placed, 1.0, 0.0).astype(bf16)
        high_ref[piece] = jnp.where(placed, dot(weight_high, spread), 0.0).astype(bf16)
        low_ref[piece] = jnp.where(placed, dot(weight_low, spread), 0.0).astype(bf16)


def route(first, info, local_experts, choices, piece_count, slots):
    shape = jax.ShapeDtypeStruct((piece_count, info.shape[0], slots), bf16)
    return pl.pallas_call(
        functools.partial(route_kernel, local_experts, choices),
        in_specs=[
            pl.BlockSpec(memory_space=pltpu.SMEM),
            pl.BlockSpec(memory_space=pltpu.VMEM),
        ],
        out_shape=(shape, shape, shape),
        compiler_params=params(32),
        name="route",
    )(first, info)


def gate_up_kernel(per_step, with_sum, piece_ref, rows_ref, place_ref, weight_ref, *rest):
    added_ref = rest[0] if with_sum else None
    out_ref, picked_ref = rest[-2:]
    width = weight_ref.shape[1]
    ff_pair = weight_ref.shape[2]
    step = pl.program_id(0)

    @pl.when(step == 0)
    def pick():
        picked_ref[...] = dot(place_ref[0], rows_ref[...], ((0,), (0,))).astype(bf16)

    count = weight_ref.shape[0]
    rows = per_step // count
    for i in range(count):
        start = pl.multiple_of(step * per_step + i * rows, rows)
        picked = picked_ref[pl.ds(start, rows), :]
        product = dot(picked[:, :width], weight_ref[i])
        squares = picked[:, width:].astype(f32)
        here = slice(i * rows, (i + 1) * rows)
        if with_sum:
            product = product + added_ref[here, :ff_pair].astype(f32)
            squares = squares + added_ref[here, ff_pair:].astype(f32)
            high, low = in_two(squares[:, :1] + squares[:, 1:2])
            lane = lane_ids((rows, LANES))
            squares = jnp.where(lane == 0, high, jnp.where(lane == 1, low, 0.0))
        out_ref[here, :ff_pair] = product.astype(bf16)
        out_ref[here, ff_pair:] = squares.astype(bf16)


def gate_up(piece, rows, place, weight, added=None):
    piece_count, tokens, slots = place.shape
    local_experts, width, ff_pair = weight.shape
    capacity = piece_count * slots // local_experts
    experts = max(1, slots // capacity)
    count = 2 if experts % 2 == 0 else 1
    steps = experts // count
    per_step = slots // steps
    columns = ff_pair + LANES

    def weight_block(step, piece_ref):
        return ((piece_ref[0] * slots // capacity) // count + step, 0, 0)

    in_specs = [
        pl.BlockSpec(rows.shape, lambda step, piece_ref: (0, 0)),
        pl.BlockSpec((1, tokens, slots), lambda step, piece_ref: (piece_ref[0], 0, 0)),
        pl.BlockSpec((count, width, ff_pair), weight_block),
    ]
    operands = [rows, place, weight]
    if added is not None:
        in_specs.append(pl.BlockSpec((per_step, columns), lambda step, piece_ref: (step, 0)))
        operands.append(added)
    return pl.pallas_call(
        functools.partial(gate_up_kernel, per_step, added is not None),
        grid_spec=pltpu.PrefetchScalarGridSpec(
            num_scalar_prefetch=1,
            grid=(steps,),
            in_specs=in_specs,
            out_specs=pl.BlockSpec((per_step, columns), lambda step, piece_ref: (step, 0)),
            scratch_shapes=[pltpu.VMEM((slots, rows.shape[1]), bf16)],
        ),
        out_shape=jax.ShapeDtypeStruct((slots, columns), bf16),
        compiler_params=params(32, 1),
        cost_estimate=pl.CostEstimate(
            flops=2 * slots * width * ff_pair,
            bytes_accessed=2 * experts * width * ff_pair,
            transcendentals=0,
        ),
        name="gate_up_sum" if added is not None else "gate_up",
    )(piece, *operands)


def hidden_kernel(part_count, model_width, *refs):
    out_ref = refs[-1]
    ff_width = out_ref.shape[1]
    total = refs[0][...].astype(f32)
    for ref in refs[1:part_count]:
        total = total + ref[...].astype(f32)
    squares = total[:, 2 * ff_width : 2 * ff_width + 1] + total[:, 2 * ff_width + 1 : 2 * ff_width + 2]
    norm = lax.rsqrt(squares / model_width + epsilon)
    gate = total[:, :ff_width] * norm
    up = total[:, ff_width : 2 * ff_width] * norm
    out_ref[...] = (gate / (1.0 + jnp.exp(-gate)) * up).astype(bf16)


def hidden_of(parts, ff_width, model_width):
    return pl.pallas_call(
        functools.partial(hidden_kernel, len(parts), model_width),
        out_shape=jax.ShapeDtypeStruct((parts[0].shape[0], ff_width), bf16),
        compiler_params=params(16),
        name="hidden",
    )(*parts)


def down_kernel(piece_ref, hidden_ref, weight_ref, high_ref, low_ref, out_ref, total_ref, held_ref):
    piece, step = pl.program_id(0), pl.program_id(1)
    rows = hidden_ref.shape[1]
    count = weight_ref.shape[0]
    each = rows // count
    for i in range(count):
        here = slice(i * each, (i + 1) * each)
        product = dot(hidden_ref[0, here, :], weight_ref[i]).astype(bf16)
        start = pl.multiple_of(step * rows + i * each, each)
        held_ref[pl.ds(start, each), :] = product

    @pl.when(step == pl.num_programs(1) - 1)
    def combine():
        held = held_ref[...]
        part = dot(high_ref[0], held) + dot(low_ref[0], held)

        @pl.when(piece == 0)
        def first():
            total_ref[...] = part

        @pl.when(piece > 0)
        def later():
            total_ref[...] += part

        @pl.when(piece == pl.num_programs(0) - 1)
        def last():
            out_ref[...] = total_ref[...].astype(bf16)


def down(pieces, hidden, weight, high, low):
    held_count, slots, ff_width = hidden.shape
    piece_count, tokens, _ = high.shape
    local_experts, _, piece_width = weight.shape
    capacity = piece_count * slots // local_experts
    experts = max(1, slots // capacity)
    count = 2 if experts % 2 == 0 else 1
    steps = experts // count
    per_step = slots // steps

    def weight_block(piece, step, piece_ref):
        return ((piece_ref[piece] * slots // capacity) // count + step, 0, 0)

    def route_block(piece, step, piece_ref):
        return (piece_ref[piece], 0, 0)

    return pl.pallas_call(
        down_kernel,
        grid_spec=pltpu.PrefetchScalarGridSpec(
            num_scalar_prefetch=1,
            grid=(held_count, steps),
            in_specs=[
                pl.BlockSpec((1, per_step, ff_width), lambda piece, step, piece_ref: (piece, step, 0)),
                pl.BlockSpec((count, ff_width, piece_width), weight_block),
                pl.BlockSpec((1, tokens, slots), route_block),
                pl.BlockSpec((1, tokens, slots), route_block),
            ],
            out_specs=pl.BlockSpec((tokens, piece_width), lambda piece, step, piece_ref: (0, 0)),
            scratch_shapes=[
                pltpu.VMEM((tokens, piece_width), f32),
                pltpu.VMEM((slots, piece_width), bf16),
            ],
        ),
        out_shape=jax.ShapeDtypeStruct((tokens, piece_width), bf16),
        compiler_params=params(32, 2),
        cost_estimate=pl.CostEstimate(
            flops=2 * held_count * slots * ff_width * piece_width,
            bytes_accessed=2 * held_count * experts * ff_width * piece_width,
            transcendentals=0,
        ),
        name="down",
    )(pieces, hidden, weight, high, low)


def body(
    queries,
    cached_keys,
    cached_values,
    key_seg,
    query_seg,
    parent,
    out_weight,
    residual,
    norm_gain,
    gate_up_weight,
    down_weight,
    expert_ids,
    route_weight,
):
    ctx_count, exp_count, tp_count = (lax.axis_size(axis) for axis in ("ctx", "exp", "tp"))
    own_ctx, own_exp, own_tp = (lax.axis_index(axis) for axis in ("ctx", "exp", "tp"))
    assert tp_count == 2 and cached_keys.shape[1] == 1
    piece_count = exp_count * tp_count
    query_rows = queries.shape[0]
    key_count, _, head_size = cached_keys.shape
    heads = queries.shape[2] // head_size
    width = heads * head_size
    model_width = out_weight.shape[2]
    local_experts, piece_width, _ = gate_up_weight.shape
    ff_width = down_weight.shape[1]
    choices = expert_ids.shape[1]
    token_count = ctx_count * query_rows
    slots = local_experts * ctx_count * MOST // piece_count
    scale = math.log2(math.e) / math.sqrt(head_size)

    route_high = route_weight.astype(bf16)
    route_low = (route_weight - lax.reduce_precision(route_weight, 8, 7)).astype(bf16)
    info = jnp.concatenate(
        [query_seg[:, None].astype(bf16), expert_ids.astype(bf16), route_high, route_low], axis=1
    )
    info = jnp.pad(info, ((0, 0), (0, LANES - info.shape[1])))
    packed = jnp.concatenate([queries.reshape(query_rows, width), info], axis=1)
    gathered = collect(packed, "ctx").reshape(token_count, width + LANES)

    sight = sight_of(parent, key_seg)
    lead = ctx_count * (key_count - query_rows) - own_ctx * key_count
    attended = attend(
        lead.astype(jnp.int32)[None],
        gathered,
        cached_keys.reshape(key_count, head_size),
        cached_values.reshape(key_count, head_size),
        sight,
        heads,
        scale,
    )
    parts = exchange(attended.reshape(ctx_count, query_rows, width + LANES), "ctx")
    place, combine_high, combine_low = route(
        (own_ctx * local_experts).astype(jnp.int32)[None],
        gathered[:, width:],
        local_experts,
        choices,
        piece_count,
        slots,
    )
    projected = project(
        parts, out_weight.reshape(width, model_width), heads, scale, piece_count
    )
    mixed, sent = mix(exchange(projected, ("exp", "tp")), residual, norm_gain)
    rows = collect(sent, "ctx").reshape(token_count, piece_width + LANES)

    def piece_at(tp_index, exp_index):
        return (tp_index * exp_count + exp_index).astype(jnp.int32)[None]

    steps = list(range(1, exp_count)) + [0]
    targets = [(own_exp + step) % exp_count for step in steps]
    away = [gate_up(piece_at(1 - own_tp, at), rows, place, gate_up_weight) for at in targets]
    arrived = [shifted(value, "tp", 1) for value in away]
    summed = [
        gate_up(piece_at(own_tp, at), rows, place, gate_up_weight, value)
        for at, value in zip(targets, arrived)
    ]
    finals = [shifted(value, "exp", step) for value, step in zip(summed[:-1], steps[:-1])]
    own_hidden = hidden_of([summed[-1]] + finals, ff_width, model_width)

    here = [own_hidden] + [shifted(own_hidden, "exp", step) for step in range(1, exp_count)]
    sources = [(own_exp - step) % exp_count for step in range(exp_count)]
    here = jnp.stack(here)
    there = shifted(here, "tp", 1)
    pieces = jnp.concatenate(
        [piece_at(own_tp, at) for at in sources] + [piece_at(1 - own_tp, at) for at in sources]
    )
    moe_part = down(
        pieces, jnp.concatenate([here, there]), down_weight, combine_high, combine_low
    )
    returned = exchange(moe_part.reshape(ctx_count, query_rows, piece_width), "ctx")
    return (mixed + jnp.sum(returned.astype(f32), axis=0)).astype(bf16)


def solution(mesh):
    in_specs = (
        P(("group", "ctx"), "tp", "exp"),
        P(("group", "ctx"), "tp", None),
        P(("group", "ctx"), "tp", None),
        P(("group", "ctx")),
        P(("group", "ctx")),
        P("group"),
        P("tp", "exp", None),
        P(("group", "ctx"), ("exp", "tp")),
        P(("exp", "tp")),
        P("ctx", ("exp", "tp"), None),
        P("ctx", None, ("exp", "tp")),
        P(("group", "ctx"), None),
        P(("group", "ctx"), None),
    )
    out_specs = P(("group", "ctx"), ("exp", "tp"))
    return jax.shard_map(body, mesh=mesh, in_specs=in_specs, out_specs=out_specs, check_vma=False)
```

```python
import functools
import math

import jax
import jax.numpy as jnp
from jax import lax
from jax.experimental import pallas as pl
from jax.experimental.pallas import tpu as pltpu
from jax.sharding import PartitionSpec as P

MOST = 8
DEPTH = 6
LANES = 128

epsilon = 1e-06
masked_score = -1e30
least_high = -1e20

f32 = jnp.float32
bf16 = jnp.bfloat16


def params(megabytes, steps=0):
    semantics = ("arbitrary",) * steps if steps else None
    return pltpu.CompilerParams(
        vmem_limit_bytes=megabytes * 1024 * 1024, dimension_semantics=semantics
    )


def cost(flops, bytes_accessed, transcendentals=0):
    return pl.CostEstimate(
        flops=flops, bytes_accessed=bytes_accessed, transcendentals=transcendentals
    )


def whole(memory_space=pltpu.VMEM):
    return pl.BlockSpec(memory_space=memory_space)


def lane_ids(shape):
    return lax.broadcasted_iota(jnp.int32, shape, len(shape) - 1)


def row_ids(shape):
    return lax.broadcasted_iota(jnp.int32, shape, len(shape) - 2)


def as_bf16(mask):
    return mask.astype(f32).astype(bf16)


def dot(left, right, dims=((1,), (0,))):
    return lax.dot_general(left, right, (dims, ((), ())), preferred_element_type=f32)


def in_two(value):
    high = value.astype(bf16).astype(f32)
    return high, value - high


def swapped(value, axes, mask):
    count = lax.axis_size(axes)
    pairs = [(source, source ^ mask) for source in range(count)]
    return lax.ppermute(value, axes, pairs)


def far_first(count):
    return list(range(count - 1, 0, -1))


def pack_kernel(width, queries_ref, seg_ref, ids_ref, weight_ref, out_ref):
    rows = out_ref.shape[0]
    choices = ids_ref.shape[0]
    out_ref[:, :width] = queries_ref[...]
    shape = (choices, LANES)

    def placed(value, first, last):
        to_lane = (lane_ids(shape) == row_ids(shape) + first) & (row_ids(shape) <= last)
        return dot(value.astype(bf16), as_bf16(to_lane), ((0,), (0,)))

    segs = jnp.broadcast_to(seg_ref[...], (choices, rows)).astype(f32)
    high, low = in_two(weight_ref[...])
    info = placed(segs, 0, 0) + placed(ids_ref[...].astype(f32), 1, choices)
    info = info + placed(high, 1 + choices, choices) + placed(low, 1 + 2 * choices, choices)
    out_ref[:, width:] = info.astype(bf16)


def pack(queries, query_seg, expert_ids, route_weight):
    rows, width = queries.shape
    return pl.pallas_call(
        functools.partial(pack_kernel, width),
        out_shape=jax.ShapeDtypeStruct((rows, width + LANES), bf16),
        compiler_params=params(4),
        name="pack",
    )(queries, query_seg[None, :], expert_ids.T, route_weight.T)


def sight_kernel(parent_ref, key_seg_ref, sight_ref):
    seg_count, key_count = sight_ref.shape
    square = (seg_count, seg_count)
    same = row_ids(square) == lane_ids(square)
    one = as_bf16((parent_ref[...] == row_ids(square)) | same)
    two = as_bf16(dot(one, one) > 0.5)
    four = as_bf16(dot(two, two) > 0.5)
    six = as_bf16(dot(four, two) > 0.5)
    keys = as_bf16(key_seg_ref[...] == row_ids((seg_count, key_count)))
    sight_ref[...] = dot(six, keys, ((0,), (0,))).astype(bf16)


def sight_of(parent, key_seg):
    assert DEPTH == 6
    return pl.pallas_call(
        sight_kernel,
        out_shape=jax.ShapeDtypeStruct((parent.shape[0], key_seg.shape[0]), bf16),
        compiler_params=params(4),
        cost_estimate=cost(2**24, 2**19),
        name="sight",
    )(parent[None, :], key_seg[None, :])


def attend_kernel(
    heads, scale, lead_at, plan_ref, queries_ref, keys_ref, values_ref, sight_ref, out_ref,
    stacked_ref, probs_ref,
):
    rows = queries_ref.shape[0]
    key_count, head_size = keys_ref.shape
    seg_count = sight_ref.shape[0]
    width = heads * head_size
    info = queries_ref[:, width:].astype(f32)
    own_seg = info[:, :1].astype(jnp.int32)
    onehot = as_bf16(own_seg == lane_ids((rows, seg_count)))
    seen = dot(onehot, sight_ref[...]) > 0.5
    place = (rows, key_count)
    causal = lane_ids(place) - row_ids(place) <= plan_ref[lead_at]
    bias = jnp.where(seen & causal, 0.0, masked_score)
    for head in range(heads):
        columns = slice(head * head_size, (head + 1) * head_size)
        stacked_ref[head * rows : (head + 1) * rows, :] = queries_ref[:, columns]
    scores = dot(stacked_ref[...], keys_ref[...], ((1,), (1,)))
    stats = jnp.zeros((rows, LANES), f32)
    lane = lane_ids((rows, LANES))
    for head in range(heads):
        here = slice(head * rows, (head + 1) * rows)
        biased = scores[here, :] + bias
        high = jnp.maximum(jnp.max(biased, axis=1, keepdims=True), least_high)
        high = high.astype(bf16).astype(f32)
        probs = jnp.exp2((biased - high) * scale)
        total_high, total_low = in_two(jnp.sum(probs, axis=1, keepdims=True))
        probs_ref[here, :] = probs.astype(bf16)
        stats = jnp.where(lane == head, high, stats)
        stats = jnp.where(lane == heads + head, total_high, stats)
        stats = jnp.where(lane == 2 * heads + head, total_low, stats)
    out_ref[:, width:] = stats.astype(bf16)
    sums = dot(probs_ref[...], values_ref[...])
    for head in range(heads):
        columns = slice(head * head_size, (head + 1) * head_size)
        out_ref[:, columns] = sums[head * rows : (head + 1) * rows, :].astype(bf16)


def attend(plan, lead_at, queries, keys, values, sight, heads, scale):
    rows, columns = queries.shape
    key_count, head_size = keys.shape
    work = rows * heads * key_count
    return pl.pallas_call(
        functools.partial(attend_kernel, heads, scale, lead_at),
        in_specs=[whole(pltpu.SMEM)] + [whole()] * 4,
        out_shape=jax.ShapeDtypeStruct((rows, columns), bf16),
        scratch_shapes=[
            pltpu.VMEM((rows * heads, head_size), bf16),
            pltpu.VMEM((rows * heads, key_count), bf16),
        ],
        compiler_params=params(12),
        cost_estimate=cost(8 * work * head_size, 2**20, work),
        name="attend",
    )(plan, queries, keys, values, sight)


def project_kernel(heads, scale, order_at, source_count, plan_ref, *refs):
    parts_refs, weight_ref = refs[:source_count], refs[source_count]
    out_refs, attention_ref = refs[source_count + 1 : -1], refs[-1]
    width = attention_ref.shape[1]
    head_size = width // heads
    stats = [ref[:, width:].astype(f32) for ref in parts_refs]
    top = functools.reduce(jnp.maximum, stats)
    factors = [jnp.exp2(jnp.minimum((stat - top) * scale, 0.0)) for stat in stats]
    total = 0.0
    for stat, factor in zip(stats, factors):
        high = pltpu.roll(stat, LANES - heads, 1)
        low = pltpu.roll(stat, LANES - 2 * heads, 1)
        total = total + factor * (high + low)
    shares = [factor / total for factor in factors]
    for head in range(heads):
        columns = slice(head * head_size, (head + 1) * head_size)
        merged = 0.0
        for ref, share in zip(parts_refs, shares):
            merged = merged + ref[:, columns].astype(f32) * share[:, head : head + 1]
        attention_ref[:, columns] = merged.astype(bf16)
    for i, out_ref in enumerate(out_refs):
        piece_width = out_ref.shape[1]
        start = pl.multiple_of(plan_ref[order_at + i] * piece_width, piece_width)
        out_ref[...] = dot(attention_ref[...], weight_ref[:, pl.ds(start, piece_width)]).astype(bf16)


def project(plan, order_at, parts, weight, heads, scale, piece_count):
    rows = parts[0].shape[0]
    width, model_width = weight.shape
    piece_width = model_width // piece_count
    return pl.pallas_call(
        functools.partial(project_kernel, heads, scale, order_at, len(parts)),
        in_specs=[whole(pltpu.SMEM)] + [whole()] * (len(parts) + 1),
        out_shape=[jax.ShapeDtypeStruct((rows, piece_width), bf16)] * piece_count,
        scratch_shapes=[pltpu.VMEM((rows, width), bf16)],
        compiler_params=params(8),
        cost_estimate=cost(2 * rows * width * model_width, 2 * width * model_width),
        name="project",
    )(plan, *parts, weight)


def mix_kernel(residual_ref, gain_ref, *refs):
    parts_refs, (mixed_ref, sent_ref) = refs[:-2], refs[-2:]
    rows, width = mixed_ref.shape
    mixed = residual_ref[...].astype(f32)
    for ref in parts_refs:
        mixed = mixed + ref[...].astype(f32)
    mixed_ref[...] = mixed
    sent_ref[:, :width] = (mixed * gain_ref[...].astype(f32)).astype(bf16)
    high, low = in_two(jnp.sum(mixed * mixed, axis=1, keepdims=True))
    lane = lane_ids((rows, LANES))
    squares = jnp.where(lane == 0, high, jnp.where(lane == 1, low, 0.0))
    sent_ref[:, width:] = squares.astype(bf16)


def mix(residual, gain, parts):
    rows, width = residual.shape
    return pl.pallas_call(
        mix_kernel,
        out_shape=(
            jax.ShapeDtypeStruct((rows, width), f32),
            jax.ShapeDtypeStruct((rows, width + LANES), bf16),
        ),
        compiler_params=params(4),
        name="mix",
    )(residual, gain[None, :], *parts)


def route_kernel(local_experts, choices, width, first_at, plan_ref, *refs):
    info_refs, (place_ref, high_ref, low_ref) = refs[:-3], refs[-3:]
    piece_count, tokens, slots = place_ref.shape
    info = jnp.concatenate([ref[:, width:] for ref in info_refs], axis=0).astype(f32)
    expert = (lane_ids((tokens, local_experts)) + plan_ref[first_at]).astype(f32)
    member = jnp.zeros((tokens, local_experts), f32)
    weight_high = jnp.zeros((tokens, local_experts), f32)
    weight_low = jnp.zeros((tokens, local_experts), f32)
    for k in range(choices):
        chosen = info[:, 1 + k : 2 + k] == expert
        high = info[:, 1 + choices + k : 2 + choices + k]
        low = info[:, 1 + 2 * choices + k : 2 + 2 * choices + k]
        member = jnp.where(chosen, 1.0, member)
        weight_high = jnp.where(chosen, high, weight_high)
        weight_low = jnp.where(chosen, low, weight_low)
    square = (tokens, tokens)
    earlier = as_bf16(lane_ids(square) < row_ids(square))
    rank = jnp.where(member > 0.5, dot(earlier, member.astype(bf16)), -1.0).astype(bf16)
    weight_high = weight_high.astype(bf16)
    weight_low = weight_low.astype(bf16)
    capacity = piece_count * slots // local_experts
    for piece in range(piece_count):
        slot = lane_ids((local_experts, slots)) + piece * slots
        spread = as_bf16(slot // capacity == row_ids((local_experts, slots)))
        wanted = (lane_ids((tokens, slots)) + piece * slots) % capacity
        placed = dot(rank, spread) == wanted.astype(f32)
        place_ref[piece] = jnp.where(placed, 1.0, 0.0).astype(bf16)
        high_ref[piece] = jnp.where(placed, dot(weight_high, spread), 0.0).astype(bf16)
        low_ref[piece] = jnp.where(placed, dot(weight_low, spread), 0.0).astype(bf16)


def route(plan, first_at, packed, width, local_experts, choices, piece_count, slots):
    tokens = sum(value.shape[0] for value in packed)
    shape = jax.ShapeDtypeStruct((piece_count, tokens, slots), bf16)
    return pl.pallas_call(
        functools.partial(route_kernel, local_experts, choices, width, first_at),
        in_specs=[whole(pltpu.SMEM)] + [whole()] * len(packed),
        out_shape=(shape, shape, shape),
        compiler_params=params(16),
        cost_estimate=cost(2**25, 2**20),
        name="route",
    )(plan, *packed)


def pick_kernel(place_ref, *refs):
    rows_refs, (out_ref, rows_ref) = refs[:-2], refs[-2:]
    rows = rows_refs[0].shape[0]
    for i, ref in enumerate(rows_refs):
        rows_ref[i * rows : (i + 1) * rows, :] = ref[...]
    for piece in range(out_ref.shape[0]):
        out_ref[piece] = dot(place_ref[piece], rows_ref[...], ((0,), (0,))).astype(bf16)


def pick(place, rows):
    piece_count, tokens, slots = place.shape
    columns = rows[0].shape[1]
    return pl.pallas_call(
        pick_kernel,
        out_shape=jax.ShapeDtypeStruct((piece_count, slots, columns), bf16),
        scratch_shapes=[pltpu.VMEM((tokens, columns), bf16)],
        compiler_params=params(8),
        cost_estimate=cost(2**26, 2**20),
        name="pick",
    )(place, *rows)


def gate_up_kernel(plan_ref, picked_ref, weight_ref, *rest):
    added_refs, out_ref = rest[:-1], rest[-1]
    _, width, ff_pair = weight_ref.shape
    picked = picked_ref[0]
    product = dot(picked[:, :width], weight_ref[0])
    squares = picked[:, width:].astype(f32)
    for ref in added_refs:
        product = product + ref[:, :ff_pair].astype(f32)
        squares = squares + ref[:, ff_pair:].astype(f32)
        high, low = in_two(squares[:, :1] + squares[:, 1:2])
        lane = lane_ids(squares.shape)
        squares = jnp.where(lane == 0, high, jnp.where(lane == 1, low, 0.0))
    out_ref[:, :ff_pair] = product.astype(bf16)
    out_ref[:, ff_pair:] = squares.astype(bf16)


def gate_up(plan, piece_at, picked, weight, added=None):
    piece_count, slots, picked_columns = picked.shape
    local_experts, width, ff_pair = weight.shape
    capacity = piece_count * slots // local_experts
    steps = max(1, slots // capacity)
    per_step = slots // steps
    columns = ff_pair + LANES

    def weight_block(step, plan_ref):
        return (plan_ref[piece_at] * slots // capacity + step, 0, 0)

    in_specs = [
        pl.BlockSpec(
            (1, per_step, picked_columns),
            lambda step, plan_ref: (plan_ref[piece_at], step, 0),
        ),
        pl.BlockSpec((1, width, ff_pair), weight_block),
    ]
    operands = [picked, weight]
    if added is not None:
        in_specs.append(pl.BlockSpec((per_step, columns), lambda step, plan_ref: (step, 0)))
        operands.append(added)
    return pl.pallas_call(
        gate_up_kernel,
        grid_spec=pltpu.PrefetchScalarGridSpec(
            num_scalar_prefetch=1,
            grid=(steps,),
            in_specs=in_specs,
            out_specs=pl.BlockSpec((per_step, columns), lambda step, plan_ref: (step, 0)),
        ),
        out_shape=jax.ShapeDtypeStruct((slots, columns), bf16),
        compiler_params=params(8, 1),
        cost_estimate=cost(2 * slots * width * ff_pair, 2 * steps * width * ff_pair),
        name="gate_up_sum" if added is not None else "gate_up",
    )(plan, *operands)


def hidden_kernel(part_count, model_width, *refs):
    out_ref = refs[-1]
    ff_width = out_ref.shape[1]
    total = refs[0][...].astype(f32)
    for ref in refs[1:part_count]:
        total = total + ref[...].astype(f32)
    squares = total[:, 2 * ff_width : 2 * ff_width + 1] + total[:, 2 * ff_width + 1 : 2 * ff_width + 2]
    norm = lax.rsqrt(squares / model_width + epsilon)
    gate = total[:, :ff_width] * norm
    up = total[:, ff_width : 2 * ff_width] * norm
    out_ref[...] = (gate / (1.0 + jnp.exp(-gate)) * up).astype(bf16)


def hidden_of(parts, ff_width, model_width):
    return pl.pallas_call(
        functools.partial(hidden_kernel, len(parts), model_width),
        out_shape=jax.ShapeDtypeStruct((parts[0].shape[0], ff_width), bf16),
        compiler_params=params(8),
        name="hidden",
    )(*parts)


def down_kernel(source_count, plan_ref, hidden_ref, weight_ref, high_ref, low_ref, *refs):
    total_ref = refs[0] if source_count else None
    *out_refs, held_ref = refs[source_count:]
    step = pl.program_id(0)
    each = hidden_ref.shape[0]
    start = pl.multiple_of(step * each, each)
    held_ref[pl.ds(start, each), :] = dot(hidden_ref[...], weight_ref[0]).astype(bf16)

    @pl.when(step == pl.num_programs(0) - 1)
    def combine():
        held = held_ref[...]
        total = dot(high_ref[0], held) + dot(low_ref[0], held)
        if total_ref is not None:
            total = total + total_ref[...]
        rows = out_refs[0].shape[0]
        for i, ref in enumerate(out_refs):
            ref[...] = total[i * rows : (i + 1) * rows, :].astype(ref.dtype)


def down(plan, piece_at, hidden, weight, high, low, total=None, out_count=1):
    slots, ff_width = hidden.shape
    piece_count, tokens, _ = high.shape
    local_experts, _, piece_width = weight.shape
    capacity = piece_count * slots // local_experts
    steps = max(1, slots // capacity)
    per_step = slots // steps
    rows = tokens // out_count

    def weight_block(step, plan_ref):
        return (plan_ref[piece_at] * slots // capacity + step, 0, 0)

    def route_block(step, plan_ref):
        return (plan_ref[piece_at], 0, 0)

    def fixed(step, plan_ref):
        return (0, 0)

    in_specs = [
        pl.BlockSpec((per_step, ff_width), lambda step, plan_ref: (step, 0)),
        pl.BlockSpec((1, ff_width, piece_width), weight_block),
        pl.BlockSpec((1, tokens, slots), route_block),
        pl.BlockSpec((1, tokens, slots), route_block),
    ]
    operands = [hidden, weight, high, low]
    if total is not None:
        in_specs.append(pl.BlockSpec((tokens, piece_width), fixed))
        operands.append(total)
    out_type = f32 if out_count == 1 else bf16
    return pl.pallas_call(
        functools.partial(down_kernel, 0 if total is None else 1),
        grid_spec=pltpu.PrefetchScalarGridSpec(
            num_scalar_prefetch=1,
            grid=(steps,),
            in_specs=in_specs,
            out_specs=[pl.BlockSpec((rows, piece_width), fixed)] * out_count,
            scratch_shapes=[pltpu.VMEM((slots, piece_width), bf16)],
        ),
        out_shape=[jax.ShapeDtypeStruct((rows, piece_width), out_type)] * out_count,
        compiler_params=params(8, 1),
        cost_estimate=cost(2 * slots * ff_width * piece_width, 2 * steps * ff_width * piece_width),
        name="down",
    )(plan, *operands)


def finish_kernel(mixed_ref, *refs):
    total = mixed_ref[...]
    for ref in refs[:-1]:
        total = total + ref[...].astype(f32)
    refs[-1][...] = total.astype(bf16)


def finish(mixed, parts):
    return pl.pallas_call(
        finish_kernel,
        out_shape=jax.ShapeDtypeStruct(mixed.shape, bf16),
        compiler_params=params(4),
        name="finish",
    )(mixed, *parts)


def body(
    queries,
    cached_keys,
    cached_values,
    key_seg,
    query_seg,
    parent,
    out_weight,
    residual,
    norm_gain,
    gate_up_weight,
    down_weight,
    expert_ids,
    route_weight,
):
    ctx_count, exp_count, tp_count = (lax.axis_size(axis) for axis in ("ctx", "exp", "tp"))
    own_ctx, own_exp, own_tp = (lax.axis_index(axis) for axis in ("ctx", "exp", "tp"))
    assert tp_count == 2 and cached_keys.shape[1] == 1
    assert ctx_count & (ctx_count - 1) == 0 and exp_count & (exp_count - 1) == 0
    piece_count = exp_count * tp_count
    query_rows = queries.shape[0]
    key_count, _, head_size = cached_keys.shape
    heads = queries.shape[2] // head_size
    width = heads * head_size
    model_width = out_weight.shape[2]
    local_experts, piece_width, _ = gate_up_weight.shape
    ff_width = down_weight.shape[1]
    choices = expert_ids.shape[1]
    slots = local_experts * ctx_count * MOST // piece_count
    scale = math.log2(math.e) / math.sqrt(head_size)

    last = ctx_count * (key_count - query_rows) - own_ctx * key_count
    leads = [last + (own_ctx ^ k) * query_rows for k in range(ctx_count)]
    own_piece = own_exp * tp_count + own_tp
    column_pieces = [own_piece ^ k for k in range(piece_count)]
    slot_pieces = [
        (own_tp ^ flip) * exp_count + (own_exp ^ k) for flip in (0, 1) for k in range(exp_count)
    ]
    scalars = [own_ctx * local_experts] + leads + column_pieces + slot_pieces
    plan = jnp.stack([jnp.asarray(value, jnp.int32) for value in scalars])
    lead_at = 1
    order_at = lead_at + ctx_count
    mine_at = order_at + piece_count
    away_at = mine_at + exp_count

    packed = pack(queries.reshape(query_rows, width), query_seg, expert_ids, route_weight)
    gathered = {0: packed}
    for k in far_first(ctx_count):
        gathered[k] = swapped(packed, "ctx", k)
    sight = sight_of(parent, key_seg)
    keys = cached_keys.reshape(key_count, head_size)
    values = cached_values.reshape(key_count, head_size)
    parts = []
    for k in range(ctx_count):
        part = attend(plan, lead_at + k, gathered[k], keys, values, sight, heads, scale)
        parts.append(swapped(part, "ctx", k) if k else part)
    place, combine_high, combine_low = route(
        plan,
        0,
        [gathered[k] for k in range(ctx_count)],
        width,
        local_experts,
        choices,
        piece_count,
        slots,
    )
    projected = project(
        plan, order_at, parts, out_weight.reshape(width, model_width), heads, scale, piece_count
    )
    pieces = [projected[0]] + [
        swapped(projected[k], ("exp", "tp"), k) for k in far_first(piece_count)
    ]
    mixed, sent = mix(residual, norm_gain, pieces)
    rows = {0: sent}
    for k in far_first(ctx_count):
        rows[k] = swapped(sent, "ctx", k)
    picked = pick(place, [rows[k] for k in range(ctx_count)])

    finals = []
    for k in far_first(exp_count) + [0]:
        away = gate_up(plan, away_at + k, picked, gate_up_weight)
        summed = gate_up(plan, mine_at + k, picked, gate_up_weight, swapped(away, "tp", 1))
        finals.append(swapped(summed, "exp", k) if k else summed)
    own_hidden = hidden_of(finals, ff_width, model_width)

    total = None
    for k in range(exp_count):
        here = swapped(own_hidden, "exp", k) if k else own_hidden
        there = swapped(here, "tp", 1)
        for piece_at, hidden in ((mine_at + k, here), (away_at + k, there)):
            ends = piece_at == away_at + exp_count - 1
            totals = down(
                plan,
                piece_at,
                hidden,
                down_weight,
                combine_high,
                combine_low,
                total,
                ctx_count if ends else 1,
            )
            total = totals[0]
    returned = [totals[0]] + [swapped(totals[k], "ctx", k) for k in far_first(ctx_count)]
    return finish(mixed, returned)


def solution(mesh):
    in_specs = (
        P(("group", "ctx"), "tp", "exp"),
        P(("group", "ctx"), "tp", None),
        P(("group", "ctx"), "tp", None),
        P(("group", "ctx")),
        P(("group", "ctx")),
        P("group"),
        P("tp", "exp", None),
        P(("group", "ctx"), ("exp", "tp")),
        P(("exp", "tp")),
        P("ctx", ("exp", "tp"), None),
        P("ctx", None, ("exp", "tp")),
        P(("group", "ctx"), None),
        P(("group", "ctx"), None),
    )
    out_specs = P(("group", "ctx"), ("exp", "tp"))
    return jax.shard_map(body, mesh=mesh, in_specs=in_specs, out_specs=out_specs, check_vma=False)
```

```python
import functools
import math

import jax
import jax.numpy as jnp
from jax import lax
from jax.experimental import pallas as pl
from jax.experimental.pallas import tpu as pltpu
from jax.sharding import PartitionSpec as P

MOST = 8
DEPTH = 6
LANES = 128

epsilon = 1e-06
masked_score = -1e30
least_high = -1e20

f32 = jnp.float32
bf16 = jnp.bfloat16


def params(megabytes, steps=0):
    semantics = ("arbitrary",) * steps if steps else None
    return pltpu.CompilerParams(
        vmem_limit_bytes=megabytes * 1024 * 1024, dimension_semantics=semantics
    )


def cost(flops, bytes_accessed, transcendentals=0):
    return pl.CostEstimate(
        flops=flops, bytes_accessed=bytes_accessed, transcendentals=transcendentals
    )


def whole(memory_space=pltpu.VMEM):
    return pl.BlockSpec(memory_space=memory_space)


def in_hbm(values):
    return [pltpu.with_memory_space_constraint(value, pltpu.HBM) for value in values]


def in_vmem(value):
    return pltpu.with_memory_space_constraint(value, pltpu.VMEM)


def lane_ids(shape):
    return lax.broadcasted_iota(jnp.int32, shape, len(shape) - 1)


def row_ids(shape):
    return lax.broadcasted_iota(jnp.int32, shape, len(shape) - 2)


def as_bf16(mask):
    return mask.astype(f32).astype(bf16)


def dot(left, right, dims=((1,), (0,))):
    return lax.dot_general(left, right, (dims, ((), ())), preferred_element_type=f32)


def in_two(value):
    high = value.astype(bf16).astype(f32)
    return high, value - high


def swapped(value, axes, mask):
    count = lax.axis_size(axes)
    pairs = [(source, source ^ mask) for source in range(count)]
    return lax.ppermute(value, axes, pairs)


def far_first(count):
    return list(range(count - 1, 0, -1))


def pack_kernel(
    queries_ref, seg_ref, ids_ref, weight_ref, out_ref, seg_here, ids_here, weight_here, done
):
    rows, width = queries_ref.shape
    choices = ids_ref.shape[0]
    copies = [
        pltpu.make_async_copy(source, target, done.at[i])
        for i, (source, target) in enumerate(
            [
                (seg_ref, seg_here),
                (ids_ref, ids_here),
                (weight_ref, weight_here),
                (queries_ref, out_ref.at[:, :width]),
            ]
        )
    ]
    for copy in copies:
        copy.start()
    shape = (choices, LANES)

    def placed(value, first, last):
        to_lane = (lane_ids(shape) == row_ids(shape) + first) & (row_ids(shape) <= last)
        return dot(value.astype(bf16), as_bf16(to_lane), ((0,), (0,)))

    for copy in copies[:3]:
        copy.wait()
    segs = jnp.broadcast_to(seg_here[...], (choices, rows)).astype(f32)
    high, low = in_two(weight_here[...])
    info = placed(segs, 0, 0) + placed(ids_here[...].astype(f32), 1, choices)
    info = info + placed(high, 1 + choices, choices) + placed(low, 1 + 2 * choices, choices)
    out_ref[:, width:] = info.astype(bf16)
    copies[3].wait()


def pack(queries, query_seg, expert_ids, route_weight):
    rows, width = queries.shape
    small = [query_seg[None, :], expert_ids.T, route_weight.T]
    return pl.pallas_call(
        pack_kernel,
        in_specs=[whole(pltpu.HBM)] * 4,
        out_shape=jax.ShapeDtypeStruct((rows, width + LANES), bf16),
        scratch_shapes=[pltpu.VMEM(value.shape, value.dtype) for value in small]
        + [pltpu.SemaphoreType.DMA((4,))],
        compiler_params=params(4),
        name="pack",
    )(*in_hbm([queries] + small))


def sight_kernel(load_count, parent_ref, key_seg_ref, *refs):
    sources, sight_ref = refs[:load_count], refs[load_count]
    targets = refs[load_count + 1 : 2 * load_count + 1]
    parent_here, key_seg_here, done = refs[2 * load_count + 1 :]
    copies = [
        pltpu.make_async_copy(source, target, done.at[i])
        for i, (source, target) in enumerate(
            zip((parent_ref, key_seg_ref) + sources, (parent_here, key_seg_here) + targets)
        )
    ]
    for copy in copies:
        copy.start()
    for copy in copies[:2]:
        copy.wait()
    seg_count, key_count = sight_ref.shape
    square = (seg_count, seg_count)
    same = row_ids(square) == lane_ids(square)
    one = as_bf16((parent_here[...] == row_ids(square)) | same)
    two = as_bf16(dot(one, one) > 0.5)
    four = as_bf16(dot(two, two) > 0.5)
    six = as_bf16(dot(four, two) > 0.5)
    keys = as_bf16(key_seg_here[...] == row_ids((seg_count, key_count)))
    sight_ref[...] = dot(six, keys, ((0,), (0,))).astype(bf16)
    for copy in copies[2:]:
        copy.wait()


def sight_of(parent, key_seg, loaded):
    assert DEPTH == 6
    small = [parent[None, :], key_seg[None, :]]
    shapes = [pltpu.VMEM(value.shape, value.dtype) for value in loaded]
    return pl.pallas_call(
        functools.partial(sight_kernel, len(loaded)),
        in_specs=[whole(pltpu.HBM)] * (2 + len(loaded)),
        out_specs=[whole()] * (1 + len(loaded)),
        out_shape=[jax.ShapeDtypeStruct((parent.shape[0], key_seg.shape[0]), bf16)] + shapes,
        scratch_shapes=[pltpu.VMEM(value.shape, value.dtype) for value in small]
        + [pltpu.SemaphoreType.DMA((2 + len(loaded),))],
        compiler_params=params(4),
        cost_estimate=cost(2**24, 2**23),
        name="sight",
    )(*in_hbm(small + loaded))


def attend_kernel(
    heads, scale, lead_at, loads, plan_ref, queries_ref, keys_ref, values_ref, sight_ref,
    weight_ref, out_ref, *refs,
):
    loaded_refs, (stacked_ref, probs_ref, done) = refs[: len(loads)], refs[len(loads) :]
    copies = []
    for target, (expert_at, spread) in zip(loaded_refs, loads):
        for i in range(target.shape[0]):
            expert = plan_ref[expert_at] // spread + i
            copies.append(
                pltpu.make_async_copy(
                    weight_ref.at[expert], target.at[i], done.at[len(copies)]
                )
            )
    for copy in copies:
        copy.start()
    rows = queries_ref.shape[0]
    key_count, head_size = keys_ref.shape
    seg_count = sight_ref.shape[0]
    width = heads * head_size
    info = queries_ref[:, width:].astype(f32)
    own_seg = info[:, :1].astype(jnp.int32)
    onehot = as_bf16(own_seg == lane_ids((rows, seg_count)))
    seen = dot(onehot, sight_ref[...]) > 0.5
    place = (rows, key_count)
    causal = lane_ids(place) - row_ids(place) <= plan_ref[lead_at]
    bias = jnp.where(seen & causal, 0.0, masked_score)
    for head in range(heads):
        columns = slice(head * head_size, (head + 1) * head_size)
        stacked_ref[head * rows : (head + 1) * rows, :] = queries_ref[:, columns]
    scores = dot(stacked_ref[...], keys_ref[...], ((1,), (1,)))
    stats = jnp.zeros((rows, LANES), f32)
    lane = lane_ids((rows, LANES))
    for head in range(heads):
        here = slice(head * rows, (head + 1) * rows)
        biased = scores[here, :] + bias
        high = jnp.maximum(jnp.max(biased, axis=1, keepdims=True), least_high)
        high = high.astype(bf16).astype(f32)
        probs = jnp.exp2((biased - high) * scale)
        total_high, total_low = in_two(jnp.sum(probs, axis=1, keepdims=True))
        probs_ref[here, :] = probs.astype(bf16)
        stats = jnp.where(lane == head, high, stats)
        stats = jnp.where(lane == heads + head, total_high, stats)
        stats = jnp.where(lane == 2 * heads + head, total_low, stats)
    out_ref[:, width:] = stats.astype(bf16)
    sums = dot(probs_ref[...], values_ref[...])
    for head in range(heads):
        columns = slice(head * head_size, (head + 1) * head_size)
        out_ref[:, columns] = sums[head * rows : (head + 1) * rows, :].astype(bf16)
    for copy in copies:
        copy.wait()


def attend(plan, lead_at, queries, keys, values, sight, heads, scale, weight, loads, experts, spread):
    rows, columns = queries.shape
    key_count, head_size = keys.shape
    work = rows * heads * key_count
    held = pltpu.VMEM((experts,) + weight.shape[1:], weight.dtype)
    part, *loaded = pl.pallas_call(
        functools.partial(
            attend_kernel, heads, scale, lead_at, [(load, spread) for load in loads]
        ),
        in_specs=[whole(pltpu.SMEM)] + [whole()] * 4 + [whole(pltpu.HBM)],
        out_specs=[whole()] * (1 + len(loads)),
        out_shape=[jax.ShapeDtypeStruct((rows, columns), bf16)] + [held] * len(loads),
        scratch_shapes=[
            pltpu.VMEM((rows * heads, head_size), bf16),
            pltpu.VMEM((rows * heads, key_count), bf16),
            pltpu.SemaphoreType.DMA((max(1, len(loads) * experts),)),
        ],
        compiler_params=params(8),
        cost_estimate=cost(8 * work * head_size, 2**20, work),
        name="attend",
    )(plan, queries, in_vmem(keys), in_vmem(values), sight, *in_hbm([weight]))
    return part, loaded


def project_kernel(heads, scale, order_at, source_count, plan_ref, *refs):
    parts_refs, weight_ref = refs[:source_count], refs[source_count]
    out_refs, attention_ref = refs[source_count + 1 : -1], refs[-1]
    width = attention_ref.shape[1]
    head_size = width // heads
    stats = [ref[:, width:].astype(f32) for ref in parts_refs]
    top = functools.reduce(jnp.maximum, stats)
    factors = [jnp.exp2(jnp.minimum((stat - top) * scale, 0.0)) for stat in stats]
    total = 0.0
    for stat, factor in zip(stats, factors):
        high = pltpu.roll(stat, LANES - heads, 1)
        low = pltpu.roll(stat, LANES - 2 * heads, 1)
        total = total + factor * (high + low)
    shares = [factor / total for factor in factors]
    for head in range(heads):
        columns = slice(head * head_size, (head + 1) * head_size)
        merged = 0.0
        for ref, share in zip(parts_refs, shares):
            merged = merged + ref[:, columns].astype(f32) * share[:, head : head + 1]
        attention_ref[:, columns] = merged.astype(bf16)
    for i, out_ref in enumerate(out_refs):
        piece_width = out_ref.shape[1]
        start = pl.multiple_of(plan_ref[order_at + i] * piece_width, piece_width)
        out_ref[...] = dot(attention_ref[...], weight_ref[:, pl.ds(start, piece_width)]).astype(bf16)


def project(plan, order_at, parts, weight, heads, scale, piece_count):
    rows = parts[0].shape[0]
    width, model_width = weight.shape
    piece_width = model_width // piece_count
    return pl.pallas_call(
        functools.partial(project_kernel, heads, scale, order_at, len(parts)),
        in_specs=[whole(pltpu.SMEM)] + [whole()] * (len(parts) + 1),
        out_shape=[jax.ShapeDtypeStruct((rows, piece_width), bf16)] * piece_count,
        scratch_shapes=[pltpu.VMEM((rows, width), bf16)],
        compiler_params=params(8),
        cost_estimate=cost(2 * rows * width * model_width, 2 * width * model_width),
        name="project",
    )(plan, *parts, in_vmem(weight))


def mix_kernel(residual_ref, gain_ref, *refs):
    parts_refs, (mixed_ref, sent_ref) = refs[:-2], refs[-2:]
    rows, width = mixed_ref.shape
    mixed = residual_ref[...].astype(f32)
    for ref in parts_refs:
        mixed = mixed + ref[...].astype(f32)
    mixed_ref[...] = mixed
    sent_ref[:, :width] = (mixed * gain_ref[...].astype(f32)).astype(bf16)
    high, low = in_two(jnp.sum(mixed * mixed, axis=1, keepdims=True))
    lane = lane_ids((rows, LANES))
    squares = jnp.where(lane == 0, high, jnp.where(lane == 1, low, 0.0))
    sent_ref[:, width:] = squares.astype(bf16)


def mix(residual, gain, parts):
    rows, width = residual.shape
    return pl.pallas_call(
        mix_kernel,
        out_shape=(
            jax.ShapeDtypeStruct((rows, width), f32),
            jax.ShapeDtypeStruct((rows, width + LANES), bf16),
        ),
        compiler_params=params(4),
        name="mix",
    )(residual, gain[None, :], *parts)


def route_kernel(local_experts, choices, width, first_at, plan_ref, *refs):
    info_refs, (place_ref, high_ref, low_ref) = refs[:-3], refs[-3:]
    piece_count, tokens, slots = place_ref.shape
    info = jnp.concatenate([ref[:, width:] for ref in info_refs], axis=0).astype(f32)
    expert = (lane_ids((tokens, local_experts)) + plan_ref[first_at]).astype(f32)
    member = jnp.zeros((tokens, local_experts), f32)
    weight_high = jnp.zeros((tokens, local_experts), f32)
    weight_low = jnp.zeros((tokens, local_experts), f32)
    for k in range(choices):
        chosen = info[:, 1 + k : 2 + k] == expert
        high = info[:, 1 + choices + k : 2 + choices + k]
        low = info[:, 1 + 2 * choices + k : 2 + 2 * choices + k]
        member = jnp.where(chosen, 1.0, member)
        weight_high = jnp.where(chosen, high, weight_high)
        weight_low = jnp.where(chosen, low, weight_low)
    square = (tokens, tokens)
    earlier = as_bf16(lane_ids(square) < row_ids(square))
    rank = jnp.where(member > 0.5, dot(earlier, member.astype(bf16)), -1.0).astype(bf16)
    weight_high = weight_high.astype(bf16)
    weight_low = weight_low.astype(bf16)
    capacity = piece_count * slots // local_experts
    for piece in range(piece_count):
        slot = lane_ids((local_experts, slots)) + piece * slots
        spread = as_bf16(slot // capacity == row_ids((local_experts, slots)))
        wanted = (lane_ids((tokens, slots)) + piece * slots) % capacity
        placed = dot(rank, spread) == wanted.astype(f32)
        place_ref[piece] = jnp.where(placed, 1.0, 0.0).astype(bf16)
        high_ref[piece] = jnp.where(placed, dot(weight_high, spread), 0.0).astype(bf16)
        low_ref[piece] = jnp.where(placed, dot(weight_low, spread), 0.0).astype(bf16)


def route(plan, first_at, packed, width, local_experts, choices, piece_count, slots):
    tokens = sum(value.shape[0] for value in packed)
    shape = jax.ShapeDtypeStruct((piece_count, tokens, slots), bf16)
    return pl.pallas_call(
        functools.partial(route_kernel, local_experts, choices, width, first_at),
        in_specs=[whole(pltpu.SMEM)] + [whole()] * len(packed),
        out_shape=(shape, shape, shape),
        compiler_params=params(16),
        cost_estimate=cost(2**25, 2**20),
        name="route",
    )(plan, *packed)


def pick_kernel(place_ref, *refs):
    rows_refs, (out_ref, rows_ref) = refs[:-2], refs[-2:]
    rows = rows_refs[0].shape[0]
    for i, ref in enumerate(rows_refs):
        rows_ref[i * rows : (i + 1) * rows, :] = ref[...]
    for piece in range(out_ref.shape[0]):
        out_ref[piece] = dot(place_ref[piece], rows_ref[...], ((0,), (0,))).astype(bf16)


def pick(place, rows):
    piece_count, tokens, slots = place.shape
    columns = rows[0].shape[1]
    return pl.pallas_call(
        pick_kernel,
        out_shape=jax.ShapeDtypeStruct((piece_count, slots, columns), bf16),
        scratch_shapes=[pltpu.VMEM((tokens, columns), bf16)],
        compiler_params=params(8),
        cost_estimate=cost(2**26, 2**20),
        name="pick",
    )(place, *rows)


def squares_joined(squares):
    high, low = in_two(squares[:, :1] + squares[:, 1:2])
    lane = lane_ids(squares.shape)
    return jnp.where(lane == 0, high, jnp.where(lane == 1, low, 0.0))


def gate_up_kernel(piece_at, plan_ref, picked_ref, weight_ref, *rest):
    added_refs, out_ref = rest[:-1], rest[-1]
    experts, width, ff_pair = weight_ref.shape
    rows = out_ref.shape[0] // experts
    piece = plan_ref[piece_at]
    for i in range(experts):
        here = slice(i * rows, (i + 1) * rows)
        picked = picked_ref[piece, here, :]
        product = dot(picked[:, :width], weight_ref[i])
        squares = picked[:, width:].astype(f32)
        for ref in added_refs:
            product = product + ref[here, :ff_pair].astype(f32)
            squares = squares_joined(squares + ref[here, ff_pair:].astype(f32))
        out_ref[here, :ff_pair] = product.astype(bf16)
        out_ref[here, ff_pair:] = squares.astype(bf16)


def gate_up(plan, piece_at, picked, weight, added=()):
    slots = picked.shape[1]
    experts, width, ff_pair = weight.shape
    return pl.pallas_call(
        functools.partial(gate_up_kernel, piece_at),
        in_specs=[whole(pltpu.SMEM)] + [whole()] * (2 + len(added)),
        out_shape=jax.ShapeDtypeStruct((slots, ff_pair + LANES), bf16),
        compiler_params=params(8),
        cost_estimate=cost(slots * width * ff_pair // 8, experts * width * ff_pair // 8),
        name="gate_up_sum" if added else "gate_up",
    )(plan, picked, in_vmem(weight), *added)


def join_kernel(left_ref, right_ref, out_ref):
    ff_pair = out_ref.shape[1] - LANES
    product = left_ref[:, :ff_pair].astype(f32) + right_ref[:, :ff_pair].astype(f32)
    out_ref[:, :ff_pair] = product.astype(bf16)
    squares = left_ref[:, ff_pair:].astype(f32) + right_ref[:, ff_pair:].astype(f32)
    out_ref[:, ff_pair:] = squares_joined(squares).astype(bf16)


def join(left, right):
    return pl.pallas_call(
        join_kernel,
        out_shape=jax.ShapeDtypeStruct(left.shape, bf16),
        compiler_params=params(4),
        name="join",
    )(left, right)


def hidden_kernel(part_count, model_width, *refs):
    out_ref = refs[-1]
    ff_width = out_ref.shape[1]
    total = refs[0][...].astype(f32)
    for ref in refs[1:part_count]:
        total = total + ref[...].astype(f32)
    squares = total[:, 2 * ff_width : 2 * ff_width + 1] + total[:, 2 * ff_width + 1 : 2 * ff_width + 2]
    norm = lax.rsqrt(squares / model_width + epsilon)
    gate = total[:, :ff_width] * norm
    up = total[:, ff_width : 2 * ff_width] * norm
    out_ref[...] = (gate / (1.0 + jnp.exp(-gate)) * up).astype(bf16)


def hidden_of(parts, ff_width, model_width):
    return pl.pallas_call(
        functools.partial(hidden_kernel, len(parts), model_width),
        out_shape=jax.ShapeDtypeStruct((parts[0].shape[0], ff_width), bf16),
        compiler_params=params(8),
        name="hidden",
    )(*parts)


def down(plan, piece_at, expert_at, spread, hidden, weight, high, low, total=None, out_count=1):
    slots, ff_width = hidden.shape
    piece_count, tokens, _ = high.shape
    local_experts, _, piece_width = weight.shape
    experts = max(1, local_experts // piece_count)
    each = slots // experts
    rows = tokens // out_count
    out_type = f32 if out_count == 1 else bf16

    def kernel(plan_ref, hidden_ref, weight_ref, high_ref, low_ref, *refs):
        total_refs, out_refs, held_ref = refs[: -1 - out_count], refs[-1 - out_count : -1], refs[-1]
        piece = plan_ref[piece_at]
        first = plan_ref[expert_at] // spread
        for i in range(experts):
            here = slice(i * each, (i + 1) * each)
            held_ref[here, :] = dot(hidden_ref[here, :], weight_ref[first + i]).astype(bf16)
        held = held_ref[...]
        summed = dot(high_ref[piece], held) + dot(low_ref[piece], held)
        for ref in total_refs:
            summed = summed + ref[...]
        for i, ref in enumerate(out_refs):
            ref[...] = summed[i * rows : (i + 1) * rows, :].astype(ref.dtype)

    before = [] if total is None else [total]
    return pl.pallas_call(
        kernel,
        in_specs=[whole(pltpu.SMEM)] + [whole()] * (4 + len(before)),
        out_shape=[jax.ShapeDtypeStruct((rows, piece_width), out_type)] * out_count,
        scratch_shapes=[pltpu.VMEM((slots, piece_width), bf16)],
        compiler_params=params(8),
        cost_estimate=cost(2 * slots * ff_width * piece_width, 2 * experts * ff_width * piece_width),
        name="down",
    )(plan, hidden, weight, high, low, *before)


def finish_kernel(mixed_ref, *refs):
    total = mixed_ref[...]
    for ref in refs[:-1]:
        total = total + ref[...].astype(f32)
    refs[-1][...] = total.astype(bf16)


def finish(mixed, parts):
    return pl.pallas_call(
        finish_kernel,
        out_shape=jax.ShapeDtypeStruct(mixed.shape, bf16),
        compiler_params=params(4),
        name="finish",
    )(mixed, *parts)


def body(
    queries,
    cached_keys,
    cached_values,
    key_seg,
    query_seg,
    parent,
    out_weight,
    residual,
    norm_gain,
    gate_up_weight,
    down_weight,
    expert_ids,
    route_weight,
):
    ctx_count, exp_count, tp_count = (lax.axis_size(axis) for axis in ("ctx", "exp", "tp"))
    own_ctx, own_exp, own_tp = (lax.axis_index(axis) for axis in ("ctx", "exp", "tp"))
    assert tp_count == 2 and cached_keys.shape[1] == 1
    assert ctx_count & (ctx_count - 1) == 0 and exp_count & (exp_count - 1) == 0
    piece_count = exp_count * tp_count
    query_rows = queries.shape[0]
    key_count, _, head_size = cached_keys.shape
    heads = queries.shape[2] // head_size
    width = heads * head_size
    model_width = out_weight.shape[2]
    local_experts, piece_width, _ = gate_up_weight.shape
    ff_width = down_weight.shape[1]
    choices = expert_ids.shape[1]
    slots = local_experts * ctx_count * MOST // piece_count
    scale = math.log2(math.e) / math.sqrt(head_size)

    last = ctx_count * (key_count - query_rows) - own_ctx * key_count
    leads = [last + (own_ctx ^ k) * query_rows for k in range(ctx_count)]
    own_piece = own_exp * tp_count + own_tp
    column_pieces = [own_piece ^ k for k in range(piece_count)]
    slot_pieces = [
        (own_tp ^ flip) * exp_count + (own_exp ^ k) for flip in (0, 1) for k in range(exp_count)
    ]
    capacity = ctx_count * MOST
    experts = max(1, slots // capacity)
    spread = max(1, capacity // slots)
    scalars = [own_ctx * local_experts] + leads + column_pieces + slot_pieces
    scalars = scalars + [piece * experts for piece in slot_pieces]
    plan = jnp.stack([jnp.asarray(value, jnp.int32) for value in scalars])
    lead_at = 1
    order_at = lead_at + ctx_count
    mine_at = order_at + piece_count
    away_at = mine_at + exp_count
    expert_at = piece_count

    packed = pack(queries.reshape(query_rows, width), query_seg, expert_ids, route_weight)
    gathered = {0: packed}
    for k in far_first(ctx_count):
        gathered[k] = swapped(packed, "ctx", k)
    sight, keys, values, out_matrix = sight_of(
        parent,
        key_seg,
        [
            cached_keys.reshape(key_count, head_size),
            cached_values.reshape(key_count, head_size),
            out_weight.reshape(width, model_width),
        ],
    )
    steps = far_first(exp_count) + [0]
    wanted = [at + k for k in steps for at in (away_at, mine_at)]
    assert ctx_count >= piece_count
    parts = {}
    held = {}
    for turn, k in enumerate(list(range(1, ctx_count)) + [0]):
        loads = wanted[turn : turn + 1]
        part, loaded = attend(
            plan,
            lead_at + k,
            gathered[k],
            keys,
            values,
            sight,
            heads,
            scale,
            gate_up_weight,
            [at + expert_at for at in loads],
            experts,
            spread,
        )
        held.update(zip(loads, loaded))
        parts[k] = swapped(part, "ctx", k) if k else part
    place, combine_high, combine_low = route(
        plan,
        0,
        [gathered[k] for k in range(ctx_count)],
        width,
        local_experts,
        choices,
        piece_count,
        slots,
    )
    projected = project(
        plan,
        order_at,
        [parts[k] for k in range(ctx_count)],
        out_matrix,
        heads,
        scale,
        piece_count,
    )
    pieces = [projected[0]] + [
        swapped(projected[k], ("exp", "tp"), k) for k in far_first(piece_count)
    ]
    mixed, sent = mix(residual, norm_gain, pieces)
    rows = {0: sent}
    for k in far_first(ctx_count):
        rows[k] = swapped(sent, "ctx", k)
    picked = pick(place, [rows[k] for k in range(ctx_count)])

    finals = []
    for k in steps:
        away = gate_up(plan, away_at + k, picked, held[away_at + k])
        arrived = swapped(away, "tp", 1)
        if k:
            mine = gate_up(plan, mine_at + k, picked, held[mine_at + k])
            joined = join(mine, arrived)
            finals.append(swapped(joined, "exp", k))
            picked, _ = lax.optimization_barrier((picked, joined))
        else:
            mine = gate_up(plan, mine_at, picked, held[mine_at])
            finals, mine = lax.optimization_barrier((finals, mine))
            finals = [arrived, mine] + finals
    own_hidden = hidden_of(finals, ff_width, model_width)

    total = None
    for k in range(exp_count):
        here = own_hidden
        if k:
            here, total = lax.optimization_barrier((swapped(own_hidden, "exp", k), total))
        there = swapped(here, "tp", 1)
        for piece_at, hidden in ((mine_at + k, here), (away_at + k, there)):
            ends = piece_at == away_at + exp_count - 1
            totals = down(
                plan,
                piece_at,
                piece_at + expert_at,
                spread,
                hidden,
                down_weight,
                combine_high,
                combine_low,
                total,
                ctx_count if ends else 1,
            )
            total = totals[0]
    returned = [totals[0]] + [swapped(totals[k], "ctx", k) for k in far_first(ctx_count)]
    return finish(mixed, returned)


def solution(mesh):
    in_specs = (
        P(("group", "ctx"), "tp", "exp"),
        P(("group", "ctx"), "tp", None),
        P(("group", "ctx"), "tp", None),
        P(("group", "ctx")),
        P(("group", "ctx")),
        P("group"),
        P("tp", "exp", None),
        P(("group", "ctx"), ("exp", "tp")),
        P(("exp", "tp")),
        P("ctx", ("exp", "tp"), None),
        P("ctx", None, ("exp", "tp")),
        P(("group", "ctx"), None),
        P(("group", "ctx"), None),
    )
    out_specs = P(("group", "ctx"), ("exp", "tp"))
    return jax.shard_map(body, mesh=mesh, in_specs=in_specs, out_specs=out_specs, check_vma=False)
```

```python
import functools
import math

import jax
import jax.numpy as jnp
from jax import lax
from jax.experimental import pallas as pl
from jax.experimental.pallas import tpu as pltpu
from jax.sharding import PartitionSpec as P

MOST = 8
DEPTH = 6
LANES = 128

epsilon = 1e-06
masked_score = -1e30
least_high = -1e20

f32 = jnp.float32
bf16 = jnp.bfloat16


def params(megabytes, steps=0):
    semantics = ("arbitrary",) * steps if steps else None
    return pltpu.CompilerParams(
        vmem_limit_bytes=megabytes * 1024 * 1024, dimension_semantics=semantics
    )


def cost(flops, bytes_accessed, transcendentals=0):
    return pl.CostEstimate(
        flops=flops, bytes_accessed=bytes_accessed, transcendentals=transcendentals
    )


def whole(memory_space=pltpu.VMEM):
    return pl.BlockSpec(memory_space=memory_space)


def in_hbm(values):
    return [pltpu.with_memory_space_constraint(value, pltpu.HBM) for value in values]


def lane_ids(shape):
    return lax.broadcasted_iota(jnp.int32, shape, len(shape) - 1)


def row_ids(shape):
    return lax.broadcasted_iota(jnp.int32, shape, len(shape) - 2)


def as_bf16(mask):
    return mask.astype(f32).astype(bf16)


def dot(left, right, dims=((1,), (0,))):
    return lax.dot_general(left, right, (dims, ((), ())), preferred_element_type=f32)


def in_two(value):
    high = value.astype(bf16).astype(f32)
    return high, value - high


def swapped(value, axes, mask):
    count = lax.axis_size(axes)
    pairs = [(source, source ^ mask) for source in range(count)]
    return lax.ppermute(value, axes, pairs)


def far_first(count):
    return list(range(count - 1, 0, -1))


def pack_kernel(
    queries_ref, seg_ref, ids_ref, weight_ref, beside_ref, out_ref,
    seg_here, ids_here, weight_here, done,
):
    rows, width = queries_ref.shape
    choices = ids_ref.shape[0]
    copies = [
        pltpu.make_async_copy(source, target, done.at[i])
        for i, (source, target) in enumerate(
            [
                (seg_ref, seg_here),
                (ids_ref, ids_here),
                (weight_ref, weight_here),
                (queries_ref, out_ref.at[:, :width]),
            ]
        )
    ]
    for copy in copies:
        copy.start()
    shape = (choices, LANES)

    def placed(value, first, last):
        to_lane = (lane_ids(shape) == row_ids(shape) + first) & (row_ids(shape) <= last)
        return dot(value.astype(bf16), as_bf16(to_lane), ((0,), (0,)))

    for copy in copies[:3]:
        copy.wait()
    segs = jnp.broadcast_to(seg_here[...], (choices, rows)).astype(f32)
    high, low = in_two(weight_here[...])
    info = placed(segs, 0, 0) + placed(ids_here[...].astype(f32), 1, choices)
    info = info + placed(high, 1 + choices, choices) + placed(low, 1 + 2 * choices, choices)
    out_ref[:, width:] = info.astype(bf16)
    copies[3].wait()


def pack(queries, query_seg, expert_ids, route_weight, beside):
    rows, width = queries.shape
    small = [query_seg[None, :], expert_ids.T, route_weight.T]
    return pl.pallas_call(
        pack_kernel,
        in_specs=[whole(pltpu.HBM)] * 5,
        out_shape=jax.ShapeDtypeStruct((rows, width + LANES), bf16),
        scratch_shapes=[pltpu.VMEM(value.shape, value.dtype) for value in small]
        + [pltpu.SemaphoreType.DMA((4,))],
        compiler_params=params(4),
        name="pack",
    )(*in_hbm([queries] + small + [beside]))


def sight_kernel(parent_ref, key_seg_ref, beside_ref, sight_ref, parent_here, key_seg_here, done):
    copies = [
        pltpu.make_async_copy(parent_ref, parent_here, done.at[0]),
        pltpu.make_async_copy(key_seg_ref, key_seg_here, done.at[1]),
    ]
    for copy in copies:
        copy.start()
    for copy in copies:
        copy.wait()
    seg_count, key_count = sight_ref.shape
    square = (seg_count, seg_count)
    same = row_ids(square) == lane_ids(square)
    one = as_bf16((parent_here[...] == row_ids(square)) | same)
    two = as_bf16(dot(one, one) > 0.5)
    four = as_bf16(dot(two, two) > 0.5)
    six = as_bf16(dot(four, two) > 0.5)
    keys = as_bf16(key_seg_here[...] == row_ids((seg_count, key_count)))
    sight_ref[...] = dot(six, keys, ((0,), (0,))).astype(bf16)


def sight_of(parent, key_seg, beside):
    assert DEPTH == 6
    small = [parent[None, :], key_seg[None, :]]
    return pl.pallas_call(
        sight_kernel,
        in_specs=[whole(pltpu.HBM)] * 3,
        out_shape=jax.ShapeDtypeStruct((parent.shape[0], key_seg.shape[0]), bf16),
        scratch_shapes=[pltpu.VMEM(value.shape, value.dtype) for value in small]
        + [pltpu.SemaphoreType.DMA((2,))],
        compiler_params=params(4),
        cost_estimate=cost(2**24, 2**19),
        name="sight",
    )(*in_hbm(small + [beside]))


def attend_kernel(
    heads, scale, lead_at, plan_ref, queries_ref, keys_ref, values_ref, sight_ref, beside_ref,
    out_ref, stacked_ref, probs_ref,
):
    rows = queries_ref.shape[0]
    key_count, head_size = keys_ref.shape
    seg_count = sight_ref.shape[0]
    width = heads * head_size
    info = queries_ref[:, width:].astype(f32)
    own_seg = info[:, :1].astype(jnp.int32)
    onehot = as_bf16(own_seg == lane_ids((rows, seg_count)))
    seen = dot(onehot, sight_ref[...]) > 0.5
    place = (rows, key_count)
    causal = lane_ids(place) - row_ids(place) <= plan_ref[lead_at]
    bias = jnp.where(seen & causal, 0.0, masked_score)
    for head in range(heads):
        columns = slice(head * head_size, (head + 1) * head_size)
        stacked_ref[head * rows : (head + 1) * rows, :] = queries_ref[:, columns]
    scores = dot(stacked_ref[...], keys_ref[...], ((1,), (1,)))
    stats = jnp.zeros((rows, LANES), f32)
    lane = lane_ids((rows, LANES))
    for head in range(heads):
        here = slice(head * rows, (head + 1) * rows)
        biased = scores[here, :] + bias
        high = jnp.maximum(jnp.max(biased, axis=1, keepdims=True), least_high)
        high = high.astype(bf16).astype(f32)
        probs = jnp.exp2((biased - high) * scale)
        total_high, total_low = in_two(jnp.sum(probs, axis=1, keepdims=True))
        probs_ref[here, :] = probs.astype(bf16)
        stats = jnp.where(lane == head, high, stats)
        stats = jnp.where(lane == heads + head, total_high, stats)
        stats = jnp.where(lane == 2 * heads + head, total_low, stats)
    out_ref[:, width:] = stats.astype(bf16)
    sums = dot(probs_ref[...], values_ref[...])
    for head in range(heads):
        columns = slice(head * head_size, (head + 1) * head_size)
        out_ref[:, columns] = sums[head * rows : (head + 1) * rows, :].astype(bf16)


def attend(plan, lead_at, queries, keys, values, sight, heads, scale, beside):
    rows, columns = queries.shape
    key_count, head_size = keys.shape
    work = rows * heads * key_count
    return pl.pallas_call(
        functools.partial(attend_kernel, heads, scale, lead_at),
        in_specs=[whole(pltpu.SMEM)] + [whole()] * 4 + [whole(pltpu.HBM)],
        out_shape=jax.ShapeDtypeStruct((rows, columns), bf16),
        scratch_shapes=[
            pltpu.VMEM((rows * heads, head_size), bf16),
            pltpu.VMEM((rows * heads, key_count), bf16),
        ],
        compiler_params=params(8),
        cost_estimate=cost(8 * work * head_size, 2**20, work),
        name="attend",
    )(plan, queries, keys, values, sight, *in_hbm([beside]))


def project_kernel(heads, scale, order_at, source_count, plan_ref, *refs):
    parts_refs, weight_ref = refs[:source_count], refs[source_count]
    out_refs, attention_ref = refs[source_count + 1 : -1], refs[-1]
    width = attention_ref.shape[1]
    head_size = width // heads
    stats = [ref[:, width:].astype(f32) for ref in parts_refs]
    top = functools.reduce(jnp.maximum, stats)
    factors = [jnp.exp2(jnp.minimum((stat - top) * scale, 0.0)) for stat in stats]
    total = 0.0
    for stat, factor in zip(stats, factors):
        high = pltpu.roll(stat, LANES - heads, 1)
        low = pltpu.roll(stat, LANES - 2 * heads, 1)
        total = total + factor * (high + low)
    shares = [factor / total for factor in factors]
    for head in range(heads):
        columns = slice(head * head_size, (head + 1) * head_size)
        merged = 0.0
        for ref, share in zip(parts_refs, shares):
            merged = merged + ref[:, columns].astype(f32) * share[:, head : head + 1]
        attention_ref[:, columns] = merged.astype(bf16)
    for i, out_ref in enumerate(out_refs):
        piece_width = out_ref.shape[1]
        start = pl.multiple_of(plan_ref[order_at + i] * piece_width, piece_width)
        out_ref[...] = dot(attention_ref[...], weight_ref[:, pl.ds(start, piece_width)]).astype(bf16)


def project(plan, order_at, parts, weight, heads, scale, piece_count):
    rows = parts[0].shape[0]
    width, model_width = weight.shape
    piece_width = model_width // piece_count
    return pl.pallas_call(
        functools.partial(project_kernel, heads, scale, order_at, len(parts)),
        in_specs=[whole(pltpu.SMEM)] + [whole()] * (len(parts) + 1),
        out_shape=[jax.ShapeDtypeStruct((rows, piece_width), bf16)] * piece_count,
        scratch_shapes=[pltpu.VMEM((rows, width), bf16)],
        compiler_params=params(8),
        cost_estimate=cost(2 * rows * width * model_width, 2 * width * model_width),
        name="project",
    )(plan, *parts, weight)


def mix_kernel(residual_ref, gain_ref, *refs):
    parts_refs, (mixed_ref, sent_ref) = refs[:-2], refs[-2:]
    rows, width = mixed_ref.shape
    mixed = residual_ref[...].astype(f32)
    for ref in parts_refs:
        mixed = mixed + ref[...].astype(f32)
    mixed_ref[...] = mixed
    sent_ref[:, :width] = (mixed * gain_ref[...].astype(f32)).astype(bf16)
    high, low = in_two(jnp.sum(mixed * mixed, axis=1, keepdims=True))
    lane = lane_ids((rows, LANES))
    squares = jnp.where(lane == 0, high, jnp.where(lane == 1, low, 0.0))
    sent_ref[:, width:] = squares.astype(bf16)


def mix(residual, gain, parts):
    rows, width = residual.shape
    return pl.pallas_call(
        mix_kernel,
        out_shape=(
            jax.ShapeDtypeStruct((rows, width), f32),
            jax.ShapeDtypeStruct((rows, width + LANES), bf16),
        ),
        compiler_params=params(4),
        name="mix",
    )(residual, gain[None, :], *parts)


def route_kernel(local_experts, choices, width, first_at, plan_ref, *refs):
    info_refs, (place_ref, high_ref, low_ref) = refs[:-3], refs[-3:]
    piece_count, tokens, slots = place_ref.shape
    info = jnp.concatenate([ref[:, width:] for ref in info_refs], axis=0).astype(f32)
    expert = (lane_ids((tokens, local_experts)) + plan_ref[first_at]).astype(f32)
    member = jnp.zeros((tokens, local_experts), f32)
    weight_high = jnp.zeros((tokens, local_experts), f32)
    weight_low = jnp.zeros((tokens, local_experts), f32)
    for k in range(choices):
        chosen = info[:, 1 + k : 2 + k] == expert
        high = info[:, 1 + choices + k : 2 + choices + k]
        low = info[:, 1 + 2 * choices + k : 2 + 2 * choices + k]
        member = jnp.where(chosen, 1.0, member)
        weight_high = jnp.where(chosen, high, weight_high)
        weight_low = jnp.where(chosen, low, weight_low)
    square = (tokens, tokens)
    earlier = as_bf16(lane_ids(square) < row_ids(square))
    rank = jnp.where(member > 0.5, dot(earlier, member.astype(bf16)), -1.0).astype(bf16)
    weight_high = weight_high.astype(bf16)
    weight_low = weight_low.astype(bf16)
    capacity = piece_count * slots // local_experts
    for piece in range(piece_count):
        slot = lane_ids((local_experts, slots)) + piece * slots
        spread = as_bf16(slot // capacity == row_ids((local_experts, slots)))
        wanted = (lane_ids((tokens, slots)) + piece * slots) % capacity
        placed = dot(rank, spread) == wanted.astype(f32)
        place_ref[piece] = jnp.where(placed, 1.0, 0.0).astype(bf16)
        high_ref[piece] = jnp.where(placed, dot(weight_high, spread), 0.0).astype(bf16)
        low_ref[piece] = jnp.where(placed, dot(weight_low, spread), 0.0).astype(bf16)


def route(plan, first_at, packed, width, local_experts, choices, piece_count, slots):
    tokens = sum(value.shape[0] for value in packed)
    shape = jax.ShapeDtypeStruct((piece_count, tokens, slots), bf16)
    return pl.pallas_call(
        functools.partial(route_kernel, local_experts, choices, width, first_at),
        in_specs=[whole(pltpu.SMEM)] + [whole()] * len(packed),
        out_shape=(shape, shape, shape),
        compiler_params=params(16),
        cost_estimate=cost(2**25, 2**20),
        name="route",
    )(plan, *packed)


def pick_kernel(beside_ref, place_ref, *refs):
    rows_refs, (out_ref, rows_ref) = refs[:-2], refs[-2:]
    rows = rows_refs[0].shape[0]
    for i, ref in enumerate(rows_refs):
        rows_ref[i * rows : (i + 1) * rows, :] = ref[...]
    for piece in range(out_ref.shape[0]):
        out_ref[piece] = dot(place_ref[piece], rows_ref[...], ((0,), (0,))).astype(bf16)


def pick(place, rows, beside):
    piece_count, tokens, slots = place.shape
    columns = rows[0].shape[1]
    return pl.pallas_call(
        pick_kernel,
        in_specs=[whole(pltpu.HBM)] + [whole()] * (1 + len(rows)),
        out_shape=jax.ShapeDtypeStruct((piece_count, slots, columns), bf16),
        scratch_shapes=[pltpu.VMEM((tokens, columns), bf16)],
        compiler_params=params(8),
        cost_estimate=cost(2**26, 2**20),
        name="pick",
    )(*in_hbm([beside]), place, *rows)


def squares_joined(squares):
    high, low = in_two(squares[:, :1] + squares[:, 1:2])
    lane = lane_ids(squares.shape)
    return jnp.where(lane == 0, high, jnp.where(lane == 1, low, 0.0))


def gate_up(plan, piece_at, expert_at, spread, picked, weight):
    piece_count, slots, _ = picked.shape
    local_experts, width, ff_pair = weight.shape
    experts = max(1, local_experts // piece_count)
    rows = slots // experts

    def kernel(plan_ref, picked_ref, weight_ref, out_ref):
        piece = plan_ref[piece_at]
        first = plan_ref[expert_at] // spread
        for i in range(experts):
            here = slice(i * rows, (i + 1) * rows)
            picked = picked_ref[piece, here, :]
            out_ref[here, :ff_pair] = dot(picked[:, :width], weight_ref[first + i]).astype(bf16)
            out_ref[here, ff_pair:] = picked[:, width:]

    return pl.pallas_call(
        kernel,
        in_specs=[whole(pltpu.SMEM)] + [whole()] * 2,
        out_shape=jax.ShapeDtypeStruct((slots, ff_pair + LANES), bf16),
        compiler_params=params(8),
        cost_estimate=cost(2 * slots * width * ff_pair, 2 * experts * width * ff_pair),
        name="gate_up",
    )(plan, picked, weight)


def join_kernel(left_ref, right_ref, out_ref):
    ff_pair = out_ref.shape[1] - LANES
    product = left_ref[:, :ff_pair].astype(f32) + right_ref[:, :ff_pair].astype(f32)
    out_ref[:, :ff_pair] = product.astype(bf16)
    squares = left_ref[:, ff_pair:].astype(f32) + right_ref[:, ff_pair:].astype(f32)
    out_ref[:, ff_pair:] = squares_joined(squares).astype(bf16)


def join(left, right):
    return pl.pallas_call(
        join_kernel,
        out_shape=jax.ShapeDtypeStruct(left.shape, bf16),
        compiler_params=params(4),
        name="join",
    )(left, right)


def hidden_kernel(part_count, model_width, *refs):
    out_ref = refs[-1]
    ff_width = out_ref.shape[1]
    refs = refs[1:]
    total = refs[0][...].astype(f32)
    for ref in refs[1:part_count]:
        total = total + ref[...].astype(f32)
    squares = total[:, 2 * ff_width : 2 * ff_width + 1] + total[:, 2 * ff_width + 1 : 2 * ff_width + 2]
    norm = lax.rsqrt(squares / model_width + epsilon)
    gate = total[:, :ff_width] * norm
    up = total[:, ff_width : 2 * ff_width] * norm
    out_ref[...] = (gate / (1.0 + jnp.exp(-gate)) * up).astype(bf16)


def hidden_of(parts, ff_width, model_width, beside):
    return pl.pallas_call(
        functools.partial(hidden_kernel, len(parts), model_width),
        in_specs=[whole(pltpu.HBM)] + [whole()] * len(parts),
        out_shape=jax.ShapeDtypeStruct((parts[0].shape[0], ff_width), bf16),
        compiler_params=params(8),
        name="hidden",
    )(*in_hbm([beside]), *parts)


def down(plan, piece_at, expert_at, spread, hidden, weight, high, low, total=None, out_count=1):
    slots, ff_width = hidden.shape
    piece_count, tokens, _ = high.shape
    local_experts, _, piece_width = weight.shape
    experts = max(1, local_experts // piece_count)
    each = slots // experts
    rows = tokens // out_count
    out_type = f32 if out_count == 1 else bf16

    def kernel(plan_ref, hidden_ref, weight_ref, high_ref, low_ref, *refs):
        total_refs, out_refs, held_ref = refs[: -1 - out_count], refs[-1 - out_count : -1], refs[-1]
        piece = plan_ref[piece_at]
        first = plan_ref[expert_at] // spread
        for i in range(experts):
            here = slice(i * each, (i + 1) * each)
            held_ref[here, :] = dot(hidden_ref[here, :], weight_ref[first + i]).astype(bf16)
        held = held_ref[...]
        summed = dot(high_ref[piece], held) + dot(low_ref[piece], held)
        for ref in total_refs:
            summed = summed + ref[...]
        for i, ref in enumerate(out_refs):
            ref[...] = summed[i * rows : (i + 1) * rows, :].astype(ref.dtype)

    before = [] if total is None else [total]
    return pl.pallas_call(
        kernel,
        in_specs=[whole(pltpu.SMEM)] + [whole()] * (4 + len(before)),
        out_shape=[jax.ShapeDtypeStruct((rows, piece_width), out_type)] * out_count,
        scratch_shapes=[pltpu.VMEM((slots, piece_width), bf16)],
        compiler_params=params(8),
        cost_estimate=cost(2 * slots * ff_width * piece_width, 2 * experts * ff_width * piece_width),
        name="down",
    )(plan, hidden, weight, high, low, *before)


def finish_kernel(mixed_ref, *refs):
    total = mixed_ref[...]
    for ref in refs[:-1]:
        total = total + ref[...].astype(f32)
    refs[-1][...] = total.astype(bf16)


def finish(mixed, parts):
    return pl.pallas_call(
        finish_kernel,
        out_shape=jax.ShapeDtypeStruct(mixed.shape, bf16),
        compiler_params=params(4),
        name="finish",
    )(mixed, *parts)


def body(
    queries,
    cached_keys,
    cached_values,
    key_seg,
    query_seg,
    parent,
    out_weight,
    residual,
    norm_gain,
    gate_up_weight,
    down_weight,
    expert_ids,
    route_weight,
):
    ctx_count, exp_count, tp_count = (lax.axis_size(axis) for axis in ("ctx", "exp", "tp"))
    own_ctx, own_exp, own_tp = (lax.axis_index(axis) for axis in ("ctx", "exp", "tp"))
    assert tp_count == 2 and cached_keys.shape[1] == 1
    assert ctx_count & (ctx_count - 1) == 0 and exp_count & (exp_count - 1) == 0
    piece_count = exp_count * tp_count
    query_rows = queries.shape[0]
    key_count, _, head_size = cached_keys.shape
    heads = queries.shape[2] // head_size
    width = heads * head_size
    model_width = out_weight.shape[2]
    local_experts, piece_width, _ = gate_up_weight.shape
    ff_width = down_weight.shape[1]
    choices = expert_ids.shape[1]
    slots = local_experts * ctx_count * MOST // piece_count
    scale = math.log2(math.e) / math.sqrt(head_size)

    last = ctx_count * (key_count - query_rows) - own_ctx * key_count
    leads = [last + (own_ctx ^ k) * query_rows for k in range(ctx_count)]
    own_piece = own_exp * tp_count + own_tp
    column_pieces = [own_piece ^ k for k in range(piece_count)]
    slot_pieces = [
        (own_tp ^ flip) * exp_count + (own_exp ^ k) for flip in (0, 1) for k in range(exp_count)
    ]
    capacity = ctx_count * MOST
    experts = max(1, slots // capacity)
    spread = max(1, capacity // slots)
    scalars = [own_ctx * local_experts] + leads + column_pieces + slot_pieces
    scalars = scalars + [piece * experts for piece in slot_pieces]
    plan = jnp.stack([jnp.asarray(value, jnp.int32) for value in scalars])
    lead_at = 1
    order_at = lead_at + ctx_count
    mine_at = order_at + piece_count
    away_at = mine_at + exp_count
    expert_at = piece_count

    packed = pack(
        queries.reshape(query_rows, width), query_seg, expert_ids, route_weight, gate_up_weight
    )
    gathered = {0: packed}
    for k in far_first(ctx_count):
        gathered[k] = swapped(packed, "ctx", k)
    sight = sight_of(parent, key_seg, gate_up_weight)
    keys = cached_keys.reshape(key_count, head_size)
    values = cached_values.reshape(key_count, head_size)
    out_matrix = out_weight.reshape(width, model_width)
    parts = {}
    for k in list(range(1, ctx_count)) + [0]:
        part = attend(
            plan, lead_at + k, gathered[k], keys, values, sight, heads, scale, gate_up_weight
        )
        parts[k] = swapped(part, "ctx", k) if k else part
    place, combine_high, combine_low = route(
        plan,
        0,
        [gathered[k] for k in range(ctx_count)],
        width,
        local_experts,
        choices,
        piece_count,
        slots,
    )
    projected = project(
        plan,
        order_at,
        [parts[k] for k in range(ctx_count)],
        out_matrix,
        heads,
        scale,
        piece_count,
    )
    pieces = [projected[0]] + [
        swapped(projected[k], ("exp", "tp"), k) for k in far_first(piece_count)
    ]
    mixed, sent = mix(residual, norm_gain, pieces)
    rows = {0: sent}
    for k in far_first(ctx_count):
        rows[k] = swapped(sent, "ctx", k)
    picked = pick(place, [rows[k] for k in range(ctx_count)], gate_up_weight)

    def first_half(piece_at):
        return gate_up(plan, piece_at, piece_at + expert_at, spread, picked, gate_up_weight)

    finals = []
    for k in far_first(exp_count) + [0]:
        arrived = swapped(first_half(away_at + k), "tp", 1)
        mine = first_half(mine_at + k)
        if k:
            joined = join(mine, arrived)
            finals.append(swapped(joined, "exp", k))
            picked, _ = lax.optimization_barrier((picked, joined))
        else:
            finals, mine = lax.optimization_barrier((finals, mine))
            finals = [arrived, mine] + finals
    own_hidden = hidden_of(finals, ff_width, model_width, gate_up_weight)

    total = None
    for k in range(exp_count):
        here = own_hidden
        if k:
            here, total = lax.optimization_barrier((swapped(own_hidden, "exp", k), total))
        there = swapped(here, "tp", 1)
        for piece_at, hidden in ((mine_at + k, here), (away_at + k, there)):
            ends = piece_at == away_at + exp_count - 1
            totals = down(
                plan,
                piece_at,
                piece_at + expert_at,
                spread,
                hidden,
                down_weight,
                combine_high,
                combine_low,
                total,
                ctx_count if ends else 1,
            )
            total = totals[0]
    returned = [totals[0]] + [swapped(totals[k], "ctx", k) for k in far_first(ctx_count)]
    return finish(mixed, returned)


def solution(mesh):
    in_specs = (
        P(("group", "ctx"), "tp", "exp"),
        P(("group", "ctx"), "tp", None),
        P(("group", "ctx"), "tp", None),
        P(("group", "ctx")),
        P(("group", "ctx")),
        P("group"),
        P("tp", "exp", None),
        P(("group", "ctx"), ("exp", "tp")),
        P(("exp", "tp")),
        P("ctx", ("exp", "tp"), None),
        P("ctx", None, ("exp", "tp")),
        P(("group", "ctx"), None),
        P(("group", "ctx"), None),
    )
    out_specs = P(("group", "ctx"), ("exp", "tp"))
    return jax.shard_map(body, mesh=mesh, in_specs=in_specs, out_specs=out_specs, check_vma=False)
```

```python
import functools
import math

import jax
import jax.numpy as jnp
from jax import lax
from jax.experimental import pallas as pl
from jax.experimental.pallas import tpu as pltpu
from jax.sharding import PartitionSpec as P

MOST = 8
DEPTH = 6
LANES = 128

epsilon = 1e-06
masked_score = -1e30
least_high = -1e20

f32 = jnp.float32
bf16 = jnp.bfloat16


def params(megabytes, steps=0):
    semantics = ("arbitrary",) * steps if steps else None
    return pltpu.CompilerParams(
        vmem_limit_bytes=megabytes * 1024 * 1024, dimension_semantics=semantics
    )


def cost(flops, bytes_accessed, transcendentals=0):
    return pl.CostEstimate(
        flops=flops, bytes_accessed=bytes_accessed, transcendentals=transcendentals
    )


def whole(memory_space=pltpu.VMEM):
    return pl.BlockSpec(memory_space=memory_space)


def in_hbm(values):
    return [pltpu.with_memory_space_constraint(value, pltpu.HBM) for value in values]


def lane_ids(shape):
    return lax.broadcasted_iota(jnp.int32, shape, len(shape) - 1)


def row_ids(shape):
    return lax.broadcasted_iota(jnp.int32, shape, len(shape) - 2)


def as_bf16(mask):
    return mask.astype(f32).astype(bf16)


def dot(left, right, dims=((1,), (0,))):
    return lax.dot_general(left, right, (dims, ((), ())), preferred_element_type=f32)


def in_two(value):
    high = value.astype(bf16).astype(f32)
    return high, value - high


def swapped(value, axes, mask):
    count = lax.axis_size(axes)
    pairs = [(source, source ^ mask) for source in range(count)]
    return lax.ppermute(value, axes, pairs)


def far_first(count):
    return list(range(count - 1, 0, -1))


def pack_kernel(
    queries_ref, seg_ref, ids_ref, weight_ref, beside_ref, out_ref,
    seg_here, ids_here, weight_here, done,
):
    rows, width = queries_ref.shape
    choices = ids_ref.shape[0]
    copies = [
        pltpu.make_async_copy(source, target, done.at[i])
        for i, (source, target) in enumerate(
            [
                (seg_ref, seg_here),
                (ids_ref, ids_here),
                (weight_ref, weight_here),
                (queries_ref, out_ref.at[:, :width]),
            ]
        )
    ]
    for copy in copies:
        copy.start()
    shape = (choices, LANES)

    def placed(value, first, last):
        to_lane = (lane_ids(shape) == row_ids(shape) + first) & (row_ids(shape) <= last)
        return dot(value.astype(bf16), as_bf16(to_lane), ((0,), (0,)))

    for copy in copies[:3]:
        copy.wait()
    segs = jnp.broadcast_to(seg_here[...], (choices, rows)).astype(f32)
    high, low = in_two(weight_here[...])
    info = placed(segs, 0, 0) + placed(ids_here[...].astype(f32), 1, choices)
    info = info + placed(high, 1 + choices, choices) + placed(low, 1 + 2 * choices, choices)
    out_ref[:, width:] = info.astype(bf16)
    copies[3].wait()


def pack(queries, query_seg, expert_ids, route_weight, beside):
    rows, width = queries.shape
    small = [query_seg[None, :], expert_ids.T, route_weight.T]
    return pl.pallas_call(
        pack_kernel,
        in_specs=[whole(pltpu.HBM)] * 5,
        out_shape=jax.ShapeDtypeStruct((rows, width + LANES), bf16),
        scratch_shapes=[pltpu.VMEM(value.shape, value.dtype) for value in small]
        + [pltpu.SemaphoreType.DMA((4,))],
        compiler_params=params(4),
        name="pack",
    )(*in_hbm([queries] + small + [beside]))


def sight_kernel(parent_ref, key_seg_ref, beside_ref, sight_ref, parent_here, key_seg_here, done):
    copies = [
        pltpu.make_async_copy(parent_ref, parent_here, done.at[0]),
        pltpu.make_async_copy(key_seg_ref, key_seg_here, done.at[1]),
    ]
    for copy in copies:
        copy.start()
    for copy in copies:
        copy.wait()
    seg_count, key_count = sight_ref.shape
    square = (seg_count, seg_count)
    same = row_ids(square) == lane_ids(square)
    one = as_bf16((parent_here[...] == row_ids(square)) | same)
    two = as_bf16(dot(one, one) > 0.5)
    four = as_bf16(dot(two, two) > 0.5)
    six = as_bf16(dot(four, two) > 0.5)
    keys = as_bf16(key_seg_here[...] == row_ids((seg_count, key_count)))
    sight_ref[...] = dot(six, keys, ((0,), (0,))).astype(bf16)


def sight_of(parent, key_seg, beside):
    assert DEPTH == 6
    small = [parent[None, :], key_seg[None, :]]
    return pl.pallas_call(
        sight_kernel,
        in_specs=[whole(pltpu.HBM)] * 3,
        out_shape=jax.ShapeDtypeStruct((parent.shape[0], key_seg.shape[0]), bf16),
        scratch_shapes=[pltpu.VMEM(value.shape, value.dtype) for value in small]
        + [pltpu.SemaphoreType.DMA((2,))],
        compiler_params=params(4),
        cost_estimate=cost(2**24, 2**19),
        name="sight",
    )(*in_hbm(small + [beside]))


def attend_kernel(
    heads, scale, lead_at, plan_ref, queries_ref, keys_ref, values_ref, sight_ref, beside_ref,
    out_ref, stacked_ref, probs_ref,
):
    rows = queries_ref.shape[0]
    key_count, head_size = keys_ref.shape
    seg_count = sight_ref.shape[0]
    width = heads * head_size
    info = queries_ref[:, width:].astype(f32)
    own_seg = info[:, :1].astype(jnp.int32)
    onehot = as_bf16(own_seg == lane_ids((rows, seg_count)))
    seen = dot(onehot, sight_ref[...]) > 0.5
    place = (rows, key_count)
    causal = lane_ids(place) - row_ids(place) <= plan_ref[lead_at]
    bias = jnp.where(seen & causal, 0.0, masked_score)
    for head in range(heads):
        columns = slice(head * head_size, (head + 1) * head_size)
        stacked_ref[head * rows : (head + 1) * rows, :] = queries_ref[:, columns]
    scores = dot(stacked_ref[...], keys_ref[...], ((1,), (1,)))
    stats = jnp.zeros((rows, LANES), f32)
    lane = lane_ids((rows, LANES))
    for head in range(heads):
        here = slice(head * rows, (head + 1) * rows)
        biased = scores[here, :] + bias
        high = jnp.maximum(jnp.max(biased, axis=1, keepdims=True), least_high)
        high = high.astype(bf16).astype(f32)
        probs = jnp.exp2((biased - high) * scale)
        total_high, total_low = in_two(jnp.sum(probs, axis=1, keepdims=True))
        probs_ref[here, :] = probs.astype(bf16)
        stats = jnp.where(lane == head, high, stats)
        stats = jnp.where(lane == heads + head, total_high, stats)
        stats = jnp.where(lane == 2 * heads + head, total_low, stats)
    out_ref[:, width:] = stats.astype(bf16)
    sums = dot(probs_ref[...], values_ref[...])
    for head in range(heads):
        columns = slice(head * head_size, (head + 1) * head_size)
        out_ref[:, columns] = sums[head * rows : (head + 1) * rows, :].astype(bf16)


def attend(plan, lead_at, queries, keys, values, sight, heads, scale, beside):
    rows, columns = queries.shape
    key_count, head_size = keys.shape
    work = rows * heads * key_count
    return pl.pallas_call(
        functools.partial(attend_kernel, heads, scale, lead_at),
        in_specs=[whole(pltpu.SMEM)] + [whole()] * 4 + [whole(pltpu.HBM)],
        out_shape=jax.ShapeDtypeStruct((rows, columns), bf16),
        scratch_shapes=[
            pltpu.VMEM((rows * heads, head_size), bf16),
            pltpu.VMEM((rows * heads, key_count), bf16),
        ],
        compiler_params=params(8),
        cost_estimate=cost(8 * work * head_size, 2**20, work),
        name="attend",
    )(plan, queries, keys, values, sight, *in_hbm([beside]))


def project_kernel(heads, scale, order_at, source_count, plan_ref, *refs):
    parts_refs, weight_ref = refs[:source_count], refs[source_count]
    out_refs, attention_ref = refs[source_count + 1 : -1], refs[-1]
    width = attention_ref.shape[1]
    head_size = width // heads
    stats = [ref[:, width:].astype(f32) for ref in parts_refs]
    top = functools.reduce(jnp.maximum, stats)
    factors = [jnp.exp2(jnp.minimum((stat - top) * scale, 0.0)) for stat in stats]
    total = 0.0
    for stat, factor in zip(stats, factors):
        high = pltpu.roll(stat, LANES - heads, 1)
        low = pltpu.roll(stat, LANES - 2 * heads, 1)
        total = total + factor * (high + low)
    shares = [factor / total for factor in factors]
    for head in range(heads):
        columns = slice(head * head_size, (head + 1) * head_size)
        merged = 0.0
        for ref, share in zip(parts_refs, shares):
            merged = merged + ref[:, columns].astype(f32) * share[:, head : head + 1]
        attention_ref[:, columns] = merged.astype(bf16)
    for i, out_ref in enumerate(out_refs):
        piece_width = out_ref.shape[1]
        start = pl.multiple_of(plan_ref[order_at + i] * piece_width, piece_width)
        out_ref[...] = dot(attention_ref[...], weight_ref[:, pl.ds(start, piece_width)]).astype(bf16)


def project(plan, order_at, parts, weight, heads, scale, piece_count):
    rows = parts[0].shape[0]
    width, model_width = weight.shape
    piece_width = model_width // piece_count
    return pl.pallas_call(
        functools.partial(project_kernel, heads, scale, order_at, len(parts)),
        in_specs=[whole(pltpu.SMEM)] + [whole()] * (len(parts) + 1),
        out_shape=[jax.ShapeDtypeStruct((rows, piece_width), bf16)] * piece_count,
        scratch_shapes=[pltpu.VMEM((rows, width), bf16)],
        compiler_params=params(8),
        cost_estimate=cost(2 * rows * width * model_width, 2 * width * model_width),
        name="project",
    )(plan, *parts, weight)


def mix_kernel(residual_ref, gain_ref, *refs):
    parts_refs, (mixed_ref, sent_ref) = refs[:-2], refs[-2:]
    rows, width = mixed_ref.shape
    mixed = residual_ref[...].astype(f32)
    for ref in parts_refs:
        mixed = mixed + ref[...].astype(f32)
    mixed_ref[...] = mixed
    sent_ref[:, :width] = (mixed * gain_ref[...].astype(f32)).astype(bf16)
    high, low = in_two(jnp.sum(mixed * mixed, axis=1, keepdims=True))
    lane = lane_ids((rows, LANES))
    squares = jnp.where(lane == 0, high, jnp.where(lane == 1, low, 0.0))
    sent_ref[:, width:] = squares.astype(bf16)


def mix(residual, gain, parts):
    rows, width = residual.shape
    return pl.pallas_call(
        mix_kernel,
        out_shape=(
            jax.ShapeDtypeStruct((rows, width), f32),
            jax.ShapeDtypeStruct((rows, width + LANES), bf16),
        ),
        compiler_params=params(4),
        name="mix",
    )(residual, gain[None, :], *parts)


def route_kernel(local_experts, choices, width, first_at, plan_ref, *refs):
    info_refs, (place_ref, high_ref, low_ref) = refs[:-3], refs[-3:]
    piece_count, tokens, slots = place_ref.shape
    info = jnp.concatenate([ref[:, width:] for ref in info_refs], axis=0).astype(f32)
    expert = (lane_ids((tokens, local_experts)) + plan_ref[first_at]).astype(f32)
    member = jnp.zeros((tokens, local_experts), f32)
    weight_high = jnp.zeros((tokens, local_experts), f32)
    weight_low = jnp.zeros((tokens, local_experts), f32)
    for k in range(choices):
        chosen = info[:, 1 + k : 2 + k] == expert
        high = info[:, 1 + choices + k : 2 + choices + k]
        low = info[:, 1 + 2 * choices + k : 2 + 2 * choices + k]
        member = jnp.where(chosen, 1.0, member)
        weight_high = jnp.where(chosen, high, weight_high)
        weight_low = jnp.where(chosen, low, weight_low)
    square = (tokens, tokens)
    earlier = as_bf16(lane_ids(square) < row_ids(square))
    rank = jnp.where(member > 0.5, dot(earlier, member.astype(bf16)), -1.0).astype(bf16)
    weight_high = weight_high.astype(bf16)
    weight_low = weight_low.astype(bf16)
    capacity = piece_count * slots // local_experts
    for piece in range(piece_count):
        slot = lane_ids((local_experts, slots)) + piece * slots
        spread = as_bf16(slot // capacity == row_ids((local_experts, slots)))
        wanted = (lane_ids((tokens, slots)) + piece * slots) % capacity
        placed = dot(rank, spread) == wanted.astype(f32)
        place_ref[piece] = jnp.where(placed, 1.0, 0.0).astype(bf16)
        high_ref[piece] = jnp.where(placed, dot(weight_high, spread), 0.0).astype(bf16)
        low_ref[piece] = jnp.where(placed, dot(weight_low, spread), 0.0).astype(bf16)


def route(plan, first_at, packed, width, local_experts, choices, piece_count, slots):
    tokens = sum(value.shape[0] for value in packed)
    shape = jax.ShapeDtypeStruct((piece_count, tokens, slots), bf16)
    return pl.pallas_call(
        functools.partial(route_kernel, local_experts, choices, width, first_at),
        in_specs=[whole(pltpu.SMEM)] + [whole()] * len(packed),
        out_shape=(shape, shape, shape),
        compiler_params=params(16),
        cost_estimate=cost(2**25, 2**20),
        name="route",
    )(plan, *packed)


def pick_kernel(place_ref, *refs):
    rows_refs, (out_ref, rows_ref) = refs[:-2], refs[-2:]
    rows = rows_refs[0].shape[0]
    for i, ref in enumerate(rows_refs):
        rows_ref[i * rows : (i + 1) * rows, :] = ref[...]
    for piece in range(out_ref.shape[0]):
        out_ref[piece] = dot(place_ref[piece], rows_ref[...], ((0,), (0,))).astype(bf16)


def pick(place, rows):
    piece_count, tokens, slots = place.shape
    columns = rows[0].shape[1]
    return pl.pallas_call(
        pick_kernel,
        out_shape=jax.ShapeDtypeStruct((piece_count, slots, columns), bf16),
        scratch_shapes=[pltpu.VMEM((tokens, columns), bf16)],
        compiler_params=params(8),
        cost_estimate=cost(2**26, 2**20),
        name="pick",
    )(place, *rows)


def squares_joined(squares):
    high, low = in_two(squares[:, :1] + squares[:, 1:2])
    lane = lane_ids(squares.shape)
    return jnp.where(lane == 0, high, jnp.where(lane == 1, low, 0.0))


def gate_up(plan, piece_at, expert_at, spread, picked, weight):
    piece_count, slots, _ = picked.shape
    local_experts, width, ff_pair = weight.shape
    experts = max(1, local_experts // piece_count)
    rows = slots // experts

    def kernel(plan_ref, picked_ref, weight_ref, out_ref):
        piece = plan_ref[piece_at]
        first = plan_ref[expert_at] // spread
        for i in range(experts):
            here = slice(i * rows, (i + 1) * rows)
            picked = picked_ref[piece, here, :]
            out_ref[here, :ff_pair] = dot(picked[:, :width], weight_ref[first + i]).astype(bf16)
            out_ref[here, ff_pair:] = picked[:, width:]

    return pl.pallas_call(
        kernel,
        in_specs=[whole(pltpu.SMEM)] + [whole()] * 2,
        out_shape=jax.ShapeDtypeStruct((slots, ff_pair + LANES), bf16),
        compiler_params=params(8),
        cost_estimate=cost(2 * slots * width * ff_pair, 2 * experts * width * ff_pair),
        name="gate_up",
    )(plan, picked, weight)


def join_kernel(left_ref, right_ref, out_ref):
    ff_pair = out_ref.shape[1] - LANES
    product = left_ref[:, :ff_pair].astype(f32) + right_ref[:, :ff_pair].astype(f32)
    out_ref[:, :ff_pair] = product.astype(bf16)
    squares = left_ref[:, ff_pair:].astype(f32) + right_ref[:, ff_pair:].astype(f32)
    out_ref[:, ff_pair:] = squares_joined(squares).astype(bf16)


def join(left, right):
    return pl.pallas_call(
        join_kernel,
        out_shape=jax.ShapeDtypeStruct(left.shape, bf16),
        compiler_params=params(4),
        name="join",
    )(left, right)


def hidden_kernel(part_count, model_width, *refs):
    out_ref = refs[-1]
    ff_width = out_ref.shape[1]
    refs = refs[1:]
    total = refs[0][...].astype(f32)
    for ref in refs[1:part_count]:
        total = total + ref[...].astype(f32)
    squares = total[:, 2 * ff_width : 2 * ff_width + 1] + total[:, 2 * ff_width + 1 : 2 * ff_width + 2]
    norm = lax.rsqrt(squares / model_width + epsilon)
    gate = total[:, :ff_width] * norm
    up = total[:, ff_width : 2 * ff_width] * norm
    out_ref[...] = (gate / (1.0 + jnp.exp(-gate)) * up).astype(bf16)


def hidden_of(parts, ff_width, model_width, beside):
    return pl.pallas_call(
        functools.partial(hidden_kernel, len(parts), model_width),
        in_specs=[whole(pltpu.HBM)] + [whole()] * len(parts),
        out_shape=jax.ShapeDtypeStruct((parts[0].shape[0], ff_width), bf16),
        compiler_params=params(8),
        name="hidden",
    )(*in_hbm([beside]), *parts)


def down(plan, piece_at, expert_at, spread, hidden, weight, high, low, total=None, out_count=1):
    slots, ff_width = hidden.shape
    piece_count, tokens, _ = high.shape
    local_experts, _, piece_width = weight.shape
    experts = max(1, local_experts // piece_count)
    each = slots // experts
    rows = tokens // out_count
    out_type = f32 if out_count == 1 else bf16

    def kernel(plan_ref, hidden_ref, weight_ref, high_ref, low_ref, *refs):
        total_refs, out_refs, held_ref = refs[: -1 - out_count], refs[-1 - out_count : -1], refs[-1]
        piece = plan_ref[piece_at]
        first = plan_ref[expert_at] // spread
        for i in range(experts):
            here = slice(i * each, (i + 1) * each)
            held_ref[here, :] = dot(hidden_ref[here, :], weight_ref[first + i]).astype(bf16)
        held = held_ref[...]
        summed = dot(high_ref[piece], held) + dot(low_ref[piece], held)
        for ref in total_refs:
            summed = summed + ref[...]
        for i, ref in enumerate(out_refs):
            ref[...] = summed[i * rows : (i + 1) * rows, :].astype(ref.dtype)

    before = [] if total is None else [total]
    return pl.pallas_call(
        kernel,
        in_specs=[whole(pltpu.SMEM)] + [whole()] * (4 + len(before)),
        out_shape=[jax.ShapeDtypeStruct((rows, piece_width), out_type)] * out_count,
        scratch_shapes=[pltpu.VMEM((slots, piece_width), bf16)],
        compiler_params=params(8),
        cost_estimate=cost(2 * slots * ff_width * piece_width, 2 * experts * ff_width * piece_width),
        name="down",
    )(plan, hidden, weight, high, low, *before)


def finish_kernel(mixed_ref, *refs):
    total = mixed_ref[...]
    for ref in refs[:-1]:
        total = total + ref[...].astype(f32)
    refs[-1][...] = total.astype(bf16)


def finish(mixed, parts):
    return pl.pallas_call(
        finish_kernel,
        out_shape=jax.ShapeDtypeStruct(mixed.shape, bf16),
        compiler_params=params(4),
        name="finish",
    )(mixed, *parts)


def body(
    queries,
    cached_keys,
    cached_values,
    key_seg,
    query_seg,
    parent,
    out_weight,
    residual,
    norm_gain,
    gate_up_weight,
    down_weight,
    expert_ids,
    route_weight,
):
    ctx_count, exp_count, tp_count = (lax.axis_size(axis) for axis in ("ctx", "exp", "tp"))
    own_ctx, own_exp, own_tp = (lax.axis_index(axis) for axis in ("ctx", "exp", "tp"))
    assert tp_count == 2 and cached_keys.shape[1] == 1
    assert ctx_count & (ctx_count - 1) == 0 and exp_count & (exp_count - 1) == 0
    piece_count = exp_count * tp_count
    query_rows = queries.shape[0]
    key_count, _, head_size = cached_keys.shape
    heads = queries.shape[2] // head_size
    width = heads * head_size
    model_width = out_weight.shape[2]
    local_experts, piece_width, _ = gate_up_weight.shape
    ff_width = down_weight.shape[1]
    choices = expert_ids.shape[1]
    slots = local_experts * ctx_count * MOST // piece_count
    scale = math.log2(math.e) / math.sqrt(head_size)

    last = ctx_count * (key_count - query_rows) - own_ctx * key_count
    leads = [last + (own_ctx ^ k) * query_rows for k in range(ctx_count)]
    own_piece = own_exp * tp_count + own_tp
    column_pieces = [own_piece ^ k for k in range(piece_count)]
    slot_pieces = [
        (own_tp ^ flip) * exp_count + (own_exp ^ k) for flip in (0, 1) for k in range(exp_count)
    ]
    capacity = ctx_count * MOST
    experts = max(1, slots // capacity)
    spread = max(1, capacity // slots)
    scalars = [own_ctx * local_experts] + leads + column_pieces + slot_pieces
    scalars = scalars + [piece * experts for piece in slot_pieces]
    plan = jnp.stack([jnp.asarray(value, jnp.int32) for value in scalars])
    lead_at = 1
    order_at = lead_at + ctx_count
    mine_at = order_at + piece_count
    away_at = mine_at + exp_count
    expert_at = piece_count

    packed = pack(
        queries.reshape(query_rows, width), query_seg, expert_ids, route_weight, gate_up_weight
    )
    gathered = {0: packed}
    for k in far_first(ctx_count):
        gathered[k] = swapped(packed, "ctx", k)
    sight = sight_of(parent, key_seg, gate_up_weight)
    keys = cached_keys.reshape(key_count, head_size)
    values = cached_values.reshape(key_count, head_size)
    out_matrix = out_weight.reshape(width, model_width)
    parts = {}
    for k in list(range(1, ctx_count)) + [0]:
        part = attend(
            plan, lead_at + k, gathered[k], keys, values, sight, heads, scale, gate_up_weight
        )
        parts[k] = swapped(part, "ctx", k) if k else part
    place, combine_high, combine_low = route(
        plan,
        0,
        [gathered[k] for k in range(ctx_count)],
        width,
        local_experts,
        choices,
        piece_count,
        slots,
    )
    projected = project(
        plan,
        order_at,
        [parts[k] for k in range(ctx_count)],
        out_matrix,
        heads,
        scale,
        piece_count,
    )
    pieces = [projected[0]] + [
        swapped(projected[k], ("exp", "tp"), k) for k in far_first(piece_count)
    ]
    mixed, sent = mix(residual, norm_gain, pieces)
    rows = {0: sent}
    for k in far_first(ctx_count):
        rows[k] = swapped(sent, "ctx", k)
    picked = pick(place, [rows[k] for k in range(ctx_count)])

    def first_half(piece_at):
        return gate_up(plan, piece_at, piece_at + expert_at, spread, picked, gate_up_weight)

    finals = []
    for k in far_first(exp_count) + [0]:
        arrived = swapped(first_half(away_at + k), "tp", 1)
        mine = first_half(mine_at + k)
        if k:
            joined = join(mine, arrived)
            finals.append(swapped(joined, "exp", k))
            picked, _ = lax.optimization_barrier((picked, joined))
        else:
            finals, mine = lax.optimization_barrier((finals, mine))
            finals = [arrived, mine] + finals
    own_hidden = hidden_of(finals, ff_width, model_width, gate_up_weight)

    total = None
    for k in range(exp_count):
        here = own_hidden
        if k:
            here, total = lax.optimization_barrier((swapped(own_hidden, "exp", k), total))
        there = swapped(here, "tp", 1)
        for piece_at, hidden in ((mine_at + k, here), (away_at + k, there)):
            ends = piece_at == away_at + exp_count - 1
            totals = down(
                plan,
                piece_at,
                piece_at + expert_at,
                spread,
                hidden,
                down_weight,
                combine_high,
                combine_low,
                total,
                ctx_count if ends else 1,
            )
            total = totals[0]
    returned = [totals[0]] + [swapped(totals[k], "ctx", k) for k in far_first(ctx_count)]
    return finish(mixed, returned)


def solution(mesh):
    in_specs = (
        P(("group", "ctx"), "tp", "exp"),
        P(("group", "ctx"), "tp", None),
        P(("group", "ctx"), "tp", None),
        P(("group", "ctx")),
        P(("group", "ctx")),
        P("group"),
        P("tp", "exp", None),
        P(("group", "ctx"), ("exp", "tp")),
        P(("exp", "tp")),
        P("ctx", ("exp", "tp"), None),
        P("ctx", None, ("exp", "tp")),
        P(("group", "ctx"), None),
        P(("group", "ctx"), None),
    )
    out_specs = P(("group", "ctx"), ("exp", "tp"))
    return jax.shard_map(body, mesh=mesh, in_specs=in_specs, out_specs=out_specs, check_vma=False)
```

```python
import functools
import math

import jax
import jax.numpy as jnp
from jax import lax
from jax.experimental import pallas as pl
from jax.experimental.pallas import tpu as pltpu
from jax.sharding import PartitionSpec as P

MOST = 8
DEPTH = 6
LANES = 128

epsilon = 1e-06
masked_score = -1e30
least_high = -1e20

f32 = jnp.float32
bf16 = jnp.bfloat16


def params(megabytes, steps=0):
    semantics = ("arbitrary",) * steps if steps else None
    return pltpu.CompilerParams(
        vmem_limit_bytes=megabytes * 1024 * 1024, dimension_semantics=semantics
    )


def cost(flops, bytes_accessed, transcendentals=0):
    return pl.CostEstimate(
        flops=flops, bytes_accessed=bytes_accessed, transcendentals=transcendentals
    )


def whole(memory_space=pltpu.VMEM):
    return pl.BlockSpec(memory_space=memory_space)


def in_hbm(values):
    return [pltpu.with_memory_space_constraint(value, pltpu.HBM) for value in values]


def lane_ids(shape):
    return lax.broadcasted_iota(jnp.int32, shape, len(shape) - 1)


def row_ids(shape):
    return lax.broadcasted_iota(jnp.int32, shape, len(shape) - 2)


def as_bf16(mask):
    return mask.astype(f32).astype(bf16)


def dot(left, right, dims=((1,), (0,))):
    return lax.dot_general(left, right, (dims, ((), ())), preferred_element_type=f32)


def in_two(value):
    high = value.astype(bf16).astype(f32)
    return high, value - high


def swapped(value, axes, mask):
    count = lax.axis_size(axes)
    pairs = [(source, source ^ mask) for source in range(count)]
    return lax.ppermute(value, axes, pairs)


def far_first(count):
    return list(range(count - 1, 0, -1))


def pack_kernel(
    queries_ref, seg_ref, ids_ref, weight_ref, beside_ref, out_ref,
    seg_here, ids_here, weight_here, done,
):
    rows, width = queries_ref.shape
    choices = ids_ref.shape[0]
    copies = [
        pltpu.make_async_copy(source, target, done.at[i])
        for i, (source, target) in enumerate(
            [
                (seg_ref, seg_here),
                (ids_ref, ids_here),
                (weight_ref, weight_here),
                (queries_ref, out_ref.at[:, :width]),
            ]
        )
    ]
    for copy in copies:
        copy.start()
    shape = (choices, LANES)

    def placed(value, first, last):
        to_lane = (lane_ids(shape) == row_ids(shape) + first) & (row_ids(shape) <= last)
        return dot(value.astype(bf16), as_bf16(to_lane), ((0,), (0,)))

    for copy in copies[:3]:
        copy.wait()
    segs = jnp.broadcast_to(seg_here[...], (choices, rows)).astype(f32)
    high, low = in_two(weight_here[...])
    info = placed(segs, 0, 0) + placed(ids_here[...].astype(f32), 1, choices)
    info = info + placed(high, 1 + choices, choices) + placed(low, 1 + 2 * choices, choices)
    out_ref[:, width:] = info.astype(bf16)
    copies[3].wait()


def pack(queries, query_seg, expert_ids, route_weight, beside):
    rows, width = queries.shape
    small = [query_seg[None, :], expert_ids.T, route_weight.T]
    return pl.pallas_call(
        pack_kernel,
        in_specs=[whole(pltpu.HBM)] * 5,
        out_shape=jax.ShapeDtypeStruct((rows, width + LANES), bf16),
        scratch_shapes=[pltpu.VMEM(value.shape, value.dtype) for value in small]
        + [pltpu.SemaphoreType.DMA((4,))],
        compiler_params=params(4),
        name="pack",
    )(*in_hbm([queries] + small + [beside]))


def sight_kernel(parent_ref, key_seg_ref, beside_ref, sight_ref, parent_here, key_seg_here, done):
    copies = [
        pltpu.make_async_copy(parent_ref, parent_here, done.at[0]),
        pltpu.make_async_copy(key_seg_ref, key_seg_here, done.at[1]),
    ]
    for copy in copies:
        copy.start()
    for copy in copies:
        copy.wait()
    seg_count, key_count = sight_ref.shape
    square = (seg_count, seg_count)
    same = row_ids(square) == lane_ids(square)
    one = as_bf16((parent_here[...] == row_ids(square)) | same)
    two = as_bf16(dot(one, one) > 0.5)
    four = as_bf16(dot(two, two) > 0.5)
    six = as_bf16(dot(four, two) > 0.5)
    keys = as_bf16(key_seg_here[...] == row_ids((seg_count, key_count)))
    sight_ref[...] = dot(six, keys, ((0,), (0,))).astype(bf16)


def sight_of(parent, key_seg, beside):
    assert DEPTH == 6
    small = [parent[None, :], key_seg[None, :]]
    return pl.pallas_call(
        sight_kernel,
        in_specs=[whole(pltpu.HBM)] * 3,
        out_shape=jax.ShapeDtypeStruct((parent.shape[0], key_seg.shape[0]), bf16),
        scratch_shapes=[pltpu.VMEM(value.shape, value.dtype) for value in small]
        + [pltpu.SemaphoreType.DMA((2,))],
        compiler_params=params(4),
        cost_estimate=cost(2**24, 2**19),
        name="sight",
    )(*in_hbm(small + [beside]))


def attend_kernel(
    heads, scale, lead_at, plan_ref, queries_ref, keys_ref, values_ref, sight_ref, beside_ref,
    out_ref, stacked_ref, probs_ref,
):
    rows = queries_ref.shape[0]
    key_count, head_size = keys_ref.shape
    seg_count = sight_ref.shape[0]
    width = heads * head_size
    info = queries_ref[:, width:].astype(f32)
    own_seg = info[:, :1].astype(jnp.int32)
    onehot = as_bf16(own_seg == lane_ids((rows, seg_count)))
    seen = dot(onehot, sight_ref[...]) > 0.5
    place = (rows, key_count)
    causal = lane_ids(place) - row_ids(place) <= plan_ref[lead_at]
    bias = jnp.where(seen & causal, 0.0, masked_score)
    for head in range(heads):
        columns = slice(head * head_size, (head + 1) * head_size)
        stacked_ref[head * rows : (head + 1) * rows, :] = queries_ref[:, columns]
    scores = dot(stacked_ref[...], keys_ref[...], ((1,), (1,)))
    stats = jnp.zeros((rows, LANES), f32)
    lane = lane_ids((rows, LANES))
    for head in range(heads):
        here = slice(head * rows, (head + 1) * rows)
        biased = scores[here, :] + bias
        high = jnp.maximum(jnp.max(biased, axis=1, keepdims=True), least_high)
        high = high.astype(bf16).astype(f32)
        probs = jnp.exp2((biased - high) * scale)
        total_high, total_low = in_two(jnp.sum(probs, axis=1, keepdims=True))
        probs_ref[here, :] = probs.astype(bf16)
        stats = jnp.where(lane == head, high, stats)
        stats = jnp.where(lane == heads + head, total_high, stats)
        stats = jnp.where(lane == 2 * heads + head, total_low, stats)
    out_ref[:, width:] = stats.astype(bf16)
    sums = dot(probs_ref[...], values_ref[...])
    for head in range(heads):
        columns = slice(head * head_size, (head + 1) * head_size)
        out_ref[:, columns] = sums[head * rows : (head + 1) * rows, :].astype(bf16)


def attend(plan, lead_at, queries, keys, values, sight, heads, scale, beside):
    rows, columns = queries.shape
    key_count, head_size = keys.shape
    work = rows * heads * key_count
    return pl.pallas_call(
        functools.partial(attend_kernel, heads, scale, lead_at),
        in_specs=[whole(pltpu.SMEM)] + [whole()] * 4 + [whole(pltpu.HBM)],
        out_shape=jax.ShapeDtypeStruct((rows, columns), bf16),
        scratch_shapes=[
            pltpu.VMEM((rows * heads, head_size), bf16),
            pltpu.VMEM((rows * heads, key_count), bf16),
        ],
        compiler_params=params(8),
        cost_estimate=cost(8 * work * head_size, 2**20, work),
        name="attend",
    )(plan, queries, keys, values, sight, *in_hbm([beside]))


def merged(parts, heads, scale, width):
    head_size = width // heads
    tops = [part[2] for part in parts]
    top = functools.reduce(jnp.maximum, tops)
    factors = [jnp.exp2(jnp.minimum((each - top) * scale, 0.0)) for each in tops]
    total = sum(part[1] * factor for part, factor in zip(parts, factors))
    columns = []
    for head in range(heads):
        here = slice(head * head_size, (head + 1) * head_size)
        columns.append(
            sum(part[0](here) * factor[:, head : head + 1] for part, factor in zip(parts, factors))
        )
    return columns, total, top


def as_part(ref, heads, width):
    stats = ref[:, width:].astype(f32)
    total = pltpu.roll(stats, LANES - heads, 1) + pltpu.roll(stats, LANES - 2 * heads, 1)
    return (lambda here: ref[:, here].astype(f32), total, stats)


def merge_kernel(heads, scale, beside_ref, *refs):
    parts_refs, (sums_ref, total_ref, top_ref) = refs[:-3], refs[-3:]
    width = sums_ref.shape[1]
    head_size = width // heads
    parts = [as_part(ref, heads, width) for ref in parts_refs]
    columns, total_ref[...], top_ref[...] = merged(parts, heads, scale, width)
    for head, column in enumerate(columns):
        sums_ref[:, head * head_size : (head + 1) * head_size] = column


def merge(parts, heads, scale, width, beside):
    rows = parts[0].shape[0]
    narrow = jax.ShapeDtypeStruct((rows, LANES), f32)
    return pl.pallas_call(
        functools.partial(merge_kernel, heads, scale),
        in_specs=[whole(pltpu.HBM)] + [whole()] * len(parts),
        out_shape=(jax.ShapeDtypeStruct((rows, width), f32), narrow, narrow),
        compiler_params=params(8),
        name="merge",
    )(*in_hbm([beside]), *parts)


def project_kernel(
    heads, scale, order_at, plan_ref, sums_ref, total_ref, top_ref, part_ref, weight_ref, *refs
):
    out_refs, attention_ref = refs[:-1], refs[-1]
    width = attention_ref.shape[1]
    head_size = width // heads
    before = (lambda here: sums_ref[:, here], total_ref[...], top_ref[...])
    columns, total, _ = merged([before, as_part(part_ref, heads, width)], heads, scale, width)
    share = 1.0 / total
    for head, column in enumerate(columns):
        here = slice(head * head_size, (head + 1) * head_size)
        attention_ref[:, here] = (column * share[:, head : head + 1]).astype(bf16)
    for i, out_ref in enumerate(out_refs):
        piece_width = out_ref.shape[1]
        start = pl.multiple_of(plan_ref[order_at + i] * piece_width, piece_width)
        out_ref[...] = dot(attention_ref[...], weight_ref[:, pl.ds(start, piece_width)]).astype(bf16)


def project(plan, order_at, before, part, weight, heads, scale, piece_count):
    rows = part.shape[0]
    width, model_width = weight.shape
    piece_width = model_width // piece_count
    return pl.pallas_call(
        functools.partial(project_kernel, heads, scale, order_at),
        in_specs=[whole(pltpu.SMEM)] + [whole()] * 5,
        out_shape=[jax.ShapeDtypeStruct((rows, piece_width), bf16)] * piece_count,
        scratch_shapes=[pltpu.VMEM((rows, width), bf16)],
        compiler_params=params(8),
        cost_estimate=cost(2 * rows * width * model_width, 2 * width * model_width),
        name="project",
    )(plan, *before, part, weight)


def mix_kernel(residual_ref, gain_ref, *refs):
    parts_refs, (mixed_ref, sent_ref) = refs[:-2], refs[-2:]
    rows, width = mixed_ref.shape
    mixed = residual_ref[...].astype(f32)
    for ref in parts_refs:
        mixed = mixed + ref[...].astype(f32)
    mixed_ref[...] = mixed
    sent_ref[:, :width] = (mixed * gain_ref[...].astype(f32)).astype(bf16)
    high, low = in_two(jnp.sum(mixed * mixed, axis=1, keepdims=True))
    lane = lane_ids((rows, LANES))
    squares = jnp.where(lane == 0, high, jnp.where(lane == 1, low, 0.0))
    sent_ref[:, width:] = squares.astype(bf16)


def mix(residual, gain, parts):
    rows, width = residual.shape
    return pl.pallas_call(
        mix_kernel,
        out_shape=(
            jax.ShapeDtypeStruct((rows, width), f32),
            jax.ShapeDtypeStruct((rows, width + LANES), bf16),
        ),
        compiler_params=params(4),
        name="mix",
    )(residual, gain[None, :], *parts)


def route_kernel(local_experts, choices, width, first_at, plan_ref, *refs):
    info_refs, (place_ref, high_ref, low_ref) = refs[:-3], refs[-3:]
    piece_count, tokens, slots = place_ref.shape
    info = jnp.concatenate([ref[:, width:] for ref in info_refs], axis=0).astype(f32)
    expert = (lane_ids((tokens, local_experts)) + plan_ref[first_at]).astype(f32)
    member = jnp.zeros((tokens, local_experts), f32)
    weight_high = jnp.zeros((tokens, local_experts), f32)
    weight_low = jnp.zeros((tokens, local_experts), f32)
    for k in range(choices):
        chosen = info[:, 1 + k : 2 + k] == expert
        high = info[:, 1 + choices + k : 2 + choices + k]
        low = info[:, 1 + 2 * choices + k : 2 + 2 * choices + k]
        member = jnp.where(chosen, 1.0, member)
        weight_high = jnp.where(chosen, high, weight_high)
        weight_low = jnp.where(chosen, low, weight_low)
    square = (tokens, tokens)
    earlier = as_bf16(lane_ids(square) < row_ids(square))
    rank = jnp.where(member > 0.5, dot(earlier, member.astype(bf16)), -1.0).astype(bf16)
    weight_high = weight_high.astype(bf16)
    weight_low = weight_low.astype(bf16)
    capacity = piece_count * slots // local_experts
    for piece in range(piece_count):
        slot = lane_ids((local_experts, slots)) + piece * slots
        spread = as_bf16(slot // capacity == row_ids((local_experts, slots)))
        wanted = (lane_ids((tokens, slots)) + piece * slots) % capacity
        placed = dot(rank, spread) == wanted.astype(f32)
        place_ref[piece] = jnp.where(placed, 1.0, 0.0).astype(bf16)
        high_ref[piece] = jnp.where(placed, dot(weight_high, spread), 0.0).astype(bf16)
        low_ref[piece] = jnp.where(placed, dot(weight_low, spread), 0.0).astype(bf16)


def route(plan, first_at, packed, width, local_experts, choices, piece_count, slots):
    tokens = sum(value.shape[0] for value in packed)
    shape = jax.ShapeDtypeStruct((piece_count, tokens, slots), bf16)
    return pl.pallas_call(
        functools.partial(route_kernel, local_experts, choices, width, first_at),
        in_specs=[whole(pltpu.SMEM)] + [whole()] * len(packed),
        out_shape=(shape, shape, shape),
        compiler_params=params(16),
        cost_estimate=cost(2**25, 2**20),
        name="route",
    )(plan, *packed)


def pick_kernel(place_ref, *refs):
    rows_refs, (out_ref, rows_ref) = refs[:-2], refs[-2:]
    rows = rows_refs[0].shape[0]
    for i, ref in enumerate(rows_refs):
        rows_ref[i * rows : (i + 1) * rows, :] = ref[...]
    for piece in range(out_ref.shape[0]):
        out_ref[piece] = dot(place_ref[piece], rows_ref[...], ((0,), (0,))).astype(bf16)


def pick(place, rows):
    piece_count, tokens, slots = place.shape
    columns = rows[0].shape[1]
    return pl.pallas_call(
        pick_kernel,
        out_shape=jax.ShapeDtypeStruct((piece_count, slots, columns), bf16),
        scratch_shapes=[pltpu.VMEM((tokens, columns), bf16)],
        compiler_params=params(8),
        cost_estimate=cost(2**26, 2**20),
        name="pick",
    )(place, *rows)


def squares_joined(squares):
    high, low = in_two(squares[:, :1] + squares[:, 1:2])
    lane = lane_ids(squares.shape)
    return jnp.where(lane == 0, high, jnp.where(lane == 1, low, 0.0))


def gate_up(plan, piece_at, expert_at, spread, picked, weight):
    piece_count, slots, _ = picked.shape
    local_experts, width, ff_pair = weight.shape
    experts = max(1, local_experts // piece_count)
    rows = slots // experts

    def kernel(plan_ref, picked_ref, weight_ref, out_ref):
        piece = plan_ref[piece_at]
        first = plan_ref[expert_at] // spread
        for i in range(experts):
            here = slice(i * rows, (i + 1) * rows)
            picked = picked_ref[piece, here, :]
            out_ref[here, :ff_pair] = dot(picked[:, :width], weight_ref[first + i]).astype(bf16)
            out_ref[here, ff_pair:] = picked[:, width:]

    return pl.pallas_call(
        kernel,
        in_specs=[whole(pltpu.SMEM)] + [whole()] * 2,
        out_shape=jax.ShapeDtypeStruct((slots, ff_pair + LANES), bf16),
        compiler_params=params(8),
        cost_estimate=cost(2 * slots * width * ff_pair, 2 * experts * width * ff_pair),
        name="gate_up",
    )(plan, picked, weight)


def join_kernel(left_ref, right_ref, out_ref):
    ff_pair = out_ref.shape[1] - LANES
    product = left_ref[:, :ff_pair].astype(f32) + right_ref[:, :ff_pair].astype(f32)
    out_ref[:, :ff_pair] = product.astype(bf16)
    squares = left_ref[:, ff_pair:].astype(f32) + right_ref[:, ff_pair:].astype(f32)
    out_ref[:, ff_pair:] = squares_joined(squares).astype(bf16)


def join(left, right):
    return pl.pallas_call(
        join_kernel,
        out_shape=jax.ShapeDtypeStruct(left.shape, bf16),
        compiler_params=params(4),
        name="join",
    )(left, right)


def hidden_kernel(part_count, model_width, *refs):
    out_ref = refs[-1]
    ff_width = out_ref.shape[1]
    refs = refs[1:]
    total = refs[0][...].astype(f32)
    for ref in refs[1:part_count]:
        total = total + ref[...].astype(f32)
    squares = total[:, 2 * ff_width : 2 * ff_width + 1] + total[:, 2 * ff_width + 1 : 2 * ff_width + 2]
    norm = lax.rsqrt(squares / model_width + epsilon)
    gate = total[:, :ff_width] * norm
    up = total[:, ff_width : 2 * ff_width] * norm
    out_ref[...] = (gate / (1.0 + jnp.exp(-gate)) * up).astype(bf16)


def hidden_of(parts, ff_width, model_width, beside):
    return pl.pallas_call(
        functools.partial(hidden_kernel, len(parts), model_width),
        in_specs=[whole(pltpu.HBM)] + [whole()] * len(parts),
        out_shape=jax.ShapeDtypeStruct((parts[0].shape[0], ff_width), bf16),
        compiler_params=params(8),
        name="hidden",
    )(*in_hbm([beside]), *parts)


def down(plan, piece_at, expert_at, spread, hidden, weight, high, low, total=None, out_count=1):
    slots, ff_width = hidden.shape
    piece_count, tokens, _ = high.shape
    local_experts, _, piece_width = weight.shape
    experts = max(1, local_experts // piece_count)
    each = slots // experts
    rows = tokens // out_count
    out_type = f32 if out_count == 1 else bf16

    def kernel(plan_ref, hidden_ref, weight_ref, high_ref, low_ref, *refs):
        total_refs, out_refs, held_ref = refs[: -1 - out_count], refs[-1 - out_count : -1], refs[-1]
        piece = plan_ref[piece_at]
        first = plan_ref[expert_at] // spread
        for i in range(experts):
            here = slice(i * each, (i + 1) * each)
            held_ref[here, :] = dot(hidden_ref[here, :], weight_ref[first + i]).astype(bf16)
        held = held_ref[...]
        summed = dot(high_ref[piece], held) + dot(low_ref[piece], held)
        for ref in total_refs:
            summed = summed + ref[...]
        for i, ref in enumerate(out_refs):
            ref[...] = summed[i * rows : (i + 1) * rows, :].astype(ref.dtype)

    before = [] if total is None else [total]
    return pl.pallas_call(
        kernel,
        in_specs=[whole(pltpu.SMEM)] + [whole()] * (4 + len(before)),
        out_shape=[jax.ShapeDtypeStruct((rows, piece_width), out_type)] * out_count,
        scratch_shapes=[pltpu.VMEM((slots, piece_width), bf16)],
        compiler_params=params(8),
        cost_estimate=cost(2 * slots * ff_width * piece_width, 2 * experts * ff_width * piece_width),
        name="down",
    )(plan, hidden, weight, high, low, *before)


def finish_kernel(mixed_ref, *refs):
    total = mixed_ref[...]
    for ref in refs[:-1]:
        total = total + ref[...].astype(f32)
    refs[-1][...] = total.astype(bf16)


def finish(mixed, parts):
    return pl.pallas_call(
        finish_kernel,
        out_shape=jax.ShapeDtypeStruct(mixed.shape, bf16),
        compiler_params=params(4),
        name="finish",
    )(mixed, *parts)


def body(
    queries,
    cached_keys,
    cached_values,
    key_seg,
    query_seg,
    parent,
    out_weight,
    residual,
    norm_gain,
    gate_up_weight,
    down_weight,
    expert_ids,
    route_weight,
):
    ctx_count, exp_count, tp_count = (lax.axis_size(axis) for axis in ("ctx", "exp", "tp"))
    own_ctx, own_exp, own_tp = (lax.axis_index(axis) for axis in ("ctx", "exp", "tp"))
    assert tp_count == 2 and cached_keys.shape[1] == 1
    assert ctx_count & (ctx_count - 1) == 0 and exp_count & (exp_count - 1) == 0
    piece_count = exp_count * tp_count
    query_rows = queries.shape[0]
    key_count, _, head_size = cached_keys.shape
    heads = queries.shape[2] // head_size
    width = heads * head_size
    model_width = out_weight.shape[2]
    local_experts, piece_width, _ = gate_up_weight.shape
    ff_width = down_weight.shape[1]
    choices = expert_ids.shape[1]
    slots = local_experts * ctx_count * MOST // piece_count
    scale = math.log2(math.e) / math.sqrt(head_size)

    last = ctx_count * (key_count - query_rows) - own_ctx * key_count
    leads = [last + (own_ctx ^ k) * query_rows for k in range(ctx_count)]
    own_piece = own_exp * tp_count + own_tp
    column_pieces = [own_piece ^ k for k in range(piece_count)]
    slot_pieces = [
        (own_tp ^ flip) * exp_count + (own_exp ^ k) for flip in (0, 1) for k in range(exp_count)
    ]
    capacity = ctx_count * MOST
    experts = max(1, slots // capacity)
    spread = max(1, capacity // slots)
    scalars = [own_ctx * local_experts] + leads + column_pieces + slot_pieces
    scalars = scalars + [piece * experts for piece in slot_pieces]
    plan = jnp.stack([jnp.asarray(value, jnp.int32) for value in scalars])
    lead_at = 1
    order_at = lead_at + ctx_count
    mine_at = order_at + piece_count
    away_at = mine_at + exp_count
    expert_at = piece_count

    packed = pack(
        queries.reshape(query_rows, width), query_seg, expert_ids, route_weight, gate_up_weight
    )
    sight = sight_of(parent, key_seg, gate_up_weight)
    gathered = {0: packed}
    for k in far_first(ctx_count):
        gathered[k] = swapped(packed, "ctx", k)
    keys = cached_keys.reshape(key_count, head_size)
    values = cached_values.reshape(key_count, head_size)
    out_matrix = out_weight.reshape(width, model_width)
    parts = {}
    for k in range(ctx_count):
        part = attend(
            plan, lead_at + k, gathered[k], keys, values, sight, heads, scale, gate_up_weight
        )
        parts[k] = swapped(part, "ctx", k) if k else part
        sight, _ = lax.optimization_barrier((sight, part))
    place, combine_high, combine_low = route(
        plan,
        0,
        [gathered[k] for k in range(ctx_count)],
        width,
        local_experts,
        choices,
        piece_count,
        slots,
    )
    last_part = parts.pop(ctx_count - 1)
    before = merge(list(parts.values()), heads, scale, width, gate_up_weight)
    projected = project(
        plan, order_at, before, last_part, out_matrix, heads, scale, piece_count
    )
    pieces = [projected[0]] + [
        swapped(projected[k], ("exp", "tp"), k) for k in far_first(piece_count)
    ]
    mixed, sent = mix(residual, norm_gain, pieces)
    rows = {0: sent}
    for k in far_first(ctx_count):
        rows[k] = swapped(sent, "ctx", k)
    picked = pick(place, [rows[k] for k in range(ctx_count)])

    def first_half(piece_at):
        return gate_up(plan, piece_at, piece_at + expert_at, spread, picked, gate_up_weight)

    finals = []
    for k in far_first(exp_count) + [0]:
        arrived = swapped(first_half(away_at + k), "tp", 1)
        mine = first_half(mine_at + k)
        if k:
            joined = join(mine, arrived)
            finals.append(swapped(joined, "exp", k))
            picked, _ = lax.optimization_barrier((picked, joined))
        else:
            finals, mine = lax.optimization_barrier((finals, mine))
            finals = [arrived, mine] + finals
    own_hidden = hidden_of(finals, ff_width, model_width, gate_up_weight)

    total = None
    for k in range(exp_count):
        here = own_hidden
        if k:
            here, total = lax.optimization_barrier((swapped(own_hidden, "exp", k), total))
        there = swapped(here, "tp", 1)
        for piece_at, hidden in ((mine_at + k, here), (away_at + k, there)):
            ends = piece_at == away_at + exp_count - 1
            totals = down(
                plan,
                piece_at,
                piece_at + expert_at,
                spread,
                hidden,
                down_weight,
                combine_high,
                combine_low,
                total,
                ctx_count if ends else 1,
            )
            total = totals[0]
    returned = [totals[0]] + [swapped(totals[k], "ctx", k) for k in far_first(ctx_count)]
    return finish(mixed, returned)


def solution(mesh):
    in_specs = (
        P(("group", "ctx"), "tp", "exp"),
        P(("group", "ctx"), "tp", None),
        P(("group", "ctx"), "tp", None),
        P(("group", "ctx")),
        P(("group", "ctx")),
        P("group"),
        P("tp", "exp", None),
        P(("group", "ctx"), ("exp", "tp")),
        P(("exp", "tp")),
        P("ctx", ("exp", "tp"), None),
        P("ctx", None, ("exp", "tp")),
        P(("group", "ctx"), None),
        P(("group", "ctx"), None),
    )
    out_specs = P(("group", "ctx"), ("exp", "tp"))
    return jax.shard_map(body, mesh=mesh, in_specs=in_specs, out_specs=out_specs, check_vma=False)
```

```python
import functools
import math

import jax
import jax.numpy as jnp
from jax import lax
from jax.experimental import pallas as pl
from jax.experimental.pallas import tpu as pltpu
from jax.sharding import PartitionSpec as P

MOST = 8
DEPTH = 6
LANES = 128
CELLS = 2

epsilon = 1e-06
masked_score = -1e30
least_high = -1e20

f32 = jnp.float32
bf16 = jnp.bfloat16


def params(megabytes, steps=0):
    semantics = ("arbitrary",) * steps if steps else None
    return pltpu.CompilerParams(
        vmem_limit_bytes=megabytes * 1024 * 1024, dimension_semantics=semantics
    )


def cost(flops, bytes_accessed, transcendentals=0):
    return pl.CostEstimate(
        flops=flops, bytes_accessed=bytes_accessed, transcendentals=transcendentals
    )


def whole(memory_space=pltpu.VMEM):
    return pl.BlockSpec(memory_space=memory_space)


def in_hbm(values):
    return [pltpu.with_memory_space_constraint(value, pltpu.HBM) for value in values]


def lane_ids(shape):
    return lax.broadcasted_iota(jnp.int32, shape, len(shape) - 1)


def row_ids(shape):
    return lax.broadcasted_iota(jnp.int32, shape, len(shape) - 2)


def as_bf16(mask):
    return mask.astype(f32).astype(bf16)


def dot(left, right, dims=((1,), (0,))):
    return lax.dot_general(left, right, (dims, ((), ())), preferred_element_type=f32)


def in_two(value):
    high = value.astype(bf16).astype(f32)
    return high, value - high


def swapped(value, axes, mask):
    count = lax.axis_size(axes)
    pairs = [(source, source ^ mask) for source in range(count)]
    return lax.ppermute(value, axes, pairs)


def far_first(count):
    return list(range(count - 1, 0, -1))


def pack_kernel(
    queries_ref, seg_ref, ids_ref, weight_ref, beside_ref, out_ref,
    seg_here, ids_here, weight_here, done,
):
    rows, width = queries_ref.shape
    choices = ids_ref.shape[0]
    copies = [
        pltpu.make_async_copy(source, target, done.at[i])
        for i, (source, target) in enumerate(
            [
                (seg_ref, seg_here),
                (ids_ref, ids_here),
                (weight_ref, weight_here),
                (queries_ref, out_ref.at[:, :width]),
            ]
        )
    ]
    for copy in copies:
        copy.start()
    shape = (choices, LANES)

    def placed(value, first, last):
        to_lane = (lane_ids(shape) == row_ids(shape) + first) & (row_ids(shape) <= last)
        return dot(value.astype(bf16), as_bf16(to_lane), ((0,), (0,)))

    for copy in copies[:3]:
        copy.wait()
    segs = jnp.broadcast_to(seg_here[...], (choices, rows)).astype(f32)
    high, low = in_two(weight_here[...])
    info = placed(segs, 0, 0) + placed(ids_here[...].astype(f32), 1, choices)
    info = info + placed(high, 1 + choices, choices) + placed(low, 1 + 2 * choices, choices)
    out_ref[:, width:] = info.astype(bf16)
    copies[3].wait()


def pack(queries, query_seg, expert_ids, route_weight, beside):
    rows, width = queries.shape
    small = [query_seg[None, :], expert_ids.T, route_weight.T]
    return pl.pallas_call(
        pack_kernel,
        in_specs=[whole(pltpu.HBM)] * 5,
        out_shape=jax.ShapeDtypeStruct((rows, width + LANES), bf16),
        scratch_shapes=[pltpu.VMEM(value.shape, value.dtype) for value in small]
        + [pltpu.SemaphoreType.DMA((4,))],
        compiler_params=params(4),
        name="pack",
    )(*in_hbm([queries] + small + [beside]))


def sight_kernel(parent_ref, key_seg_ref, beside_ref, sight_ref, parent_here, key_seg_here, done):
    copies = [
        pltpu.make_async_copy(parent_ref, parent_here, done.at[0]),
        pltpu.make_async_copy(key_seg_ref, key_seg_here, done.at[1]),
    ]
    for copy in copies:
        copy.start()
    for copy in copies:
        copy.wait()
    seg_count, key_count = sight_ref.shape
    square = (seg_count, seg_count)
    same = row_ids(square) == lane_ids(square)
    one = as_bf16((parent_here[...] == row_ids(square)) | same)
    two = as_bf16(dot(one, one) > 0.5)
    four = as_bf16(dot(two, two) > 0.5)
    six = as_bf16(dot(four, two) > 0.5)
    keys = as_bf16(key_seg_here[...] == row_ids((seg_count, key_count)))
    sight_ref[...] = dot(six, keys, ((0,), (0,))).astype(bf16)


def sight_of(parent, key_seg, beside):
    assert DEPTH == 6
    small = [parent[None, :], key_seg[None, :]]
    return pl.pallas_call(
        sight_kernel,
        in_specs=[whole(pltpu.HBM)] * 3,
        out_shape=jax.ShapeDtypeStruct((parent.shape[0], key_seg.shape[0]), bf16),
        scratch_shapes=[pltpu.VMEM(value.shape, value.dtype) for value in small]
        + [pltpu.SemaphoreType.DMA((2,))],
        compiler_params=params(4),
        cost_estimate=cost(2**24, 2**19),
        name="sight",
    )(*in_hbm(small + [beside]))


def attend_kernel(
    heads, scale, lead_at, plan_ref, queries_ref, keys_ref, values_ref, sight_ref, beside_ref,
    out_ref, stacked_ref, probs_ref,
):
    rows = queries_ref.shape[0]
    key_count, head_size = keys_ref.shape
    seg_count = sight_ref.shape[0]
    width = heads * head_size
    info = queries_ref[:, width:].astype(f32)
    own_seg = info[:, :1].astype(jnp.int32)
    onehot = as_bf16(own_seg == lane_ids((rows, seg_count)))
    seen = dot(onehot, sight_ref[...]) > 0.5
    place = (rows, key_count)
    causal = lane_ids(place) - row_ids(place) <= plan_ref[lead_at]
    bias = jnp.where(seen & causal, 0.0, masked_score)
    for head in range(heads):
        columns = slice(head * head_size, (head + 1) * head_size)
        stacked_ref[head * rows : (head + 1) * rows, :] = queries_ref[:, columns]
    scores = dot(stacked_ref[...], keys_ref[...], ((1,), (1,)))
    stats = jnp.zeros((rows, LANES), f32)
    lane = lane_ids((rows, LANES))
    for head in range(heads):
        here = slice(head * rows, (head + 1) * rows)
        biased = scores[here, :] + bias
        high = jnp.maximum(jnp.max(biased, axis=1, keepdims=True), least_high)
        high = high.astype(bf16).astype(f32)
        probs = jnp.exp2((biased - high) * scale)
        total_high, total_low = in_two(jnp.sum(probs, axis=1, keepdims=True))
        probs_ref[here, :] = probs.astype(bf16)
        stats = jnp.where(lane == head, high, stats)
        stats = jnp.where(lane == heads + head, total_high, stats)
        stats = jnp.where(lane == 2 * heads + head, total_low, stats)
    out_ref[:, width:] = stats.astype(bf16)
    sums = dot(probs_ref[...], values_ref[...])
    for head in range(heads):
        columns = slice(head * head_size, (head + 1) * head_size)
        out_ref[:, columns] = sums[head * rows : (head + 1) * rows, :].astype(bf16)


def attend(plan, lead_at, queries, keys, values, sight, heads, scale, beside):
    rows, columns = queries.shape
    key_count, head_size = keys.shape
    work = rows * heads * key_count
    return pl.pallas_call(
        functools.partial(attend_kernel, heads, scale, lead_at),
        in_specs=[whole(pltpu.SMEM)] + [whole()] * 4 + [whole(pltpu.HBM)],
        out_shape=jax.ShapeDtypeStruct((rows, columns), bf16),
        scratch_shapes=[
            pltpu.VMEM((rows * heads, head_size), bf16),
            pltpu.VMEM((rows * heads, key_count), bf16),
        ],
        compiler_params=params(8),
        cost_estimate=cost(8 * work * head_size, 2**20, work),
        name="attend",
    )(plan, queries, keys, values, sight, *in_hbm([beside]))


def project_kernel(heads, scale, order_at, source_count, plan_ref, *refs):
    parts_refs, weight_ref = refs[:source_count], refs[source_count]
    out_refs, attention_ref = refs[source_count + 1 : -1], refs[-1]
    width = attention_ref.shape[1]
    head_size = width // heads
    stats = [ref[:, width:].astype(f32) for ref in parts_refs]
    top = functools.reduce(jnp.maximum, stats)
    factors = [jnp.exp2(jnp.minimum((stat - top) * scale, 0.0)) for stat in stats]
    total = 0.0
    for stat, factor in zip(stats, factors):
        high = pltpu.roll(stat, LANES - heads, 1)
        low = pltpu.roll(stat, LANES - 2 * heads, 1)
        total = total + factor * (high + low)
    shares = [factor / total for factor in factors]
    for head in range(heads):
        columns = slice(head * head_size, (head + 1) * head_size)
        merged = 0.0
        for ref, share in zip(parts_refs, shares):
            merged = merged + ref[:, columns].astype(f32) * share[:, head : head + 1]
        attention_ref[:, columns] = merged.astype(bf16)
    for i, out_ref in enumerate(out_refs):
        piece_width = out_ref.shape[1]
        start = pl.multiple_of(plan_ref[order_at + i] * piece_width, piece_width)
        out_ref[...] = dot(attention_ref[...], weight_ref[:, pl.ds(start, piece_width)]).astype(bf16)


def project(plan, order_at, parts, weight, heads, scale, piece_count):
    rows = parts[0].shape[0]
    width, model_width = weight.shape
    piece_width = model_width // piece_count
    return pl.pallas_call(
        functools.partial(project_kernel, heads, scale, order_at, len(parts)),
        in_specs=[whole(pltpu.SMEM)] + [whole()] * (len(parts) + 1),
        out_shape=[jax.ShapeDtypeStruct((rows, piece_width), bf16)] * piece_count,
        scratch_shapes=[pltpu.VMEM((rows, width), bf16)],
        compiler_params=params(8),
        cost_estimate=cost(2 * rows * width * model_width, 2 * width * model_width),
        name="project",
    )(plan, *parts, weight)


def mix_kernel(residual_ref, gain_ref, *refs):
    parts_refs, (mixed_ref, sent_ref) = refs[:-2], refs[-2:]
    rows, width = mixed_ref.shape
    mixed = residual_ref[...].astype(f32)
    for ref in parts_refs:
        mixed = mixed + ref[...].astype(f32)
    mixed_ref[...] = mixed
    sent_ref[:, :width] = (mixed * gain_ref[...].astype(f32)).astype(bf16)
    high, low = in_two(jnp.sum(mixed * mixed, axis=1, keepdims=True))
    lane = lane_ids((rows, LANES))
    squares = jnp.where(lane == 0, high, jnp.where(lane == 1, low, 0.0))
    sent_ref[:, width:] = squares.astype(bf16)


def mix(residual, gain, parts):
    rows, width = residual.shape
    return pl.pallas_call(
        mix_kernel,
        out_shape=(
            jax.ShapeDtypeStruct((rows, width), f32),
            jax.ShapeDtypeStruct((rows, width + LANES), bf16),
        ),
        compiler_params=params(4),
        name="mix",
    )(residual, gain[None, :], *parts)


def route_kernel(local_experts, choices, width, first_at, plan_ref, *refs):
    info_refs, (place_ref, high_ref, low_ref) = refs[:-3], refs[-3:]
    piece_count, tokens, slots = place_ref.shape
    info = jnp.concatenate([ref[:, width:] for ref in info_refs], axis=0).astype(f32)
    expert = (lane_ids((tokens, local_experts)) + plan_ref[first_at]).astype(f32)
    member = jnp.zeros((tokens, local_experts), f32)
    weight_high = jnp.zeros((tokens, local_experts), f32)
    weight_low = jnp.zeros((tokens, local_experts), f32)
    for k in range(choices):
        chosen = info[:, 1 + k : 2 + k] == expert
        high = info[:, 1 + choices + k : 2 + choices + k]
        low = info[:, 1 + 2 * choices + k : 2 + 2 * choices + k]
        member = jnp.where(chosen, 1.0, member)
        weight_high = jnp.where(chosen, high, weight_high)
        weight_low = jnp.where(chosen, low, weight_low)
    square = (tokens, tokens)
    earlier = as_bf16(lane_ids(square) < row_ids(square))
    rank = jnp.where(member > 0.5, dot(earlier, member.astype(bf16)), -1.0).astype(bf16)
    weight_high = weight_high.astype(bf16)
    weight_low = weight_low.astype(bf16)
    capacity = piece_count * slots // local_experts
    for piece in range(piece_count):
        slot = lane_ids((local_experts, slots)) + piece * slots
        spread = as_bf16(slot // capacity == row_ids((local_experts, slots)))
        wanted = (lane_ids((tokens, slots)) + piece * slots) % capacity
        placed = dot(rank, spread) == wanted.astype(f32)
        place_ref[piece] = jnp.where(placed, 1.0, 0.0).astype(bf16)
        high_ref[piece] = jnp.where(placed, dot(weight_high, spread), 0.0).astype(bf16)
        low_ref[piece] = jnp.where(placed, dot(weight_low, spread), 0.0).astype(bf16)


def route(plan, first_at, packed, width, local_experts, choices, piece_count, slots):
    tokens = sum(value.shape[0] for value in packed)
    shape = jax.ShapeDtypeStruct((piece_count, tokens, slots), bf16)
    return pl.pallas_call(
        functools.partial(route_kernel, local_experts, choices, width, first_at),
        in_specs=[whole(pltpu.SMEM)] + [whole()] * len(packed),
        out_shape=(shape, shape, shape),
        compiler_params=params(16),
        cost_estimate=cost(2**25, 2**20),
        name="route",
    )(plan, *packed)


def pick_kernel(place_ref, *refs):
    rows_refs, (out_ref, rows_ref) = refs[:-2], refs[-2:]
    rows = rows_refs[0].shape[0]
    for i, ref in enumerate(rows_refs):
        rows_ref[i * rows : (i + 1) * rows, :] = ref[...]
    for piece in range(out_ref.shape[0]):
        out_ref[piece] = dot(place_ref[piece], rows_ref[...], ((0,), (0,))).astype(bf16)


def pick(place, rows):
    piece_count, tokens, slots = place.shape
    columns = rows[0].shape[1]
    return pl.pallas_call(
        pick_kernel,
        out_shape=jax.ShapeDtypeStruct((piece_count, slots, columns), bf16),
        scratch_shapes=[pltpu.VMEM((tokens, columns), bf16)],
        compiler_params=params(8),
        cost_estimate=cost(2**26, 2**20),
        name="pick",
    )(place, *rows)


def squares_joined(squares):
    high, low = in_two(squares[:, :1] + squares[:, 1:2])
    lane = lane_ids(squares.shape)
    return jnp.where(lane == 0, high, jnp.where(lane == 1, low, 0.0))


class Layout:
    def __init__(self, local_experts, piece_count, capacity):
        slots = local_experts * capacity // piece_count
        self.rows = slots // CELLS
        self.experts = max(1, slots // capacity)
        self.spread = max(1, capacity // slots)
        self.each = max(1, self.experts // CELLS)
        self.cell_count = piece_count * CELLS

    def first_expert(self, piece, cell):
        within = cell * self.each if self.experts > 1 else 0
        return (piece * self.experts + within) // self.spread


def gate_up(plan, piece_at, cells, layout, picked, weight):
    _, width, ff_pair = weight.shape
    rows = layout.rows // layout.each

    def kernel(plan_ref, picked_ref, weight_ref, out_ref):
        piece = plan_ref[piece_at]
        for place, cell in enumerate(cells):
            first = layout.first_expert(piece, cell)
            for i in range(layout.each):
                picked = picked_ref[piece * CELLS + cell, i * rows : (i + 1) * rows, :]
                start = place * layout.rows + i * rows
                here = slice(start, start + rows)
                product = dot(picked[:, :width], weight_ref[first + i])
                out_ref[here, :ff_pair] = product.astype(bf16)
                out_ref[here, ff_pair:] = picked[:, width:]

    total = len(cells) * layout.rows
    return pl.pallas_call(
        kernel,
        in_specs=[whole(pltpu.SMEM)] + [whole()] * 2,
        out_shape=jax.ShapeDtypeStruct((total, ff_pair + LANES), bf16),
        compiler_params=params(8),
        cost_estimate=cost(2 * total * width * ff_pair, 2 * total * ff_pair),
        name="gate_up",
    )(plan, picked, weight)


def join_kernel(left_ref, right_ref, out_ref):
    ff_pair = out_ref.shape[1] - LANES
    product = left_ref[:, :ff_pair].astype(f32) + right_ref[:, :ff_pair].astype(f32)
    out_ref[:, :ff_pair] = product.astype(bf16)
    squares = left_ref[:, ff_pair:].astype(f32) + right_ref[:, ff_pair:].astype(f32)
    out_ref[:, ff_pair:] = squares_joined(squares).astype(bf16)


def join(left, right):
    return pl.pallas_call(
        join_kernel,
        out_shape=jax.ShapeDtypeStruct(left.shape, bf16),
        compiler_params=params(4),
        name="join",
    )(left, right)


def hidden_of(parts, starts, layout, ff_width, model_width, beside):
    def kernel(beside_ref, *refs):
        out_ref = refs[-1]
        total = 0.0
        for ref, start in zip(refs, starts):
            total = total + ref[start : start + layout.rows, :].astype(f32)
        high = total[:, 2 * ff_width : 2 * ff_width + 1]
        low = total[:, 2 * ff_width + 1 : 2 * ff_width + 2]
        norm = lax.rsqrt((high + low) / model_width + epsilon)
        gate = total[:, :ff_width] * norm
        up = total[:, ff_width : 2 * ff_width] * norm
        out_ref[...] = (gate / (1.0 + jnp.exp(-gate)) * up).astype(bf16)

    return pl.pallas_call(
        kernel,
        in_specs=[whole(pltpu.HBM)] + [whole()] * len(parts),
        out_shape=jax.ShapeDtypeStruct((layout.rows, ff_width), bf16),
        compiler_params=params(8),
        name="hidden",
    )(*in_hbm([beside]), *parts)


def down(plan, cells, layout, hidden, weight, high, low, total=None, out_count=1):
    ff_width = hidden[0].shape[1]
    tokens = high.shape[1]
    piece_width = weight.shape[2]
    each = layout.rows // layout.each
    rows = tokens // out_count
    out_type = f32 if out_count == 1 else bf16

    def kernel(plan_ref, weight_ref, high_ref, low_ref, *refs):
        hidden_refs, refs = refs[: len(cells)], refs[len(cells) :]
        total_refs, out_refs, held_ref = refs[: -1 - out_count], refs[-1 - out_count : -1], refs[-1]
        summed = 0.0
        for ref, (piece_at, cell) in zip(hidden_refs, cells):
            piece = plan_ref[piece_at]
            first = layout.first_expert(piece, cell)
            for i in range(layout.each):
                here = slice(i * each, (i + 1) * each)
                held_ref[here, :] = dot(ref[here, :], weight_ref[first + i]).astype(bf16)
            held = held_ref[...]
            at = piece * CELLS + cell
            summed = summed + dot(high_ref[at], held) + dot(low_ref[at], held)
        for ref in total_refs:
            summed = summed + ref[...]
        for i, ref in enumerate(out_refs):
            ref[...] = summed[i * rows : (i + 1) * rows, :].astype(ref.dtype)

    before = [] if total is None else [total]
    return pl.pallas_call(
        kernel,
        in_specs=[whole(pltpu.SMEM)] + [whole()] * (3 + len(cells) + len(before)),
        out_shape=[jax.ShapeDtypeStruct((rows, piece_width), out_type)] * out_count,
        scratch_shapes=[pltpu.VMEM((layout.rows, piece_width), bf16)],
        compiler_params=params(8),
        cost_estimate=cost(2 * layout.rows * ff_width * piece_width, 2**20),
        name="down",
    )(plan, weight, high, low, *hidden, *before)


def finish_kernel(mixed_ref, *refs):
    total = mixed_ref[...]
    for ref in refs[:-1]:
        total = total + ref[...].astype(f32)
    refs[-1][...] = total.astype(bf16)


def finish(mixed, parts):
    return pl.pallas_call(
        finish_kernel,
        out_shape=jax.ShapeDtypeStruct(mixed.shape, bf16),
        compiler_params=params(4),
        name="finish",
    )(mixed, *parts)


def body(
    queries,
    cached_keys,
    cached_values,
    key_seg,
    query_seg,
    parent,
    out_weight,
    residual,
    norm_gain,
    gate_up_weight,
    down_weight,
    expert_ids,
    route_weight,
):
    ctx_count, exp_count, tp_count = (lax.axis_size(axis) for axis in ("ctx", "exp", "tp"))
    own_ctx, own_exp, own_tp = (lax.axis_index(axis) for axis in ("ctx", "exp", "tp"))
    assert tp_count == 2 and cached_keys.shape[1] == 1
    assert ctx_count & (ctx_count - 1) == 0 and exp_count & (exp_count - 1) == 0
    piece_count = exp_count * tp_count
    query_rows = queries.shape[0]
    key_count, _, head_size = cached_keys.shape
    heads = queries.shape[2] // head_size
    width = heads * head_size
    model_width = out_weight.shape[2]
    local_experts, piece_width, _ = gate_up_weight.shape
    ff_width = down_weight.shape[1]
    choices = expert_ids.shape[1]
    scale = math.log2(math.e) / math.sqrt(head_size)

    last = ctx_count * (key_count - query_rows) - own_ctx * key_count
    leads = [last + (own_ctx ^ k) * query_rows for k in range(ctx_count)]
    own_piece = own_exp * tp_count + own_tp
    column_pieces = [own_piece ^ k for k in range(piece_count)]
    slot_pieces = [
        (own_tp ^ flip) * exp_count + (own_exp ^ k) for flip in (0, 1) for k in range(exp_count)
    ]
    layout = Layout(local_experts, piece_count, ctx_count * MOST)
    scalars = [own_ctx * local_experts] + leads + column_pieces + slot_pieces
    plan = jnp.stack([jnp.asarray(value, jnp.int32) for value in scalars])
    lead_at = 1
    order_at = lead_at + ctx_count
    mine_at = order_at + piece_count
    away_at = mine_at + exp_count

    packed = pack(
        queries.reshape(query_rows, width), query_seg, expert_ids, route_weight, gate_up_weight
    )
    gathered = {0: packed}
    for k in far_first(ctx_count):
        gathered[k] = swapped(packed, "ctx", k)
    sight = sight_of(parent, key_seg, gate_up_weight)
    keys = cached_keys.reshape(key_count, head_size)
    values = cached_values.reshape(key_count, head_size)
    out_matrix = out_weight.reshape(width, model_width)
    parts = {}
    for k in list(range(1, ctx_count)) + [0]:
        part = attend(
            plan, lead_at + k, gathered[k], keys, values, sight, heads, scale, gate_up_weight
        )
        parts[k] = swapped(part, "ctx", k) if k else part
    place, combine_high, combine_low = route(
        plan,
        0,
        [gathered[k] for k in range(ctx_count)],
        width,
        local_experts,
        choices,
        layout.cell_count,
        layout.rows,
    )
    projected = project(
        plan,
        order_at,
        [parts[k] for k in range(ctx_count)],
        out_matrix,
        heads,
        scale,
        piece_count,
    )
    pieces = [projected[0]] + [
        swapped(projected[k], ("exp", "tp"), k) for k in far_first(piece_count)
    ]
    mixed, sent = mix(residual, norm_gain, pieces)
    rows = {0: sent}
    for k in far_first(ctx_count):
        rows[k] = swapped(sent, "ctx", k)
    picked = pick(place, [rows[k] for k in range(ctx_count)])

    def after(value, *others):
        return lax.optimization_barrier((value,) + others)[0]

    def first_half(piece_at, cells):
        return gate_up(plan, piece_at, cells, layout, picked, gate_up_weight)

    crossed = [[] for _ in range(CELLS)]
    arrived = [None] * CELLS
    for k in far_first(exp_count):
        near = [swapped(first_half(away_at + k, (0,)), "tp", 1)]
        mine = first_half(mine_at + k, (0,))
        picked = after(picked, mine)
        near.append(swapped(first_half(away_at + k, (1,)), "tp", 1))
        for cell in range(CELLS):
            if cell:
                mine = first_half(mine_at + k, (cell,))
            joined = join(mine, near[cell])
            picked = after(picked, joined)
            crossed[cell].append(swapped(joined, "exp", k))
            if k == 1:
                arrived[cell] = swapped(first_half(away_at, (cell,)), "tp", 1)
    kept = first_half(mine_at, tuple(range(CELLS)))

    def add(cells, hidden, total, out_count=1):
        return down(
            plan, cells, layout, hidden, down_weight, combine_high, combine_low, total, out_count
        )

    total = None
    own_hidden = []
    for cell in range(CELLS):
        if total is not None:
            kept = after(kept, total)
        crossed[cell], kept = lax.optimization_barrier((crossed[cell], kept))
        parts = [kept, arrived[cell]] + crossed[cell]
        starts = [cell * layout.rows] + [0] * (len(parts) - 1)
        hidden = hidden_of(parts, starts, layout, ff_width, model_width, gate_up_weight)
        own_hidden.append(hidden)
        if cell == 0:
            cells = [(mine_at, 0), (away_at, 0)]
            total = add(cells, [hidden, swapped(hidden, "tp", 1)], total)[0]
    far = {
        (k, cell): swapped(own_hidden[cell], "exp", k)
        for cell in range(CELLS)
        for k in range(1, exp_count)
    }
    cells = [(mine_at, 1), (away_at, 1)]
    total = add(cells, [own_hidden[1], swapped(own_hidden[1], "tp", 1)], total)[0]
    last = {}
    for (k, cell), hidden in far.items():
        if last:
            hidden = after(hidden, total)
        last[k, cell] = swapped(hidden, "tp", 1)
        total = add([(mine_at + k, cell)], [hidden], total)[0]
    totals = add(
        [(away_at + k, cell) for k, cell in last], list(last.values()), total, ctx_count
    )
    returned = [totals[0]] + [swapped(totals[k], "ctx", k) for k in far_first(ctx_count)]
    return finish(mixed, returned)


def solution(mesh):
    in_specs = (
        P(("group", "ctx"), "tp", "exp"),
        P(("group", "ctx"), "tp", None),
        P(("group", "ctx"), "tp", None),
        P(("group", "ctx")),
        P(("group", "ctx")),
        P("group"),
        P("tp", "exp", None),
        P(("group", "ctx"), ("exp", "tp")),
        P(("exp", "tp")),
        P("ctx", ("exp", "tp"), None),
        P("ctx", None, ("exp", "tp")),
        P(("group", "ctx"), None),
        P(("group", "ctx"), None),
    )
    out_specs = P(("group", "ctx"), ("exp", "tp"))
    return jax.shard_map(body, mesh=mesh, in_specs=in_specs, out_specs=out_specs, check_vma=False)
```

```python
import functools
import math

import jax
import jax.numpy as jnp
from jax import lax
from jax.experimental import pallas as pl
from jax.experimental.pallas import tpu as pltpu
from jax.sharding import PartitionSpec as P

MOST = 8
DEPTH = 6
LANES = 128
CELLS = 2

epsilon = 1e-06
masked_score = -1e30
least_high = -1e20

f32 = jnp.float32
bf16 = jnp.bfloat16


def params(megabytes, steps=0):
    semantics = ("arbitrary",) * steps if steps else None
    return pltpu.CompilerParams(
        vmem_limit_bytes=megabytes * 1024 * 1024, dimension_semantics=semantics
    )


def cost(flops, bytes_accessed, transcendentals=0):
    return pl.CostEstimate(
        flops=flops, bytes_accessed=bytes_accessed, transcendentals=transcendentals
    )


def whole(memory_space=pltpu.VMEM):
    return pl.BlockSpec(memory_space=memory_space)


def in_hbm(values):
    return [pltpu.with_memory_space_constraint(value, pltpu.HBM) for value in values]


class Layout:
    def __init__(self, local_experts, key_count, query_rows):
        self.ctx, self.exp, self.tp = (lax.axis_size(axis) for axis in ("ctx", "exp", "tp"))
        self.key_count, self.query_rows = key_count, query_rows
        self.local_experts = local_experts
        self.piece_count = self.exp * self.tp
        capacity = self.ctx * MOST
        slots = local_experts * capacity // self.piece_count
        self.rows = slots // CELLS
        self.experts = max(1, slots // capacity)
        self.spread = max(1, capacity // slots)
        self.each = max(1, self.experts // CELLS)
        self.cell_count = self.piece_count * CELLS

    def lead(self, k):
        own = lax.axis_index("ctx")
        start = self.ctx * (self.key_count - self.query_rows)
        return start + (own ^ k) * self.query_rows - own * self.key_count

    def column_piece(self, k):
        return (lax.axis_index("exp") * self.tp + lax.axis_index("tp")) ^ k

    def first_local_expert(self):
        return lax.axis_index("ctx") * self.local_experts

    def cell(self, name):
        flip, k, cell = name
        piece = (lax.axis_index("tp") ^ flip) * self.exp + (lax.axis_index("exp") ^ k)
        within = cell * self.each if self.experts > 1 else 0
        return piece * CELLS + cell, lax.div(piece * self.experts + within, self.spread)


def lane_ids(shape):
    return lax.broadcasted_iota(jnp.int32, shape, len(shape) - 1)


def row_ids(shape):
    return lax.broadcasted_iota(jnp.int32, shape, len(shape) - 2)


def as_bf16(mask):
    return mask.astype(f32).astype(bf16)


def dot(left, right, dims=((1,), (0,))):
    return lax.dot_general(left, right, (dims, ((), ())), preferred_element_type=f32)


def in_two(value):
    high = value.astype(bf16).astype(f32)
    return high, value - high


def swapped(value, axes, mask):
    count = lax.axis_size(axes)
    pairs = [(source, source ^ mask) for source in range(count)]
    return lax.ppermute(value, axes, pairs)


def far_first(count):
    return list(range(count - 1, 0, -1))


def pack_kernel(
    queries_ref, seg_ref, ids_ref, weight_ref, beside_ref, out_ref,
    seg_here, ids_here, weight_here, done,
):
    rows, width = queries_ref.shape
    choices = ids_ref.shape[0]
    copies = [
        pltpu.make_async_copy(source, target, done.at[i])
        for i, (source, target) in enumerate(
            [
                (seg_ref, seg_here),
                (ids_ref, ids_here),
                (weight_ref, weight_here),
                (queries_ref, out_ref.at[:, :width]),
            ]
        )
    ]
    for copy in copies:
        copy.start()
    shape = (choices, LANES)

    def placed(value, first, last):
        to_lane = (lane_ids(shape) == row_ids(shape) + first) & (row_ids(shape) <= last)
        return dot(value.astype(bf16), as_bf16(to_lane), ((0,), (0,)))

    for copy in copies[:3]:
        copy.wait()
    segs = jnp.broadcast_to(seg_here[...], (choices, rows)).astype(f32)
    high, low = in_two(weight_here[...])
    info = placed(segs, 0, 0) + placed(ids_here[...].astype(f32), 1, choices)
    info = info + placed(high, 1 + choices, choices) + placed(low, 1 + 2 * choices, choices)
    out_ref[:, width:] = info.astype(bf16)
    copies[3].wait()


def pack(queries, query_seg, expert_ids, route_weight, beside):
    rows, width = queries.shape
    small = [query_seg[None, :], expert_ids.T, route_weight.T]
    return pl.pallas_call(
        pack_kernel,
        in_specs=[whole(pltpu.HBM)] * 5,
        out_shape=jax.ShapeDtypeStruct((rows, width + LANES), bf16),
        scratch_shapes=[pltpu.VMEM(value.shape, value.dtype) for value in small]
        + [pltpu.SemaphoreType.DMA((4,))],
        compiler_params=params(4),
        name="pack",
    )(*in_hbm([queries] + small + [beside]))


def sight_kernel(parent_ref, key_seg_ref, sight_ref):
    seg_count, key_count = sight_ref.shape
    square = (seg_count, seg_count)
    same = row_ids(square) == lane_ids(square)
    one = as_bf16((parent_ref[...] == row_ids(square)) | same)
    two = as_bf16(dot(one, one) > 0.5)
    four = as_bf16(dot(two, two) > 0.5)
    six = as_bf16(dot(four, two) > 0.5)
    keys = as_bf16(key_seg_ref[...] == row_ids((seg_count, key_count)))
    sight_ref[...] = dot(six, keys, ((0,), (0,))).astype(bf16)


def sight_of(parent, key_seg):
    assert DEPTH == 6
    return pl.pallas_call(
        sight_kernel,
        out_shape=jax.ShapeDtypeStruct((parent.shape[0], key_seg.shape[0]), bf16),
        compiler_params=params(4),
        cost_estimate=cost(2**24, 2**19),
        name="sight",
    )(parent[None, :], key_seg[None, :])


def attend_kernel(
    heads, scale, layout, k, queries_ref, keys_ref, values_ref, sight_ref, beside_ref,
    out_ref, stacked_ref, probs_ref,
):
    rows = queries_ref.shape[0]
    key_count, head_size = keys_ref.shape
    seg_count = sight_ref.shape[0]
    width = heads * head_size
    info = queries_ref[:, width:].astype(f32)
    own_seg = info[:, :1].astype(jnp.int32)
    onehot = as_bf16(own_seg == lane_ids((rows, seg_count)))
    seen = dot(onehot, sight_ref[...]) > 0.5
    place = (rows, key_count)
    causal = lane_ids(place) - row_ids(place) <= layout.lead(k)
    bias = jnp.where(seen & causal, 0.0, masked_score)
    for head in range(heads):
        columns = slice(head * head_size, (head + 1) * head_size)
        stacked_ref[head * rows : (head + 1) * rows, :] = queries_ref[:, columns]
    scores = dot(stacked_ref[...], keys_ref[...], ((1,), (1,)))
    stats = jnp.zeros((rows, LANES), f32)
    lane = lane_ids((rows, LANES))
    for head in range(heads):
        here = slice(head * rows, (head + 1) * rows)
        biased = scores[here, :] + bias
        high = jnp.maximum(jnp.max(biased, axis=1, keepdims=True), least_high)
        high = high.astype(bf16).astype(f32)
        probs = jnp.exp2((biased - high) * scale)
        total_high, total_low = in_two(jnp.sum(probs, axis=1, keepdims=True))
        probs_ref[here, :] = probs.astype(bf16)
        stats = jnp.where(lane == head, high, stats)
        stats = jnp.where(lane == heads + head, total_high, stats)
        stats = jnp.where(lane == 2 * heads + head, total_low, stats)
    out_ref[:, width:] = stats.astype(bf16)
    sums = dot(probs_ref[...], values_ref[...])
    for head in range(heads):
        columns = slice(head * head_size, (head + 1) * head_size)
        out_ref[:, columns] = sums[head * rows : (head + 1) * rows, :].astype(bf16)


def attend(layout, k, queries, keys, values, sight, heads, scale, beside):
    rows, columns = queries.shape
    key_count, head_size = keys.shape
    work = rows * heads * key_count
    return pl.pallas_call(
        functools.partial(attend_kernel, heads, scale, layout, k),
        in_specs=[whole()] * 4 + [whole(pltpu.HBM)],
        out_shape=jax.ShapeDtypeStruct((rows, columns), bf16),
        scratch_shapes=[
            pltpu.VMEM((rows * heads, head_size), bf16),
            pltpu.VMEM((rows * heads, key_count), bf16),
        ],
        compiler_params=params(8),
        cost_estimate=cost(8 * work * head_size, 2**20, work),
        name="attend",
    )(queries, keys, values, sight, *in_hbm([beside]))


def project_kernel(heads, scale, layout, source_count, *refs):
    parts_refs, weight_ref = refs[:source_count], refs[source_count]
    out_refs, attention_ref = refs[source_count + 1 : -1], refs[-1]
    width = attention_ref.shape[1]
    head_size = width // heads
    stats = [ref[:, width:].astype(f32) for ref in parts_refs]
    top = functools.reduce(jnp.maximum, stats)
    factors = [jnp.exp2(jnp.minimum((stat - top) * scale, 0.0)) for stat in stats]
    total = 0.0
    for stat, factor in zip(stats, factors):
        high = pltpu.roll(stat, LANES - heads, 1)
        low = pltpu.roll(stat, LANES - 2 * heads, 1)
        total = total + factor * (high + low)
    shares = [factor / total for factor in factors]
    for head in range(heads):
        columns = slice(head * head_size, (head + 1) * head_size)
        merged = 0.0
        for ref, share in zip(parts_refs, shares):
            merged = merged + ref[:, columns].astype(f32) * share[:, head : head + 1]
        attention_ref[:, columns] = merged.astype(bf16)
    for i, out_ref in enumerate(out_refs):
        piece_width = out_ref.shape[1]
        start = pl.multiple_of(layout.column_piece(i) * piece_width, piece_width)
        out_ref[...] = dot(attention_ref[...], weight_ref[:, pl.ds(start, piece_width)]).astype(bf16)


def project(layout, parts, weight, heads, scale):
    rows = parts[0].shape[0]
    width, model_width = weight.shape
    piece_width = model_width // layout.piece_count
    return pl.pallas_call(
        functools.partial(project_kernel, heads, scale, layout, len(parts)),
        out_shape=[jax.ShapeDtypeStruct((rows, piece_width), bf16)] * layout.piece_count,
        scratch_shapes=[pltpu.VMEM((rows, width), bf16)],
        compiler_params=params(8),
        cost_estimate=cost(2 * rows * width * model_width, 2 * width * model_width),
        name="project",
    )(*parts, weight)


def mix_kernel(residual_ref, gain_ref, *refs):
    parts_refs, (mixed_ref, sent_ref) = refs[:-2], refs[-2:]
    rows, width = mixed_ref.shape
    mixed = residual_ref[...].astype(f32)
    for ref in parts_refs:
        mixed = mixed + ref[...].astype(f32)
    mixed_ref[...] = mixed
    sent_ref[:, :width] = (mixed * gain_ref[...].astype(f32)).astype(bf16)
    high, low = in_two(jnp.sum(mixed * mixed, axis=1, keepdims=True))
    lane = lane_ids((rows, LANES))
    squares = jnp.where(lane == 0, high, jnp.where(lane == 1, low, 0.0))
    sent_ref[:, width:] = squares.astype(bf16)


def mix(residual, gain, parts):
    rows, width = residual.shape
    return pl.pallas_call(
        mix_kernel,
        out_shape=(
            jax.ShapeDtypeStruct((rows, width), f32),
            jax.ShapeDtypeStruct((rows, width + LANES), bf16),
        ),
        compiler_params=params(4),
        name="mix",
    )(residual, gain[None, :], *parts)


def route_kernel(layout, choices, width, *refs):
    info_refs, (place_ref, high_ref, low_ref) = refs[:-3], refs[-3:]
    cell_count, tokens, slots = place_ref.shape
    local_experts = layout.local_experts
    info = jnp.concatenate([ref[:, width:] for ref in info_refs], axis=0).astype(f32)
    expert = (lane_ids((tokens, local_experts)) + layout.first_local_expert()).astype(f32)
    member = jnp.zeros((tokens, local_experts), f32)
    weight_high = jnp.zeros((tokens, local_experts), f32)
    weight_low = jnp.zeros((tokens, local_experts), f32)
    for k in range(choices):
        chosen = info[:, 1 + k : 2 + k] == expert
        high = info[:, 1 + choices + k : 2 + choices + k]
        low = info[:, 1 + 2 * choices + k : 2 + 2 * choices + k]
        member = jnp.where(chosen, 1.0, member)
        weight_high = jnp.where(chosen, high, weight_high)
        weight_low = jnp.where(chosen, low, weight_low)
    square = (tokens, tokens)
    earlier = as_bf16(lane_ids(square) < row_ids(square))
    rank = jnp.where(member > 0.5, dot(earlier, member.astype(bf16)), -1.0).astype(bf16)
    weight_high = weight_high.astype(bf16)
    weight_low = weight_low.astype(bf16)
    capacity = cell_count * slots // local_experts
    for piece in range(cell_count):
        slot = lane_ids((local_experts, slots)) + piece * slots
        spread = as_bf16(slot // capacity == row_ids((local_experts, slots)))
        wanted = (lane_ids((tokens, slots)) + piece * slots) % capacity
        placed = dot(rank, spread) == wanted.astype(f32)
        place_ref[piece] = jnp.where(placed, 1.0, 0.0).astype(bf16)
        high_ref[piece] = jnp.where(placed, dot(weight_high, spread), 0.0).astype(bf16)
        low_ref[piece] = jnp.where(placed, dot(weight_low, spread), 0.0).astype(bf16)


def route(layout, packed, width, choices):
    tokens = sum(value.shape[0] for value in packed)
    shape = jax.ShapeDtypeStruct((layout.cell_count, tokens, layout.rows), bf16)
    return pl.pallas_call(
        functools.partial(route_kernel, layout, choices, width),
        out_shape=(shape, shape, shape),
        compiler_params=params(16),
        cost_estimate=cost(2**25, 2**20),
        name="route",
    )(*packed)


def pick_kernel(place_ref, *refs):
    rows_refs, (out_ref, rows_ref) = refs[:-2], refs[-2:]
    rows = rows_refs[0].shape[0]
    for i, ref in enumerate(rows_refs):
        rows_ref[i * rows : (i + 1) * rows, :] = ref[...]
    for piece in range(out_ref.shape[0]):
        out_ref[piece] = dot(place_ref[piece], rows_ref[...], ((0,), (0,))).astype(bf16)


def pick(place, rows):
    piece_count, tokens, slots = place.shape
    columns = rows[0].shape[1]
    return pl.pallas_call(
        pick_kernel,
        out_shape=jax.ShapeDtypeStruct((piece_count, slots, columns), bf16),
        scratch_shapes=[pltpu.VMEM((tokens, columns), bf16)],
        compiler_params=params(8),
        cost_estimate=cost(2**26, 2**20),
        name="pick",
    )(place, *rows)


def squares_joined(squares):
    high, low = in_two(squares[:, :1] + squares[:, 1:2])
    lane = lane_ids(squares.shape)
    return jnp.where(lane == 0, high, jnp.where(lane == 1, low, 0.0))


def gate_up(names, layout, picked, weight):
    _, width, ff_pair = weight.shape
    rows = layout.rows // layout.each

    def kernel(picked_ref, weight_ref, out_ref):
        for place, name in enumerate(names):
            at, first = layout.cell(name)
            for i in range(layout.each):
                picked = picked_ref[at, i * rows : (i + 1) * rows, :]
                start = place * layout.rows + i * rows
                here = slice(start, start + rows)
                product = dot(picked[:, :width], weight_ref[first + i])
                out_ref[here, :ff_pair] = product.astype(bf16)
                out_ref[here, ff_pair:] = picked[:, width:]

    total = len(names) * layout.rows
    return pl.pallas_call(
        kernel,
        out_shape=jax.ShapeDtypeStruct((total, ff_pair + LANES), bf16),
        compiler_params=params(8),
        cost_estimate=cost(2 * total * width * ff_pair, 2 * total * ff_pair),
        name="gate_up",
    )(picked, weight)


def join_kernel(left_ref, right_ref, out_ref):
    ff_pair = out_ref.shape[1] - LANES
    product = left_ref[:, :ff_pair].astype(f32) + right_ref[:, :ff_pair].astype(f32)
    out_ref[:, :ff_pair] = product.astype(bf16)
    squares = left_ref[:, ff_pair:].astype(f32) + right_ref[:, ff_pair:].astype(f32)
    out_ref[:, ff_pair:] = squares_joined(squares).astype(bf16)


def join(left, right):
    return pl.pallas_call(
        join_kernel,
        out_shape=jax.ShapeDtypeStruct(left.shape, bf16),
        compiler_params=params(4),
        name="join",
    )(left, right)


def hidden_of(parts, starts, layout, ff_width, model_width, beside):
    def kernel(beside_ref, *refs):
        out_ref = refs[-1]
        total = 0.0
        for ref, start in zip(refs, starts):
            total = total + ref[start : start + layout.rows, :].astype(f32)
        high = total[:, 2 * ff_width : 2 * ff_width + 1]
        low = total[:, 2 * ff_width + 1 : 2 * ff_width + 2]
        norm = lax.rsqrt((high + low) / model_width + epsilon)
        gate = total[:, :ff_width] * norm
        up = total[:, ff_width : 2 * ff_width] * norm
        out_ref[...] = (gate / (1.0 + jnp.exp(-gate)) * up).astype(bf16)

    return pl.pallas_call(
        kernel,
        in_specs=[whole(pltpu.HBM)] + [whole()] * len(parts),
        out_shape=jax.ShapeDtypeStruct((layout.rows, ff_width), bf16),
        compiler_params=params(8),
        name="hidden",
    )(*in_hbm([beside]), *parts)


def down(names, layout, hidden, weight, high, low, total=None, out_count=1):
    ff_width = hidden[0].shape[1]
    tokens = high.shape[1]
    piece_width = weight.shape[2]
    each = layout.rows // layout.each
    rows = tokens // out_count
    out_type = f32 if out_count == 1 else bf16

    def kernel(weight_ref, high_ref, low_ref, *refs):
        hidden_refs, refs = refs[: len(names)], refs[len(names) :]
        total_refs, out_refs, held_ref = refs[: -1 - out_count], refs[-1 - out_count : -1], refs[-1]
        summed = 0.0
        for ref, name in zip(hidden_refs, names):
            at, first = layout.cell(name)
            for i in range(layout.each):
                here = slice(i * each, (i + 1) * each)
                held_ref[here, :] = dot(ref[here, :], weight_ref[first + i]).astype(bf16)
            held = held_ref[...]
            summed = summed + dot(high_ref[at], held) + dot(low_ref[at], held)
        for ref in total_refs:
            summed = summed + ref[...]
        for i, ref in enumerate(out_refs):
            ref[...] = summed[i * rows : (i + 1) * rows, :].astype(ref.dtype)

    before = [] if total is None else [total]
    return pl.pallas_call(
        kernel,
        out_shape=[jax.ShapeDtypeStruct((rows, piece_width), out_type)] * out_count,
        scratch_shapes=[pltpu.VMEM((layout.rows, piece_width), bf16)],
        compiler_params=params(8),
        cost_estimate=cost(2 * layout.rows * ff_width * piece_width, 2**20),
        name="down",
    )(weight, high, low, *hidden, *before)


def finish_kernel(mixed_ref, *refs):
    total = mixed_ref[...]
    for ref in refs[:-1]:
        total = total + ref[...].astype(f32)
    refs[-1][...] = total.astype(bf16)


def finish(mixed, parts):
    return pl.pallas_call(
        finish_kernel,
        out_shape=jax.ShapeDtypeStruct(mixed.shape, bf16),
        compiler_params=params(4),
        name="finish",
    )(mixed, *parts)


def body(
    queries,
    cached_keys,
    cached_values,
    key_seg,
    query_seg,
    parent,
    out_weight,
    residual,
    norm_gain,
    gate_up_weight,
    down_weight,
    expert_ids,
    route_weight,
):
    ctx_count, exp_count, tp_count = (lax.axis_size(axis) for axis in ("ctx", "exp", "tp"))
    assert tp_count == 2 and cached_keys.shape[1] == 1
    assert ctx_count & (ctx_count - 1) == 0 and exp_count & (exp_count - 1) == 0
    piece_count = exp_count * tp_count
    query_rows = queries.shape[0]
    key_count, _, head_size = cached_keys.shape
    heads = queries.shape[2] // head_size
    width = heads * head_size
    model_width = out_weight.shape[2]
    local_experts, piece_width, _ = gate_up_weight.shape
    ff_width = down_weight.shape[1]
    choices = expert_ids.shape[1]
    scale = math.log2(math.e) / math.sqrt(head_size)

    layout = Layout(local_experts, key_count, query_rows)

    packed = pack(
        queries.reshape(query_rows, width), query_seg, expert_ids, route_weight, gate_up_weight
    )
    gathered = {0: packed}
    for k in far_first(ctx_count):
        gathered[k] = swapped(packed, "ctx", k)
    sight = sight_of(parent, key_seg)
    keys = cached_keys.reshape(key_count, head_size)
    values = cached_values.reshape(key_count, head_size)
    out_matrix = out_weight.reshape(width, model_width)
    parts = {}
    for k in list(range(1, ctx_count)) + [0]:
        part = attend(
            layout, k, gathered[k], keys, values, sight, heads, scale, gate_up_weight
        )
        parts[k] = swapped(part, "ctx", k) if k else part
    place, combine_high, combine_low = route(
        layout, [gathered[k] for k in range(ctx_count)], width, choices
    )
    projected = project(
        layout, [parts[k] for k in range(ctx_count)], out_matrix, heads, scale
    )
    pieces = [projected[0]] + [
        swapped(projected[k], ("exp", "tp"), k) for k in far_first(piece_count)
    ]
    mixed, sent = mix(residual, norm_gain, pieces)
    rows = {0: sent}
    for k in far_first(ctx_count):
        rows[k] = swapped(sent, "ctx", k)
    picked = pick(place, [rows[k] for k in range(ctx_count)])

    def after(value, *others):
        return lax.optimization_barrier((value,) + others)[0]

    def first_half(*names):
        return gate_up(names, layout, picked, gate_up_weight)

    crossed = [[] for _ in range(CELLS)]
    arrived = [None] * CELLS
    for k in far_first(exp_count):
        near = [swapped(first_half((1, k, 0)), "tp", 1)]
        mine = first_half((0, k, 0))
        picked = after(picked, mine)
        near.append(swapped(first_half((1, k, 1)), "tp", 1))
        for cell in range(CELLS):
            if cell:
                mine = first_half((0, k, cell))
            joined = join(mine, near[cell])
            picked = after(picked, joined)
            crossed[cell].append(swapped(joined, "exp", k))
            if k == 1:
                arrived[cell] = swapped(first_half((1, 0, cell)), "tp", 1)
    kept = first_half((0, 0, 0), (0, 0, 1))

    own_hidden = []
    for cell in range(CELLS):
        crossed[cell], kept = lax.optimization_barrier((crossed[cell], kept))
        parts = [kept, arrived[cell]] + crossed[cell]
        starts = [cell * layout.rows] + [0] * (len(parts) - 1)
        hidden = hidden_of(parts, starts, layout, ff_width, model_width, gate_up_weight)
        kept = after(kept, hidden)
        own_hidden.append(hidden)

    def add(hidden, total, out_count=1):
        return down(
            list(hidden),
            layout,
            list(hidden.values()),
            down_weight,
            combine_high,
            combine_low,
            total,
            out_count,
        )

    near = {
        (flip, 0, cell): swapped(hidden, "tp", 1) if flip else hidden
        for cell, hidden in enumerate(own_hidden)
        for flip in (0, 1)
    }
    far = {
        (0, k, cell): swapped(own_hidden[cell], "exp", k)
        for cell in range(CELLS)
        for k in range(1, exp_count)
    }
    total = add({name: near[name] for name in list(near)[:2]}, None)[0]
    names = list(near)[2:]
    near[names[0]] = after(near[names[0]], total)
    first = next(iter(far))
    total = add({**{name: near[name] for name in names}, first: far[first]}, total)[0]
    last = {}
    for turn, ((_, k, cell), hidden) in enumerate(far.items()):
        if turn:
            hidden = after(hidden, total)
            total = add({(0, k, cell): hidden}, total)[0]
        last[1, k, cell] = swapped(hidden, "tp", 1)
    totals = add(last, total, ctx_count)
    returned = [totals[0]] + [swapped(totals[k], "ctx", k) for k in far_first(ctx_count)]
    return finish(mixed, returned)


def solution(mesh):
    in_specs = (
        P(("group", "ctx"), "tp", "exp"),
        P(("group", "ctx"), "tp", None),
        P(("group", "ctx"), "tp", None),
        P(("group", "ctx")),
        P(("group", "ctx")),
        P("group"),
        P("tp", "exp", None),
        P(("group", "ctx"), ("exp", "tp")),
        P(("exp", "tp")),
        P("ctx", ("exp", "tp"), None),
        P("ctx", None, ("exp", "tp")),
        P(("group", "ctx"), None),
        P(("group", "ctx"), None),
    )
    out_specs = P(("group", "ctx"), ("exp", "tp"))
    return jax.shard_map(body, mesh=mesh, in_specs=in_specs, out_specs=out_specs, check_vma=False)
```

```python
import functools
import math

import jax
import jax.numpy as jnp
from jax import lax
from jax.experimental import pallas as pl
from jax.experimental.pallas import tpu as pltpu
from jax.sharding import PartitionSpec as P

MOST = 8
DEPTH = 6
LANES = 128
CELLS = 2

epsilon = 1e-06
masked_score = -1e30
least_high = -1e20

f32 = jnp.float32
bf16 = jnp.bfloat16


def params(megabytes, steps=0):
    semantics = ("arbitrary",) * steps if steps else None
    return pltpu.CompilerParams(
        vmem_limit_bytes=megabytes * 1024 * 1024, dimension_semantics=semantics
    )


def cost(flops, bytes_accessed, transcendentals=0):
    return pl.CostEstimate(
        flops=flops, bytes_accessed=bytes_accessed, transcendentals=transcendentals
    )


def whole(memory_space=pltpu.VMEM):
    return pl.BlockSpec(memory_space=memory_space)


def in_hbm(values):
    return [pltpu.with_memory_space_constraint(value, pltpu.HBM) for value in values]


class Layout:
    def __init__(self, local_experts, key_count, query_rows):
        self.ctx, self.exp, self.tp = (lax.axis_size(axis) for axis in ("ctx", "exp", "tp"))
        self.key_count, self.query_rows = key_count, query_rows
        self.local_experts = local_experts
        self.piece_count = self.exp * self.tp
        self.capacity = self.ctx * MOST // CELLS
        self.rows = local_experts * self.capacity // self.piece_count
        self.experts = max(1, self.rows // self.capacity)
        self.spread = max(1, self.capacity // self.rows)
        self.cell_count = self.piece_count * CELLS

    def lead(self, k):
        own = lax.axis_index("ctx")
        start = self.ctx * (self.key_count - self.query_rows)
        return start + (own ^ k) * self.query_rows - own * self.key_count

    def column_piece(self, k):
        return (lax.axis_index("exp") * self.tp + lax.axis_index("tp")) ^ k

    def first_local_expert(self):
        return lax.axis_index("ctx") * self.local_experts

    def cell(self, flip, k, cell):
        piece = (lax.axis_index("tp") ^ flip) * self.exp + (lax.axis_index("exp") ^ k)
        return piece * CELLS + cell, lax.div(piece * self.experts, self.spread)


def lane_ids(shape):
    return lax.broadcasted_iota(jnp.int32, shape, len(shape) - 1)


def row_ids(shape):
    return lax.broadcasted_iota(jnp.int32, shape, len(shape) - 2)


def as_bf16(mask):
    return mask.astype(f32).astype(bf16)


def dot(left, right, dims=((1,), (0,))):
    return lax.dot_general(left, right, (dims, ((), ())), preferred_element_type=f32)


def in_two(value):
    high = value.astype(bf16).astype(f32)
    return high, value - high


def swapped(value, axes, mask):
    count = lax.axis_size(axes)
    pairs = [(source, source ^ mask) for source in range(count)]
    return lax.ppermute(value, axes, pairs)


def far_first(count):
    return list(range(count - 1, 0, -1))


def pack_kernel(
    queries_ref, seg_ref, ids_ref, weight_ref, beside_ref, out_ref,
    seg_here, ids_here, weight_here, done,
):
    rows, width = queries_ref.shape
    choices = ids_ref.shape[0]
    copies = [
        pltpu.make_async_copy(source, target, done.at[i])
        for i, (source, target) in enumerate(
            [
                (seg_ref, seg_here),
                (ids_ref, ids_here),
                (weight_ref, weight_here),
                (queries_ref, out_ref.at[:, :width]),
            ]
        )
    ]
    for copy in copies:
        copy.start()
    shape = (choices, LANES)

    def placed(value, first, last):
        to_lane = (lane_ids(shape) == row_ids(shape) + first) & (row_ids(shape) <= last)
        return dot(value.astype(bf16), as_bf16(to_lane), ((0,), (0,)))

    for copy in copies[:3]:
        copy.wait()
    segs = jnp.broadcast_to(seg_here[...], (choices, rows)).astype(f32)
    high, low = in_two(weight_here[...])
    info = placed(segs, 0, 0) + placed(ids_here[...].astype(f32), 1, choices)
    info = info + placed(high, 1 + choices, choices) + placed(low, 1 + 2 * choices, choices)
    out_ref[:, width:] = info.astype(bf16)
    copies[3].wait()


def pack(queries, query_seg, expert_ids, route_weight, beside):
    rows, width = queries.shape
    small = [query_seg[None, :], expert_ids.T, route_weight.T]
    return pl.pallas_call(
        pack_kernel,
        in_specs=[whole(pltpu.HBM)] * 5,
        out_shape=jax.ShapeDtypeStruct((rows, width + LANES), bf16),
        scratch_shapes=[pltpu.VMEM(value.shape, value.dtype) for value in small]
        + [pltpu.SemaphoreType.DMA((4,))],
        compiler_params=params(4),
        name="pack",
    )(*in_hbm([queries] + small + [beside]))


def sight_kernel(parent_ref, key_seg_ref, sight_ref):
    seg_count, key_count = sight_ref.shape
    square = (seg_count, seg_count)
    same = row_ids(square) == lane_ids(square)
    one = as_bf16((parent_ref[...] == row_ids(square)) | same)
    two = as_bf16(dot(one, one) > 0.5)
    four = as_bf16(dot(two, two) > 0.5)
    six = as_bf16(dot(four, two) > 0.5)
    keys = as_bf16(key_seg_ref[...] == row_ids((seg_count, key_count)))
    sight_ref[...] = dot(six, keys, ((0,), (0,))).astype(bf16)


def sight_of(parent, key_seg):
    assert DEPTH == 6
    return pl.pallas_call(
        sight_kernel,
        out_shape=jax.ShapeDtypeStruct((parent.shape[0], key_seg.shape[0]), bf16),
        compiler_params=params(4),
        cost_estimate=cost(2**24, 2**19),
        name="sight",
    )(parent[None, :], key_seg[None, :])


def attend_kernel(
    heads, scale, layout, k, queries_ref, keys_ref, values_ref, sight_ref, beside_ref,
    out_ref, stacked_ref, probs_ref,
):
    rows = queries_ref.shape[0]
    key_count, head_size = keys_ref.shape
    seg_count = sight_ref.shape[0]
    width = heads * head_size
    info = queries_ref[:, width:].astype(f32)
    own_seg = info[:, :1].astype(jnp.int32)
    onehot = as_bf16(own_seg == lane_ids((rows, seg_count)))
    seen = dot(onehot, sight_ref[...]) > 0.5
    place = (rows, key_count)
    causal = lane_ids(place) - row_ids(place) <= layout.lead(k)
    bias = jnp.where(seen & causal, 0.0, masked_score)
    for head in range(heads):
        columns = slice(head * head_size, (head + 1) * head_size)
        stacked_ref[head * rows : (head + 1) * rows, :] = queries_ref[:, columns]
    scores = dot(stacked_ref[...], keys_ref[...], ((1,), (1,)))
    stats = jnp.zeros((rows, LANES), f32)
    lane = lane_ids((rows, LANES))
    for head in range(heads):
        here = slice(head * rows, (head + 1) * rows)
        biased = scores[here, :] + bias
        high = jnp.maximum(jnp.max(biased, axis=1, keepdims=True), least_high)
        high = high.astype(bf16).astype(f32)
        probs = jnp.exp2((biased - high) * scale)
        total_high, total_low = in_two(jnp.sum(probs, axis=1, keepdims=True))
        probs_ref[here, :] = probs.astype(bf16)
        stats = jnp.where(lane == head, high, stats)
        stats = jnp.where(lane == heads + head, total_high, stats)
        stats = jnp.where(lane == 2 * heads + head, total_low, stats)
    out_ref[:, width:] = stats.astype(bf16)
    sums = dot(probs_ref[...], values_ref[...])
    for head in range(heads):
        columns = slice(head * head_size, (head + 1) * head_size)
        out_ref[:, columns] = sums[head * rows : (head + 1) * rows, :].astype(bf16)


def attend(layout, k, queries, keys, values, sight, heads, scale, beside):
    rows, columns = queries.shape
    key_count, head_size = keys.shape
    work = rows * heads * key_count
    return pl.pallas_call(
        functools.partial(attend_kernel, heads, scale, layout, k),
        in_specs=[whole()] * 4 + [whole(pltpu.HBM)],
        out_shape=jax.ShapeDtypeStruct((rows, columns), bf16),
        scratch_shapes=[
            pltpu.VMEM((rows * heads, head_size), bf16),
            pltpu.VMEM((rows * heads, key_count), bf16),
        ],
        compiler_params=params(8),
        cost_estimate=cost(8 * work * head_size, 2**20, work),
        name="attend",
    )(queries, keys, values, sight, *in_hbm([beside]))


def project_kernel(heads, scale, layout, source_count, *refs):
    parts_refs, weight_ref = refs[:source_count], refs[source_count]
    out_refs, attention_ref = refs[source_count + 1 : -1], refs[-1]
    width = attention_ref.shape[1]
    head_size = width // heads
    stats = [ref[:, width:].astype(f32) for ref in parts_refs]
    top = functools.reduce(jnp.maximum, stats)
    factors = [jnp.exp2(jnp.minimum((stat - top) * scale, 0.0)) for stat in stats]
    total = 0.0
    for stat, factor in zip(stats, factors):
        high = pltpu.roll(stat, LANES - heads, 1)
        low = pltpu.roll(stat, LANES - 2 * heads, 1)
        total = total + factor * (high + low)
    shares = [factor / total for factor in factors]
    for head in range(heads):
        columns = slice(head * head_size, (head + 1) * head_size)
        merged = 0.0
        for ref, share in zip(parts_refs, shares):
            merged = merged + ref[:, columns].astype(f32) * share[:, head : head + 1]
        attention_ref[:, columns] = merged.astype(bf16)
    for i, out_ref in enumerate(out_refs):
        piece_width = out_ref.shape[1]
        start = pl.multiple_of(layout.column_piece(i) * piece_width, piece_width)
        out_ref[...] = dot(attention_ref[...], weight_ref[:, pl.ds(start, piece_width)]).astype(bf16)


def project(layout, parts, weight, heads, scale):
    rows = parts[0].shape[0]
    width, model_width = weight.shape
    piece_width = model_width // layout.piece_count
    return pl.pallas_call(
        functools.partial(project_kernel, heads, scale, layout, len(parts)),
        out_shape=[jax.ShapeDtypeStruct((rows, piece_width), bf16)] * layout.piece_count,
        scratch_shapes=[pltpu.VMEM((rows, width), bf16)],
        compiler_params=params(8),
        cost_estimate=cost(2 * rows * width * model_width, 2 * width * model_width),
        name="project",
    )(*parts, weight)


def mix_kernel(residual_ref, gain_ref, *refs):
    parts_refs, (mixed_ref, sent_ref) = refs[:-2], refs[-2:]
    rows, width = mixed_ref.shape
    mixed = residual_ref[...].astype(f32)
    for ref in parts_refs:
        mixed = mixed + ref[...].astype(f32)
    mixed_ref[...] = mixed
    sent_ref[:, :width] = (mixed * gain_ref[...].astype(f32)).astype(bf16)
    high, low = in_two(jnp.sum(mixed * mixed, axis=1, keepdims=True))
    lane = lane_ids((rows, LANES))
    squares = jnp.where(lane == 0, high, jnp.where(lane == 1, low, 0.0))
    sent_ref[:, width:] = squares.astype(bf16)


def mix(residual, gain, parts):
    rows, width = residual.shape
    return pl.pallas_call(
        mix_kernel,
        out_shape=(
            jax.ShapeDtypeStruct((rows, width), f32),
            jax.ShapeDtypeStruct((rows, width + LANES), bf16),
        ),
        compiler_params=params(4),
        name="mix",
    )(residual, gain[None, :], *parts)


def route_kernel(layout, choices, width, *refs):
    info_refs, (place_ref, high_ref, low_ref) = refs[:-3], refs[-3:]
    cell_count, tokens, slots = place_ref.shape
    local_experts, capacity = layout.local_experts, layout.capacity
    expert = (lane_ids((tokens, local_experts)) + layout.first_local_expert()).astype(f32)
    square = (tokens, tokens)
    earlier = as_bf16(lane_ids(square) < row_ids(square))
    count = len(info_refs) // CELLS
    for cell in range(CELLS):
        sources = info_refs[cell * count : (cell + 1) * count]
        info = jnp.concatenate([ref[:, width:] for ref in sources], axis=0).astype(f32)
        member = jnp.zeros((tokens, local_experts), f32)
        weight_high = jnp.zeros((tokens, local_experts), f32)
        weight_low = jnp.zeros((tokens, local_experts), f32)
        for k in range(choices):
            chosen = info[:, 1 + k : 2 + k] == expert
            high = info[:, 1 + choices + k : 2 + choices + k]
            low = info[:, 1 + 2 * choices + k : 2 + 2 * choices + k]
            member = jnp.where(chosen, 1.0, member)
            weight_high = jnp.where(chosen, high, weight_high)
            weight_low = jnp.where(chosen, low, weight_low)
        rank = jnp.where(member > 0.5, dot(earlier, member.astype(bf16)), -1.0).astype(bf16)
        weight_high = weight_high.astype(bf16)
        weight_low = weight_low.astype(bf16)
        for piece in range(layout.piece_count):
            slot = lane_ids((local_experts, slots)) + piece * slots
            spread = as_bf16(slot // capacity == row_ids((local_experts, slots)))
            wanted = (lane_ids((tokens, slots)) + piece * slots) % capacity
            placed = dot(rank, spread) == wanted.astype(f32)
            at = piece * CELLS + cell
            place_ref[at] = jnp.where(placed, 1.0, 0.0).astype(bf16)
            high_ref[at] = jnp.where(placed, dot(weight_high, spread), 0.0).astype(bf16)
            low_ref[at] = jnp.where(placed, dot(weight_low, spread), 0.0).astype(bf16)


def route(layout, packed, width, choices):
    tokens = sum(value.shape[0] for value in packed) // CELLS
    shape = jax.ShapeDtypeStruct((layout.cell_count, tokens, layout.rows), bf16)
    return pl.pallas_call(
        functools.partial(route_kernel, layout, choices, width),
        out_shape=(shape, shape, shape),
        compiler_params=params(16),
        cost_estimate=cost(2**25, 2**20),
        name="route",
    )(*packed)


def squares_joined(squares):
    high, low = in_two(squares[:, :1] + squares[:, 1:2])
    lane = lane_ids(squares.shape)
    return jnp.where(lane == 0, high, jnp.where(lane == 1, low, 0.0))


def gate_up(names, layout, place, rows, weight):
    _, width, ff_pair = weight.shape
    each = layout.rows // layout.experts
    row_count = len(rows)

    def kernel(place_ref, weight_ref, *refs):
        for name, out_ref in zip(names, refs[row_count:]):
            at, first = layout.cell(*name)
            picked = 0.0
            for i, ref in enumerate(refs[:row_count]):
                count = ref.shape[0]
                here = place_ref[at, i * count : (i + 1) * count, :]
                picked = picked + dot(here, ref[...], ((0,), (0,)))
            picked = picked.astype(bf16)
            for i in range(layout.experts):
                here = slice(i * each, (i + 1) * each)
                product = dot(picked[here, :width], weight_ref[first + i])
                out_ref[here, :ff_pair] = product.astype(bf16)
            out_ref[:, ff_pair:] = picked[:, width:]

    out = jax.ShapeDtypeStruct((layout.rows, ff_pair + LANES), bf16)
    return pl.pallas_call(
        kernel,
        out_shape=[out] * len(names),
        compiler_params=params(8),
        cost_estimate=cost(2 * layout.rows * width * ff_pair, 2 * layout.rows * ff_pair),
        name="gate_up",
    )(place, weight, *rows)


def join_kernel(left_ref, right_ref, out_ref):
    ff_pair = out_ref.shape[1] - LANES
    product = left_ref[:, :ff_pair].astype(f32) + right_ref[:, :ff_pair].astype(f32)
    out_ref[:, :ff_pair] = product.astype(bf16)
    squares = left_ref[:, ff_pair:].astype(f32) + right_ref[:, ff_pair:].astype(f32)
    out_ref[:, ff_pair:] = squares_joined(squares).astype(bf16)


def join(left, right):
    return pl.pallas_call(
        join_kernel,
        out_shape=jax.ShapeDtypeStruct(left.shape, bf16),
        compiler_params=params(4),
        name="join",
    )(left, right)


def hidden_of(parts, ff_width, model_width, beside):
    def kernel(*refs):
        refs, out_ref = refs[len(beside) : -1], refs[-1]
        total = 0.0
        for ref in refs:
            total = total + ref[...].astype(f32)
        high = total[:, 2 * ff_width : 2 * ff_width + 1]
        low = total[:, 2 * ff_width + 1 : 2 * ff_width + 2]
        norm = lax.rsqrt((high + low) / model_width + epsilon)
        gate = total[:, :ff_width] * norm
        up = total[:, ff_width : 2 * ff_width] * norm
        out_ref[...] = (gate / (1.0 + jnp.exp(-gate)) * up).astype(bf16)

    return pl.pallas_call(
        kernel,
        in_specs=[whole(pltpu.HBM)] * len(beside) + [whole()] * len(parts),
        out_shape=jax.ShapeDtypeStruct((parts[0].shape[0], ff_width), bf16),
        compiler_params=params(8),
        name="hidden",
    )(*in_hbm(beside), *parts)


def down(pieces, layout, weight, high, low, total=None, out_count=1):
    first_cells = next(iter(pieces.values()))
    ff_width = first_cells[0].shape[1]
    tokens = high.shape[1]
    piece_width = weight.shape[2]
    each = layout.rows // layout.experts
    rows = tokens * CELLS // out_count
    out_type = f32 if out_count == 1 else bf16

    def kernel(weight_ref, high_ref, low_ref, *refs):
        hidden_refs, refs = refs[: len(pieces) * CELLS], refs[len(pieces) * CELLS :]
        total_refs, out_refs, held_ref = refs[: -1 - out_count], refs[-1 - out_count : -1], refs[-1]
        summed = [0.0] * CELLS
        for turn, name in enumerate(pieces):
            cells = hidden_refs[turn * CELLS : (turn + 1) * CELLS]
            _, first = layout.cell(*name, 0)
            for i in range(layout.experts):
                here = slice(i * each, (i + 1) * each)
                rows_in = jnp.concatenate([ref[here, :] for ref in cells], axis=0)
                product = dot(rows_in, weight_ref[first + i]).astype(bf16)
                for cell in range(CELLS):
                    held_ref[cell, here, :] = product[cell * each : (cell + 1) * each, :]
            for cell in range(CELLS):
                at, _ = layout.cell(*name, cell)
                held = held_ref[cell]
                summed[cell] = summed[cell] + dot(high_ref[at], held) + dot(low_ref[at], held)
        whole_sum = jnp.concatenate(summed, axis=0)
        for ref in total_refs:
            whole_sum = whole_sum + ref[...]
        for i, ref in enumerate(out_refs):
            ref[...] = whole_sum[i * rows : (i + 1) * rows, :].astype(ref.dtype)

    before = [] if total is None else [total]
    hidden = [value for cells in pieces.values() for value in cells]
    return pl.pallas_call(
        kernel,
        out_shape=[jax.ShapeDtypeStruct((rows, piece_width), out_type)] * out_count,
        scratch_shapes=[pltpu.VMEM((CELLS, layout.rows, piece_width), bf16)],
        compiler_params=params(8),
        cost_estimate=cost(4 * layout.rows * ff_width * piece_width, 2**20),
        name="down",
    )(weight, high, low, *hidden, *before)


def finish_kernel(mixed_ref, *refs):
    total = mixed_ref[...]
    for ref in refs[:-1]:
        total = total + ref[...].astype(f32)
    refs[-1][...] = total.astype(bf16)


def finish(mixed, parts):
    return pl.pallas_call(
        finish_kernel,
        out_shape=jax.ShapeDtypeStruct(mixed.shape, bf16),
        compiler_params=params(4),
        name="finish",
    )(mixed, *parts)


def body(
    queries,
    cached_keys,
    cached_values,
    key_seg,
    query_seg,
    parent,
    out_weight,
    residual,
    norm_gain,
    gate_up_weight,
    down_weight,
    expert_ids,
    route_weight,
):
    ctx_count, exp_count, tp_count = (lax.axis_size(axis) for axis in ("ctx", "exp", "tp"))
    assert tp_count == 2 and cached_keys.shape[1] == 1
    assert ctx_count & (ctx_count - 1) == 0 and exp_count & (exp_count - 1) == 0
    piece_count = exp_count * tp_count
    query_rows = queries.shape[0]
    key_count, _, head_size = cached_keys.shape
    heads = queries.shape[2] // head_size
    width = heads * head_size
    model_width = out_weight.shape[2]
    local_experts, piece_width, _ = gate_up_weight.shape
    ff_width = down_weight.shape[1]
    choices = expert_ids.shape[1]
    scale = math.log2(math.e) / math.sqrt(head_size)

    layout = Layout(local_experts, key_count, query_rows)

    packed = pack(
        queries.reshape(query_rows, width), query_seg, expert_ids, route_weight, gate_up_weight
    )
    gathered = {0: packed}
    for k in far_first(ctx_count):
        gathered[k] = swapped(packed, "ctx", k)
    sight = sight_of(parent, key_seg)
    keys = cached_keys.reshape(key_count, head_size)
    values = cached_values.reshape(key_count, head_size)
    out_matrix = out_weight.reshape(width, model_width)
    parts = {}
    for k in list(range(1, ctx_count)) + [0]:
        part = attend(
            layout, k, gathered[k], keys, values, sight, heads, scale, gate_up_weight
        )
        parts[k] = swapped(part, "ctx", k) if k else part
    place, combine_high, combine_low = route(
        layout, [gathered[k] for k in range(ctx_count)], width, choices
    )
    def after(value, *others):
        return lax.optimization_barrier((value,) + others)[0]

    projected = project(
        layout,
        [parts[k] for k in range(ctx_count)],
        after(out_matrix, place),
        heads,
        scale,
    )
    pieces = [projected[0]] + [
        swapped(projected[k], ("exp", "tp"), k) for k in far_first(piece_count)
    ]
    mixed, sent = mix(residual, norm_gain, pieces)
    rows = {0: sent}
    for k in far_first(ctx_count):
        rows[k] = swapped(sent, "ctx", k)
    half = ctx_count // CELLS
    sources = [[rows[k] for k in range(half * i, half * (i + 1))] for i in range(CELLS)]

    def first_half(k, cell, flips):
        names = [(flip, k, cell) for flip in flips]
        return gate_up(names, layout, place, sources[cell], gate_up_weight)

    crossed = [[] for _ in range(CELLS)]
    for k in far_first(exp_count):
        away, mine = first_half(k, 0, (1, 0))
        here = [swapped(away, "tp", 1)]
        sources[1] = list(lax.optimization_barrier(tuple(sources[1]) + (mine,)))[:-1]
        here.append(swapped(first_half(k, 1, (1,))[0], "tp", 1))
        for cell in range(CELLS):
            if cell:
                mine = first_half(k, cell, (0,))[0]
            joined = join(mine, here[cell])
            place = after(place, joined)
            crossed[cell].append(swapped(joined, "exp", k))
    own_hidden = []
    for cell in range(CELLS):
        arrived = swapped(first_half(0, cell, (1,))[0], "tp", 1)
        kept = first_half(0, cell, (0,))[0]
        crossed[cell], kept = lax.optimization_barrier((crossed[cell], kept))
        beside = [gate_up_weight] if cell == CELLS - 1 else []
        hidden = hidden_of([kept, arrived] + crossed[cell], ff_width, model_width, beside)
        place = after(place, hidden)
        own_hidden.append(hidden)

    near = [swapped(hidden, "tp", 1) for hidden in own_hidden]
    far = {
        k: [swapped(hidden, "exp", k) for hidden in own_hidden] for k in range(1, exp_count)
    }
    own_hidden[-1] = after(own_hidden[-1], far[1][0])

    def add(pieces, total, out_count=1):
        return down(pieces, layout, down_weight, combine_high, combine_low, total, out_count)

    total = add({(0, 0): own_hidden, (1, 0): near}, None)[0]
    last = {}
    for k in far:
        far[k][-1] = after(far[k][-1], total)
        last[1, k] = [swapped(hidden, "tp", 1) for hidden in far[k]]
        total = add({(0, k): far[k]}, total)[0]
    totals = add(last, total, ctx_count)
    returned = [totals[0]] + [swapped(totals[k], "ctx", k) for k in far_first(ctx_count)]
    return finish(mixed, returned)


def solution(mesh):
    in_specs = (
        P(("group", "ctx"), "tp", "exp"),
        P(("group", "ctx"), "tp", None),
        P(("group", "ctx"), "tp", None),
        P(("group", "ctx")),
        P(("group", "ctx")),
        P("group"),
        P("tp", "exp", None),
        P(("group", "ctx"), ("exp", "tp")),
        P(("exp", "tp")),
        P("ctx", ("exp", "tp"), None),
        P("ctx", None, ("exp", "tp")),
        P(("group", "ctx"), None),
        P(("group", "ctx"), None),
    )
    out_specs = P(("group", "ctx"), ("exp", "tp"))
    return jax.shard_map(body, mesh=mesh, in_specs=in_specs, out_specs=out_specs, check_vma=False)
```

```python
import functools
import math

import jax
import jax.numpy as jnp
from jax import lax
from jax.experimental import pallas as pl
from jax.experimental.pallas import tpu as pltpu
from jax.sharding import PartitionSpec as P

MOST = 8
DEPTH = 6
LANES = 128
CELLS = 2

epsilon = 1e-06
masked_score = -1e30
least_high = -1e20

f32 = jnp.float32
bf16 = jnp.bfloat16


def params(megabytes, steps=0):
    semantics = ("arbitrary",) * steps if steps else None
    return pltpu.CompilerParams(
        vmem_limit_bytes=megabytes * 1024 * 1024, dimension_semantics=semantics
    )


def cost(flops, bytes_accessed, transcendentals=0):
    return pl.CostEstimate(
        flops=flops, bytes_accessed=bytes_accessed, transcendentals=transcendentals
    )


def whole(memory_space=pltpu.VMEM):
    return pl.BlockSpec(memory_space=memory_space)


def in_hbm(values):
    return [pltpu.with_memory_space_constraint(value, pltpu.HBM) for value in values]


class Layout:
    def __init__(self, local_experts, key_count, query_rows):
        self.ctx, self.exp, self.tp = (lax.axis_size(axis) for axis in ("ctx", "exp", "tp"))
        self.key_count, self.query_rows = key_count, query_rows
        self.local_experts = local_experts
        self.piece_count = self.exp * self.tp
        self.capacity = self.ctx * MOST // CELLS
        self.rows = local_experts * self.capacity // self.piece_count
        self.experts = max(1, self.rows // self.capacity)
        self.spread = max(1, self.capacity // self.rows)
        self.cell_count = self.piece_count * CELLS

    def lead(self, k):
        own = lax.axis_index("ctx")
        start = self.ctx * (self.key_count - self.query_rows)
        return start + (own ^ k) * self.query_rows - own * self.key_count

    def column_piece(self, k):
        return (lax.axis_index("exp") * self.tp + lax.axis_index("tp")) ^ k

    def first_local_expert(self):
        return lax.axis_index("ctx") * self.local_experts

    def cell(self, flip, k, cell):
        piece = (lax.axis_index("tp") ^ flip) * self.exp + (lax.axis_index("exp") ^ k)
        return piece * CELLS + cell, lax.div(piece * self.experts, self.spread)


def lane_ids(shape):
    return lax.broadcasted_iota(jnp.int32, shape, len(shape) - 1)


def row_ids(shape):
    return lax.broadcasted_iota(jnp.int32, shape, len(shape) - 2)


def as_bf16(mask):
    return mask.astype(f32).astype(bf16)


def dot(left, right, dims=((1,), (0,))):
    return lax.dot_general(left, right, (dims, ((), ())), preferred_element_type=f32)


def in_two(value):
    high = value.astype(bf16).astype(f32)
    return high, value - high


def swapped(value, axes, mask):
    count = lax.axis_size(axes)
    pairs = [(source, source ^ mask) for source in range(count)]
    return lax.ppermute(value, axes, pairs)


def far_first(count):
    return list(range(count - 1, 0, -1))


def pack_kernel(
    queries_ref, seg_ref, ids_ref, weight_ref, beside_ref, out_ref,
    seg_here, ids_here, weight_here, done,
):
    rows, width = queries_ref.shape
    choices = ids_ref.shape[0]
    copies = [
        pltpu.make_async_copy(source, target, done.at[i])
        for i, (source, target) in enumerate(
            [
                (seg_ref, seg_here),
                (ids_ref, ids_here),
                (weight_ref, weight_here),
                (queries_ref, out_ref.at[:, :width]),
            ]
        )
    ]
    for copy in copies:
        copy.start()
    shape = (choices, LANES)

    def placed(value, first, last):
        to_lane = (lane_ids(shape) == row_ids(shape) + first) & (row_ids(shape) <= last)
        return dot(value.astype(bf16), as_bf16(to_lane), ((0,), (0,)))

    for copy in copies[:3]:
        copy.wait()
    segs = jnp.broadcast_to(seg_here[...], (choices, rows)).astype(f32)
    high, low = in_two(weight_here[...])
    info = placed(segs, 0, 0) + placed(ids_here[...].astype(f32), 1, choices)
    info = info + placed(high, 1 + choices, choices) + placed(low, 1 + 2 * choices, choices)
    out_ref[:, width:] = info.astype(bf16)
    copies[3].wait()


def pack(queries, query_seg, expert_ids, route_weight, beside):
    rows, width = queries.shape
    small = [query_seg[None, :], expert_ids.T, route_weight.T]
    return pl.pallas_call(
        pack_kernel,
        in_specs=[whole(pltpu.HBM)] * 5,
        out_shape=jax.ShapeDtypeStruct((rows, width + LANES), bf16),
        scratch_shapes=[pltpu.VMEM(value.shape, value.dtype) for value in small]
        + [pltpu.SemaphoreType.DMA((4,))],
        compiler_params=params(4),
        name="pack",
    )(*in_hbm([queries] + small + [beside]))


def sight_kernel(parent_ref, key_seg_ref, sight_ref):
    seg_count, key_count = sight_ref.shape
    square = (seg_count, seg_count)
    same = row_ids(square) == lane_ids(square)
    one = as_bf16((parent_ref[...] == row_ids(square)) | same)
    two = as_bf16(dot(one, one) > 0.5)
    four = as_bf16(dot(two, two) > 0.5)
    six = as_bf16(dot(four, two) > 0.5)
    keys = as_bf16(key_seg_ref[...] == row_ids((seg_count, key_count)))
    sight_ref[...] = dot(six, keys, ((0,), (0,))).astype(bf16)


def sight_of(parent, key_seg):
    assert DEPTH == 6
    return pl.pallas_call(
        sight_kernel,
        out_shape=jax.ShapeDtypeStruct((parent.shape[0], key_seg.shape[0]), bf16),
        compiler_params=params(4),
        cost_estimate=cost(2**24, 2**19),
        name="sight",
    )(parent[None, :], key_seg[None, :])


def attend_kernel(
    heads, scale, layout, k, queries_ref, keys_ref, values_ref, sight_ref, beside_ref,
    out_ref, stacked_ref, probs_ref,
):
    rows = queries_ref.shape[0]
    key_count, head_size = keys_ref.shape
    seg_count = sight_ref.shape[0]
    width = heads * head_size
    info = queries_ref[:, width:].astype(f32)
    own_seg = info[:, :1].astype(jnp.int32)
    onehot = as_bf16(own_seg == lane_ids((rows, seg_count)))
    seen = dot(onehot, sight_ref[...]) > 0.5
    place = (rows, key_count)
    causal = lane_ids(place) - row_ids(place) <= layout.lead(k)
    bias = jnp.where(seen & causal, 0.0, masked_score)
    for head in range(heads):
        columns = slice(head * head_size, (head + 1) * head_size)
        stacked_ref[head * rows : (head + 1) * rows, :] = queries_ref[:, columns]
    scores = dot(stacked_ref[...], keys_ref[...], ((1,), (1,)))
    stats = jnp.zeros((rows, LANES), f32)
    lane = lane_ids((rows, LANES))
    for head in range(heads):
        here = slice(head * rows, (head + 1) * rows)
        biased = scores[here, :] + bias
        high = jnp.maximum(jnp.max(biased, axis=1, keepdims=True), least_high)
        high = high.astype(bf16).astype(f32)
        probs = jnp.exp2((biased - high) * scale)
        total_high, total_low = in_two(jnp.sum(probs, axis=1, keepdims=True))
        probs_ref[here, :] = probs.astype(bf16)
        stats = jnp.where(lane == head, high, stats)
        stats = jnp.where(lane == heads + head, total_high, stats)
        stats = jnp.where(lane == 2 * heads + head, total_low, stats)
    out_ref[:, width:] = stats.astype(bf16)
    sums = dot(probs_ref[...], values_ref[...])
    for head in range(heads):
        columns = slice(head * head_size, (head + 1) * head_size)
        out_ref[:, columns] = sums[head * rows : (head + 1) * rows, :].astype(bf16)


def attend(layout, k, queries, keys, values, sight, heads, scale, beside):
    rows, columns = queries.shape
    key_count, head_size = keys.shape
    work = rows * heads * key_count
    return pl.pallas_call(
        functools.partial(attend_kernel, heads, scale, layout, k),
        in_specs=[whole()] * 4 + [whole(pltpu.HBM)],
        out_shape=jax.ShapeDtypeStruct((rows, columns), bf16),
        scratch_shapes=[
            pltpu.VMEM((rows * heads, head_size), bf16),
            pltpu.VMEM((rows * heads, key_count), bf16),
        ],
        compiler_params=params(8),
        cost_estimate=cost(8 * work * head_size, 2**20, work),
        name="attend",
    )(queries, keys, values, sight, *in_hbm([beside]))


def project_kernel(heads, scale, layout, source_count, *refs):
    parts_refs, weight_ref = refs[:source_count], refs[source_count]
    out_refs, attention_ref = refs[source_count + 1 : -1], refs[-1]
    width = attention_ref.shape[1]
    head_size = width // heads
    stats = [ref[:, width:].astype(f32) for ref in parts_refs]
    top = functools.reduce(jnp.maximum, stats)
    factors = [jnp.exp2(jnp.minimum((stat - top) * scale, 0.0)) for stat in stats]
    total = 0.0
    for stat, factor in zip(stats, factors):
        high = pltpu.roll(stat, LANES - heads, 1)
        low = pltpu.roll(stat, LANES - 2 * heads, 1)
        total = total + factor * (high + low)
    shares = [factor / total for factor in factors]
    for head in range(heads):
        columns = slice(head * head_size, (head + 1) * head_size)
        merged = 0.0
        for ref, share in zip(parts_refs, shares):
            merged = merged + ref[:, columns].astype(f32) * share[:, head : head + 1]
        attention_ref[:, columns] = merged.astype(bf16)
    for i, out_ref in enumerate(out_refs):
        piece_width = out_ref.shape[1]
        start = pl.multiple_of(layout.column_piece(i) * piece_width, piece_width)
        out_ref[...] = dot(attention_ref[...], weight_ref[:, pl.ds(start, piece_width)]).astype(bf16)


def project(layout, parts, weight, heads, scale):
    rows = parts[0].shape[0]
    width, model_width = weight.shape
    piece_width = model_width // layout.piece_count
    return pl.pallas_call(
        functools.partial(project_kernel, heads, scale, layout, len(parts)),
        out_shape=[jax.ShapeDtypeStruct((rows, piece_width), bf16)] * layout.piece_count,
        scratch_shapes=[pltpu.VMEM((rows, width), bf16)],
        compiler_params=params(8),
        cost_estimate=cost(2 * rows * width * model_width, 2 * width * model_width),
        name="project",
    )(*parts, weight)


def mix_kernel(residual_ref, gain_ref, *refs):
    parts_refs, (mixed_ref, sent_ref) = refs[:-2], refs[-2:]
    rows, width = mixed_ref.shape
    mixed = residual_ref[...].astype(f32)
    for ref in parts_refs:
        mixed = mixed + ref[...].astype(f32)
    mixed_ref[...] = mixed
    sent_ref[:, :width] = (mixed * gain_ref[...].astype(f32)).astype(bf16)
    high, low = in_two(jnp.sum(mixed * mixed, axis=1, keepdims=True))
    lane = lane_ids((rows, LANES))
    squares = jnp.where(lane == 0, high, jnp.where(lane == 1, low, 0.0))
    sent_ref[:, width:] = squares.astype(bf16)


def mix(residual, gain, parts):
    rows, width = residual.shape
    return pl.pallas_call(
        mix_kernel,
        out_shape=(
            jax.ShapeDtypeStruct((rows, width), f32),
            jax.ShapeDtypeStruct((rows, width + LANES), bf16),
        ),
        compiler_params=params(4),
        name="mix",
    )(residual, gain[None, :], *parts)


def route_kernel(layout, choices, width, *refs):
    info_refs, (place_ref, high_ref, low_ref) = refs[:-3], refs[-3:]
    cell_count, tokens, slots = place_ref.shape
    local_experts, capacity = layout.local_experts, layout.capacity
    expert = (lane_ids((tokens, local_experts)) + layout.first_local_expert()).astype(f32)
    square = (tokens, tokens)
    earlier = as_bf16(lane_ids(square) < row_ids(square))
    count = len(info_refs) // CELLS
    for cell in range(CELLS):
        sources = info_refs[cell * count : (cell + 1) * count]
        info = jnp.concatenate([ref[:, width:] for ref in sources], axis=0).astype(f32)
        member = jnp.zeros((tokens, local_experts), f32)
        weight_high = jnp.zeros((tokens, local_experts), f32)
        weight_low = jnp.zeros((tokens, local_experts), f32)
        for k in range(choices):
            chosen = info[:, 1 + k : 2 + k] == expert
            high = info[:, 1 + choices + k : 2 + choices + k]
            low = info[:, 1 + 2 * choices + k : 2 + 2 * choices + k]
            member = jnp.where(chosen, 1.0, member)
            weight_high = jnp.where(chosen, high, weight_high)
            weight_low = jnp.where(chosen, low, weight_low)
        rank = jnp.where(member > 0.5, dot(earlier, member.astype(bf16)), -1.0).astype(bf16)
        weight_high = weight_high.astype(bf16)
        weight_low = weight_low.astype(bf16)
        for piece in range(layout.piece_count):
            slot = lane_ids((local_experts, slots)) + piece * slots
            spread = as_bf16(slot // capacity == row_ids((local_experts, slots)))
            wanted = (lane_ids((tokens, slots)) + piece * slots) % capacity
            placed = dot(rank, spread) == wanted.astype(f32)
            at = piece * CELLS + cell
            place_ref[at] = jnp.where(placed, 1.0, 0.0).astype(bf16)
            high_ref[at] = jnp.where(placed, dot(weight_high, spread), 0.0).astype(bf16)
            low_ref[at] = jnp.where(placed, dot(weight_low, spread), 0.0).astype(bf16)


def route(layout, packed, width, choices):
    tokens = sum(value.shape[0] for value in packed) // CELLS
    shape = jax.ShapeDtypeStruct((layout.cell_count, tokens, layout.rows), bf16)
    return pl.pallas_call(
        functools.partial(route_kernel, layout, choices, width),
        out_shape=(shape, shape, shape),
        compiler_params=params(16),
        cost_estimate=cost(2**25, 2**20),
        name="route",
    )(*packed)


def squares_joined(squares):
    high, low = in_two(squares[:, :1] + squares[:, 1:2])
    lane = lane_ids(squares.shape)
    return jnp.where(lane == 0, high, jnp.where(lane == 1, low, 0.0))


def gate_up(names, layout, place, rows, weight):
    _, width, ff_pair = weight.shape
    each = layout.rows // layout.experts
    row_count = len(rows)

    def kernel(place_ref, weight_ref, *refs):
        for name, out_ref in zip(names, refs[row_count:]):
            at, first = layout.cell(*name)
            picked = 0.0
            for i, ref in enumerate(refs[:row_count]):
                count = ref.shape[0]
                here = place_ref[at, i * count : (i + 1) * count, :]
                picked = picked + dot(here, ref[...], ((0,), (0,)))
            picked = picked.astype(bf16)
            for i in range(layout.experts):
                here = slice(i * each, (i + 1) * each)
                product = dot(picked[here, :width], weight_ref[first + i])
                out_ref[here, :ff_pair] = product.astype(bf16)
            out_ref[:, ff_pair:] = picked[:, width:]

    out = jax.ShapeDtypeStruct((layout.rows, ff_pair + LANES), bf16)
    return pl.pallas_call(
        kernel,
        out_shape=[out] * len(names),
        compiler_params=params(8),
        cost_estimate=cost(2 * layout.rows * width * ff_pair, 2 * layout.rows * ff_pair),
        name="gate_up",
    )(place, weight, *rows)


def join_kernel(left_ref, right_ref, out_ref):
    ff_pair = out_ref.shape[1] - LANES
    product = left_ref[:, :ff_pair].astype(f32) + right_ref[:, :ff_pair].astype(f32)
    out_ref[:, :ff_pair] = product.astype(bf16)
    squares = left_ref[:, ff_pair:].astype(f32) + right_ref[:, ff_pair:].astype(f32)
    out_ref[:, ff_pair:] = squares_joined(squares).astype(bf16)


def join(left, right):
    return pl.pallas_call(
        join_kernel,
        out_shape=jax.ShapeDtypeStruct(left.shape, bf16),
        compiler_params=params(4),
        name="join",
    )(left, right)


def hidden_of(parts, ff_width, model_width, beside):
    def kernel(*refs):
        refs, out_ref = refs[len(beside) : -1], refs[-1]
        total = 0.0
        for ref in refs:
            total = total + ref[...].astype(f32)
        high = total[:, 2 * ff_width : 2 * ff_width + 1]
        low = total[:, 2 * ff_width + 1 : 2 * ff_width + 2]
        norm = lax.rsqrt((high + low) / model_width + epsilon)
        gate = total[:, :ff_width] * norm
        up = total[:, ff_width : 2 * ff_width] * norm
        out_ref[...] = (gate / (1.0 + jnp.exp(-gate)) * up).astype(bf16)

    return pl.pallas_call(
        kernel,
        in_specs=[whole(pltpu.HBM)] * len(beside) + [whole()] * len(parts),
        out_shape=jax.ShapeDtypeStruct((parts[0].shape[0], ff_width), bf16),
        compiler_params=params(8),
        name="hidden",
    )(*in_hbm(beside), *parts)


def down(pieces, layout, weight, high, low, total=None, out_count=1):
    first_cells = next(iter(pieces.values()))
    ff_width = first_cells[0].shape[1]
    tokens = high.shape[1]
    piece_width = weight.shape[2]
    each = layout.rows // layout.experts
    rows = tokens * CELLS // out_count
    out_type = f32 if out_count == 1 else bf16

    def kernel(weight_ref, high_ref, low_ref, *refs):
        hidden_refs, refs = refs[: len(pieces) * CELLS], refs[len(pieces) * CELLS :]
        total_refs, out_refs, held_ref = refs[: -1 - out_count], refs[-1 - out_count : -1], refs[-1]
        summed = [0.0] * CELLS
        for turn, name in enumerate(pieces):
            cells = hidden_refs[turn * CELLS : (turn + 1) * CELLS]
            _, first = layout.cell(*name, 0)
            for i in range(layout.experts):
                here = slice(i * each, (i + 1) * each)
                rows_in = jnp.concatenate([ref[here, :] for ref in cells], axis=0)
                product = dot(rows_in, weight_ref[first + i]).astype(bf16)
                for cell in range(CELLS):
                    held_ref[cell, here, :] = product[cell * each : (cell + 1) * each, :]
            for cell in range(CELLS):
                at, _ = layout.cell(*name, cell)
                held = held_ref[cell]
                summed[cell] = summed[cell] + dot(high_ref[at], held) + dot(low_ref[at], held)
        whole_sum = jnp.concatenate(summed, axis=0)
        for ref in total_refs:
            whole_sum = whole_sum + ref[...]
        for i, ref in enumerate(out_refs):
            ref[...] = whole_sum[i * rows : (i + 1) * rows, :].astype(ref.dtype)

    before = [] if total is None else [total]
    hidden = [value for cells in pieces.values() for value in cells]
    return pl.pallas_call(
        kernel,
        out_shape=[jax.ShapeDtypeStruct((rows, piece_width), out_type)] * out_count,
        scratch_shapes=[pltpu.VMEM((CELLS, layout.rows, piece_width), bf16)],
        compiler_params=params(8),
        cost_estimate=cost(4 * layout.rows * ff_width * piece_width, 2**20),
        name="down",
    )(weight, high, low, *hidden, *before)


def finish_kernel(mixed_ref, *refs):
    total = mixed_ref[...]
    for ref in refs[:-1]:
        total = total + ref[...].astype(f32)
    refs[-1][...] = total.astype(bf16)


def finish(mixed, parts):
    return pl.pallas_call(
        finish_kernel,
        out_shape=jax.ShapeDtypeStruct(mixed.shape, bf16),
        compiler_params=params(4),
        name="finish",
    )(mixed, *parts)


def body(
    queries,
    cached_keys,
    cached_values,
    key_seg,
    query_seg,
    parent,
    out_weight,
    residual,
    norm_gain,
    gate_up_weight,
    down_weight,
    expert_ids,
    route_weight,
):
    ctx_count, exp_count, tp_count = (lax.axis_size(axis) for axis in ("ctx", "exp", "tp"))
    assert tp_count == 2 and cached_keys.shape[1] == 1
    assert ctx_count & (ctx_count - 1) == 0 and exp_count & (exp_count - 1) == 0
    piece_count = exp_count * tp_count
    query_rows = queries.shape[0]
    key_count, _, head_size = cached_keys.shape
    heads = queries.shape[2] // head_size
    width = heads * head_size
    model_width = out_weight.shape[2]
    local_experts, piece_width, _ = gate_up_weight.shape
    ff_width = down_weight.shape[1]
    choices = expert_ids.shape[1]
    scale = math.log2(math.e) / math.sqrt(head_size)

    layout = Layout(local_experts, key_count, query_rows)

    packed = pack(
        queries.reshape(query_rows, width), query_seg, expert_ids, route_weight, gate_up_weight
    )
    gathered = {0: packed}
    for k in far_first(ctx_count):
        gathered[k] = swapped(packed, "ctx", k)
    sight = sight_of(parent, key_seg)
    keys = cached_keys.reshape(key_count, head_size)
    values = cached_values.reshape(key_count, head_size)
    out_matrix = out_weight.reshape(width, model_width)
    parts = {}
    for k in list(range(1, ctx_count)) + [0]:
        part = attend(
            layout, k, gathered[k], keys, values, sight, heads, scale, gate_up_weight
        )
        parts[k] = swapped(part, "ctx", k) if k else part
    place, combine_high, combine_low = route(
        layout, [gathered[k] for k in range(ctx_count)], width, choices
    )
    def after(value, *others):
        return lax.optimization_barrier((value,) + others)[0]

    projected = project(
        layout,
        [parts[k] for k in range(ctx_count)],
        after(out_matrix, place),
        heads,
        scale,
    )
    pieces = [projected[0]] + [
        swapped(projected[k], ("exp", "tp"), k) for k in far_first(piece_count)
    ]
    mixed, sent = mix(residual, norm_gain, pieces)
    rows = {0: sent}
    for k in far_first(ctx_count):
        rows[k] = swapped(sent, "ctx", k)
    half = ctx_count // CELLS
    sources = [[rows[k] for k in range(half * i, half * (i + 1))] for i in range(CELLS)]

    def first_half(names):
        cell = names[0][2]
        return gate_up(names, layout, place, sources[cell], gate_up_weight)

    crossed = [[] for _ in range(CELLS)]
    arrived, kept = [None] * CELLS, [None] * CELLS
    for k in far_first(exp_count):
        names = [(1, k, 0), (0, k, 0)] + ([(1, 0, 0)] if k == 1 else [])
        away, mine, *staying = first_half(names)
        here = [swapped(away, "tp", 1)]
        if staying:
            arrived[0] = swapped(staying[0], "tp", 1)
        sources[1] = list(lax.optimization_barrier(tuple(sources[1]) + (mine,)))[:-1]
        here.append(swapped(first_half([(1, k, 1)])[0], "tp", 1))
        for cell in range(CELLS):
            if cell:
                mine = first_half([(0, k, cell)])[0]
            joined = join(mine, here[cell])
            place = after(place, joined)
            crossed[cell].append(swapped(joined, "exp", k))
    away, kept[1] = first_half([(1, 0, 1), (0, 0, 1)])
    arrived[1] = swapped(away, "tp", 1)
    place = after(place, kept[1])
    kept[0] = first_half([(0, 0, 0)])[0]
    own_hidden = []
    for cell in range(CELLS):
        if cell:
            arrived[cell] = after(arrived[cell], kept[cell], *own_hidden)
        else:
            crossed[cell], kept[cell] = lax.optimization_barrier((crossed[cell], kept[cell]))
        beside = [] if cell else [gate_up_weight]
        hidden = hidden_of(
            [kept[cell], arrived[cell]] + crossed[cell], ff_width, model_width, beside
        )
        own_hidden.append(hidden)

    near = [swapped(hidden, "tp", 1) for hidden in own_hidden]
    far = {
        k: [swapped(hidden, "exp", k) for hidden in own_hidden] for k in range(1, exp_count)
    }
    own_hidden[-1] = after(own_hidden[-1], far[1][0])

    def add(pieces, total, out_count=1):
        return down(pieces, layout, down_weight, combine_high, combine_low, total, out_count)

    total = add({(0, 0): own_hidden, (1, 0): near}, None)[0]
    last = {}
    for k in far:
        far[k][-1] = after(far[k][-1], total)
        last[1, k] = [swapped(hidden, "tp", 1) for hidden in far[k]]
        total = add({(0, k): far[k]}, total)[0]
    totals = add(last, total, ctx_count)
    returned = [totals[0]] + [swapped(totals[k], "ctx", k) for k in far_first(ctx_count)]
    return finish(mixed, returned)


def solution(mesh):
    in_specs = (
        P(("group", "ctx"), "tp", "exp"),
        P(("group", "ctx"), "tp", None),
        P(("group", "ctx"), "tp", None),
        P(("group", "ctx")),
        P(("group", "ctx")),
        P("group"),
        P("tp", "exp", None),
        P(("group", "ctx"), ("exp", "tp")),
        P(("exp", "tp")),
        P("ctx", ("exp", "tp"), None),
        P("ctx", None, ("exp", "tp")),
        P(("group", "ctx"), None),
        P(("group", "ctx"), None),
    )
    out_specs = P(("group", "ctx"), ("exp", "tp"))
    return jax.shard_map(body, mesh=mesh, in_specs=in_specs, out_specs=out_specs, check_vma=False)
```

```python
import functools
import math

import jax
import jax.numpy as jnp
from jax import lax
from jax.experimental import pallas as pl
from jax.experimental.pallas import tpu as pltpu
from jax.sharding import PartitionSpec as P

MOST = 8
DEPTH = 6
LANES = 128
CELLS = 2

epsilon = 1e-06
masked_score = -1e30
least_high = -1e20

f32 = jnp.float32
bf16 = jnp.bfloat16


def params(megabytes, steps=0):
    semantics = ("arbitrary",) * steps if steps else None
    return pltpu.CompilerParams(
        vmem_limit_bytes=megabytes * 1024 * 1024, dimension_semantics=semantics
    )


def cost(flops, bytes_accessed, transcendentals=0):
    return pl.CostEstimate(
        flops=flops, bytes_accessed=bytes_accessed, transcendentals=transcendentals
    )


def whole(memory_space=pltpu.VMEM):
    return pl.BlockSpec(memory_space=memory_space)


def in_hbm(values):
    return [pltpu.with_memory_space_constraint(value, pltpu.HBM) for value in values]


class Layout:
    def __init__(self, local_experts, key_count, query_rows):
        self.ctx, self.exp, self.tp = (lax.axis_size(axis) for axis in ("ctx", "exp", "tp"))
        self.key_count, self.query_rows = key_count, query_rows
        self.local_experts = local_experts
        self.piece_count = self.exp * self.tp
        self.capacity = self.ctx * MOST // CELLS
        self.rows = local_experts * self.capacity // self.piece_count
        self.experts = max(1, self.rows // self.capacity)
        self.spread = max(1, self.capacity // self.rows)
        self.cell_count = self.piece_count * CELLS

    def lead(self, k):
        own = lax.axis_index("ctx")
        start = self.ctx * (self.key_count - self.query_rows)
        return start + (own ^ k) * self.query_rows - own * self.key_count

    def column_piece(self, k):
        return (lax.axis_index("exp") * self.tp + lax.axis_index("tp")) ^ k

    def first_local_expert(self):
        return lax.axis_index("ctx") * self.local_experts

    def cell(self, flip, k, cell):
        piece = (lax.axis_index("tp") ^ flip) * self.exp + (lax.axis_index("exp") ^ k)
        return piece * CELLS + cell, lax.div(piece * self.experts, self.spread)


def lane_ids(shape):
    return lax.broadcasted_iota(jnp.int32, shape, len(shape) - 1)


def row_ids(shape):
    return lax.broadcasted_iota(jnp.int32, shape, len(shape) - 2)


def as_bf16(mask):
    return mask.astype(f32).astype(bf16)


def dot(left, right, dims=((1,), (0,))):
    return lax.dot_general(left, right, (dims, ((), ())), preferred_element_type=f32)


def in_two(value):
    high = value.astype(bf16).astype(f32)
    return high, value - high


def swapped(value, axes, mask):
    count = lax.axis_size(axes)
    pairs = [(source, source ^ mask) for source in range(count)]
    return lax.ppermute(value, axes, pairs)


def far_first(count):
    return list(range(count - 1, 0, -1))


def pack_kernel(
    queries_ref, seg_ref, ids_ref, weight_ref, beside_ref, out_ref,
    seg_here, ids_here, weight_here, done,
):
    rows, width = queries_ref.shape
    choices = ids_ref.shape[0]
    copies = [
        pltpu.make_async_copy(source, target, done.at[i])
        for i, (source, target) in enumerate(
            [
                (seg_ref, seg_here),
                (ids_ref, ids_here),
                (weight_ref, weight_here),
                (queries_ref, out_ref.at[:, :width]),
            ]
        )
    ]
    for copy in copies:
        copy.start()
    shape = (choices, LANES)

    def placed(value, first, last):
        to_lane = (lane_ids(shape) == row_ids(shape) + first) & (row_ids(shape) <= last)
        return dot(value.astype(bf16), as_bf16(to_lane), ((0,), (0,)))

    for copy in copies[:3]:
        copy.wait()
    segs = jnp.broadcast_to(seg_here[...], (choices, rows)).astype(f32)
    high, low = in_two(weight_here[...])
    info = placed(segs, 0, 0) + placed(ids_here[...].astype(f32), 1, choices)
    info = info + placed(high, 1 + choices, choices) + placed(low, 1 + 2 * choices, choices)
    out_ref[:, width:] = info.astype(bf16)
    copies[3].wait()


def pack(queries, query_seg, expert_ids, route_weight, beside):
    rows, width = queries.shape
    small = [query_seg[None, :], expert_ids.T, route_weight.T]
    return pl.pallas_call(
        pack_kernel,
        in_specs=[whole(pltpu.HBM)] * 5,
        out_shape=jax.ShapeDtypeStruct((rows, width + LANES), bf16),
        scratch_shapes=[pltpu.VMEM(value.shape, value.dtype) for value in small]
        + [pltpu.SemaphoreType.DMA((4,))],
        compiler_params=params(4),
        name="pack",
    )(*in_hbm([queries] + small + [beside]))


def sight_kernel(parent_ref, key_seg_ref, sight_ref):
    seg_count, key_count = sight_ref.shape
    square = (seg_count, seg_count)
    same = row_ids(square) == lane_ids(square)
    one = as_bf16((parent_ref[...] == row_ids(square)) | same)
    two = as_bf16(dot(one, one) > 0.5)
    four = as_bf16(dot(two, two) > 0.5)
    six = as_bf16(dot(four, two) > 0.5)
    keys = as_bf16(key_seg_ref[...] == row_ids((seg_count, key_count)))
    sight_ref[...] = dot(six, keys, ((0,), (0,))).astype(bf16)


def sight_of(parent, key_seg):
    assert DEPTH == 6
    return pl.pallas_call(
        sight_kernel,
        out_shape=jax.ShapeDtypeStruct((parent.shape[0], key_seg.shape[0]), bf16),
        compiler_params=params(4),
        cost_estimate=cost(2**24, 2**19),
        name="sight",
    )(parent[None, :], key_seg[None, :])


def attend_kernel(
    heads, scale, layout, k, queries_ref, keys_ref, values_ref, sight_ref, beside_ref,
    out_ref, stacked_ref, probs_ref,
):
    rows = queries_ref.shape[0]
    key_count, head_size = keys_ref.shape
    seg_count = sight_ref.shape[0]
    width = heads * head_size
    info = queries_ref[:, width:].astype(f32)
    own_seg = info[:, :1].astype(jnp.int32)
    onehot = as_bf16(own_seg == lane_ids((rows, seg_count)))
    seen = dot(onehot, sight_ref[...]) > 0.5
    place = (rows, key_count)
    causal = lane_ids(place) - row_ids(place) <= layout.lead(k)
    bias = jnp.where(seen & causal, 0.0, masked_score)
    for head in range(heads):
        columns = slice(head * head_size, (head + 1) * head_size)
        stacked_ref[head * rows : (head + 1) * rows, :] = queries_ref[:, columns]
    scores = dot(stacked_ref[...], keys_ref[...], ((1,), (1,)))
    stats = jnp.zeros((rows, LANES), f32)
    lane = lane_ids((rows, LANES))
    for head in range(heads):
        here = slice(head * rows, (head + 1) * rows)
        biased = scores[here, :] + bias
        high = jnp.maximum(jnp.max(biased, axis=1, keepdims=True), least_high)
        high = high.astype(bf16).astype(f32)
        probs = jnp.exp2((biased - high) * scale)
        total_high, total_low = in_two(jnp.sum(probs, axis=1, keepdims=True))
        probs_ref[here, :] = probs.astype(bf16)
        stats = jnp.where(lane == head, high, stats)
        stats = jnp.where(lane == heads + head, total_high, stats)
        stats = jnp.where(lane == 2 * heads + head, total_low, stats)
    out_ref[:, width:] = stats.astype(bf16)
    sums = dot(probs_ref[...], values_ref[...])
    for head in range(heads):
        columns = slice(head * head_size, (head + 1) * head_size)
        out_ref[:, columns] = sums[head * rows : (head + 1) * rows, :].astype(bf16)


def attend(layout, k, queries, keys, values, sight, heads, scale, beside):
    rows, columns = queries.shape
    key_count, head_size = keys.shape
    work = rows * heads * key_count
    return pl.pallas_call(
        functools.partial(attend_kernel, heads, scale, layout, k),
        in_specs=[whole()] * 4 + [whole(pltpu.HBM)],
        out_shape=jax.ShapeDtypeStruct((rows, columns), bf16),
        scratch_shapes=[
            pltpu.VMEM((rows * heads, head_size), bf16),
            pltpu.VMEM((rows * heads, key_count), bf16),
        ],
        compiler_params=params(8),
        cost_estimate=cost(8 * work * head_size, 2**20, work),
        name="attend",
    )(queries, keys, values, sight, *in_hbm([beside]))


def project_kernel(heads, scale, layout, source_count, *refs):
    parts_refs, weight_ref = refs[:source_count], refs[source_count]
    out_refs, attention_ref = refs[source_count + 1 : -1], refs[-1]
    width = attention_ref.shape[1]
    head_size = width // heads
    stats = [ref[:, width:].astype(f32) for ref in parts_refs]
    top = functools.reduce(jnp.maximum, stats)
    factors = [jnp.exp2(jnp.minimum((stat - top) * scale, 0.0)) for stat in stats]
    total = 0.0
    for stat, factor in zip(stats, factors):
        high = pltpu.roll(stat, LANES - heads, 1)
        low = pltpu.roll(stat, LANES - 2 * heads, 1)
        total = total + factor * (high + low)
    shares = [factor / total for factor in factors]
    for head in range(heads):
        columns = slice(head * head_size, (head + 1) * head_size)
        merged = 0.0
        for ref, share in zip(parts_refs, shares):
            merged = merged + ref[:, columns].astype(f32) * share[:, head : head + 1]
        attention_ref[:, columns] = merged.astype(bf16)
    for i, out_ref in enumerate(out_refs):
        piece_width = out_ref.shape[1]
        start = pl.multiple_of(layout.column_piece(i) * piece_width, piece_width)
        out_ref[...] = dot(attention_ref[...], weight_ref[:, pl.ds(start, piece_width)]).astype(bf16)


def project(layout, parts, weight, heads, scale):
    rows = parts[0].shape[0]
    width, model_width = weight.shape
    piece_width = model_width // layout.piece_count
    return pl.pallas_call(
        functools.partial(project_kernel, heads, scale, layout, len(parts)),
        out_shape=[jax.ShapeDtypeStruct((rows, piece_width), bf16)] * layout.piece_count,
        scratch_shapes=[pltpu.VMEM((rows, width), bf16)],
        compiler_params=params(8),
        cost_estimate=cost(2 * rows * width * model_width, 2 * width * model_width),
        name="project",
    )(*parts, weight)


def mix_kernel(residual_ref, gain_ref, *refs):
    parts_refs, (mixed_ref, sent_ref) = refs[:-2], refs[-2:]
    rows, width = mixed_ref.shape
    mixed = residual_ref[...].astype(f32)
    for ref in parts_refs:
        mixed = mixed + ref[...].astype(f32)
    mixed_ref[...] = mixed
    sent_ref[:, :width] = (mixed * gain_ref[...].astype(f32)).astype(bf16)
    high, low = in_two(jnp.sum(mixed * mixed, axis=1, keepdims=True))
    lane = lane_ids((rows, LANES))
    squares = jnp.where(lane == 0, high, jnp.where(lane == 1, low, 0.0))
    sent_ref[:, width:] = squares.astype(bf16)


def mix(residual, gain, parts):
    rows, width = residual.shape
    return pl.pallas_call(
        mix_kernel,
        out_shape=(
            jax.ShapeDtypeStruct((rows, width), f32),
            jax.ShapeDtypeStruct((rows, width + LANES), bf16),
        ),
        compiler_params=params(4),
        name="mix",
    )(residual, gain[None, :], *parts)


def route_kernel(layout, choices, width, *refs):
    info_refs, (place_ref, high_ref, low_ref) = refs[:-3], refs[-3:]
    cell_count, tokens, slots = place_ref.shape
    local_experts, capacity = layout.local_experts, layout.capacity
    expert = (lane_ids((tokens, local_experts)) + layout.first_local_expert()).astype(f32)
    square = (tokens, tokens)
    earlier = as_bf16(lane_ids(square) < row_ids(square))
    count = len(info_refs) // CELLS
    for cell in range(CELLS):
        sources = info_refs[cell * count : (cell + 1) * count]
        info = jnp.concatenate([ref[:, width:] for ref in sources], axis=0).astype(f32)
        member = jnp.zeros((tokens, local_experts), f32)
        weight_high = jnp.zeros((tokens, local_experts), f32)
        weight_low = jnp.zeros((tokens, local_experts), f32)
        for k in range(choices):
            chosen = info[:, 1 + k : 2 + k] == expert
            high = info[:, 1 + choices + k : 2 + choices + k]
            low = info[:, 1 + 2 * choices + k : 2 + 2 * choices + k]
            member = jnp.where(chosen, 1.0, member)
            weight_high = jnp.where(chosen, high, weight_high)
            weight_low = jnp.where(chosen, low, weight_low)
        rank = jnp.where(member > 0.5, dot(earlier, member.astype(bf16)), -1.0).astype(bf16)
        weight_high = weight_high.astype(bf16)
        weight_low = weight_low.astype(bf16)
        for piece in range(layout.piece_count):
            slot = lane_ids((local_experts, slots)) + piece * slots
            spread = as_bf16(slot // capacity == row_ids((local_experts, slots)))
            wanted = (lane_ids((tokens, slots)) + piece * slots) % capacity
            placed = dot(rank, spread) == wanted.astype(f32)
            at = piece * CELLS + cell
            place_ref[at] = jnp.where(placed, 1.0, 0.0).astype(bf16)
            high_ref[at] = jnp.where(placed, dot(weight_high, spread), 0.0).astype(bf16)
            low_ref[at] = jnp.where(placed, dot(weight_low, spread), 0.0).astype(bf16)


def route(layout, packed, width, choices):
    tokens = sum(value.shape[0] for value in packed) // CELLS
    shape = jax.ShapeDtypeStruct((layout.cell_count, tokens, layout.rows), bf16)
    return pl.pallas_call(
        functools.partial(route_kernel, layout, choices, width),
        out_shape=(shape, shape, shape),
        compiler_params=params(16),
        cost_estimate=cost(2**25, 2**20),
        name="route",
    )(*packed)


def squares_joined(squares):
    high, low = in_two(squares[:, :1] + squares[:, 1:2])
    lane = lane_ids(squares.shape)
    return jnp.where(lane == 0, high, jnp.where(lane == 1, low, 0.0))


def gate_up(names, layout, place, sources, weight):
    _, width, ff_pair = weight.shape
    each = layout.rows // layout.experts
    cells = sorted({name[2] for name in names})
    count = len(sources[0])

    def kernel(place_ref, weight_ref, *refs):
        for name, out_ref in zip(names, refs[len(cells) * count :]):
            at, first = layout.cell(*name)
            turn = cells.index(name[2])
            picked = 0.0
            for i, ref in enumerate(refs[turn * count : (turn + 1) * count]):
                tokens = ref.shape[0]
                here = place_ref[at, i * tokens : (i + 1) * tokens, :]
                picked = picked + dot(here, ref[...], ((0,), (0,)))
            picked = picked.astype(bf16)
            for i in range(layout.experts):
                here = slice(i * each, (i + 1) * each)
                product = dot(picked[here, :width], weight_ref[first + i])
                out_ref[here, :ff_pair] = product.astype(bf16)
            out_ref[:, ff_pair:] = picked[:, width:]

    out = jax.ShapeDtypeStruct((layout.rows, ff_pair + LANES), bf16)
    return pl.pallas_call(
        kernel,
        out_shape=[out] * len(names),
        compiler_params=params(8),
        cost_estimate=cost(2 * layout.rows * width * ff_pair, 2 * layout.rows * ff_pair),
        name="gate_up",
    )(place, weight, *[value for cell in cells for value in sources[cell]])


def join_kernel(left_ref, right_ref, out_ref):
    ff_pair = out_ref.shape[1] - LANES
    product = left_ref[:, :ff_pair].astype(f32) + right_ref[:, :ff_pair].astype(f32)
    out_ref[:, :ff_pair] = product.astype(bf16)
    squares = left_ref[:, ff_pair:].astype(f32) + right_ref[:, ff_pair:].astype(f32)
    out_ref[:, ff_pair:] = squares_joined(squares).astype(bf16)


def join(left, right):
    return pl.pallas_call(
        join_kernel,
        out_shape=jax.ShapeDtypeStruct(left.shape, bf16),
        compiler_params=params(4),
        name="join",
    )(left, right)


def hidden_of(parts, ff_width, model_width, beside):
    def kernel(*refs):
        refs, out_ref = refs[len(beside) : -1], refs[-1]
        total = 0.0
        for ref in refs:
            total = total + ref[...].astype(f32)
        high = total[:, 2 * ff_width : 2 * ff_width + 1]
        low = total[:, 2 * ff_width + 1 : 2 * ff_width + 2]
        norm = lax.rsqrt((high + low) / model_width + epsilon)
        gate = total[:, :ff_width] * norm
        up = total[:, ff_width : 2 * ff_width] * norm
        out_ref[...] = (gate / (1.0 + jnp.exp(-gate)) * up).astype(bf16)

    return pl.pallas_call(
        kernel,
        in_specs=[whole(pltpu.HBM)] * len(beside) + [whole()] * len(parts),
        out_shape=jax.ShapeDtypeStruct((parts[0].shape[0], ff_width), bf16),
        compiler_params=params(8),
        name="hidden",
    )(*in_hbm(beside), *parts)


def down(pieces, layout, weight, high, low, total=None, out_count=1):
    first_cells = next(iter(pieces.values()))
    ff_width = first_cells[0].shape[1]
    tokens = high.shape[1]
    piece_width = weight.shape[2]
    each = layout.rows // layout.experts
    rows = tokens * CELLS // out_count
    out_type = f32 if out_count == 1 else bf16

    def kernel(weight_ref, high_ref, low_ref, *refs):
        hidden_refs, refs = refs[: len(pieces) * CELLS], refs[len(pieces) * CELLS :]
        total_refs, out_refs, held_ref = refs[: -1 - out_count], refs[-1 - out_count : -1], refs[-1]
        summed = [0.0] * CELLS
        for turn, name in enumerate(pieces):
            cells = hidden_refs[turn * CELLS : (turn + 1) * CELLS]
            _, first = layout.cell(*name, 0)
            for i in range(layout.experts):
                here = slice(i * each, (i + 1) * each)
                rows_in = jnp.concatenate([ref[here, :] for ref in cells], axis=0)
                product = dot(rows_in, weight_ref[first + i]).astype(bf16)
                for cell in range(CELLS):
                    held_ref[cell, here, :] = product[cell * each : (cell + 1) * each, :]
            for cell in range(CELLS):
                at, _ = layout.cell(*name, cell)
                held = held_ref[cell]
                summed[cell] = summed[cell] + dot(high_ref[at], held) + dot(low_ref[at], held)
        whole_sum = jnp.concatenate(summed, axis=0)
        for ref in total_refs:
            whole_sum = whole_sum + ref[...]
        for i, ref in enumerate(out_refs):
            ref[...] = whole_sum[i * rows : (i + 1) * rows, :].astype(ref.dtype)

    before = [] if total is None else [total]
    hidden = [value for cells in pieces.values() for value in cells]
    return pl.pallas_call(
        kernel,
        out_shape=[jax.ShapeDtypeStruct((rows, piece_width), out_type)] * out_count,
        scratch_shapes=[pltpu.VMEM((CELLS, layout.rows, piece_width), bf16)],
        compiler_params=params(8),
        cost_estimate=cost(4 * layout.rows * ff_width * piece_width, 2**20),
        name="down",
    )(weight, high, low, *hidden, *before)


def finish_kernel(mixed_ref, *refs):
    total = mixed_ref[...]
    for ref in refs[:-1]:
        total = total + ref[...].astype(f32)
    refs[-1][...] = total.astype(bf16)


def finish(mixed, parts):
    return pl.pallas_call(
        finish_kernel,
        out_shape=jax.ShapeDtypeStruct(mixed.shape, bf16),
        compiler_params=params(4),
        name="finish",
    )(mixed, *parts)


def body(
    queries,
    cached_keys,
    cached_values,
    key_seg,
    query_seg,
    parent,
    out_weight,
    residual,
    norm_gain,
    gate_up_weight,
    down_weight,
    expert_ids,
    route_weight,
):
    ctx_count, exp_count, tp_count = (lax.axis_size(axis) for axis in ("ctx", "exp", "tp"))
    assert tp_count == 2 and cached_keys.shape[1] == 1
    assert ctx_count & (ctx_count - 1) == 0 and exp_count & (exp_count - 1) == 0
    piece_count = exp_count * tp_count
    query_rows = queries.shape[0]
    key_count, _, head_size = cached_keys.shape
    heads = queries.shape[2] // head_size
    width = heads * head_size
    model_width = out_weight.shape[2]
    local_experts, piece_width, _ = gate_up_weight.shape
    ff_width = down_weight.shape[1]
    choices = expert_ids.shape[1]
    scale = math.log2(math.e) / math.sqrt(head_size)

    layout = Layout(local_experts, key_count, query_rows)

    packed = pack(
        queries.reshape(query_rows, width), query_seg, expert_ids, route_weight, gate_up_weight
    )
    gathered = {0: packed}
    for k in far_first(ctx_count):
        gathered[k] = swapped(packed, "ctx", k)
    sight = sight_of(parent, key_seg)
    keys = cached_keys.reshape(key_count, head_size)
    values = cached_values.reshape(key_count, head_size)
    out_matrix = out_weight.reshape(width, model_width)
    parts = {}
    for k in list(range(1, ctx_count)) + [0]:
        part = attend(
            layout, k, gathered[k], keys, values, sight, heads, scale, gate_up_weight
        )
        parts[k] = swapped(part, "ctx", k) if k else part
    place, combine_high, combine_low = route(
        layout, [gathered[k] for k in range(ctx_count)], width, choices
    )
    def after(value, *others):
        return lax.optimization_barrier((value,) + others)[0]

    projected = project(
        layout,
        [parts[k] for k in range(ctx_count)],
        after(out_matrix, place),
        heads,
        scale,
    )
    pieces = [projected[0]] + [
        swapped(projected[k], ("exp", "tp"), k) for k in far_first(piece_count)
    ]
    mixed, sent = mix(residual, norm_gain, pieces)
    rows = {0: sent}
    for k in far_first(ctx_count):
        rows[k] = swapped(sent, "ctx", k)
    half = ctx_count // CELLS
    sources = [[rows[k] for k in range(half * i, half * (i + 1))] for i in range(CELLS)]

    def first_half(*names):
        return gate_up(names, layout, place, sources, gate_up_weight)

    crossed = [[] for _ in range(CELLS)]
    for k in far_first(exp_count):
        away, mine = first_half((1, k, 0), (0, k, 0))
        here = [swapped(away, "tp", 1)]
        sources[1] = list(lax.optimization_barrier(tuple(sources[1]) + (mine,)))[:-1]
        here.append(swapped(first_half((1, k, 1))[0], "tp", 1))
        for cell in range(CELLS):
            if cell:
                mine = first_half((0, k, cell))[0]
            joined = join(mine, here[cell])
            place = after(place, joined)
            crossed[cell].append(swapped(joined, "exp", k))
    arrived = [swapped(first_half((1, 0, 0))[0], "tp", 1)]
    kept = list(first_half((0, 0, 0), (0, 0, 1)))
    own_hidden = []
    for cell in range(CELLS):
        if cell:
            arrived.append(swapped(first_half((1, 0, cell))[0], "tp", 1))
        crossed[cell], kept[cell] = lax.optimization_barrier((crossed[cell], kept[cell]))
        beside = [out_matrix] * 3
        hidden = hidden_of([kept[cell], arrived[cell]] + crossed[cell], ff_width, model_width, beside)
        place = after(place, hidden)
        own_hidden.append(hidden)

    near = [swapped(hidden, "tp", 1) for hidden in own_hidden]
    far = {
        k: [swapped(hidden, "exp", k) for hidden in own_hidden] for k in range(1, exp_count)
    }
    own_hidden[-1] = after(own_hidden[-1], far[1][0])

    def add(pieces, total, out_count=1):
        return down(pieces, layout, down_weight, combine_high, combine_low, total, out_count)

    total = add({(0, 0): own_hidden, (1, 0): near}, None)[0]
    last = {}
    for k in far:
        far[k][-1] = after(far[k][-1], total)
        last[1, k] = [swapped(hidden, "tp", 1) for hidden in far[k]]
        total = add({(0, k): far[k]}, total)[0]
    totals = add(last, total, ctx_count)
    returned = [totals[0]] + [swapped(totals[k], "ctx", k) for k in far_first(ctx_count)]
    return finish(mixed, returned)


def solution(mesh):
    in_specs = (
        P(("group", "ctx"), "tp", "exp"),
        P(("group", "ctx"), "tp", None),
        P(("group", "ctx"), "tp", None),
        P(("group", "ctx")),
        P(("group", "ctx")),
        P("group"),
        P("tp", "exp", None),
        P(("group", "ctx"), ("exp", "tp")),
        P(("exp", "tp")),
        P("ctx", ("exp", "tp"), None),
        P("ctx", None, ("exp", "tp")),
        P(("group", "ctx"), None),
        P(("group", "ctx"), None),
    )
    out_specs = P(("group", "ctx"), ("exp", "tp"))
    return jax.shard_map(body, mesh=mesh, in_specs=in_specs, out_specs=out_specs, check_vma=False)
```

```python
import functools
import math

import jax
import jax.numpy as jnp
from jax import lax
from jax.experimental import pallas as pl
from jax.experimental.pallas import tpu as pltpu
from jax.sharding import PartitionSpec as P

MOST = 8
DEPTH = 6
LANES = 128
CELLS = 2

epsilon = 1e-06
masked_score = -1e30
least_high = -1e20

f32 = jnp.float32
bf16 = jnp.bfloat16


def params(megabytes, steps=0):
    semantics = ("arbitrary",) * steps if steps else None
    return pltpu.CompilerParams(
        vmem_limit_bytes=megabytes * 1024 * 1024, dimension_semantics=semantics
    )


def cost(flops, bytes_accessed, transcendentals=0):
    return pl.CostEstimate(
        flops=flops, bytes_accessed=bytes_accessed, transcendentals=transcendentals
    )


def whole(memory_space=pltpu.VMEM):
    return pl.BlockSpec(memory_space=memory_space)


def in_hbm(values):
    return [pltpu.with_memory_space_constraint(value, pltpu.HBM) for value in values]


class Layout:
    def __init__(self, local_experts, key_count, query_rows):
        self.ctx, self.exp, self.tp = (lax.axis_size(axis) for axis in ("ctx", "exp", "tp"))
        self.key_count, self.query_rows = key_count, query_rows
        self.local_experts = local_experts
        self.piece_count = self.exp * self.tp
        self.capacity = self.ctx * MOST // CELLS
        self.rows = local_experts * self.capacity // self.piece_count
        self.experts = max(1, self.rows // self.capacity)
        self.spread = max(1, self.capacity // self.rows)
        self.cell_count = self.piece_count * CELLS

    def lead(self, k):
        own = lax.axis_index("ctx")
        start = self.ctx * (self.key_count - self.query_rows)
        return start + (own ^ k) * self.query_rows - own * self.key_count

    def column_piece(self, k):
        return (lax.axis_index("exp") * self.tp + lax.axis_index("tp")) ^ k

    def first_local_expert(self):
        return lax.axis_index("ctx") * self.local_experts

    def cell(self, flip, k, cell):
        piece = (lax.axis_index("tp") ^ flip) * self.exp + (lax.axis_index("exp") ^ k)
        return piece * CELLS + cell, lax.div(piece * self.experts, self.spread)


def lane_ids(shape):
    return lax.broadcasted_iota(jnp.int32, shape, len(shape) - 1)


def row_ids(shape):
    return lax.broadcasted_iota(jnp.int32, shape, len(shape) - 2)


def as_bf16(mask):
    return mask.astype(f32).astype(bf16)


def dot(left, right, dims=((1,), (0,))):
    return lax.dot_general(left, right, (dims, ((), ())), preferred_element_type=f32)


def in_two(value):
    high = value.astype(bf16).astype(f32)
    return high, value - high


def swapped(value, axes, mask):
    count = lax.axis_size(axes)
    pairs = [(source, source ^ mask) for source in range(count)]
    return lax.ppermute(value, axes, pairs)


def far_first(count):
    return list(range(count - 1, 0, -1))


def pack_kernel(
    queries_ref, seg_ref, ids_ref, weight_ref, beside_ref, out_ref,
    seg_here, ids_here, weight_here, done,
):
    rows, width = queries_ref.shape
    choices = ids_ref.shape[0]
    copies = [
        pltpu.make_async_copy(source, target, done.at[i])
        for i, (source, target) in enumerate(
            [
                (seg_ref, seg_here),
                (ids_ref, ids_here),
                (weight_ref, weight_here),
                (queries_ref, out_ref.at[:, :width]),
            ]
        )
    ]
    for copy in copies:
        copy.start()
    shape = (choices, LANES)

    def placed(value, first, last):
        to_lane = (lane_ids(shape) == row_ids(shape) + first) & (row_ids(shape) <= last)
        return dot(value.astype(bf16), as_bf16(to_lane), ((0,), (0,)))

    for copy in copies[:3]:
        copy.wait()
    segs = jnp.broadcast_to(seg_here[...], (choices, rows)).astype(f32)
    high, low = in_two(weight_here[...])
    info = placed(segs, 0, 0) + placed(ids_here[...].astype(f32), 1, choices)
    info = info + placed(high, 1 + choices, choices) + placed(low, 1 + 2 * choices, choices)
    out_ref[:, width:] = info.astype(bf16)
    copies[3].wait()


def pack(queries, query_seg, expert_ids, route_weight, beside):
    rows, width = queries.shape
    small = [query_seg[None, :], expert_ids.T, route_weight.T]
    return pl.pallas_call(
        pack_kernel,
        in_specs=[whole(pltpu.HBM)] * 5,
        out_shape=jax.ShapeDtypeStruct((rows, width + LANES), bf16),
        scratch_shapes=[pltpu.VMEM(value.shape, value.dtype) for value in small]
        + [pltpu.SemaphoreType.DMA((4,))],
        compiler_params=params(4),
        name="pack",
    )(*in_hbm([queries] + small + [beside]))


def sight_kernel(parent_ref, key_seg_ref, sight_ref):
    seg_count, key_count = sight_ref.shape
    square = (seg_count, seg_count)
    same = row_ids(square) == lane_ids(square)
    one = as_bf16((parent_ref[...] == row_ids(square)) | same)
    two = as_bf16(dot(one, one) > 0.5)
    four = as_bf16(dot(two, two) > 0.5)
    six = as_bf16(dot(four, two) > 0.5)
    keys = as_bf16(key_seg_ref[...] == row_ids((seg_count, key_count)))
    sight_ref[...] = dot(six, keys, ((0,), (0,))).astype(bf16)


def sight_of(parent, key_seg):
    assert DEPTH == 6
    return pl.pallas_call(
        sight_kernel,
        out_shape=jax.ShapeDtypeStruct((parent.shape[0], key_seg.shape[0]), bf16),
        compiler_params=params(4),
        cost_estimate=cost(2**24, 2**19),
        name="sight",
    )(parent[None, :], key_seg[None, :])


def attend_kernel(
    heads, scale, layout, k, queries_ref, keys_ref, values_ref, sight_ref, beside_ref,
    out_ref, stacked_ref, probs_ref,
):
    rows = queries_ref.shape[0]
    key_count, head_size = keys_ref.shape
    seg_count = sight_ref.shape[0]
    width = heads * head_size
    info = queries_ref[:, width:].astype(f32)
    own_seg = info[:, :1].astype(jnp.int32)
    onehot = as_bf16(own_seg == lane_ids((rows, seg_count)))
    seen = dot(onehot, sight_ref[...]) > 0.5
    place = (rows, key_count)
    causal = lane_ids(place) - row_ids(place) <= layout.lead(k)
    bias = jnp.where(seen & causal, 0.0, masked_score)
    for head in range(heads):
        columns = slice(head * head_size, (head + 1) * head_size)
        stacked_ref[head * rows : (head + 1) * rows, :] = queries_ref[:, columns]
    scores = dot(stacked_ref[...], keys_ref[...], ((1,), (1,)))
    stats = jnp.zeros((rows, LANES), f32)
    lane = lane_ids((rows, LANES))
    for head in range(heads):
        here = slice(head * rows, (head + 1) * rows)
        biased = scores[here, :] + bias
        high = jnp.maximum(jnp.max(biased, axis=1, keepdims=True), least_high)
        high = high.astype(bf16).astype(f32)
        probs = jnp.exp2((biased - high) * scale)
        total_high, total_low = in_two(jnp.sum(probs, axis=1, keepdims=True))
        probs_ref[here, :] = probs.astype(bf16)
        stats = jnp.where(lane == head, high, stats)
        stats = jnp.where(lane == heads + head, total_high, stats)
        stats = jnp.where(lane == 2 * heads + head, total_low, stats)
    out_ref[:, width:] = stats.astype(bf16)
    sums = dot(probs_ref[...], values_ref[...])
    for head in range(heads):
        columns = slice(head * head_size, (head + 1) * head_size)
        out_ref[:, columns] = sums[head * rows : (head + 1) * rows, :].astype(bf16)


def attend(layout, k, queries, keys, values, sight, heads, scale, beside):
    rows, columns = queries.shape
    key_count, head_size = keys.shape
    work = rows * heads * key_count
    return pl.pallas_call(
        functools.partial(attend_kernel, heads, scale, layout, k),
        in_specs=[whole()] * 4 + [whole(pltpu.HBM)],
        out_shape=jax.ShapeDtypeStruct((rows, columns), bf16),
        scratch_shapes=[
            pltpu.VMEM((rows * heads, head_size), bf16),
            pltpu.VMEM((rows * heads, key_count), bf16),
        ],
        compiler_params=params(8),
        cost_estimate=cost(8 * work * head_size, 2**20, work),
        name="attend",
    )(queries, keys, values, sight, *in_hbm([beside]))


def project_kernel(heads, scale, layout, source_count, *refs):
    parts_refs, weight_ref = refs[:source_count], refs[source_count]
    out_refs, attention_ref = refs[source_count + 1 : -1], refs[-1]
    width = attention_ref.shape[1]
    head_size = width // heads
    stats = [ref[:, width:].astype(f32) for ref in parts_refs]
    top = functools.reduce(jnp.maximum, stats)
    factors = [jnp.exp2(jnp.minimum((stat - top) * scale, 0.0)) for stat in stats]
    total = 0.0
    for stat, factor in zip(stats, factors):
        high = pltpu.roll(stat, LANES - heads, 1)
        low = pltpu.roll(stat, LANES - 2 * heads, 1)
        total = total + factor * (high + low)
    shares = [factor / total for factor in factors]
    for head in range(heads):
        columns = slice(head * head_size, (head + 1) * head_size)
        merged = 0.0
        for ref, share in zip(parts_refs, shares):
            merged = merged + ref[:, columns].astype(f32) * share[:, head : head + 1]
        attention_ref[:, columns] = merged.astype(bf16)
    for i, out_ref in enumerate(out_refs):
        piece_width = out_ref.shape[1]
        start = pl.multiple_of(layout.column_piece(i) * piece_width, piece_width)
        out_ref[...] = dot(attention_ref[...], weight_ref[:, pl.ds(start, piece_width)]).astype(bf16)


def project(layout, parts, weight, heads, scale):
    rows = parts[0].shape[0]
    width, model_width = weight.shape
    piece_width = model_width // layout.piece_count
    return pl.pallas_call(
        functools.partial(project_kernel, heads, scale, layout, len(parts)),
        out_shape=[jax.ShapeDtypeStruct((rows, piece_width), bf16)] * layout.piece_count,
        scratch_shapes=[pltpu.VMEM((rows, width), bf16)],
        compiler_params=params(8),
        cost_estimate=cost(2 * rows * width * model_width, 2 * width * model_width),
        name="project",
    )(*parts, weight)


def mix_kernel(residual_ref, gain_ref, *refs):
    parts_refs, (mixed_ref, sent_ref) = refs[:-2], refs[-2:]
    rows, width = mixed_ref.shape
    mixed = residual_ref[...].astype(f32)
    for ref in parts_refs:
        mixed = mixed + ref[...].astype(f32)
    mixed_ref[...] = mixed
    sent_ref[:, :width] = (mixed * gain_ref[...].astype(f32)).astype(bf16)
    high, low = in_two(jnp.sum(mixed * mixed, axis=1, keepdims=True))
    lane = lane_ids((rows, LANES))
    squares = jnp.where(lane == 0, high, jnp.where(lane == 1, low, 0.0))
    sent_ref[:, width:] = squares.astype(bf16)


def mix(residual, gain, parts):
    rows, width = residual.shape
    return pl.pallas_call(
        mix_kernel,
        out_shape=(
            jax.ShapeDtypeStruct((rows, width), f32),
            jax.ShapeDtypeStruct((rows, width + LANES), bf16),
        ),
        compiler_params=params(4),
        name="mix",
    )(residual, gain[None, :], *parts)


def route_kernel(layout, choices, width, *refs):
    info_refs, (place_ref, high_ref, low_ref) = refs[:-3], refs[-3:]
    cell_count, tokens, slots = place_ref.shape
    local_experts, capacity = layout.local_experts, layout.capacity
    expert = (lane_ids((tokens, local_experts)) + layout.first_local_expert()).astype(f32)
    square = (tokens, tokens)
    earlier = as_bf16(lane_ids(square) < row_ids(square))
    count = len(info_refs) // CELLS
    for cell in range(CELLS):
        sources = info_refs[cell * count : (cell + 1) * count]
        info = jnp.concatenate([ref[:, width:] for ref in sources], axis=0).astype(f32)
        member = jnp.zeros((tokens, local_experts), f32)
        weight_high = jnp.zeros((tokens, local_experts), f32)
        weight_low = jnp.zeros((tokens, local_experts), f32)
        for k in range(choices):
            chosen = info[:, 1 + k : 2 + k] == expert
            high = info[:, 1 + choices + k : 2 + choices + k]
            low = info[:, 1 + 2 * choices + k : 2 + 2 * choices + k]
            member = jnp.where(chosen, 1.0, member)
            weight_high = jnp.where(chosen, high, weight_high)
            weight_low = jnp.where(chosen, low, weight_low)
        rank = jnp.where(member > 0.5, dot(earlier, member.astype(bf16)), -1.0).astype(bf16)
        weight_high = weight_high.astype(bf16)
        weight_low = weight_low.astype(bf16)
        for piece in range(layout.piece_count):
            slot = lane_ids((local_experts, slots)) + piece * slots
            spread = as_bf16(slot // capacity == row_ids((local_experts, slots)))
            wanted = (lane_ids((tokens, slots)) + piece * slots) % capacity
            placed = dot(rank, spread) == wanted.astype(f32)
            at = piece * CELLS + cell
            place_ref[at] = jnp.where(placed, 1.0, 0.0).astype(bf16)
            high_ref[at] = jnp.where(placed, dot(weight_high, spread), 0.0).astype(bf16)
            low_ref[at] = jnp.where(placed, dot(weight_low, spread), 0.0).astype(bf16)


def route(layout, packed, width, choices):
    tokens = sum(value.shape[0] for value in packed) // CELLS
    shape = jax.ShapeDtypeStruct((layout.cell_count, tokens, layout.rows), bf16)
    return pl.pallas_call(
        functools.partial(route_kernel, layout, choices, width),
        out_shape=(shape, shape, shape),
        compiler_params=params(16),
        cost_estimate=cost(2**25, 2**20),
        name="route",
    )(*packed)


def squares_joined(squares):
    high, low = in_two(squares[:, :1] + squares[:, 1:2])
    lane = lane_ids(squares.shape)
    return jnp.where(lane == 0, high, jnp.where(lane == 1, low, 0.0))


def gate_up(names, layout, place, sources, weight):
    _, width, ff_pair = weight.shape
    each = layout.rows // layout.experts
    cells = sorted({name[2] for name in names})
    count = len(sources[0])

    def kernel(place_ref, weight_ref, *refs):
        for name, out_ref in zip(names, refs[len(cells) * count :]):
            at, first = layout.cell(*name)
            turn = cells.index(name[2])
            picked = 0.0
            for i, ref in enumerate(refs[turn * count : (turn + 1) * count]):
                tokens = ref.shape[0]
                here = place_ref[at, i * tokens : (i + 1) * tokens, :]
                picked = picked + dot(here, ref[...], ((0,), (0,)))
            picked = picked.astype(bf16)
            for i in range(layout.experts):
                here = slice(i * each, (i + 1) * each)
                product = dot(picked[here, :width], weight_ref[first + i])
                out_ref[here, :ff_pair] = product.astype(bf16)
            out_ref[:, ff_pair:] = picked[:, width:]

    out = jax.ShapeDtypeStruct((layout.rows, ff_pair + LANES), bf16)
    return pl.pallas_call(
        kernel,
        out_shape=[out] * len(names),
        compiler_params=params(8),
        cost_estimate=cost(2 * layout.rows * width * ff_pair, 2 * layout.rows * ff_pair),
        name="gate_up",
    )(place, weight, *[value for cell in cells for value in sources[cell]])


def join_kernel(left_ref, right_ref, out_ref):
    ff_pair = out_ref.shape[1] - LANES
    product = left_ref[:, :ff_pair].astype(f32) + right_ref[:, :ff_pair].astype(f32)
    out_ref[:, :ff_pair] = product.astype(bf16)
    squares = left_ref[:, ff_pair:].astype(f32) + right_ref[:, ff_pair:].astype(f32)
    out_ref[:, ff_pair:] = squares_joined(squares).astype(bf16)


def join(left, right):
    return pl.pallas_call(
        join_kernel,
        out_shape=jax.ShapeDtypeStruct(left.shape, bf16),
        compiler_params=params(4),
        name="join",
    )(left, right)


def hidden_of(parts, ff_width, model_width, beside):
    def kernel(*refs):
        refs, out_ref = refs[len(beside) : -1], refs[-1]
        total = 0.0
        for ref in refs:
            total = total + ref[...].astype(f32)
        high = total[:, 2 * ff_width : 2 * ff_width + 1]
        low = total[:, 2 * ff_width + 1 : 2 * ff_width + 2]
        norm = lax.rsqrt((high + low) / model_width + epsilon)
        gate = total[:, :ff_width] * norm
        up = total[:, ff_width : 2 * ff_width] * norm
        out_ref[...] = (gate / (1.0 + jnp.exp(-gate)) * up).astype(bf16)

    return pl.pallas_call(
        kernel,
        in_specs=[whole(pltpu.HBM)] * len(beside) + [whole()] * len(parts),
        out_shape=jax.ShapeDtypeStruct((parts[0].shape[0], ff_width), bf16),
        compiler_params=params(8),
        name="hidden",
    )(*in_hbm(beside), *parts)


def down(pieces, layout, weight, high, low, total=None, out_count=1):
    first_cells = next(iter(pieces.values()))
    ff_width = first_cells[0].shape[1]
    tokens = high.shape[1]
    piece_width = weight.shape[2]
    each = layout.rows // layout.experts
    rows = tokens * CELLS // out_count
    out_type = f32 if out_count == 1 else bf16

    def kernel(weight_ref, high_ref, low_ref, *refs):
        hidden_refs, refs = refs[: len(pieces) * CELLS], refs[len(pieces) * CELLS :]
        total_refs, out_refs, held_ref = refs[: -1 - out_count], refs[-1 - out_count : -1], refs[-1]
        summed = [0.0] * CELLS
        for turn, name in enumerate(pieces):
            cells = hidden_refs[turn * CELLS : (turn + 1) * CELLS]
            _, first = layout.cell(*name, 0)
            for i in range(layout.experts):
                here = slice(i * each, (i + 1) * each)
                rows_in = jnp.concatenate([ref[here, :] for ref in cells], axis=0)
                product = dot(rows_in, weight_ref[first + i]).astype(bf16)
                for cell in range(CELLS):
                    held_ref[cell, here, :] = product[cell * each : (cell + 1) * each, :]
            for cell in range(CELLS):
                at, _ = layout.cell(*name, cell)
                held = held_ref[cell]
                summed[cell] = summed[cell] + dot(high_ref[at], held) + dot(low_ref[at], held)
        whole_sum = jnp.concatenate(summed, axis=0)
        for ref in total_refs:
            whole_sum = whole_sum + ref[...]
        for i, ref in enumerate(out_refs):
            ref[...] = whole_sum[i * rows : (i + 1) * rows, :].astype(ref.dtype)

    before = [] if total is None else [total]
    hidden = [value for cells in pieces.values() for value in cells]
    return pl.pallas_call(
        kernel,
        out_shape=[jax.ShapeDtypeStruct((rows, piece_width), out_type)] * out_count,
        scratch_shapes=[pltpu.VMEM((CELLS, layout.rows, piece_width), bf16)],
        compiler_params=params(8),
        cost_estimate=cost(4 * layout.rows * ff_width * piece_width, 2**20),
        name="down",
    )(weight, high, low, *hidden, *before)


def finish_kernel(mixed_ref, *refs):
    total = mixed_ref[...]
    for ref in refs[:-1]:
        total = total + ref[...].astype(f32)
    refs[-1][...] = total.astype(bf16)


def finish(mixed, parts):
    return pl.pallas_call(
        finish_kernel,
        out_shape=jax.ShapeDtypeStruct(mixed.shape, bf16),
        compiler_params=params(4),
        name="finish",
    )(mixed, *parts)


def body(
    queries,
    cached_keys,
    cached_values,
    key_seg,
    query_seg,
    parent,
    out_weight,
    residual,
    norm_gain,
    gate_up_weight,
    down_weight,
    expert_ids,
    route_weight,
):
    ctx_count, exp_count, tp_count = (lax.axis_size(axis) for axis in ("ctx", "exp", "tp"))
    assert tp_count == 2 and cached_keys.shape[1] == 1
    assert ctx_count & (ctx_count - 1) == 0 and exp_count & (exp_count - 1) == 0
    piece_count = exp_count * tp_count
    query_rows = queries.shape[0]
    key_count, _, head_size = cached_keys.shape
    heads = queries.shape[2] // head_size
    width = heads * head_size
    model_width = out_weight.shape[2]
    local_experts, piece_width, _ = gate_up_weight.shape
    ff_width = down_weight.shape[1]
    choices = expert_ids.shape[1]
    scale = math.log2(math.e) / math.sqrt(head_size)

    layout = Layout(local_experts, key_count, query_rows)

    packed = pack(
        queries.reshape(query_rows, width), query_seg, expert_ids, route_weight, gate_up_weight
    )
    gathered = {0: packed}
    for k in far_first(ctx_count):
        gathered[k] = swapped(packed, "ctx", k)
    sight = sight_of(parent, key_seg)
    keys = cached_keys.reshape(key_count, head_size)
    values = cached_values.reshape(key_count, head_size)
    out_matrix = out_weight.reshape(width, model_width)
    parts = {}
    for k in far_first(ctx_count) + [0]:
        part = attend(
            layout, k, gathered[k], keys, values, sight, heads, scale, gate_up_weight
        )
        parts[k] = swapped(part, "ctx", k) if k else part
    place, combine_high, combine_low = route(
        layout, [gathered[k] for k in range(ctx_count)], width, choices
    )
    def after(value, *others):
        return lax.optimization_barrier((value,) + others)[0]

    projected = project(
        layout,
        list(parts.values()),
        after(out_matrix, place),
        heads,
        scale,
    )
    pieces = [projected[0]] + [
        swapped(projected[k], ("exp", "tp"), k) for k in far_first(piece_count)
    ]
    mixed, sent = mix(residual, norm_gain, pieces)
    rows = {0: sent}
    for k in far_first(ctx_count):
        rows[k] = swapped(sent, "ctx", k)
    half = ctx_count // CELLS
    sources = [[rows[k] for k in range(half * i, half * (i + 1))] for i in range(CELLS)]

    def first_half(*names):
        return gate_up(names, layout, place, sources, gate_up_weight)

    crossed = [[] for _ in range(CELLS)]
    for k in far_first(exp_count):
        away, mine = first_half((1, k, 0), (0, k, 0))
        here = [swapped(away, "tp", 1)]
        sources[1] = list(lax.optimization_barrier(tuple(sources[1]) + (mine,)))[:-1]
        here.append(swapped(first_half((1, k, 1))[0], "tp", 1))
        for cell in range(CELLS):
            if cell:
                mine = first_half((0, k, cell))[0]
            joined = join(mine, here[cell])
            place = after(place, joined)
            crossed[cell].append(swapped(joined, "exp", k))
    arrived = [swapped(first_half((1, 0, 0))[0], "tp", 1)]
    kept = list(first_half((0, 0, 0), (0, 0, 1)))
    own_hidden = []
    for cell in range(CELLS):
        if cell:
            arrived.append(swapped(first_half((1, 0, cell))[0], "tp", 1))
        crossed[cell], kept[cell] = lax.optimization_barrier((crossed[cell], kept[cell]))
        beside = [out_matrix] * 3
        hidden = hidden_of([kept[cell], arrived[cell]] + crossed[cell], ff_width, model_width, beside)
        place = after(place, hidden)
        own_hidden.append(hidden)

    near = [swapped(hidden, "tp", 1) for hidden in own_hidden]
    far = {
        k: [swapped(hidden, "exp", k) for hidden in own_hidden] for k in range(1, exp_count)
    }
    own_hidden[-1] = after(own_hidden[-1], far[1][0])

    def add(pieces, total, out_count=1):
        return down(pieces, layout, down_weight, combine_high, combine_low, total, out_count)

    total = add({(0, 0): own_hidden, (1, 0): near}, None)[0]
    last = {}
    for k in far:
        far[k][-1] = after(far[k][-1], total)
        last[1, k] = [swapped(hidden, "tp", 1) for hidden in far[k]]
        total = add({(0, k): far[k]}, total)[0]
    totals = add(last, total, ctx_count)
    returned = [totals[0]] + [swapped(totals[k], "ctx", k) for k in far_first(ctx_count)]
    return finish(mixed, returned)


def solution(mesh):
    in_specs = (
        P(("group", "ctx"), "tp", "exp"),
        P(("group", "ctx"), "tp", None),
        P(("group", "ctx"), "tp", None),
        P(("group", "ctx")),
        P(("group", "ctx")),
        P("group"),
        P("tp", "exp", None),
        P(("group", "ctx"), ("exp", "tp")),
        P(("exp", "tp")),
        P("ctx", ("exp", "tp"), None),
        P("ctx", None, ("exp", "tp")),
        P(("group", "ctx"), None),
        P(("group", "ctx"), None),
    )
    out_specs = P(("group", "ctx"), ("exp", "tp"))
    return jax.shard_map(body, mesh=mesh, in_specs=in_specs, out_specs=out_specs, check_vma=False)
```

```python
import functools
import math

import jax
import jax.numpy as jnp
from jax import lax
from jax.experimental import pallas as pl
from jax.experimental.pallas import tpu as pltpu
from jax.sharding import PartitionSpec as P

MOST = 8
DEPTH = 6
LANES = 128
CELLS = 2

epsilon = 1e-06
masked_score = -1e30
least_high = -1e20

f32 = jnp.float32
bf16 = jnp.bfloat16


def params(megabytes, steps=0):
    semantics = ("arbitrary",) * steps if steps else None
    return pltpu.CompilerParams(
        vmem_limit_bytes=megabytes * 1024 * 1024, dimension_semantics=semantics
    )


def cost(flops, bytes_accessed, transcendentals=0):
    return pl.CostEstimate(
        flops=flops, bytes_accessed=bytes_accessed, transcendentals=transcendentals
    )


def whole(memory_space=pltpu.VMEM):
    return pl.BlockSpec(memory_space=memory_space)


def in_hbm(values):
    return [pltpu.with_memory_space_constraint(value, pltpu.HBM) for value in values]


class Layout:
    def __init__(self, local_experts, key_count, query_rows):
        self.ctx, self.exp, self.tp = (lax.axis_size(axis) for axis in ("ctx", "exp", "tp"))
        self.key_count, self.query_rows = key_count, query_rows
        self.local_experts = local_experts
        self.piece_count = self.exp * self.tp
        self.capacity = self.ctx * MOST // CELLS
        self.rows = local_experts * self.capacity // self.piece_count
        self.experts = max(1, self.rows // self.capacity)
        self.spread = max(1, self.capacity // self.rows)
        self.cell_count = self.piece_count * CELLS

    def lead(self, k):
        own = lax.axis_index("ctx")
        start = self.ctx * (self.key_count - self.query_rows)
        return start + (own ^ k) * self.query_rows - own * self.key_count

    def column_piece(self, k):
        return (lax.axis_index("exp") * self.tp + lax.axis_index("tp")) ^ k

    def first_local_expert(self):
        return lax.axis_index("ctx") * self.local_experts

    def cell(self, flip, k, cell):
        piece = (lax.axis_index("tp") ^ flip) * self.exp + (lax.axis_index("exp") ^ k)
        return piece * CELLS + cell, lax.div(piece * self.experts, self.spread)


def lane_ids(shape):
    return lax.broadcasted_iota(jnp.int32, shape, len(shape) - 1)


def row_ids(shape):
    return lax.broadcasted_iota(jnp.int32, shape, len(shape) - 2)


def as_bf16(mask):
    return mask.astype(f32).astype(bf16)


def dot(left, right, dims=((1,), (0,))):
    return lax.dot_general(left, right, (dims, ((), ())), preferred_element_type=f32)


def in_two(value):
    high = value.astype(bf16).astype(f32)
    return high, value - high


def swapped(value, axes, mask):
    count = lax.axis_size(axes)
    pairs = [(source, source ^ mask) for source in range(count)]
    return lax.ppermute(value, axes, pairs)


def far_first(count):
    return list(range(count - 1, 0, -1))


def pack_kernel(
    queries_ref, seg_ref, ids_ref, weight_ref, beside_ref, out_ref,
    seg_here, ids_here, weight_here, done,
):
    rows, width = queries_ref.shape
    choices = ids_ref.shape[0]
    copies = [
        pltpu.make_async_copy(source, target, done.at[i])
        for i, (source, target) in enumerate(
            [
                (seg_ref, seg_here),
                (ids_ref, ids_here),
                (weight_ref, weight_here),
                (queries_ref, out_ref.at[:, :width]),
            ]
        )
    ]
    for copy in copies:
        copy.start()
    shape = (choices, LANES)

    def placed(value, first, last):
        to_lane = (lane_ids(shape) == row_ids(shape) + first) & (row_ids(shape) <= last)
        return dot(value.astype(bf16), as_bf16(to_lane), ((0,), (0,)))

    for copy in copies[:3]:
        copy.wait()
    segs = jnp.broadcast_to(seg_here[...], (choices, rows)).astype(f32)
    high, low = in_two(weight_here[...])
    info = placed(segs, 0, 0) + placed(ids_here[...].astype(f32), 1, choices)
    info = info + placed(high, 1 + choices, choices) + placed(low, 1 + 2 * choices, choices)
    out_ref[:, width:] = info.astype(bf16)
    copies[3].wait()


def pack(queries, query_seg, expert_ids, route_weight, beside):
    rows, width = queries.shape
    small = [query_seg[None, :], expert_ids.T, route_weight.T]
    return pl.pallas_call(
        pack_kernel,
        in_specs=[whole(pltpu.HBM)] * 5,
        out_shape=jax.ShapeDtypeStruct((rows, width + LANES), bf16),
        scratch_shapes=[pltpu.VMEM(value.shape, value.dtype) for value in small]
        + [pltpu.SemaphoreType.DMA((4,))],
        compiler_params=params(4),
        name="pack",
    )(*in_hbm([queries] + small + [beside]))


def sight_kernel(parent_ref, key_seg_ref, sight_ref):
    seg_count, key_count = sight_ref.shape
    square = (seg_count, seg_count)
    same = row_ids(square) == lane_ids(square)
    one = as_bf16((parent_ref[...] == row_ids(square)) | same)
    two = as_bf16(dot(one, one) > 0.5)
    four = as_bf16(dot(two, two) > 0.5)
    six = as_bf16(dot(four, two) > 0.5)
    keys = as_bf16(key_seg_ref[...] == row_ids((seg_count, key_count)))
    sight_ref[...] = dot(six, keys, ((0,), (0,))).astype(bf16)


def sight_of(parent, key_seg):
    assert DEPTH == 6
    return pl.pallas_call(
        sight_kernel,
        out_shape=jax.ShapeDtypeStruct((parent.shape[0], key_seg.shape[0]), bf16),
        compiler_params=params(4),
        cost_estimate=cost(2**24, 2**19),
        name="sight",
    )(parent[None, :], key_seg[None, :])


def attend_kernel(
    heads, scale, layout, k, queries_ref, keys_ref, values_ref, sight_ref, beside_ref,
    out_ref, stacked_ref, probs_ref,
):
    rows = queries_ref.shape[0]
    key_count, head_size = keys_ref.shape
    seg_count = sight_ref.shape[0]
    width = heads * head_size
    info = queries_ref[:, width:].astype(f32)
    own_seg = info[:, :1].astype(jnp.int32)
    onehot = as_bf16(own_seg == lane_ids((rows, seg_count)))
    seen = dot(onehot, sight_ref[...]) > 0.5
    place = (rows, key_count)
    causal = lane_ids(place) - row_ids(place) <= layout.lead(k)
    bias = jnp.where(seen & causal, 0.0, masked_score)
    for head in range(heads):
        columns = slice(head * head_size, (head + 1) * head_size)
        stacked_ref[head * rows : (head + 1) * rows, :] = queries_ref[:, columns]
    scores = dot(stacked_ref[...], keys_ref[...], ((1,), (1,)))
    stats = jnp.zeros((rows, LANES), f32)
    lane = lane_ids((rows, LANES))
    for head in range(heads):
        here = slice(head * rows, (head + 1) * rows)
        biased = scores[here, :] + bias
        high = jnp.maximum(jnp.max(biased, axis=1, keepdims=True), least_high)
        high = high.astype(bf16).astype(f32)
        probs = jnp.exp2((biased - high) * scale)
        total_high, total_low = in_two(jnp.sum(probs, axis=1, keepdims=True))
        probs_ref[here, :] = probs.astype(bf16)
        stats = jnp.where(lane == head, high, stats)
        stats = jnp.where(lane == heads + head, total_high, stats)
        stats = jnp.where(lane == 2 * heads + head, total_low, stats)
    out_ref[:, width:] = stats.astype(bf16)
    sums = dot(probs_ref[...], values_ref[...])
    for head in range(heads):
        columns = slice(head * head_size, (head + 1) * head_size)
        out_ref[:, columns] = sums[head * rows : (head + 1) * rows, :].astype(bf16)


def attend(layout, k, queries, keys, values, sight, heads, scale, beside):
    rows, columns = queries.shape
    key_count, head_size = keys.shape
    work = rows * heads * key_count
    return pl.pallas_call(
        functools.partial(attend_kernel, heads, scale, layout, k),
        in_specs=[whole()] * 4 + [whole(pltpu.HBM)],
        out_shape=jax.ShapeDtypeStruct((rows, columns), bf16),
        scratch_shapes=[
            pltpu.VMEM((rows * heads, head_size), bf16),
            pltpu.VMEM((rows * heads, key_count), bf16),
        ],
        compiler_params=params(8),
        cost_estimate=cost(8 * work * head_size, 2**20, work),
        name="attend",
    )(queries, keys, values, sight, *in_hbm([beside]))


def project_kernel(heads, scale, layout, source_count, *refs):
    parts_refs, weight_ref = refs[:source_count], refs[source_count]
    out_refs, attention_ref = refs[source_count + 1 : -1], refs[-1]
    width = attention_ref.shape[1]
    head_size = width // heads
    stats = [ref[:, width:].astype(f32) for ref in parts_refs]
    top = functools.reduce(jnp.maximum, stats)
    factors = [jnp.exp2(jnp.minimum((stat - top) * scale, 0.0)) for stat in stats]
    total = 0.0
    for stat, factor in zip(stats, factors):
        high = pltpu.roll(stat, LANES - heads, 1)
        low = pltpu.roll(stat, LANES - 2 * heads, 1)
        total = total + factor * (high + low)
    shares = [factor / total for factor in factors]
    for head in range(heads):
        columns = slice(head * head_size, (head + 1) * head_size)
        merged = 0.0
        for ref, share in zip(parts_refs, shares):
            merged = merged + ref[:, columns].astype(f32) * share[:, head : head + 1]
        attention_ref[:, columns] = merged.astype(bf16)
    for i, out_ref in enumerate(out_refs):
        piece_width = out_ref.shape[1]
        start = pl.multiple_of(layout.column_piece(i) * piece_width, piece_width)
        out_ref[...] = dot(attention_ref[...], weight_ref[:, pl.ds(start, piece_width)]).astype(bf16)


def project(layout, parts, weight, heads, scale):
    rows = parts[0].shape[0]
    width, model_width = weight.shape
    piece_width = model_width // layout.piece_count
    return pl.pallas_call(
        functools.partial(project_kernel, heads, scale, layout, len(parts)),
        out_shape=[jax.ShapeDtypeStruct((rows, piece_width), bf16)] * layout.piece_count,
        scratch_shapes=[pltpu.VMEM((rows, width), bf16)],
        compiler_params=params(8),
        cost_estimate=cost(2 * rows * width * model_width, 2 * width * model_width),
        name="project",
    )(*parts, weight)


def mix_kernel(residual_ref, gain_ref, *refs):
    parts_refs, (mixed_ref, sent_ref) = refs[:-2], refs[-2:]
    rows, width = mixed_ref.shape
    mixed = residual_ref[...].astype(f32)
    for ref in parts_refs:
        mixed = mixed + ref[...].astype(f32)
    mixed_ref[...] = mixed
    sent_ref[:, :width] = (mixed * gain_ref[...].astype(f32)).astype(bf16)
    high, low = in_two(jnp.sum(mixed * mixed, axis=1, keepdims=True))
    lane = lane_ids((rows, LANES))
    squares = jnp.where(lane == 0, high, jnp.where(lane == 1, low, 0.0))
    sent_ref[:, width:] = squares.astype(bf16)


def mix(residual, gain, parts):
    rows, width = residual.shape
    return pl.pallas_call(
        mix_kernel,
        out_shape=(
            jax.ShapeDtypeStruct((rows, width), f32),
            jax.ShapeDtypeStruct((rows, width + LANES), bf16),
        ),
        compiler_params=params(4),
        name="mix",
    )(residual, gain[None, :], *parts)


def route_kernel(layout, choices, width, *refs):
    info_refs, (place_ref, high_ref, low_ref) = refs[:-3], refs[-3:]
    cell_count, tokens, slots = place_ref.shape
    local_experts, capacity = layout.local_experts, layout.capacity
    expert = (lane_ids((tokens, local_experts)) + layout.first_local_expert()).astype(f32)
    square = (tokens, tokens)
    earlier = as_bf16(lane_ids(square) < row_ids(square))
    count = len(info_refs) // CELLS
    for cell in range(CELLS):
        sources = info_refs[cell * count : (cell + 1) * count]
        info = jnp.concatenate([ref[:, width:] for ref in sources], axis=0).astype(f32)
        member = jnp.zeros((tokens, local_experts), f32)
        weight_high = jnp.zeros((tokens, local_experts), f32)
        weight_low = jnp.zeros((tokens, local_experts), f32)
        for k in range(choices):
            chosen = info[:, 1 + k : 2 + k] == expert
            high = info[:, 1 + choices + k : 2 + choices + k]
            low = info[:, 1 + 2 * choices + k : 2 + 2 * choices + k]
            member = jnp.where(chosen, 1.0, member)
            weight_high = jnp.where(chosen, high, weight_high)
            weight_low = jnp.where(chosen, low, weight_low)
        rank = jnp.where(member > 0.5, dot(earlier, member.astype(bf16)), -1.0).astype(bf16)
        weight_high = weight_high.astype(bf16)
        weight_low = weight_low.astype(bf16)
        for piece in range(layout.piece_count):
            slot = lane_ids((local_experts, slots)) + piece * slots
            spread = as_bf16(slot // capacity == row_ids((local_experts, slots)))
            wanted = (lane_ids((tokens, slots)) + piece * slots) % capacity
            placed = dot(rank, spread) == wanted.astype(f32)
            at = piece * CELLS + cell
            place_ref[at] = jnp.where(placed, 1.0, 0.0).astype(bf16)
            high_ref[at] = jnp.where(placed, dot(weight_high, spread), 0.0).astype(bf16)
            low_ref[at] = jnp.where(placed, dot(weight_low, spread), 0.0).astype(bf16)


def route(layout, packed, width, choices):
    tokens = sum(value.shape[0] for value in packed) // CELLS
    shape = jax.ShapeDtypeStruct((layout.cell_count, tokens, layout.rows), bf16)
    return pl.pallas_call(
        functools.partial(route_kernel, layout, choices, width),
        out_shape=(shape, shape, shape),
        compiler_params=params(16),
        cost_estimate=cost(2**25, 2**20),
        name="route",
    )(*packed)


def squares_joined(squares):
    high, low = in_two(squares[:, :1] + squares[:, 1:2])
    lane = lane_ids(squares.shape)
    return jnp.where(lane == 0, high, jnp.where(lane == 1, low, 0.0))


def gate_up(names, layout, place, sources, weight):
    _, width, ff_pair = weight.shape
    each = layout.rows // layout.experts
    cells = sorted({name[2] for name in names})
    count = len(sources[0])

    def kernel(place_ref, weight_ref, *refs):
        for name, out_ref in zip(names, refs[len(cells) * count :]):
            at, first = layout.cell(*name)
            turn = cells.index(name[2])
            picked = 0.0
            for i, ref in enumerate(refs[turn * count : (turn + 1) * count]):
                tokens = ref.shape[0]
                here = place_ref[at, i * tokens : (i + 1) * tokens, :]
                picked = picked + dot(here, ref[...], ((0,), (0,)))
            picked = picked.astype(bf16)
            for i in range(layout.experts):
                here = slice(i * each, (i + 1) * each)
                product = dot(picked[here, :width], weight_ref[first + i])
                out_ref[here, :ff_pair] = product.astype(bf16)
            out_ref[:, ff_pair:] = picked[:, width:]

    out = jax.ShapeDtypeStruct((layout.rows, ff_pair + LANES), bf16)
    return pl.pallas_call(
        kernel,
        out_shape=[out] * len(names),
        compiler_params=params(8),
        cost_estimate=cost(2 * layout.rows * width * ff_pair, 2 * layout.rows * ff_pair),
        name="gate_up",
    )(place, weight, *[value for cell in cells for value in sources[cell]])


def join_kernel(left_ref, right_ref, out_ref):
    ff_pair = out_ref.shape[1] - LANES
    product = left_ref[:, :ff_pair].astype(f32) + right_ref[:, :ff_pair].astype(f32)
    out_ref[:, :ff_pair] = product.astype(bf16)
    squares = left_ref[:, ff_pair:].astype(f32) + right_ref[:, ff_pair:].astype(f32)
    out_ref[:, ff_pair:] = squares_joined(squares).astype(bf16)


def join(left, right):
    return pl.pallas_call(
        join_kernel,
        out_shape=jax.ShapeDtypeStruct(left.shape, bf16),
        compiler_params=params(4),
        name="join",
    )(left, right)


def hidden_of(parts, ff_width, model_width, beside):
    def kernel(*refs):
        refs, out_ref = refs[len(beside) : -1], refs[-1]
        total = 0.0
        for ref in refs:
            total = total + ref[...].astype(f32)
        high = total[:, 2 * ff_width : 2 * ff_width + 1]
        low = total[:, 2 * ff_width + 1 : 2 * ff_width + 2]
        norm = lax.rsqrt((high + low) / model_width + epsilon)
        gate = total[:, :ff_width] * norm
        up = total[:, ff_width : 2 * ff_width] * norm
        out_ref[...] = (gate / (1.0 + jnp.exp(-gate)) * up).astype(bf16)

    return pl.pallas_call(
        kernel,
        in_specs=[whole(pltpu.HBM)] * len(beside) + [whole()] * len(parts),
        out_shape=jax.ShapeDtypeStruct((parts[0].shape[0], ff_width), bf16),
        compiler_params=params(8),
        name="hidden",
    )(*in_hbm(beside), *parts)


def down(pieces, layout, weight, high, low, total=None, out_count=1):
    first_cells = next(iter(pieces.values()))
    ff_width = first_cells[0].shape[1]
    tokens = high.shape[1]
    piece_width = weight.shape[2]
    each = layout.rows // layout.experts
    rows = tokens * CELLS // out_count
    out_type = f32 if out_count == 1 else bf16

    def kernel(weight_ref, high_ref, low_ref, *refs):
        hidden_refs, refs = refs[: len(pieces) * CELLS], refs[len(pieces) * CELLS :]
        total_refs, out_refs, held_ref = refs[: -1 - out_count], refs[-1 - out_count : -1], refs[-1]
        summed = [0.0] * CELLS
        for turn, name in enumerate(pieces):
            cells = hidden_refs[turn * CELLS : (turn + 1) * CELLS]
            _, first = layout.cell(*name, 0)
            for i in range(layout.experts):
                here = slice(i * each, (i + 1) * each)
                rows_in = jnp.concatenate([ref[here, :] for ref in cells], axis=0)
                product = dot(rows_in, weight_ref[first + i]).astype(bf16)
                for cell in range(CELLS):
                    held_ref[cell, here, :] = product[cell * each : (cell + 1) * each, :]
            for cell in range(CELLS):
                at, _ = layout.cell(*name, cell)
                held = held_ref[cell]
                summed[cell] = summed[cell] + dot(high_ref[at], held) + dot(low_ref[at], held)
        whole_sum = jnp.concatenate(summed, axis=0)
        for ref in total_refs:
            whole_sum = whole_sum + ref[...]
        for i, ref in enumerate(out_refs):
            ref[...] = whole_sum[i * rows : (i + 1) * rows, :].astype(ref.dtype)

    before = [] if total is None else [total]
    hidden = [value for cells in pieces.values() for value in cells]
    return pl.pallas_call(
        kernel,
        out_shape=[jax.ShapeDtypeStruct((rows, piece_width), out_type)] * out_count,
        scratch_shapes=[pltpu.VMEM((CELLS, layout.rows, piece_width), bf16)],
        compiler_params=params(8),
        cost_estimate=cost(4 * layout.rows * ff_width * piece_width, 2**20),
        name="down",
    )(weight, high, low, *hidden, *before)


def finish_kernel(mixed_ref, *refs):
    total = mixed_ref[...]
    for ref in refs[:-1]:
        total = total + ref[...].astype(f32)
    refs[-1][...] = total.astype(bf16)


def finish(mixed, parts):
    return pl.pallas_call(
        finish_kernel,
        out_shape=jax.ShapeDtypeStruct(mixed.shape, bf16),
        compiler_params=params(4),
        name="finish",
    )(mixed, *parts)


def body(
    queries,
    cached_keys,
    cached_values,
    key_seg,
    query_seg,
    parent,
    out_weight,
    residual,
    norm_gain,
    gate_up_weight,
    down_weight,
    expert_ids,
    route_weight,
):
    ctx_count, exp_count, tp_count = (lax.axis_size(axis) for axis in ("ctx", "exp", "tp"))
    assert tp_count == 2 and cached_keys.shape[1] == 1
    assert ctx_count & (ctx_count - 1) == 0 and exp_count & (exp_count - 1) == 0
    piece_count = exp_count * tp_count
    query_rows = queries.shape[0]
    key_count, _, head_size = cached_keys.shape
    heads = queries.shape[2] // head_size
    width = heads * head_size
    model_width = out_weight.shape[2]
    local_experts, piece_width, _ = gate_up_weight.shape
    ff_width = down_weight.shape[1]
    choices = expert_ids.shape[1]
    scale = math.log2(math.e) / math.sqrt(head_size)

    layout = Layout(local_experts, key_count, query_rows)

    packed = pack(
        queries.reshape(query_rows, width), query_seg, expert_ids, route_weight, gate_up_weight
    )
    sight = sight_of(parent, key_seg)
    keys = cached_keys.reshape(key_count, head_size)
    values = cached_values.reshape(key_count, head_size)
    out_matrix = out_weight.reshape(width, model_width)

    def attend_block(k):
        return attend(
            layout, k, gathered[k], keys, values, sight, heads, scale, gate_up_weight
        )

    gathered = {0: packed}
    for k in range(1, ctx_count):
        if k == 1 or k % 2 == 0:
            gathered[k] = swapped(packed, "ctx", k)
    parts = {1: attend_block(1)}
    for k in range(3, ctx_count, 2):
        gathered[k] = swapped(
            lax.optimization_barrier((gathered[k - 1], parts[1]))[0], "ctx", 1
        )
    for k in list(range(2, ctx_count)) + [0]:
        parts[k] = attend_block(k)
    for k in range(1, ctx_count):
        parts[k] = swapped(parts[k], "ctx", k)
    place, combine_high, combine_low = route(
        layout, [gathered[k] for k in range(ctx_count)], width, choices
    )
    def after(value, *others):
        return lax.optimization_barrier((value,) + others)[0]

    projected = project(
        layout,
        [parts[k] for k in range(ctx_count)],
        after(out_matrix, place),
        heads,
        scale,
    )
    pieces = [projected[0]] + [
        swapped(projected[k], ("exp", "tp"), k) for k in far_first(piece_count)
    ]
    mixed, sent = mix(residual, norm_gain, pieces)
    rows = {0: sent}
    for k in far_first(ctx_count):
        rows[k] = swapped(sent, "ctx", k)
    half = ctx_count // CELLS
    sources = [[rows[k] for k in range(half * i, half * (i + 1))] for i in range(CELLS)]

    def first_half(*names):
        return gate_up(names, layout, place, sources, gate_up_weight)

    crossed = [[] for _ in range(CELLS)]
    for k in far_first(exp_count):
        away, mine = first_half((1, k, 0), (0, k, 0))
        here = [swapped(away, "tp", 1)]
        sources[1] = list(lax.optimization_barrier(tuple(sources[1]) + (mine,)))[:-1]
        here.append(swapped(first_half((1, k, 1))[0], "tp", 1))
        for cell in range(CELLS):
            if cell:
                mine = first_half((0, k, cell))[0]
            joined = join(mine, here[cell])
            place = after(place, joined)
            crossed[cell].append(swapped(joined, "exp", k))
    arrived = [swapped(first_half((1, 0, 0))[0], "tp", 1)]
    kept = list(first_half((0, 0, 0), (0, 0, 1)))
    own_hidden = []
    for cell in range(CELLS):
        if cell:
            arrived.append(swapped(first_half((1, 0, cell))[0], "tp", 1))
        crossed[cell], kept[cell] = lax.optimization_barrier((crossed[cell], kept[cell]))
        beside = [out_matrix] * 3
        hidden = hidden_of([kept[cell], arrived[cell]] + crossed[cell], ff_width, model_width, beside)
        place = after(place, hidden)
        own_hidden.append(hidden)

    near = [swapped(hidden, "tp", 1) for hidden in own_hidden]
    far = {
        k: [swapped(hidden, "exp", k) for hidden in own_hidden] for k in range(1, exp_count)
    }
    own_hidden[-1] = after(own_hidden[-1], far[1][0])

    def add(pieces, total, out_count=1):
        return down(pieces, layout, down_weight, combine_high, combine_low, total, out_count)

    total = add({(0, 0): own_hidden, (1, 0): near}, None)[0]
    last = {}
    for k in far:
        far[k][-1] = after(far[k][-1], total)
        last[1, k] = [swapped(hidden, "tp", 1) for hidden in far[k]]
        total = add({(0, k): far[k]}, total)[0]
    totals = add(last, total, ctx_count)
    returned = [totals[0]] + [swapped(totals[k], "ctx", k) for k in far_first(ctx_count)]
    return finish(mixed, returned)


def solution(mesh):
    in_specs = (
        P(("group", "ctx"), "tp", "exp"),
        P(("group", "ctx"), "tp", None),
        P(("group", "ctx"), "tp", None),
        P(("group", "ctx")),
        P(("group", "ctx")),
        P("group"),
        P("tp", "exp", None),
        P(("group", "ctx"), ("exp", "tp")),
        P(("exp", "tp")),
        P("ctx", ("exp", "tp"), None),
        P("ctx", None, ("exp", "tp")),
        P(("group", "ctx"), None),
        P(("group", "ctx"), None),
    )
    out_specs = P(("group", "ctx"), ("exp", "tp"))
    return jax.shard_map(body, mesh=mesh, in_specs=in_specs, out_specs=out_specs, check_vma=False)
```

```python
import functools
import math

import jax
import jax.numpy as jnp
from jax import lax
from jax.experimental import pallas as pl
from jax.experimental.pallas import tpu as pltpu
from jax.sharding import PartitionSpec as P

MOST = 8
DEPTH = 6
LANES = 128
CELLS = 2

epsilon = 1e-06
masked_score = -1e30
least_high = -1e20

f32 = jnp.float32
bf16 = jnp.bfloat16


def params(megabytes, steps=0):
    semantics = ("arbitrary",) * steps if steps else None
    return pltpu.CompilerParams(
        vmem_limit_bytes=megabytes * 1024 * 1024, dimension_semantics=semantics
    )


def cost(flops, bytes_accessed, transcendentals=0):
    return pl.CostEstimate(
        flops=flops, bytes_accessed=bytes_accessed, transcendentals=transcendentals
    )


def whole(memory_space=pltpu.VMEM):
    return pl.BlockSpec(memory_space=memory_space)


def in_hbm(values):
    return [pltpu.with_memory_space_constraint(value, pltpu.HBM) for value in values]


class Layout:
    def __init__(self, local_experts, key_count, query_rows):
        self.ctx, self.exp, self.tp = (lax.axis_size(axis) for axis in ("ctx", "exp", "tp"))
        self.key_count, self.query_rows = key_count, query_rows
        self.local_experts = local_experts
        self.piece_count = self.exp * self.tp
        self.capacity = self.ctx * MOST // CELLS
        self.rows = local_experts * self.capacity // self.piece_count
        self.experts = max(1, self.rows // self.capacity)
        self.spread = max(1, self.capacity // self.rows)
        self.cell_count = self.piece_count * CELLS

    def lead(self, k):
        own = lax.axis_index("ctx")
        start = self.ctx * (self.key_count - self.query_rows)
        return start + (own ^ k) * self.query_rows - own * self.key_count

    def column_piece(self, k):
        return (lax.axis_index("exp") * self.tp + lax.axis_index("tp")) ^ k

    def first_local_expert(self):
        return lax.axis_index("ctx") * self.local_experts

    def cell(self, flip, k, cell):
        piece = (lax.axis_index("tp") ^ flip) * self.exp + (lax.axis_index("exp") ^ k)
        return piece * CELLS + cell, lax.div(piece * self.experts, self.spread)


def lane_ids(shape):
    return lax.broadcasted_iota(jnp.int32, shape, len(shape) - 1)


def row_ids(shape):
    return lax.broadcasted_iota(jnp.int32, shape, len(shape) - 2)


def as_bf16(mask):
    return mask.astype(f32).astype(bf16)


def dot(left, right, dims=((1,), (0,))):
    return lax.dot_general(left, right, (dims, ((), ())), preferred_element_type=f32)


def in_two(value):
    high = value.astype(bf16).astype(f32)
    return high, value - high


def swapped(value, axes, mask):
    count = lax.axis_size(axes)
    pairs = [(source, source ^ mask) for source in range(count)]
    return lax.ppermute(value, axes, pairs)


def far_first(count):
    return list(range(count - 1, 0, -1))


def pack_kernel(
    queries_ref, seg_ref, ids_ref, weight_ref, beside_ref, out_ref,
    seg_here, ids_here, weight_here, done,
):
    rows, width = queries_ref.shape
    choices = ids_ref.shape[0]
    copies = [
        pltpu.make_async_copy(source, target, done.at[i])
        for i, (source, target) in enumerate(
            [
                (seg_ref, seg_here),
                (ids_ref, ids_here),
                (weight_ref, weight_here),
                (queries_ref, out_ref.at[:, :width]),
            ]
        )
    ]
    for copy in copies:
        copy.start()
    shape = (choices, LANES)

    def placed(value, first, last):
        to_lane = (lane_ids(shape) == row_ids(shape) + first) & (row_ids(shape) <= last)
        return dot(value.astype(bf16), as_bf16(to_lane), ((0,), (0,)))

    for copy in copies[:3]:
        copy.wait()
    segs = jnp.broadcast_to(seg_here[...], (choices, rows)).astype(f32)
    high, low = in_two(weight_here[...])
    info = placed(segs, 0, 0) + placed(ids_here[...].astype(f32), 1, choices)
    info = info + placed(high, 1 + choices, choices) + placed(low, 1 + 2 * choices, choices)
    out_ref[:, width:] = info.astype(bf16)
    copies[3].wait()


def pack(queries, query_seg, expert_ids, route_weight, beside):
    rows, width = queries.shape
    small = [query_seg[None, :], expert_ids.T, route_weight.T]
    return pl.pallas_call(
        pack_kernel,
        in_specs=[whole(pltpu.HBM)] * 5,
        out_shape=jax.ShapeDtypeStruct((rows, width + LANES), bf16),
        scratch_shapes=[pltpu.VMEM(value.shape, value.dtype) for value in small]
        + [pltpu.SemaphoreType.DMA((4,))],
        compiler_params=params(4),
        name="pack",
    )(*in_hbm([queries] + small + [beside]))


def sight_kernel(parent_ref, key_seg_ref, sight_ref):
    seg_count, key_count = sight_ref.shape
    square = (seg_count, seg_count)
    same = row_ids(square) == lane_ids(square)
    one = as_bf16((parent_ref[...] == row_ids(square)) | same)
    two = as_bf16(dot(one, one) > 0.5)
    four = as_bf16(dot(two, two) > 0.5)
    six = as_bf16(dot(four, two) > 0.5)
    keys = as_bf16(key_seg_ref[...] == row_ids((seg_count, key_count)))
    sight_ref[...] = dot(six, keys, ((0,), (0,))).astype(bf16)


def sight_of(parent, key_seg):
    assert DEPTH == 6
    return pl.pallas_call(
        sight_kernel,
        out_shape=jax.ShapeDtypeStruct((parent.shape[0], key_seg.shape[0]), bf16),
        compiler_params=params(4),
        cost_estimate=cost(2**24, 2**19),
        name="sight",
    )(parent[None, :], key_seg[None, :])


def attend_kernel(
    heads, scale, layout, k, queries_ref, keys_ref, values_ref, sight_ref, beside_ref,
    out_ref, stacked_ref, probs_ref,
):
    rows = queries_ref.shape[0]
    key_count, head_size = keys_ref.shape
    seg_count = sight_ref.shape[0]
    width = heads * head_size
    info = queries_ref[:, width:].astype(f32)
    own_seg = info[:, :1].astype(jnp.int32)
    onehot = as_bf16(own_seg == lane_ids((rows, seg_count)))
    seen = dot(onehot, sight_ref[...]) > 0.5
    place = (rows, key_count)
    causal = lane_ids(place) - row_ids(place) <= layout.lead(k)
    bias = jnp.where(seen & causal, 0.0, masked_score)
    for head in range(heads):
        columns = slice(head * head_size, (head + 1) * head_size)
        stacked_ref[head * rows : (head + 1) * rows, :] = queries_ref[:, columns]
    scores = dot(stacked_ref[...], keys_ref[...], ((1,), (1,)))
    stats = jnp.zeros((rows, LANES), f32)
    lane = lane_ids((rows, LANES))
    for head in range(heads):
        here = slice(head * rows, (head + 1) * rows)
        biased = scores[here, :] + bias
        high = jnp.maximum(jnp.max(biased, axis=1, keepdims=True), least_high)
        high = high.astype(bf16).astype(f32)
        probs = jnp.exp2((biased - high) * scale)
        total_high, total_low = in_two(jnp.sum(probs, axis=1, keepdims=True))
        probs_ref[here, :] = probs.astype(bf16)
        stats = jnp.where(lane == head, high, stats)
        stats = jnp.where(lane == heads + head, total_high, stats)
        stats = jnp.where(lane == 2 * heads + head, total_low, stats)
    out_ref[:, width:] = stats.astype(bf16)
    sums = dot(probs_ref[...], values_ref[...])
    for head in range(heads):
        columns = slice(head * head_size, (head + 1) * head_size)
        out_ref[:, columns] = sums[head * rows : (head + 1) * rows, :].astype(bf16)


def attend(layout, k, queries, keys, values, sight, heads, scale, beside):
    rows, columns = queries.shape
    key_count, head_size = keys.shape
    work = rows * heads * key_count
    return pl.pallas_call(
        functools.partial(attend_kernel, heads, scale, layout, k),
        in_specs=[whole()] * 4 + [whole(pltpu.HBM)],
        out_shape=jax.ShapeDtypeStruct((rows, columns), bf16),
        scratch_shapes=[
            pltpu.VMEM((rows * heads, head_size), bf16),
            pltpu.VMEM((rows * heads, key_count), bf16),
        ],
        compiler_params=params(8),
        cost_estimate=cost(8 * work * head_size, 2**20, work),
        name="attend",
    )(queries, keys, values, sight, *in_hbm([beside]))


def project_kernel(heads, scale, layout, source_count, *refs):
    parts_refs, weight_ref = refs[:source_count], refs[source_count]
    out_refs, attention_ref = refs[source_count + 1 : -1], refs[-1]
    width = attention_ref.shape[1]
    head_size = width // heads
    stats = [ref[:, width:].astype(f32) for ref in parts_refs]
    top = functools.reduce(jnp.maximum, stats)
    factors = [jnp.exp2(jnp.minimum((stat - top) * scale, 0.0)) for stat in stats]
    total = 0.0
    for stat, factor in zip(stats, factors):
        high = pltpu.roll(stat, LANES - heads, 1)
        low = pltpu.roll(stat, LANES - 2 * heads, 1)
        total = total + factor * (high + low)
    shares = [factor / total for factor in factors]
    for head in range(heads):
        columns = slice(head * head_size, (head + 1) * head_size)
        merged = 0.0
        for ref, share in zip(parts_refs, shares):
            merged = merged + ref[:, columns].astype(f32) * share[:, head : head + 1]
        attention_ref[:, columns] = merged.astype(bf16)
    for i, out_ref in enumerate(out_refs):
        piece_width = out_ref.shape[1]
        start = pl.multiple_of(layout.column_piece(i) * piece_width, piece_width)
        out_ref[...] = dot(attention_ref[...], weight_ref[:, pl.ds(start, piece_width)]).astype(bf16)


def project(layout, parts, weight, heads, scale):
    rows = parts[0].shape[0]
    width, model_width = weight.shape
    piece_width = model_width // layout.piece_count
    return pl.pallas_call(
        functools.partial(project_kernel, heads, scale, layout, len(parts)),
        out_shape=[jax.ShapeDtypeStruct((rows, piece_width), bf16)] * layout.piece_count,
        scratch_shapes=[pltpu.VMEM((rows, width), bf16)],
        compiler_params=params(8),
        cost_estimate=cost(2 * rows * width * model_width, 2 * width * model_width),
        name="project",
    )(*parts, weight)


def mix_kernel(residual_ref, gain_ref, *refs):
    parts_refs, (mixed_ref, sent_ref) = refs[:-2], refs[-2:]
    mixed = residual_ref[...].astype(f32)
    for ref in parts_refs:
        mixed = mixed + ref[...].astype(f32)
    mixed_ref[...] = mixed
    sent_ref[...] = (mixed * gain_ref[...].astype(f32)).astype(bf16)


def mix(residual, gain, parts):
    rows, width = residual.shape
    return pl.pallas_call(
        mix_kernel,
        out_shape=(
            jax.ShapeDtypeStruct((rows, width), f32),
            jax.ShapeDtypeStruct((rows, width), bf16),
        ),
        compiler_params=params(4),
        name="mix",
    )(residual, gain[None, :], *parts)


def route_kernel(layout, choices, width, *refs):
    info_refs, (place_ref, high_ref, low_ref) = refs[:-3], refs[-3:]
    cell_count, tokens, slots = place_ref.shape
    local_experts, capacity = layout.local_experts, layout.capacity
    expert = (lane_ids((tokens, local_experts)) + layout.first_local_expert()).astype(f32)
    square = (tokens, tokens)
    earlier = as_bf16(lane_ids(square) < row_ids(square))
    count = len(info_refs) // CELLS
    for cell in range(CELLS):
        sources = info_refs[cell * count : (cell + 1) * count]
        info = jnp.concatenate([ref[:, width:] for ref in sources], axis=0).astype(f32)
        member = jnp.zeros((tokens, local_experts), f32)
        weight_high = jnp.zeros((tokens, local_experts), f32)
        weight_low = jnp.zeros((tokens, local_experts), f32)
        for k in range(choices):
            chosen = info[:, 1 + k : 2 + k] == expert
            high = info[:, 1 + choices + k : 2 + choices + k]
            low = info[:, 1 + 2 * choices + k : 2 + 2 * choices + k]
            member = jnp.where(chosen, 1.0, member)
            weight_high = jnp.where(chosen, high, weight_high)
            weight_low = jnp.where(chosen, low, weight_low)
        rank = jnp.where(member > 0.5, dot(earlier, member.astype(bf16)), -1.0).astype(bf16)
        weight_high = weight_high.astype(bf16)
        weight_low = weight_low.astype(bf16)
        for piece in range(layout.piece_count):
            slot = lane_ids((local_experts, slots)) + piece * slots
            spread = as_bf16(slot // capacity == row_ids((local_experts, slots)))
            wanted = (lane_ids((tokens, slots)) + piece * slots) % capacity
            placed = dot(rank, spread) == wanted.astype(f32)
            at = piece * CELLS + cell
            place_ref[at] = jnp.where(placed, 1.0, 0.0).astype(bf16)
            high_ref[at] = jnp.where(placed, dot(weight_high, spread), 0.0).astype(bf16)
            low_ref[at] = jnp.where(placed, dot(weight_low, spread), 0.0).astype(bf16)


def route(layout, packed, width, choices):
    tokens = sum(value.shape[0] for value in packed) // CELLS
    shape = jax.ShapeDtypeStruct((layout.cell_count, tokens, layout.rows), bf16)
    return pl.pallas_call(
        functools.partial(route_kernel, layout, choices, width),
        out_shape=(shape, shape, shape),
        compiler_params=params(16),
        cost_estimate=cost(2**25, 2**20),
        name="route",
    )(*packed)


def squares_joined(squares):
    high, low = in_two(squares[:, :1] + squares[:, 1:2])
    lane = lane_ids(squares.shape)
    return jnp.where(lane == 0, high, jnp.where(lane == 1, low, 0.0))


def gate_up(names, layout, place, sources, weight, gain):
    _, width, ff_pair = weight.shape
    each = layout.rows // layout.experts
    cells = sorted({name[2] for name in names})
    count = len(sources[0])

    def kernel(place_ref, gain_ref, weight_ref, *refs):
        inverse_gain = 1.0 / gain_ref[...].astype(f32)
        for name, out_ref in zip(names, refs[len(cells) * count :]):
            at, first = layout.cell(*name)
            turn = cells.index(name[2])
            picked = 0.0
            for i, ref in enumerate(refs[turn * count : (turn + 1) * count]):
                tokens = ref.shape[0]
                here = place_ref[at, i * tokens : (i + 1) * tokens, :]
                picked = picked + dot(here, ref[...], ((0,), (0,)))
            picked = picked.astype(bf16)
            for i in range(layout.experts):
                here = slice(i * each, (i + 1) * each)
                out_ref[here, :ff_pair] = dot(picked[here, :], weight_ref[first + i]).astype(bf16)
            mixed = picked.astype(f32) * inverse_gain
            high, low = in_two(jnp.sum(mixed * mixed, axis=1, keepdims=True))
            lane = lane_ids((layout.rows, LANES))
            squares = jnp.where(lane == 0, high, jnp.where(lane == 1, low, 0.0))
            out_ref[:, ff_pair:] = squares.astype(bf16)

    out = jax.ShapeDtypeStruct((layout.rows, ff_pair + LANES), bf16)
    return pl.pallas_call(
        kernel,
        out_shape=[out] * len(names),
        compiler_params=params(8),
        cost_estimate=cost(2 * layout.rows * width * ff_pair, 2 * layout.rows * ff_pair),
        name="gate_up",
    )(place, gain, weight, *[value for cell in cells for value in sources[cell]])


def join_kernel(left_ref, right_ref, out_ref):
    ff_pair = out_ref.shape[1] - LANES
    product = left_ref[:, :ff_pair].astype(f32) + right_ref[:, :ff_pair].astype(f32)
    out_ref[:, :ff_pair] = product.astype(bf16)
    squares = left_ref[:, ff_pair:].astype(f32) + right_ref[:, ff_pair:].astype(f32)
    out_ref[:, ff_pair:] = squares_joined(squares).astype(bf16)


def join(left, right):
    return pl.pallas_call(
        join_kernel,
        out_shape=jax.ShapeDtypeStruct(left.shape, bf16),
        compiler_params=params(4),
        name="join",
    )(left, right)


def hidden_of(parts, ff_width, model_width, beside):
    def kernel(*refs):
        refs, out_ref = refs[len(beside) : -1], refs[-1]
        total = 0.0
        for ref in refs:
            total = total + ref[...].astype(f32)
        high = total[:, 2 * ff_width : 2 * ff_width + 1]
        low = total[:, 2 * ff_width + 1 : 2 * ff_width + 2]
        norm = lax.rsqrt((high + low) / model_width + epsilon)
        gate = total[:, :ff_width] * norm
        up = total[:, ff_width : 2 * ff_width] * norm
        out_ref[...] = (gate / (1.0 + jnp.exp(-gate)) * up).astype(bf16)

    return pl.pallas_call(
        kernel,
        in_specs=[whole(pltpu.HBM)] * len(beside) + [whole()] * len(parts),
        out_shape=jax.ShapeDtypeStruct((parts[0].shape[0], ff_width), bf16),
        compiler_params=params(8),
        name="hidden",
    )(*in_hbm(beside), *parts)


def down(pieces, layout, weight, high, low, total=None, out_count=1):
    first_cells = next(iter(pieces.values()))
    ff_width = first_cells[0].shape[1]
    tokens = high.shape[1]
    piece_width = weight.shape[2]
    each = layout.rows // layout.experts
    rows = tokens * CELLS // out_count
    out_type = f32 if out_count == 1 else bf16

    def kernel(weight_ref, high_ref, low_ref, *refs):
        hidden_refs, refs = refs[: len(pieces) * CELLS], refs[len(pieces) * CELLS :]
        total_refs, out_refs, held_ref = refs[: -1 - out_count], refs[-1 - out_count : -1], refs[-1]
        summed = [0.0] * CELLS
        for turn, name in enumerate(pieces):
            cells = hidden_refs[turn * CELLS : (turn + 1) * CELLS]
            _, first = layout.cell(*name, 0)
            for i in range(layout.experts):
                here = slice(i * each, (i + 1) * each)
                rows_in = jnp.concatenate([ref[here, :] for ref in cells], axis=0)
                product = dot(rows_in, weight_ref[first + i]).astype(bf16)
                for cell in range(CELLS):
                    held_ref[cell, here, :] = product[cell * each : (cell + 1) * each, :]
            for cell in range(CELLS):
                at, _ = layout.cell(*name, cell)
                held = held_ref[cell]
                summed[cell] = summed[cell] + dot(high_ref[at], held) + dot(low_ref[at], held)
        whole_sum = jnp.concatenate(summed, axis=0)
        for ref in total_refs:
            whole_sum = whole_sum + ref[...]
        for i, ref in enumerate(out_refs):
            ref[...] = whole_sum[i * rows : (i + 1) * rows, :].astype(ref.dtype)

    before = [] if total is None else [total]
    hidden = [value for cells in pieces.values() for value in cells]
    return pl.pallas_call(
        kernel,
        out_shape=[jax.ShapeDtypeStruct((rows, piece_width), out_type)] * out_count,
        scratch_shapes=[pltpu.VMEM((CELLS, layout.rows, piece_width), bf16)],
        compiler_params=params(8),
        cost_estimate=cost(4 * layout.rows * ff_width * piece_width, 2**20),
        name="down",
    )(weight, high, low, *hidden, *before)


def finish_kernel(mixed_ref, *refs):
    total = mixed_ref[...]
    for ref in refs[:-1]:
        total = total + ref[...].astype(f32)
    refs[-1][...] = total.astype(bf16)


def finish(mixed, parts):
    return pl.pallas_call(
        finish_kernel,
        out_shape=jax.ShapeDtypeStruct(mixed.shape, bf16),
        compiler_params=params(4),
        name="finish",
    )(mixed, *parts)


def body(
    queries,
    cached_keys,
    cached_values,
    key_seg,
    query_seg,
    parent,
    out_weight,
    residual,
    norm_gain,
    gate_up_weight,
    down_weight,
    expert_ids,
    route_weight,
):
    ctx_count, exp_count, tp_count = (lax.axis_size(axis) for axis in ("ctx", "exp", "tp"))
    assert tp_count == 2 and cached_keys.shape[1] == 1
    assert ctx_count & (ctx_count - 1) == 0 and exp_count & (exp_count - 1) == 0
    piece_count = exp_count * tp_count
    query_rows = queries.shape[0]
    key_count, _, head_size = cached_keys.shape
    heads = queries.shape[2] // head_size
    width = heads * head_size
    model_width = out_weight.shape[2]
    local_experts, piece_width, _ = gate_up_weight.shape
    ff_width = down_weight.shape[1]
    choices = expert_ids.shape[1]
    scale = math.log2(math.e) / math.sqrt(head_size)

    layout = Layout(local_experts, key_count, query_rows)

    packed = pack(
        queries.reshape(query_rows, width), query_seg, expert_ids, route_weight, gate_up_weight
    )
    gathered = {0: packed}
    for k in far_first(ctx_count):
        gathered[k] = swapped(packed, "ctx", k)
    sight = sight_of(parent, key_seg)
    keys = cached_keys.reshape(key_count, head_size)
    values = cached_values.reshape(key_count, head_size)
    out_matrix = out_weight.reshape(width, model_width)
    parts = {}
    for k in list(range(1, ctx_count)) + [0]:
        part = attend(
            layout, k, gathered[k], keys, values, sight, heads, scale, gate_up_weight
        )
        parts[k] = swapped(part, "ctx", k) if k else part
    place, combine_high, combine_low = route(
        layout, [gathered[k] for k in range(ctx_count)], width, choices
    )
    def after(value, *others):
        return lax.optimization_barrier((value,) + others)[0]

    projected = project(
        layout,
        [parts[k] for k in range(ctx_count)],
        after(out_matrix, place),
        heads,
        scale,
    )
    pieces = [projected[0]] + [
        swapped(projected[k], ("exp", "tp"), k) for k in far_first(piece_count)
    ]
    mixed, sent = mix(residual, norm_gain, pieces)
    rows = {0: sent}
    for k in far_first(ctx_count):
        rows[k] = swapped(sent, "ctx", k)
    half = ctx_count // CELLS
    sources = [[rows[k] for k in range(half * i, half * (i + 1))] for i in range(CELLS)]

    def first_half(*names):
        return gate_up(names, layout, place, sources, gate_up_weight, norm_gain[None, :])

    crossed = [[] for _ in range(CELLS)]
    for k in far_first(exp_count):
        away, mine = first_half((1, k, 0), (0, k, 0))
        here = [swapped(away, "tp", 1)]
        sources[1] = list(lax.optimization_barrier(tuple(sources[1]) + (mine,)))[:-1]
        here.append(swapped(first_half((1, k, 1))[0], "tp", 1))
        for cell in range(CELLS):
            if cell:
                mine = first_half((0, k, cell))[0]
            joined = join(mine, here[cell])
            place = after(place, joined)
            crossed[cell].append(swapped(joined, "exp", k))
    arrived = [swapped(first_half((1, 0, 0))[0], "tp", 1)]
    kept = list(first_half((0, 0, 0), (0, 0, 1)))
    own_hidden = []
    for cell in range(CELLS):
        if cell:
            arrived.append(swapped(first_half((1, 0, cell))[0], "tp", 1))
        crossed[cell], kept[cell] = lax.optimization_barrier((crossed[cell], kept[cell]))
        beside = [out_matrix] * 3
        hidden = hidden_of([kept[cell], arrived[cell]] + crossed[cell], ff_width, model_width, beside)
        place = after(place, hidden)
        own_hidden.append(hidden)

    near = [swapped(hidden, "tp", 1) for hidden in own_hidden]
    far = {
        k: [swapped(hidden, "exp", k) for hidden in own_hidden] for k in range(1, exp_count)
    }
    own_hidden[-1] = after(own_hidden[-1], far[1][0])

    def add(pieces, total, out_count=1):
        return down(pieces, layout, down_weight, combine_high, combine_low, total, out_count)

    total = add({(0, 0): own_hidden, (1, 0): near}, None)[0]
    last = {}
    for k in far:
        far[k][-1] = after(far[k][-1], total)
        last[1, k] = [swapped(hidden, "tp", 1) for hidden in far[k]]
        total = add({(0, k): far[k]}, total)[0]
    totals = add(last, total, ctx_count)
    returned = [totals[0]] + [swapped(totals[k], "ctx", k) for k in far_first(ctx_count)]
    return finish(mixed, returned)


def solution(mesh):
    in_specs = (
        P(("group", "ctx"), "tp", "exp"),
        P(("group", "ctx"), "tp", None),
        P(("group", "ctx"), "tp", None),
        P(("group", "ctx")),
        P(("group", "ctx")),
        P("group"),
        P("tp", "exp", None),
        P(("group", "ctx"), ("exp", "tp")),
        P(("exp", "tp")),
        P("ctx", ("exp", "tp"), None),
        P("ctx", None, ("exp", "tp")),
        P(("group", "ctx"), None),
        P(("group", "ctx"), None),
    )
    out_specs = P(("group", "ctx"), ("exp", "tp"))
    return jax.shard_map(body, mesh=mesh, in_specs=in_specs, out_specs=out_specs, check_vma=False)
```

```python
import functools
import math

import jax
import jax.numpy as jnp
from jax import lax
from jax.experimental import pallas as pl
from jax.experimental.pallas import tpu as pltpu
from jax.sharding import PartitionSpec as P

MOST = 8
DEPTH = 6
LANES = 128
CELLS = 2

epsilon = 1e-06
masked_score = -1e30
least_high = -1e20

f32 = jnp.float32
bf16 = jnp.bfloat16


def params(megabytes, steps=0):
    semantics = ("arbitrary",) * steps if steps else None
    return pltpu.CompilerParams(
        vmem_limit_bytes=megabytes * 1024 * 1024, dimension_semantics=semantics
    )


def cost(flops, bytes_accessed, transcendentals=0):
    return pl.CostEstimate(
        flops=flops, bytes_accessed=bytes_accessed, transcendentals=transcendentals
    )


def whole(memory_space=pltpu.VMEM):
    return pl.BlockSpec(memory_space=memory_space)


def in_hbm(values):
    return [pltpu.with_memory_space_constraint(value, pltpu.HBM) for value in values]


class Layout:
    def __init__(self, local_experts, key_count, query_rows):
        self.ctx, self.exp, self.tp = (lax.axis_size(axis) for axis in ("ctx", "exp", "tp"))
        self.key_count, self.query_rows = key_count, query_rows
        self.local_experts = local_experts
        self.piece_count = self.exp * self.tp
        self.capacity = self.ctx * MOST // CELLS
        self.rows = local_experts * self.capacity // self.piece_count
        self.experts = max(1, self.rows // self.capacity)
        self.spread = max(1, self.capacity // self.rows)
        self.cell_count = self.piece_count * CELLS

    def lead(self, k):
        own = lax.axis_index("ctx")
        start = self.ctx * (self.key_count - self.query_rows)
        return start + (own ^ k) * self.query_rows - own * self.key_count

    def column_piece(self, k):
        return (lax.axis_index("exp") * self.tp + lax.axis_index("tp")) ^ k

    def first_local_expert(self):
        return lax.axis_index("ctx") * self.local_experts

    def cell(self, flip, k, cell):
        piece = (lax.axis_index("tp") ^ flip) * self.exp + (lax.axis_index("exp") ^ k)
        return piece * CELLS + cell, lax.div(piece * self.experts, self.spread)


def lane_ids(shape):
    return lax.broadcasted_iota(jnp.int32, shape, len(shape) - 1)


def row_ids(shape):
    return lax.broadcasted_iota(jnp.int32, shape, len(shape) - 2)


def as_bf16(mask):
    return mask.astype(f32).astype(bf16)


def dot(left, right, dims=((1,), (0,))):
    return lax.dot_general(left, right, (dims, ((), ())), preferred_element_type=f32)


def in_two(value):
    high = value.astype(bf16).astype(f32)
    return high, value - high


def swapped(value, axes, mask):
    count = lax.axis_size(axes)
    pairs = [(source, source ^ mask) for source in range(count)]
    return lax.ppermute(value, axes, pairs)


def far_first(count):
    return list(range(count - 1, 0, -1))


def pack_kernel(
    queries_ref, seg_ref, ids_ref, weight_ref, beside_ref, out_ref,
    seg_here, ids_here, weight_here, done,
):
    rows, width = queries_ref.shape
    choices = ids_ref.shape[0]
    copies = [
        pltpu.make_async_copy(source, target, done.at[i])
        for i, (source, target) in enumerate(
            [
                (seg_ref, seg_here),
                (ids_ref, ids_here),
                (weight_ref, weight_here),
                (queries_ref, out_ref.at[:, :width]),
            ]
        )
    ]
    for copy in copies:
        copy.start()
    shape = (choices, LANES)

    def placed(value, first, last):
        to_lane = (lane_ids(shape) == row_ids(shape) + first) & (row_ids(shape) <= last)
        return dot(value.astype(bf16), as_bf16(to_lane), ((0,), (0,)))

    for copy in copies[:3]:
        copy.wait()
    segs = jnp.broadcast_to(seg_here[...], (choices, rows)).astype(f32)
    high, low = in_two(weight_here[...])
    info = placed(segs, 0, 0) + placed(ids_here[...].astype(f32), 1, choices)
    info = info + placed(high, 1 + choices, choices) + placed(low, 1 + 2 * choices, choices)
    out_ref[:, width:] = info.astype(bf16)
    copies[3].wait()


def pack(queries, query_seg, expert_ids, route_weight, beside):
    rows, width = queries.shape
    small = [query_seg[None, :], expert_ids.T, route_weight.T]
    return pl.pallas_call(
        pack_kernel,
        in_specs=[whole(pltpu.HBM)] * 5,
        out_shape=jax.ShapeDtypeStruct((rows, width + LANES), bf16),
        scratch_shapes=[pltpu.VMEM(value.shape, value.dtype) for value in small]
        + [pltpu.SemaphoreType.DMA((4,))],
        compiler_params=params(4),
        name="pack",
    )(*in_hbm([queries] + small + [beside]))


def sight_kernel(parent_ref, key_seg_ref, sight_ref):
    seg_count, key_count = sight_ref.shape
    square = (seg_count, seg_count)
    same = row_ids(square) == lane_ids(square)
    one = as_bf16((parent_ref[...] == row_ids(square)) | same)
    two = as_bf16(dot(one, one) > 0.5)
    four = as_bf16(dot(two, two) > 0.5)
    six = as_bf16(dot(four, two) > 0.5)
    keys = as_bf16(key_seg_ref[...] == row_ids((seg_count, key_count)))
    sight_ref[...] = dot(six, keys, ((0,), (0,))).astype(bf16)


def sight_of(parent, key_seg):
    assert DEPTH == 6
    return pl.pallas_call(
        sight_kernel,
        out_shape=jax.ShapeDtypeStruct((parent.shape[0], key_seg.shape[0]), bf16),
        compiler_params=params(4),
        cost_estimate=cost(2**24, 2**19),
        name="sight",
    )(parent[None, :], key_seg[None, :])


def attend_kernel(
    heads, scale, layout, k, queries_ref, keys_ref, values_ref, sight_ref, beside_ref,
    out_ref, stacked_ref, probs_ref,
):
    rows = queries_ref.shape[0]
    key_count, head_size = keys_ref.shape
    seg_count = sight_ref.shape[0]
    width = heads * head_size
    info = queries_ref[:, width:].astype(f32)
    own_seg = info[:, :1].astype(jnp.int32)
    onehot = as_bf16(own_seg == lane_ids((rows, seg_count)))
    seen = dot(onehot, sight_ref[...]) > 0.5
    place = (rows, key_count)
    causal = lane_ids(place) - row_ids(place) <= layout.lead(k)
    bias = jnp.where(seen & causal, 0.0, masked_score)
    for head in range(heads):
        columns = slice(head * head_size, (head + 1) * head_size)
        stacked_ref[head * rows : (head + 1) * rows, :] = queries_ref[:, columns]
    scores = dot(stacked_ref[...], keys_ref[...], ((1,), (1,)))
    stats = jnp.zeros((rows, LANES), f32)
    lane = lane_ids((rows, LANES))
    for head in range(heads):
        here = slice(head * rows, (head + 1) * rows)
        biased = scores[here, :] + bias
        high = jnp.maximum(jnp.max(biased, axis=1, keepdims=True), least_high)
        high = high.astype(bf16).astype(f32)
        probs = jnp.exp2((biased - high) * scale)
        total_high, total_low = in_two(jnp.sum(probs, axis=1, keepdims=True))
        probs_ref[here, :] = probs.astype(bf16)
        stats = jnp.where(lane == head, high, stats)
        stats = jnp.where(lane == heads + head, total_high, stats)
        stats = jnp.where(lane == 2 * heads + head, total_low, stats)
    out_ref[:, width:] = stats.astype(bf16)
    sums = dot(probs_ref[...], values_ref[...])
    for head in range(heads):
        columns = slice(head * head_size, (head + 1) * head_size)
        out_ref[:, columns] = sums[head * rows : (head + 1) * rows, :].astype(bf16)


def attend(layout, k, queries, keys, values, sight, heads, scale, beside):
    rows, columns = queries.shape
    key_count, head_size = keys.shape
    work = rows * heads * key_count
    return pl.pallas_call(
        functools.partial(attend_kernel, heads, scale, layout, k),
        in_specs=[whole()] * 4 + [whole(pltpu.HBM)],
        out_shape=jax.ShapeDtypeStruct((rows, columns), bf16),
        scratch_shapes=[
            pltpu.VMEM((rows * heads, head_size), bf16),
            pltpu.VMEM((rows * heads, key_count), bf16),
        ],
        compiler_params=params(8),
        cost_estimate=cost(8 * work * head_size, 2**20, work),
        name="attend",
    )(queries, keys, values, sight, *in_hbm([beside]))


def project_kernel(heads, scale, layout, source_count, *refs):
    parts_refs, weight_ref = refs[:source_count], refs[source_count]
    out_refs, attention_ref = refs[source_count + 1 : -1], refs[-1]
    width = attention_ref.shape[1]
    head_size = width // heads
    stats = [ref[:, width:].astype(f32) for ref in parts_refs]
    top = functools.reduce(jnp.maximum, stats)
    factors = [jnp.exp2(jnp.minimum((stat - top) * scale, 0.0)) for stat in stats]
    total = 0.0
    for stat, factor in zip(stats, factors):
        high = pltpu.roll(stat, LANES - heads, 1)
        low = pltpu.roll(stat, LANES - 2 * heads, 1)
        total = total + factor * (high + low)
    shares = [factor / total for factor in factors]
    for head in range(heads):
        columns = slice(head * head_size, (head + 1) * head_size)
        merged = 0.0
        for ref, share in zip(parts_refs, shares):
            merged = merged + ref[:, columns].astype(f32) * share[:, head : head + 1]
        attention_ref[:, columns] = merged.astype(bf16)
    for i, out_ref in enumerate(out_refs):
        piece_width = out_ref.shape[1]
        start = pl.multiple_of(layout.column_piece(i) * piece_width, piece_width)
        out_ref[...] = dot(attention_ref[...], weight_ref[:, pl.ds(start, piece_width)]).astype(bf16)


def project(layout, parts, weight, heads, scale):
    rows = parts[0].shape[0]
    width, model_width = weight.shape
    piece_width = model_width // layout.piece_count
    return pl.pallas_call(
        functools.partial(project_kernel, heads, scale, layout, len(parts)),
        out_shape=[jax.ShapeDtypeStruct((rows, piece_width), bf16)] * layout.piece_count,
        scratch_shapes=[pltpu.VMEM((rows, width), bf16)],
        compiler_params=params(8),
        cost_estimate=cost(2 * rows * width * model_width, 2 * width * model_width),
        name="project",
    )(*parts, weight)


def mix_kernel(residual_ref, gain_ref, *refs):
    parts_refs, (mixed_ref, sent_ref) = refs[:-2], refs[-2:]
    mixed = residual_ref[...].astype(f32)
    for ref in parts_refs:
        mixed = mixed + ref[...].astype(f32)
    mixed_ref[...] = mixed
    sent_ref[...] = (mixed * gain_ref[...].astype(f32)).astype(bf16)


def mix(residual, gain, parts):
    rows, width = residual.shape
    return pl.pallas_call(
        mix_kernel,
        out_shape=(
            jax.ShapeDtypeStruct((rows, width), f32),
            jax.ShapeDtypeStruct((rows, width), bf16),
        ),
        compiler_params=params(4),
        name="mix",
    )(residual, gain[None, :], *parts)


def route_kernel(layout, choices, width, *refs):
    info_refs, (place_ref, high_ref, low_ref) = refs[:-3], refs[-3:]
    cell_count, tokens, slots = place_ref.shape
    local_experts, capacity = layout.local_experts, layout.capacity
    expert = (lane_ids((tokens, local_experts)) + layout.first_local_expert()).astype(f32)
    square = (tokens, tokens)
    earlier = as_bf16(lane_ids(square) < row_ids(square))
    count = len(info_refs) // CELLS
    for cell in range(CELLS):
        sources = info_refs[cell * count : (cell + 1) * count]
        info = jnp.concatenate([ref[:, width:] for ref in sources], axis=0).astype(f32)
        member = jnp.zeros((tokens, local_experts), f32)
        weight_high = jnp.zeros((tokens, local_experts), f32)
        weight_low = jnp.zeros((tokens, local_experts), f32)
        for k in range(choices):
            chosen = info[:, 1 + k : 2 + k] == expert
            high = info[:, 1 + choices + k : 2 + choices + k]
            low = info[:, 1 + 2 * choices + k : 2 + 2 * choices + k]
            member = jnp.where(chosen, 1.0, member)
            weight_high = jnp.where(chosen, high, weight_high)
            weight_low = jnp.where(chosen, low, weight_low)
        rank = jnp.where(member > 0.5, dot(earlier, member.astype(bf16)), -1.0).astype(bf16)
        weight_high = weight_high.astype(bf16)
        weight_low = weight_low.astype(bf16)
        for piece in range(layout.piece_count):
            slot = lane_ids((local_experts, slots)) + piece * slots
            spread = as_bf16(slot // capacity == row_ids((local_experts, slots)))
            wanted = (lane_ids((tokens, slots)) + piece * slots) % capacity
            placed = dot(rank, spread) == wanted.astype(f32)
            at = piece * CELLS + cell
            place_ref[at] = jnp.where(placed, 1.0, 0.0).astype(bf16)
            high_ref[at] = jnp.where(placed, dot(weight_high, spread), 0.0).astype(bf16)
            low_ref[at] = jnp.where(placed, dot(weight_low, spread), 0.0).astype(bf16)


def route(layout, packed, width, choices):
    tokens = sum(value.shape[0] for value in packed) // CELLS
    shape = jax.ShapeDtypeStruct((layout.cell_count, tokens, layout.rows), bf16)
    return pl.pallas_call(
        functools.partial(route_kernel, layout, choices, width),
        out_shape=(shape, shape, shape),
        compiler_params=params(16),
        cost_estimate=cost(2**25, 2**20),
        name="route",
    )(*packed)


def squares_joined(squares):
    high, low = in_two(squares[:, :1] + squares[:, 1:2])
    lane = lane_ids(squares.shape)
    return jnp.where(lane == 0, high, jnp.where(lane == 1, low, 0.0))


def gate_up(names, layout, place, sources, weight, gain):
    _, width, ff_pair = weight.shape
    each = layout.rows // layout.experts
    cells = sorted({name[2] for name in names})
    count = len(sources[0])

    def kernel(place_ref, gain_ref, weight_ref, *refs):
        inverse_gain = 1.0 / gain_ref[...].astype(f32)
        for name, out_ref in zip(names, refs[len(cells) * count :]):
            at, first = layout.cell(*name)
            turn = cells.index(name[2])
            picked = 0.0
            for i, ref in enumerate(refs[turn * count : (turn + 1) * count]):
                tokens = ref.shape[0]
                here = place_ref[at, i * tokens : (i + 1) * tokens, :]
                picked = picked + dot(here, ref[...], ((0,), (0,)))
            picked = picked.astype(bf16)
            for i in range(layout.experts):
                here = slice(i * each, (i + 1) * each)
                out_ref[here, :ff_pair] = dot(picked[here, :], weight_ref[first + i]).astype(bf16)
            mixed = picked.astype(f32) * inverse_gain
            high, low = in_two(jnp.sum(mixed * mixed, axis=1, keepdims=True))
            lane = lane_ids((layout.rows, LANES))
            squares = jnp.where(lane == 0, high, jnp.where(lane == 1, low, 0.0))
            out_ref[:, ff_pair:] = squares.astype(bf16)

    out = jax.ShapeDtypeStruct((layout.rows, ff_pair + LANES), bf16)
    return pl.pallas_call(
        kernel,
        out_shape=[out] * len(names),
        compiler_params=params(8),
        cost_estimate=cost(2 * layout.rows * width * ff_pair, 2 * layout.rows * ff_pair),
        name="gate_up",
    )(place, gain, weight, *[value for cell in cells for value in sources[cell]])


def join_kernel(left_ref, right_ref, out_ref):
    ff_pair = out_ref.shape[1] - LANES
    product = left_ref[:, :ff_pair].astype(f32) + right_ref[:, :ff_pair].astype(f32)
    out_ref[:, :ff_pair] = product.astype(bf16)
    squares = left_ref[:, ff_pair:].astype(f32) + right_ref[:, ff_pair:].astype(f32)
    out_ref[:, ff_pair:] = squares_joined(squares).astype(bf16)


def join(left, right):
    return pl.pallas_call(
        join_kernel,
        out_shape=jax.ShapeDtypeStruct(left.shape, bf16),
        compiler_params=params(4),
        name="join",
    )(left, right)


def hidden_of(parts, ff_width, model_width, beside):
    def kernel(*refs):
        refs, out_ref = refs[len(beside) : -1], refs[-1]
        total = 0.0
        for ref in refs:
            total = total + ref[...].astype(f32)
        high = total[:, 2 * ff_width : 2 * ff_width + 1]
        low = total[:, 2 * ff_width + 1 : 2 * ff_width + 2]
        norm = lax.rsqrt((high + low) / model_width + epsilon)
        gate = total[:, :ff_width] * norm
        up = total[:, ff_width : 2 * ff_width] * norm
        out_ref[...] = (gate / (1.0 + jnp.exp(-gate)) * up).astype(bf16)

    return pl.pallas_call(
        kernel,
        in_specs=[whole(pltpu.HBM)] * len(beside) + [whole()] * len(parts),
        out_shape=jax.ShapeDtypeStruct((parts[0].shape[0], ff_width), bf16),
        compiler_params=params(8),
        name="hidden",
    )(*in_hbm(beside), *parts)


def down(pieces, layout, weight, high, low, total=None, out_count=1):
    first_cells = next(iter(pieces.values()))
    ff_width = first_cells[0].shape[1]
    tokens = high.shape[1]
    piece_width = weight.shape[2]
    each = layout.rows // layout.experts
    rows = tokens * CELLS // out_count
    out_type = f32 if out_count == 1 else bf16

    def kernel(weight_ref, high_ref, low_ref, *refs):
        hidden_refs, refs = refs[: len(pieces) * CELLS], refs[len(pieces) * CELLS :]
        total_refs, out_refs, held_ref = refs[: -1 - out_count], refs[-1 - out_count : -1], refs[-1]
        summed = [0.0] * CELLS
        for turn, name in enumerate(pieces):
            cells = hidden_refs[turn * CELLS : (turn + 1) * CELLS]
            _, first = layout.cell(*name, 0)
            for i in range(layout.experts):
                here = slice(i * each, (i + 1) * each)
                rows_in = jnp.concatenate([ref[here, :] for ref in cells], axis=0)
                product = dot(rows_in, weight_ref[first + i]).astype(bf16)
                for cell in range(CELLS):
                    held_ref[cell, here, :] = product[cell * each : (cell + 1) * each, :]
            for cell in range(CELLS):
                at, _ = layout.cell(*name, cell)
                held = held_ref[cell]
                summed[cell] = summed[cell] + dot(high_ref[at], held) + dot(low_ref[at], held)
        whole_sum = jnp.concatenate(summed, axis=0)
        for ref in total_refs:
            whole_sum = whole_sum + ref[...]
        for i, ref in enumerate(out_refs):
            ref[...] = whole_sum[i * rows : (i + 1) * rows, :].astype(ref.dtype)

    before = [] if total is None else [total]
    hidden = [value for cells in pieces.values() for value in cells]
    return pl.pallas_call(
        kernel,
        out_shape=[jax.ShapeDtypeStruct((rows, piece_width), out_type)] * out_count,
        scratch_shapes=[pltpu.VMEM((CELLS, layout.rows, piece_width), bf16)],
        compiler_params=params(8),
        cost_estimate=cost(4 * layout.rows * ff_width * piece_width, 2**20),
        name="down",
    )(weight, high, low, *hidden, *before)


def finish_kernel(mixed_ref, *refs):
    total = mixed_ref[...]
    for ref in refs[:-1]:
        total = total + ref[...].astype(f32)
    refs[-1][...] = total.astype(bf16)


def finish(mixed, parts):
    return pl.pallas_call(
        finish_kernel,
        out_shape=jax.ShapeDtypeStruct(mixed.shape, bf16),
        compiler_params=params(4),
        name="finish",
    )(mixed, *parts)


def body(
    queries,
    cached_keys,
    cached_values,
    key_seg,
    query_seg,
    parent,
    out_weight,
    residual,
    norm_gain,
    gate_up_weight,
    down_weight,
    expert_ids,
    route_weight,
):
    ctx_count, exp_count, tp_count = (lax.axis_size(axis) for axis in ("ctx", "exp", "tp"))
    assert tp_count == 2 and cached_keys.shape[1] == 1
    assert ctx_count & (ctx_count - 1) == 0 and exp_count & (exp_count - 1) == 0
    piece_count = exp_count * tp_count
    query_rows = queries.shape[0]
    key_count, _, head_size = cached_keys.shape
    heads = queries.shape[2] // head_size
    width = heads * head_size
    model_width = out_weight.shape[2]
    local_experts, piece_width, _ = gate_up_weight.shape
    ff_width = down_weight.shape[1]
    choices = expert_ids.shape[1]
    scale = math.log2(math.e) / math.sqrt(head_size)

    layout = Layout(local_experts, key_count, query_rows)

    packed = pack(
        queries.reshape(query_rows, width), query_seg, expert_ids, route_weight, gate_up_weight
    )
    gathered = {0: packed}
    for k in far_first(ctx_count):
        gathered[k] = swapped(packed, "ctx", k)
    sight = sight_of(parent, key_seg)
    keys = cached_keys.reshape(key_count, head_size)
    values = cached_values.reshape(key_count, head_size)
    out_matrix = out_weight.reshape(width, model_width)
    parts = {}
    for k in list(range(1, ctx_count)) + [0]:
        part = attend(
            layout, k, gathered[k], keys, values, sight, heads, scale, gate_up_weight
        )
        parts[k] = swapped(part, "ctx", k) if k else part
    place, combine_high, combine_low = route(
        layout, [gathered[k] for k in range(ctx_count)], width, choices
    )
    def after(value, *others):
        return lax.optimization_barrier((value,) + others)[0]

    projected = project(
        layout,
        [parts[k] for k in range(ctx_count)],
        after(out_matrix, place),
        heads,
        scale,
    )
    pieces = [projected[0]] + [
        swapped(projected[k], ("exp", "tp"), k) for k in far_first(piece_count)
    ]
    mixed, sent = mix(residual, norm_gain, pieces)
    rows = {0: sent}
    for k in far_first(ctx_count):
        rows[k] = swapped(sent, "ctx", k)
    half = ctx_count // CELLS
    sources = [[rows[k] for k in range(half * i, half * (i + 1))] for i in range(CELLS)]

    def first_half(*names):
        return gate_up(names, layout, place, sources, gate_up_weight, norm_gain[None, :])

    crossed = [[] for _ in range(CELLS)]
    for k in far_first(exp_count):
        away, mine = first_half((1, k, 0), (0, k, 0))
        here = [swapped(away, "tp", 1)]
        sources[1] = list(lax.optimization_barrier(tuple(sources[1]) + (mine,)))[:-1]
        here.append(swapped(first_half((1, k, 1))[0], "tp", 1))
        for cell in range(CELLS):
            if cell:
                mine = first_half((0, k, cell))[0]
            joined = join(mine, here[cell])
            place = after(place, joined)
            crossed[cell].append(swapped(joined, "exp", k))
    arrived = [swapped(first_half((1, 0, 0))[0], "tp", 1)]
    kept = list(first_half((0, 0, 0), (0, 0, 1)))
    own_hidden = []
    for cell in range(CELLS):
        if cell:
            arrived.append(swapped(first_half((1, 0, cell))[0], "tp", 1))
        crossed[cell], kept[cell] = lax.optimization_barrier((crossed[cell], kept[cell]))
        beside = [out_matrix] * 3
        hidden = hidden_of([kept[cell], arrived[cell]] + crossed[cell], ff_width, model_width, beside)
        place = after(place, hidden)
        own_hidden.append(hidden)

    near = [swapped(hidden, "tp", 1) for hidden in own_hidden]
    far = {
        k: [swapped(hidden, "exp", k) for hidden in own_hidden] for k in range(1, exp_count)
    }
    own_hidden[-1] = after(own_hidden[-1], far[1][0])

    def add(pieces, total, out_count=1):
        return down(pieces, layout, down_weight, combine_high, combine_low, total, out_count)

    total = add({(0, 0): own_hidden, (1, 0): near}, None)[0]
    last = {}
    for k in far:
        far[k][-1] = after(far[k][-1], total)
        last[1, k] = [swapped(hidden, "tp", 1) for hidden in far[k]]
        total = add({(0, k): far[k]}, total)[0]
    totals = add(last, total, ctx_count)
    returned = [totals[0]] + [swapped(totals[k], "ctx", k) for k in range(1, ctx_count)]
    return finish(mixed, returned)


def solution(mesh):
    in_specs = (
        P(("group", "ctx"), "tp", "exp"),
        P(("group", "ctx"), "tp", None),
        P(("group", "ctx"), "tp", None),
        P(("group", "ctx")),
        P(("group", "ctx")),
        P("group"),
        P("tp", "exp", None),
        P(("group", "ctx"), ("exp", "tp")),
        P(("exp", "tp")),
        P("ctx", ("exp", "tp"), None),
        P("ctx", None, ("exp", "tp")),
        P(("group", "ctx"), None),
        P(("group", "ctx"), None),
    )
    out_specs = P(("group", "ctx"), ("exp", "tp"))
    return jax.shard_map(body, mesh=mesh, in_specs=in_specs, out_specs=out_specs, check_vma=False)
```

```python
import functools
import math

import jax
import jax.numpy as jnp
from jax import lax
from jax.experimental import pallas as pl
from jax.experimental.pallas import tpu as pltpu
from jax.sharding import PartitionSpec as P

MOST = 8
DEPTH = 6
LANES = 128
CELLS = 2

epsilon = 1e-06
masked_score = -1e30
least_high = -1e20

f32 = jnp.float32
bf16 = jnp.bfloat16


def params(megabytes, steps=0):
    semantics = ("arbitrary",) * steps if steps else None
    return pltpu.CompilerParams(
        vmem_limit_bytes=megabytes * 1024 * 1024, dimension_semantics=semantics
    )


def cost(flops, bytes_accessed, transcendentals=0):
    return pl.CostEstimate(
        flops=flops, bytes_accessed=bytes_accessed, transcendentals=transcendentals
    )


def whole(memory_space=pltpu.VMEM):
    return pl.BlockSpec(memory_space=memory_space)


def in_hbm(values):
    return [pltpu.with_memory_space_constraint(value, pltpu.HBM) for value in values]


class Layout:
    def __init__(self, local_experts, key_count, query_rows):
        self.ctx, self.exp, self.tp = (lax.axis_size(axis) for axis in ("ctx", "exp", "tp"))
        self.key_count, self.query_rows = key_count, query_rows
        self.local_experts = local_experts
        self.piece_count = self.exp * self.tp
        self.capacity = self.ctx * MOST // CELLS
        self.rows = local_experts * self.capacity // self.piece_count
        self.experts = max(1, self.rows // self.capacity)
        self.spread = max(1, self.capacity // self.rows)
        self.cell_count = self.piece_count * CELLS

    def lead(self, k):
        own = lax.axis_index("ctx")
        start = self.ctx * (self.key_count - self.query_rows)
        return start + (own ^ k) * self.query_rows - own * self.key_count

    def column_piece(self, k):
        return (lax.axis_index("exp") * self.tp + lax.axis_index("tp")) ^ k

    def first_local_expert(self):
        return lax.axis_index("ctx") * self.local_experts

    def cell(self, flip, k, cell):
        piece = (lax.axis_index("tp") ^ flip) * self.exp + (lax.axis_index("exp") ^ k)
        return piece * CELLS + cell, lax.div(piece * self.experts, self.spread)


def lane_ids(shape):
    return lax.broadcasted_iota(jnp.int32, shape, len(shape) - 1)


def row_ids(shape):
    return lax.broadcasted_iota(jnp.int32, shape, len(shape) - 2)


def as_bf16(mask):
    return mask.astype(f32).astype(bf16)


def dot(left, right, dims=((1,), (0,))):
    return lax.dot_general(left, right, (dims, ((), ())), preferred_element_type=f32)


def in_two(value):
    high = value.astype(bf16).astype(f32)
    return high, value - high


def swapped(value, axes, mask):
    count = lax.axis_size(axes)
    pairs = [(source, source ^ mask) for source in range(count)]
    return lax.ppermute(value, axes, pairs)


def far_first(count):
    return list(range(count - 1, 0, -1))


def pack_kernel(
    queries_ref, seg_ref, ids_ref, weight_ref, beside_ref, out_ref,
    seg_here, ids_here, weight_here, done,
):
    rows, width = queries_ref.shape
    choices = ids_ref.shape[0]
    copies = [
        pltpu.make_async_copy(source, target, done.at[i])
        for i, (source, target) in enumerate(
            [
                (seg_ref, seg_here),
                (ids_ref, ids_here),
                (weight_ref, weight_here),
                (queries_ref, out_ref.at[:, :width]),
            ]
        )
    ]
    for copy in copies:
        copy.start()
    shape = (choices, LANES)

    def placed(value, first, last):
        to_lane = (lane_ids(shape) == row_ids(shape) + first) & (row_ids(shape) <= last)
        return dot(value.astype(bf16), as_bf16(to_lane), ((0,), (0,)))

    for copy in copies[:3]:
        copy.wait()
    segs = jnp.broadcast_to(seg_here[...], (choices, rows)).astype(f32)
    high, low = in_two(weight_here[...])
    info = placed(segs, 0, 0) + placed(ids_here[...].astype(f32), 1, choices)
    info = info + placed(high, 1 + choices, choices) + placed(low, 1 + 2 * choices, choices)
    out_ref[:, width:] = info.astype(bf16)
    copies[3].wait()


def pack(queries, query_seg, expert_ids, route_weight, beside):
    rows, width = queries.shape
    small = [query_seg[None, :], expert_ids.T, route_weight.T]
    return pl.pallas_call(
        pack_kernel,
        in_specs=[whole(pltpu.HBM)] * 5,
        out_shape=jax.ShapeDtypeStruct((rows, width + LANES), bf16),
        scratch_shapes=[pltpu.VMEM(value.shape, value.dtype) for value in small]
        + [pltpu.SemaphoreType.DMA((4,))],
        compiler_params=params(4),
        name="pack",
    )(*in_hbm([queries] + small + [beside]))


def sight_kernel(parent_ref, key_seg_ref, sight_ref):
    seg_count, key_count = sight_ref.shape
    square = (seg_count, seg_count)
    same = row_ids(square) == lane_ids(square)
    one = as_bf16((parent_ref[...] == row_ids(square)) | same)
    two = as_bf16(dot(one, one) > 0.5)
    four = as_bf16(dot(two, two) > 0.5)
    six = as_bf16(dot(four, two) > 0.5)
    keys = as_bf16(key_seg_ref[...] == row_ids((seg_count, key_count)))
    sight_ref[...] = dot(six, keys, ((0,), (0,))).astype(bf16)


def sight_of(parent, key_seg):
    assert DEPTH == 6
    return pl.pallas_call(
        sight_kernel,
        out_shape=jax.ShapeDtypeStruct((parent.shape[0], key_seg.shape[0]), bf16),
        compiler_params=params(4),
        cost_estimate=cost(2**24, 2**19),
        name="sight",
    )(parent[None, :], key_seg[None, :])


def attend_kernel(
    heads, scale, layout, k, queries_ref, keys_ref, values_ref, sight_ref, beside_ref,
    out_ref, stacked_ref, probs_ref,
):
    rows = queries_ref.shape[0]
    key_count, head_size = keys_ref.shape
    seg_count = sight_ref.shape[0]
    width = heads * head_size
    info = queries_ref[:, width:].astype(f32)
    own_seg = info[:, :1].astype(jnp.int32)
    onehot = as_bf16(own_seg == lane_ids((rows, seg_count)))
    seen = dot(onehot, sight_ref[...]) > 0.5
    place = (rows, key_count)
    causal = lane_ids(place) - row_ids(place) <= layout.lead(k)
    bias = jnp.where(seen & causal, 0.0, masked_score)
    for head in range(heads):
        columns = slice(head * head_size, (head + 1) * head_size)
        stacked_ref[head * rows : (head + 1) * rows, :] = queries_ref[:, columns]
    scores = dot(stacked_ref[...], keys_ref[...], ((1,), (1,)))
    stats = jnp.zeros((rows, LANES), f32)
    lane = lane_ids((rows, LANES))
    for head in range(heads):
        here = slice(head * rows, (head + 1) * rows)
        biased = scores[here, :] + bias
        high = jnp.maximum(jnp.max(biased, axis=1, keepdims=True), least_high)
        high = high.astype(bf16).astype(f32)
        probs = jnp.exp2((biased - high) * scale)
        total_high, total_low = in_two(jnp.sum(probs, axis=1, keepdims=True))
        probs_ref[here, :] = probs.astype(bf16)
        stats = jnp.where(lane == head, high, stats)
        stats = jnp.where(lane == heads + head, total_high, stats)
        stats = jnp.where(lane == 2 * heads + head, total_low, stats)
    out_ref[:, width:] = stats.astype(bf16)
    sums = dot(probs_ref[...], values_ref[...])
    for head in range(heads):
        columns = slice(head * head_size, (head + 1) * head_size)
        out_ref[:, columns] = sums[head * rows : (head + 1) * rows, :].astype(bf16)


def attend(layout, k, queries, keys, values, sight, heads, scale, beside):
    rows, columns = queries.shape
    key_count, head_size = keys.shape
    work = rows * heads * key_count
    return pl.pallas_call(
        functools.partial(attend_kernel, heads, scale, layout, k),
        in_specs=[whole()] * 4 + [whole(pltpu.HBM)],
        out_shape=jax.ShapeDtypeStruct((rows, columns), bf16),
        scratch_shapes=[
            pltpu.VMEM((rows * heads, head_size), bf16),
            pltpu.VMEM((rows * heads, key_count), bf16),
        ],
        compiler_params=params(8),
        cost_estimate=cost(8 * work * head_size, 2**20, work),
        name="attend",
    )(queries, keys, values, sight, *in_hbm([beside]))


def project_kernel(heads, scale, layout, source_count, *refs):
    parts_refs, weight_ref = refs[:source_count], refs[source_count]
    out_refs, attention_ref = refs[source_count + 1 : -1], refs[-1]
    width = attention_ref.shape[1]
    head_size = width // heads
    stats = [ref[:, width:].astype(f32) for ref in parts_refs]
    top = functools.reduce(jnp.maximum, stats)
    factors = [jnp.exp2(jnp.minimum((stat - top) * scale, 0.0)) for stat in stats]
    total = 0.0
    for stat, factor in zip(stats, factors):
        high = pltpu.roll(stat, LANES - heads, 1)
        low = pltpu.roll(stat, LANES - 2 * heads, 1)
        total = total + factor * (high + low)
    shares = [factor / total for factor in factors]
    for head in range(heads):
        columns = slice(head * head_size, (head + 1) * head_size)
        merged = 0.0
        for ref, share in zip(parts_refs, shares):
            merged = merged + ref[:, columns].astype(f32) * share[:, head : head + 1]
        attention_ref[:, columns] = merged.astype(bf16)
    for i, out_ref in enumerate(out_refs):
        piece_width = out_ref.shape[1]
        start = pl.multiple_of(layout.column_piece(i) * piece_width, piece_width)
        out_ref[...] = dot(attention_ref[...], weight_ref[:, pl.ds(start, piece_width)]).astype(bf16)


def project(layout, parts, weight, heads, scale):
    rows = parts[0].shape[0]
    width, model_width = weight.shape
    piece_width = model_width // layout.piece_count
    return pl.pallas_call(
        functools.partial(project_kernel, heads, scale, layout, len(parts)),
        out_shape=[jax.ShapeDtypeStruct((rows, piece_width), bf16)] * layout.piece_count,
        scratch_shapes=[pltpu.VMEM((rows, width), bf16)],
        compiler_params=params(8),
        cost_estimate=cost(2 * rows * width * model_width, 2 * width * model_width),
        name="project",
    )(*parts, weight)


def mix_kernel(residual_ref, gain_ref, *refs):
    parts_refs, (mixed_ref, sent_ref) = refs[:-2], refs[-2:]
    mixed = residual_ref[...].astype(f32)
    for ref in parts_refs:
        mixed = mixed + ref[...].astype(f32)
    mixed_ref[...] = mixed
    sent_ref[...] = (mixed * gain_ref[...].astype(f32)).astype(bf16)


def mix(residual, gain, parts):
    rows, width = residual.shape
    return pl.pallas_call(
        mix_kernel,
        out_shape=(
            jax.ShapeDtypeStruct((rows, width), f32),
            jax.ShapeDtypeStruct((rows, width), bf16),
        ),
        compiler_params=params(4),
        name="mix",
    )(residual, gain[None, :], *parts)


def route_kernel(layout, choices, width, *refs):
    info_refs, (place_ref, high_ref, low_ref) = refs[:-3], refs[-3:]
    cell_count, tokens, slots = place_ref.shape
    local_experts, capacity = layout.local_experts, layout.capacity
    expert = (lane_ids((tokens, local_experts)) + layout.first_local_expert()).astype(f32)
    square = (tokens, tokens)
    earlier = as_bf16(lane_ids(square) < row_ids(square))
    count = len(info_refs) // CELLS
    for cell in range(CELLS):
        sources = info_refs[cell * count : (cell + 1) * count]
        info = jnp.concatenate([ref[:, width:] for ref in sources], axis=0).astype(f32)
        member = jnp.zeros((tokens, local_experts), f32)
        weight_high = jnp.zeros((tokens, local_experts), f32)
        weight_low = jnp.zeros((tokens, local_experts), f32)
        for k in range(choices):
            chosen = info[:, 1 + k : 2 + k] == expert
            high = info[:, 1 + choices + k : 2 + choices + k]
            low = info[:, 1 + 2 * choices + k : 2 + 2 * choices + k]
            member = jnp.where(chosen, 1.0, member)
            weight_high = jnp.where(chosen, high, weight_high)
            weight_low = jnp.where(chosen, low, weight_low)
        rank = jnp.where(member > 0.5, dot(earlier, member.astype(bf16)), -1.0).astype(bf16)
        weight_high = weight_high.astype(bf16)
        weight_low = weight_low.astype(bf16)
        for piece in range(layout.piece_count):
            slot = lane_ids((local_experts, slots)) + piece * slots
            spread = as_bf16(slot // capacity == row_ids((local_experts, slots)))
            wanted = (lane_ids((tokens, slots)) + piece * slots) % capacity
            placed = dot(rank, spread) == wanted.astype(f32)
            at = piece * CELLS + cell
            place_ref[at] = jnp.where(placed, 1.0, 0.0).astype(bf16)
            high_ref[at] = jnp.where(placed, dot(weight_high, spread), 0.0).astype(bf16)
            low_ref[at] = jnp.where(placed, dot(weight_low, spread), 0.0).astype(bf16)


def route(layout, packed, width, choices):
    tokens = sum(value.shape[0] for value in packed) // CELLS
    shape = jax.ShapeDtypeStruct((layout.cell_count, tokens, layout.rows), bf16)
    return pl.pallas_call(
        functools.partial(route_kernel, layout, choices, width),
        out_shape=(shape, shape, shape),
        compiler_params=params(16),
        cost_estimate=cost(2**25, 2**20),
        name="route",
    )(*packed)


def squares_joined(squares):
    high, low = in_two(squares[:, :1] + squares[:, 1:2])
    lane = lane_ids(squares.shape)
    return jnp.where(lane == 0, high, jnp.where(lane == 1, low, 0.0))


def gate_up(names, layout, place, sources, weight, gain):
    _, width, ff_pair = weight.shape
    each = layout.rows // layout.experts
    cells = sorted({name[2] for name in names})
    count = len(sources[0])

    def kernel(place_ref, gain_ref, weight_ref, *refs):
        inverse_gain = 1.0 / gain_ref[...].astype(f32)
        for name, out_ref in zip(names, refs[len(cells) * count :]):
            at, first = layout.cell(*name)
            turn = cells.index(name[2])
            picked = 0.0
            for i, ref in enumerate(refs[turn * count : (turn + 1) * count]):
                tokens = ref.shape[0]
                here = place_ref[at, i * tokens : (i + 1) * tokens, :]
                picked = picked + dot(here, ref[...], ((0,), (0,)))
            picked = picked.astype(bf16)
            for i in range(layout.experts):
                here = slice(i * each, (i + 1) * each)
                out_ref[here, :ff_pair] = dot(picked[here, :], weight_ref[first + i]).astype(bf16)
            mixed = picked.astype(f32) * inverse_gain
            high, low = in_two(jnp.sum(mixed * mixed, axis=1, keepdims=True))
            lane = lane_ids((layout.rows, LANES))
            squares = jnp.where(lane == 0, high, jnp.where(lane == 1, low, 0.0))
            out_ref[:, ff_pair:] = squares.astype(bf16)

    out = jax.ShapeDtypeStruct((layout.rows, ff_pair + LANES), bf16)
    return pl.pallas_call(
        kernel,
        out_shape=[out] * len(names),
        compiler_params=params(8),
        cost_estimate=cost(2 * layout.rows * width * ff_pair, 2 * layout.rows * ff_pair),
        name="gate_up",
    )(place, gain, weight, *[value for cell in cells for value in sources[cell]])


def join_kernel(left_ref, right_ref, out_ref):
    ff_pair = out_ref.shape[1] - LANES
    product = left_ref[:, :ff_pair].astype(f32) + right_ref[:, :ff_pair].astype(f32)
    out_ref[:, :ff_pair] = product.astype(bf16)
    squares = left_ref[:, ff_pair:].astype(f32) + right_ref[:, ff_pair:].astype(f32)
    out_ref[:, ff_pair:] = squares_joined(squares).astype(bf16)


def join(left, right):
    return pl.pallas_call(
        join_kernel,
        out_shape=jax.ShapeDtypeStruct(left.shape, bf16),
        compiler_params=params(4),
        name="join",
    )(left, right)


def hidden_of(parts, ff_width, model_width, beside):
    def kernel(*refs):
        refs, out_ref = refs[len(beside) : -1], refs[-1]
        total = 0.0
        for ref in refs:
            total = total + ref[...].astype(f32)
        high = total[:, 2 * ff_width : 2 * ff_width + 1]
        low = total[:, 2 * ff_width + 1 : 2 * ff_width + 2]
        norm = lax.rsqrt((high + low) / model_width + epsilon)
        gate = total[:, :ff_width] * norm
        up = total[:, ff_width : 2 * ff_width] * norm
        out_ref[...] = (gate / (1.0 + jnp.exp(-gate)) * up).astype(bf16)

    return pl.pallas_call(
        kernel,
        in_specs=[whole(pltpu.HBM)] * len(beside) + [whole()] * len(parts),
        out_shape=jax.ShapeDtypeStruct((parts[0].shape[0], ff_width), bf16),
        compiler_params=params(8),
        name="hidden",
    )(*in_hbm(beside), *parts)


def down(pieces, layout, weight, high, low, total=None, out_count=1):
    first_cells = next(iter(pieces.values()))
    ff_width = first_cells[0].shape[1]
    tokens = high.shape[1]
    piece_width = weight.shape[2]
    each = layout.rows // layout.experts
    rows = tokens * CELLS // out_count
    out_type = f32 if out_count == 1 else bf16

    def kernel(weight_ref, high_ref, low_ref, *refs):
        hidden_refs, refs = refs[: len(pieces) * CELLS], refs[len(pieces) * CELLS :]
        total_refs, out_refs, held_ref = refs[: -1 - out_count], refs[-1 - out_count : -1], refs[-1]
        summed = [0.0] * CELLS
        for turn, name in enumerate(pieces):
            cells = hidden_refs[turn * CELLS : (turn + 1) * CELLS]
            _, first = layout.cell(*name, 0)
            for i in range(layout.experts):
                here = slice(i * each, (i + 1) * each)
                rows_in = jnp.concatenate([ref[here, :] for ref in cells], axis=0)
                product = dot(rows_in, weight_ref[first + i]).astype(bf16)
                for cell in range(CELLS):
                    held_ref[cell, here, :] = product[cell * each : (cell + 1) * each, :]
            for cell in range(CELLS):
                at, _ = layout.cell(*name, cell)
                held = held_ref[cell]
                summed[cell] = summed[cell] + dot(high_ref[at], held) + dot(low_ref[at], held)
        whole_sum = jnp.concatenate(summed, axis=0)
        for ref in total_refs:
            whole_sum = whole_sum + ref[...]
        for i, ref in enumerate(out_refs):
            ref[...] = whole_sum[i * rows : (i + 1) * rows, :].astype(ref.dtype)

    before = [] if total is None else [total]
    hidden = [value for cells in pieces.values() for value in cells]
    return pl.pallas_call(
        kernel,
        out_shape=[jax.ShapeDtypeStruct((rows, piece_width), out_type)] * out_count,
        scratch_shapes=[pltpu.VMEM((CELLS, layout.rows, piece_width), bf16)],
        compiler_params=params(8),
        cost_estimate=cost(4 * layout.rows * ff_width * piece_width, 2**20),
        name="down",
    )(weight, high, low, *hidden, *before)


def finish_kernel(mixed_ref, *refs):
    total = mixed_ref[...]
    for ref in refs[:-1]:
        total = total + ref[...].astype(f32)
    refs[-1][...] = total.astype(bf16)


def finish(mixed, parts):
    return pl.pallas_call(
        finish_kernel,
        out_shape=jax.ShapeDtypeStruct(mixed.shape, bf16),
        compiler_params=params(4),
        name="finish",
    )(mixed, *parts)


def body(
    queries,
    cached_keys,
    cached_values,
    key_seg,
    query_seg,
    parent,
    out_weight,
    residual,
    norm_gain,
    gate_up_weight,
    down_weight,
    expert_ids,
    route_weight,
):
    ctx_count, exp_count, tp_count = (lax.axis_size(axis) for axis in ("ctx", "exp", "tp"))
    assert tp_count == 2 and cached_keys.shape[1] == 1
    assert ctx_count & (ctx_count - 1) == 0 and exp_count & (exp_count - 1) == 0
    piece_count = exp_count * tp_count
    query_rows = queries.shape[0]
    key_count, _, head_size = cached_keys.shape
    heads = queries.shape[2] // head_size
    width = heads * head_size
    model_width = out_weight.shape[2]
    local_experts, piece_width, _ = gate_up_weight.shape
    ff_width = down_weight.shape[1]
    choices = expert_ids.shape[1]
    scale = math.log2(math.e) / math.sqrt(head_size)

    layout = Layout(local_experts, key_count, query_rows)

    packed = pack(
        queries.reshape(query_rows, width), query_seg, expert_ids, route_weight, gate_up_weight
    )
    gathered = {0: packed}
    for k in far_first(ctx_count):
        gathered[k] = swapped(packed, "ctx", k)
    sight = sight_of(parent, key_seg)
    keys = cached_keys.reshape(key_count, head_size)
    values = cached_values.reshape(key_count, head_size)
    out_matrix = out_weight.reshape(width, model_width)
    parts = {}
    for k in list(range(1, ctx_count)) + [0]:
        part = attend(
            layout, k, gathered[k], keys, values, sight, heads, scale, gate_up_weight
        )
        parts[k] = swapped(part, "ctx", k) if k else part
    place, combine_high, combine_low = route(
        layout, [gathered[k] for k in range(ctx_count)], width, choices
    )
    def after(value, *others):
        return lax.optimization_barrier((value,) + others)[0]

    projected = project(
        layout,
        [parts[k] for k in range(ctx_count)],
        after(out_matrix, place),
        heads,
        scale,
    )
    pieces = [projected[0]] + [
        swapped(projected[k], ("exp", "tp"), k) for k in far_first(piece_count)
    ]
    mixed, sent = mix(residual, norm_gain, pieces)
    rows = {0: sent}
    for k in far_first(ctx_count):
        rows[k] = swapped(sent, "ctx", k)
    half = ctx_count // CELLS
    sources = [[rows[k] for k in range(half * i, half * (i + 1))] for i in range(CELLS)]

    def first_half(*names):
        return gate_up(names, layout, place, sources, gate_up_weight, norm_gain[None, :])

    crossed = [[] for _ in range(CELLS)]
    for k in far_first(exp_count):
        away, mine = first_half((1, k, 0), (0, k, 0))
        here = [swapped(away, "tp", 1)]
        sources[1] = list(lax.optimization_barrier(tuple(sources[1]) + (mine,)))[:-1]
        here.append(swapped(first_half((1, k, 1))[0], "tp", 1))
        for cell in range(CELLS):
            if cell:
                mine = first_half((0, k, cell))[0]
            joined = join(mine, here[cell])
            place = after(place, joined)
            crossed[cell].append(swapped(joined, "exp", k))
    arrived = [swapped(first_half((1, 0, 0))[0], "tp", 1)]
    kept = list(first_half((0, 0, 0), (0, 0, 1)))
    own_hidden = []
    for cell in range(CELLS):
        if cell:
            arrived.append(swapped(first_half((1, 0, cell))[0], "tp", 1))
        crossed[cell], kept[cell] = lax.optimization_barrier((crossed[cell], kept[cell]))
        beside = [out_matrix] * 3
        hidden = hidden_of([kept[cell], arrived[cell]] + crossed[cell], ff_width, model_width, beside)
        place = after(place, hidden)
        own_hidden.append(hidden)

    near = [swapped(hidden, "tp", 1) for hidden in own_hidden]
    far = {
        k: [swapped(hidden, "exp", k) for hidden in own_hidden] for k in range(1, exp_count)
    }
    own_hidden[-1] = after(own_hidden[-1], far[1][0])

    def add(pieces, total, out_count=1):
        return down(pieces, layout, down_weight, combine_high, combine_low, total, out_count)

    total = add({(0, 0): own_hidden, (1, 0): near}, None)[0]
    last = {}
    for k in far:
        far[k][-1] = after(far[k][-1], total)
        last[1, k] = [swapped(hidden, "tp", 1) for hidden in far[k]]
        total = add({(0, k): far[k]}, total)[0]
    totals = add(last, total, ctx_count)
    order = far_first(ctx_count)
    order = order[:1] + order[:0:-1]
    returned = [totals[0]] + [swapped(totals[k], "ctx", k) for k in order]
    return finish(mixed, returned)


def solution(mesh):
    in_specs = (
        P(("group", "ctx"), "tp", "exp"),
        P(("group", "ctx"), "tp", None),
        P(("group", "ctx"), "tp", None),
        P(("group", "ctx")),
        P(("group", "ctx")),
        P("group"),
        P("tp", "exp", None),
        P(("group", "ctx"), ("exp", "tp")),
        P(("exp", "tp")),
        P("ctx", ("exp", "tp"), None),
        P("ctx", None, ("exp", "tp")),
        P(("group", "ctx"), None),
        P(("group", "ctx"), None),
    )
    out_specs = P(("group", "ctx"), ("exp", "tp"))
    return jax.shard_map(body, mesh=mesh, in_specs=in_specs, out_specs=out_specs, check_vma=False)
```
